32 devices in a mesh: ens: 2 (over x), space: 4 (over y, core), bin: 4 (over z).
Axes of the slice: x: 2, y: 2, z: 4, core: 2. Of those that a mesh axis runs over, the one named last changes fastest.
Arguments:
- spectrum: float32 [1296, 32768], P('bin', ('ens', 'space')), parts along dimension 1, may hold values from 0.05 to 1
- wind: float32 [2, 32768], P(None, ('ens', 'space')), parts along dimension 1, may hold values from -6 to 6
- sea_mask: int32 [16384], P('space'), may hold values 0 or 1
- neighbours: int32 [4, 16384], P(None, 'space'), may hold values from -4096 to 20479, as said below
- metric_x: float32 [16384], P('space'), may hold values from 0.05 to 0.3
- metric_y: float32 [16384], P('space'), may hold values from 0.05 to 0.3
- refraction: float32 [16384], P('space'), may hold values from -0.15 to 0.15
- freq_shift: float32 [16384], P('space'), may hold values from -0.15 to 0.15
- dia_bins: int32 [4, 1296], replicated, may hold values from 0 to 1295
- dia_wts: float32 [2, 1296], replicated, may hold values from 0 to 1
Outputs:
- spectrum_next: float32 [1296, 32768], P(None, ('ens', 'space', 'bin')), parts along dimension 1
The draws below stay inside these ranges and needn't reach their ends.
There are 2 independent parts, one for each index of `ens`. The reference program is written for one: setup_inputs(seed, part) draws one part's arguments, and reference() takes and returns one part's arrays. A program takes and returns all parts, laid end to end along the dimension named above; an argument that names none is the same for every part. Nothing has to cross between parts.
Inputs may be any that keep to these rules, and one draw needn't show every extreme that they name: `neighbours`: row 0 is p + 1 to p + 3 and row 1 is p - 3 to p - 1 for point p; row 2 is p + k and row 3 is p - k with k from 2048 to 4096. Indices outside 0 to 16383 mean open boundary.
All inputs are finite; a program needn't handle non-finite values. No bound on the sum of `sea_mask` on one device may be relied on, other than what follows from the above.
Results may differ from the reference program's by a relative error of at most 0.0003.
Values sent between devices are 32-bit elements; how exact they have to be, the bound alone decides.
No kernel may reach another device: no remote copies, remote signals or barrier semaphores. Data moves between devices by JAX's collectives and lax.ppermute only.
A program may use at most 192 MiB of HBM per device.

```python
import math
import jax
import jax.numpy as jnp
from jax import lax

NF = 36
ND = 36
NBINS = 1296
PTS_DEV = 4096
POINTS = 16384


def draw_neighbours(key, part):
    key = jax.random.fold_in(key, 11)
    key_e, key_w, key_n, key_s = jax.random.split(key, 4)
    places = jnp.arange(POINTS, dtype=jnp.int32)
    east = places + jax.random.randint(key_e, (POINTS,), 1, 4)
    west = places - jax.random.randint(key_w, (POINTS,), 1, 4)
    north = places + jax.random.randint(key_n, (POINTS,), PTS_DEV // 2, PTS_DEV + 1)
    south = places - jax.random.randint(key_s, (POINTS,), PTS_DEV // 2, PTS_DEV + 1)
    north = north.at[POINTS - 1].set(POINTS - 1 + PTS_DEV)
    south = south.at[0].set(0 - PTS_DEV)
    return jnp.stack([east, west, north, south]).astype(jnp.int32)


def with_ends(result, rng, low, top_value):
    extent = result.shape
    index_at = [jax.random.randint(jax.random.fold_in(rng, axis), (), 0, extent[axis]) for axis in range(len(extent))]
    result = result.at[tuple(index_at)].set(low)
    longest = extent.index(max(extent))
    index_at[longest] = (index_at[longest] + 1) % extent[longest]
    return result.at[tuple(index_at)].set(top_value)


def shard_levels(own_key, dims, shards, smallest, top_value):
    def one(position, blocks):
        steps = jax.random.uniform(jax.random.fold_in(jax.random.fold_in(own_key, 6), position), (blocks,), jnp.float32, smallest / len(shards), top_value / len(shards))
        return jnp.repeat(jnp.exp(steps), dims[position] // blocks).reshape((-1,) + (1,) * (len(dims) - position - 1))

    gain = one(*shards[0])
    for cut in shards[1:]:
        gain = gain * one(*cut)
    return gain


def normal_values(own_key, shape, scale, reach, cuts=(), kind=jnp.bfloat16):
    level = shard_levels(own_key, shape, cuts, -0.22, 0.18) if cuts else 1.0
    array = jax.random.normal(own_key, shape, jnp.float32) * scale * level
    return jnp.minimum(jnp.maximum(array, -reach), reach).astype(kind)


def setup_inputs(seed: int = 0, part: int = 0) -> dict:
    streams_of = jax.random.split(jax.random.key(seed), 11)
    part_splits = jax.random.split(jax.random.fold_in(streams_of[10], part), 11)
    return {
        "spectrum": jnp.clip(jnp.exp(math.log(1.0) - 2.9957323 * jax.random.uniform(part_splits[0], (NBINS, POINTS), jnp.float32) ** shard_levels(part_splits[0], (NBINS, POINTS), ((0, 4), (1, 4)), -0.2, 0.2)), 0.05, 1.0),
        "wind": normal_values(part_splits[1], (2, POINTS), 1.5, 6.0, ((1, 4),), jnp.float32),
        "sea_mask": with_ends((jax.random.randint(streams_of[2], (POINTS,), 0, 4) < 3).astype(jnp.int32), jax.random.fold_in(streams_of[2], 1), 0, 1),
        "neighbours": draw_neighbours(jax.random.fold_in(streams_of[10], 71), part),
        "metric_x": jnp.clip(0.05 + 0.25 * jax.random.uniform(streams_of[4], (POINTS,), jnp.float32) ** shard_levels(streams_of[4], (POINTS,), ((0, 4),), -0.2, 0.2), 0.05, 0.3),
        "metric_y": jnp.clip(0.05 + 0.25 * jax.random.uniform(streams_of[5], (POINTS,), jnp.float32) ** shard_levels(streams_of[5], (POINTS,), ((0, 4),), -0.2, 0.2), 0.05, 0.3),
        "refraction": jnp.clip(jax.random.uniform(streams_of[6], (POINTS,), jnp.float32, -0.15, 0.15) * shard_levels(streams_of[6], (POINTS,), ((0, 4),), -0.4, 0.0), -0.15, 0.15),
        "freq_shift": jnp.clip(jax.random.uniform(streams_of[7], (POINTS,), jnp.float32, -0.15, 0.15) * shard_levels(streams_of[7], (POINTS,), ((0, 4),), -0.4, 0.0), -0.15, 0.15),
        "dia_bins": with_ends(jax.random.randint(streams_of[8], (4, NBINS), 0, NBINS), jax.random.fold_in(streams_of[8], 1), 0, NBINS - 1).astype(jnp.int32),
        "dia_wts": jnp.clip(jax.random.uniform(streams_of[9], (2, NBINS), jnp.float32, 0.0, 1.0), 0.0, 1.0),
    }


def bin_tables(index, nfreq, ndir):
    freq = (index // ndir).astype(jnp.float32)
    direc = index % ndir
    fratio = jnp.exp(jnp.log(1.1) * (freq - (nfreq - 1)))
    speed = jnp.exp(-jnp.log(1.1) * freq)
    theta = 2.0 * jnp.pi * (direc.astype(jnp.float32) + 0.5) / ndir
    return fratio, speed, jnp.cos(theta), jnp.sin(theta), direc == 0, direc == ndir - 1


def spatial_term(wet, padded, local, metric_x, metric_y, speed, cosv, sinv):
    east = jnp.take(padded, local[0], axis=1)
    west = jnp.take(padded, local[1], axis=1)
    north = jnp.take(padded, local[2], axis=1)
    south = jnp.take(padded, local[3], axis=1)
    along_x = metric_x[None, :] * (speed * cosv)[:, None]
    along_y = metric_y[None, :] * (speed * sinv)[:, None]
    flux_x = jnp.abs(along_x) * (wet - jnp.where(along_x > 0, west, east))
    flux_y = jnp.abs(along_y) * (wet - jnp.where(along_y > 0, south, north))
    return flux_x + flux_y


def spectral_term(wet, padded, ndir, first, last, refraction, freq_shift, speed, cosv):
    rows = wet.shape[0]

    def moved_rows(offset):
        return lax.slice_in_dim(padded, ndir + offset, ndir + offset + rows, axis=0)

    prev_dir = jnp.where(first[:, None], moved_rows(ndir - 1), moved_rows(-1))
    next_dir = jnp.where(last[:, None], moved_rows(1 - ndir), moved_rows(1))
    lower = moved_rows(-ndir)
    upper = moved_rows(ndir)
    turning = refraction[None, :] * cosv[:, None]
    shifting = freq_shift[None, :] * speed[:, None]
    flux_t = jnp.abs(turning) * (wet - jnp.where(turning > 0, prev_dir, next_dir))
    flux_s = jnp.abs(shifting) * (wet - jnp.where(shifting > 0, lower, upper))
    return flux_t + flux_s


def source_step(moved, wind, maskf, fratio, speed, cosv, sinv, plus_fwd, minus_fwd, plus_back, minus_back):
    steep = jnp.mean(moved * (fratio * fratio)[:, None], axis=0)
    drive = jnp.maximum(0.0, wind[0][None, :] * cosv[:, None] + wind[1][None, :] * sinv[:, None] - 0.5 * speed[:, None])
    s_in = 0.3 * drive * drive * moved
    s_ds = -6.0 * fratio[:, None] * steep[None, :] * moved
    e_plus = plus_fwd(moved)
    e_minus = minus_fwd(moved)
    delta = 8.0 * (fratio ** 4)[:, None] * (moved * moved * (e_plus / 1.25 ** 4 + e_minus / 0.75 ** 4) - 2.0 * moved * e_plus * e_minus / 0.9375 ** 4)
    s_nl = -2.0 * delta + plus_back(delta) + minus_back(delta)
    return (moved + 0.5 * (s_in + s_ds + s_nl)) * maskf[None, :]


def lookup_pair(values, first_bins, second_bins, weight):
    return weight[:, None] * values[first_bins] + (1.0 - weight)[:, None] * values[second_bins]


def spread_pair(values, first_bins, second_bins, weight, count):
    return jax.ops.segment_sum(weight[:, None] * values, first_bins, count) + jax.ops.segment_sum((1.0 - weight)[:, None] * values, second_bins, count)


def reference(spectrum, wind, sea_mask, neighbours, metric_x, metric_y, refraction, freq_shift, dia_bins, dia_wts):
    maskf = sea_mask.astype(jnp.float32)
    wet = spectrum * maskf[None, :]
    index = jnp.arange(NBINS, dtype=jnp.int32)
    fratio, speed, cosv, sinv, first, last = bin_tables(index, NF, ND)
    padded = jnp.pad(wet, ((0, 0), (PTS_DEV, PTS_DEV)))
    local = (neighbours + PTS_DEV).astype(jnp.int32)
    spatial = spatial_term(wet, padded, local, metric_x, metric_y, speed, cosv, sinv)
    bin_pad = jnp.pad(wet, ((ND, ND), (0, 0)))
    spectral = spectral_term(wet, bin_pad, ND, first, last, refraction, freq_shift, speed, cosv)
    moved = wet - spatial - spectral
    return source_step(
        moved, wind, maskf, fratio, speed, cosv, sinv,
        lambda v: lookup_pair(v, dia_bins[0], dia_bins[1], dia_wts[0]),
        lambda v: lookup_pair(v, dia_bins[2], dia_bins[3], dia_wts[1]),
        lambda v: spread_pair(v, dia_bins[0], dia_bins[1], dia_wts[0], NBINS),
        lambda v: spread_pair(v, dia_bins[2], dia_bins[3], dia_wts[1], NBINS))
```

```python
import functools

import jax
import jax.numpy as jnp
import numpy as np
from jax import lax
from jax.experimental import pallas as pl
from jax.experimental.pallas import tpu as pltpu
from jax.sharding import PartitionSpec as P

ND = 36


def extended(array, sides, width):
    for axis, dim in sides:
        peers, length = (lax.axis_size(axis), array.shape[dim])
        up = [(i, (i + 1) % peers) for i in range(peers - 1)]
        down = [(j, i) for i, j in up]
        last = lax.slice_in_dim(array, length - width, length, axis=dim)
        initial = lax.slice_in_dim(array, 0, width, axis=dim)
        before = lax.ppermute(last, axis, up)
        after = lax.ppermute(initial, axis, down)
        array = jnp.concatenate([before, array, after], axis=dim)
    return array


def bin_tables(index, nfreq, ndir):
    freq = (index // ndir).astype(jnp.float32)
    direc = index % ndir
    fratio = jnp.exp(jnp.log(1.1) * (freq - (nfreq - 1)))
    speed = jnp.exp(-jnp.log(1.1) * freq)
    theta = 2.0 * jnp.pi * (direc.astype(jnp.float32) + 0.5) / ndir
    return (fratio, speed, jnp.cos(theta), jnp.sin(theta), direc == 0, direc == ndir - 1)


def spatial_term(wet, padded, local, metric_x, metric_y, speed, cosv, sinv):
    east = jnp.take(padded, local[0], axis=1)
    west = jnp.take(padded, local[1], axis=1)
    north = jnp.take(padded, local[2], axis=1)
    south = jnp.take(padded, local[3], axis=1)
    along_x = metric_x[None, :] * (speed * cosv)[:, None]
    along_y = metric_y[None, :] * (speed * sinv)[:, None]
    flux_x = jnp.abs(along_x) * (wet - jnp.where(along_x > 0, west, east))
    flux_y = jnp.abs(along_y) * (wet - jnp.where(along_y > 0, south, north))
    return flux_x + flux_y


def spectral_term(wet, padded, ndir, first, last, refraction, freq_shift, speed, cosv):
    rows = wet.shape[0]

    def moved_rows(offset):
        return lax.slice_in_dim(padded, ndir + offset, ndir + offset + rows, axis=0)

    prev_dir = jnp.where(first[:, None], moved_rows(ndir - 1), moved_rows(-1))
    next_dir = jnp.where(last[:, None], moved_rows(1 - ndir), moved_rows(1))
    lower = moved_rows(-ndir)
    upper = moved_rows(ndir)
    turning = refraction[None, :] * cosv[:, None]
    shifting = freq_shift[None, :] * speed[:, None]
    flux_t = jnp.abs(turning) * (wet - jnp.where(turning > 0, prev_dir, next_dir))
    flux_s = jnp.abs(shifting) * (wet - jnp.where(shifting > 0, lower, upper))
    return flux_t + flux_s


def source_step(
    moved, wind, maskf, fratio, speed, cosv, sinv, plus_fwd, minus_fwd, plus_back, minus_back
):
    steep = jnp.mean(moved * (fratio * fratio)[:, None], axis=0)
    drive = jnp.maximum(
        0.0,
        wind[0][None, :] * cosv[:, None] + wind[1][None, :] * sinv[:, None] - 0.5 * speed[:, None],
    )
    s_in = 0.3 * drive * drive * moved
    s_ds = -6.0 * fratio[:, None] * steep[None, :] * moved
    e_plus = plus_fwd(moved)
    e_minus = minus_fwd(moved)
    delta = (
        8.0
        * (fratio**4)[:, None]
        * (
            moved * moved * (e_plus / 1.25**4 + e_minus / 0.75**4)
            - 2.0 * moved * e_plus * e_minus / 0.9375**4
        )
    )
    s_nl = -2.0 * delta + plus_back(delta) + minus_back(delta)
    return (moved + 0.5 * (s_in + s_ds + s_nl)) * maskf[None, :]


def pair_matrix(first_bins, second_bins, weight, count):
    columns = jnp.arange(count, dtype=jnp.int32)[None, :]
    return weight[:, None] * (first_bins[:, None] == columns).astype(jnp.float32) + (1.0 - weight)[
        :, None
    ] * (second_bins[:, None] == columns).astype(jnp.float32)


def forward_product(matrix, values):
    return jnp.dot(
        matrix, values, precision=lax.Precision.HIGHEST, preferred_element_type=jnp.float32
    )


def backward_product(matrix, values):
    return lax.dot_general(
        matrix,
        values,
        (((0,), (0,)), ((), ())),
        precision=lax.Precision.HIGHEST,
        preferred_element_type=jnp.float32,
    )


def on_device(
    spectrum,
    wind,
    sea_mask,
    neighbours,
    metric_x,
    metric_y,
    refraction,
    freq_shift,
    dia_bins,
    dia_wts,
):
    bins_dev, points_dev = spectrum.shape
    nbins = dia_bins.shape[1]
    ndir = ND
    nfreq = nbins // ndir
    space_pos = lax.axis_index("space")
    bin_pos = lax.axis_index("bin")
    maskf = sea_mask.astype(jnp.float32)
    wet = spectrum * maskf[None, :]
    padded = extended(wet, (("space", 1),), points_dev)
    base = space_pos * points_dev - points_dev
    local = neighbours - base
    own_bins = bin_pos * bins_dev + jnp.arange(bins_dev, dtype=jnp.int32)
    fratio, speed, cosv, sinv, first, last = bin_tables(own_bins, nfreq, ndir)
    spatial = spatial_term(wet, padded, local, metric_x, metric_y, speed, cosv, sinv)
    share = points_dev // lax.axis_size("bin")
    start = bin_pos * share
    all_bins = jnp.arange(nbins, dtype=jnp.int32)
    fratio_all, speed_all, cos_all, sin_all, first_all, last_all = bin_tables(all_bins, nfreq, ndir)
    bin_pad = extended(wet, (("bin", 0),), ndir)
    spectral = spectral_term(wet, bin_pad, ndir, first, last, refraction, freq_shift, speed, cosv)
    moved_own = wet - spatial - spectral
    moved = lax.all_to_all(moved_own, "bin", split_axis=1, concat_axis=0, tiled=True)
    wind_part = lax.dynamic_slice_in_dim(wind, start, share, 1)
    mask_part = lax.dynamic_slice_in_dim(maskf, start, share, 0)
    plus_matrix = pair_matrix(dia_bins[0], dia_bins[1], dia_wts[0], nbins)
    minus_matrix = pair_matrix(dia_bins[2], dia_bins[3], dia_wts[1], nbins)
    result = source_step(
        moved,
        wind_part,
        mask_part,
        fratio_all,
        speed_all,
        cos_all,
        sin_all,
        lambda v: forward_product(plus_matrix, v),
        lambda v: forward_product(minus_matrix, v),
        lambda v: backward_product(plus_matrix, v),
        lambda v: backward_product(minus_matrix, v),
    )
    return result


LANES = 128
ROWS = 8
EDGE = 16
QUART = ND // 4
PIECES = 3


def chunk_plan(nloc):
    mid = nloc // 2
    plan = [(mid, mid + 1)]
    if mid > 1:
        plan.append((1, mid))
    if mid + 1 < nloc - 1:
        plan.append((mid + 1, nloc - 1))
    plan += [(0, 1), (nloc - 1, nloc)]
    return plan


def prep_kernel(nloc, points, plan, spec_hbm, mask_ref, *refs):
    nch = len(plan)
    wet_hbm, low_hbm, high_hbm = refs[0:3]
    hs_hbm = refs[3 : 3 + nch]
    hn_hbm = refs[3 + nch : 3 + 2 * nch]
    spec_v, wet_v, edge_v, in_sem, out_sem = refs[3 + 2 * nch :]
    tiles = points // LANES
    half = ND // 2
    where = {}
    for c, (lo, hi) in enumerate(plan):
        for f in range(lo, hi):
            where[f] = (c, f - lo)
    blocks = [(f, min(f + 2, nloc)) for f in range(0, nloc, 2)]
    first = plan[0][0] // 2
    order = [first] + [b for b in range(len(blocks)) if b != first]
    loads = {}
    for b in order:
        lo, hi = blocks[b]
        rows = pl.ds(lo * ND, (hi - lo) * ND)
        loads[b] = pltpu.make_async_copy(spec_hbm.at[rows], spec_v.at[rows], in_sem.at[b])
        loads[b].start()
    masks = [mask_ref[:, c * LANES : (c + 1) * LANES].astype(jnp.float32) for c in range(tiles)]
    copies = []

    def send(src, dst):
        copy = pltpu.make_async_copy(src, dst, out_sem.at[len(copies)])
        copy.start()
        copies.append(copy)

    for b in order:
        lo, hi = blocks[b]
        loads[b].wait()
        start, rows = lo * ND, (hi - lo) * ND

        def relayout(t, _):
            g0 = pl.multiple_of(start + t * ROWS, ROWS)
            for c in range(tiles):
                tile = spec_v[pl.ds(g0, ROWS), c * LANES : (c + 1) * LANES]
                wet_v[pl.ds(g0 * tiles + c, ROWS, stride=tiles), :] = tile * masks[c]
            return 0

        lax.fori_loop(0, rows // ROWS, relayout, 0)
        rest = rows % ROWS
        if rest:
            g0 = start + rows - rest
            for c in range(tiles):
                tile = spec_v[pl.ds(g0, rest), c * LANES : (c + 1) * LANES]
                wet_v[pl.ds(g0 * tiles + c, rest, stride=tiles), :] = tile * masks[c]
        for f in range(lo, hi):
            c, k = where[f]
            base = f * ND * tiles
            for side, (j0, row) in enumerate(((3 * QUART, tiles - 1), (QUART, 0))):
                at = base + j0 * tiles + row
                edge_v[f, side, ROWS:EDGE, :] = jnp.zeros((EDGE - ROWS, LANES), jnp.float32)
                edge_v[f, side, 0:ROWS, :] = wet_v[pl.ds(at, ROWS, stride=tiles), :]
                edge_v[f, side, ROWS : ROWS + 1, :] = wet_v[pl.ds(at + ROWS * tiles, 1), :]
            send(wet_v.at[pl.ds(base, half * tiles)], hs_hbm[c].at[k, pl.ds(0, half * tiles)])
            send(wet_v.at[pl.ds(base + half * tiles, half * tiles)], hn_hbm[c].at[k, pl.ds(0, half * tiles)])
            send(edge_v.at[f, 0], hs_hbm[c].at[k, pl.ds(half * tiles, EDGE)])
            send(edge_v.at[f, 1], hn_hbm[c].at[k, pl.ds(half * tiles, EDGE)])
            if f == nloc - 1:
                send(wet_v.at[pl.ds(base, ND * tiles)], low_hbm)
            if f == 0:
                send(wet_v.at[pl.ds(base, ND * tiles)], high_hbm)
        span = pl.ds(start * tiles, rows * tiles)
        send(wet_v.at[span], wet_hbm.at[span])
    for copy in copies:
        copy.wait()


def prep(spectrum, mask, plan):
    bins, points = spectrum.shape
    nloc = bins // ND
    tiles = points // LANES
    halo_rows = ND // 2 * tiles + EDGE
    halos = [jax.ShapeDtypeStruct((hi - lo, halo_rows, LANES), jnp.float32) for lo, hi in plan]
    one = jax.ShapeDtypeStruct((ND * tiles, LANES), jnp.float32)
    outs = [jax.ShapeDtypeStruct((bins * tiles, LANES), jnp.float32), one, one] + halos + halos
    nblocks = -(-nloc // 2)
    anywhere = pl.BlockSpec(memory_space=pl.ANY)
    res = pl.pallas_call(
        functools.partial(prep_kernel, nloc, points, plan),
        out_shape=outs,
        in_specs=[anywhere, pl.BlockSpec(memory_space=pltpu.VMEM)],
        out_specs=[anywhere] * len(outs),
        scratch_shapes=[
            pltpu.VMEM((bins, points), jnp.float32),
            pltpu.VMEM((bins * tiles, LANES), jnp.float32),
            pltpu.VMEM((nloc, 2, EDGE, LANES), jnp.float32),
            pltpu.SemaphoreType.DMA((nblocks,)),
            pltpu.SemaphoreType.DMA((4 * nloc + 2 + nblocks,)),
        ],
        compiler_params=pltpu.CompilerParams(vmem_limit_bytes=40 << 20),
        cost_estimate=pl.CostEstimate(flops=bins * points, bytes_accessed=bins * points * 12, transcendentals=0),
        name="prep",
    )(spectrum, mask)
    nch = len(plan)
    return res[0], res[1], res[2], res[3 : 3 + nch], res[3 + nch : 3 + 2 * nch]


def front_kernel(
    shares, tiles, kmin, kmax, tab_ref, dir_ref, nbr_ref, par_ref, wet_ref, low_ref, high_ref, hs_ref, hn_ref, out_ref, ext_ref
):
    speed = tab_ref[pl.program_id(0)]
    half = ND // 2
    span = half * tiles
    south, north = tiles, ROWS
    ext_ref[0:half, 0:tiles, :] = hs_ref[0, 0:span, :].reshape(half, tiles, LANES)
    ext_ref[0:half, south : south + tiles, :] = wet_ref[0, 0:half]
    ext_ref[half:ND, north : north + tiles, :] = wet_ref[0, half:ND]
    ext_ref[half:ND, north + tiles : north + 2 * tiles, :] = hn_ref[0, 0:span, :].reshape(half, tiles, LANES)
    for q in range(QUART):
        ext_ref[QUART + q, south + tiles : south + tiles + 1, :] = hn_ref[0, span + q : span + q + 1, :]
        ext_ref[3 * QUART + q, north - 1 : north, :] = hs_ref[0, span + q : span + q + 1, :]

    nblk = tiles // ROWS
    sub = lax.broadcasted_iota(jnp.int32, (ROWS, LANES), 0)
    lanes, rels = {}, {}
    for d in range(4):
        for b in range(nblk):
            src = nbr_ref[d, b * ROWS : (b + 1) * ROWS, :]
            lanes[d, b] = src & (LANES - 1)
            rels[d, b] = (src >> 7) - (sub + b * ROWS)

    def picked(j, own, b, d, offsets):
        out = None
        for r in offsets:
            window = ext_ref[j, own + b * ROWS + r : own + b * ROWS + r + ROWS, :]
            got = jnp.take_along_axis(window, lanes[d, b], axis=1, mode="promise_in_bounds")
            out = got if out is None else jnp.where(rels[d, b] == r, got, out)
        return out

    per_share = nblk // shares
    for quad in range(4):
        cos_up = quad in (0, 3)
        own, dy, off_y = (
            (south, 3, range(-(kmax // LANES), -(kmin // LANES) + 1))
            if quad < 2
            else (north, 2, range(kmin // LANES, kmax // LANES + 1))
        )
        dx, off_x = (1, (-1, 0)) if cos_up else (0, (0, 1))

        def body(q, _):
            j = quad * QUART + q
            jprev = jnp.where(j == 0, ND - 1, j - 1)
            jnext = jnp.where(j == ND - 1, 0, j + 1)
            acos = jnp.abs(dir_ref[0, j])
            asin = jnp.abs(dir_ref[1, j])
            ax, ay = speed * acos, speed * asin
            for b in range(nblk):
                at = slice(b * ROWS, (b + 1) * ROWS)
                wet = wet_ref[0, j, at, :]
                e_y = picked(j, own, b, dy, off_y)
                e_x = picked(j, own, b, dx, off_x)
                rf, fs = par_ref[2, at, :], par_ref[3, at, :]
                e_prev, e_next = wet_ref[0, jprev, at, :], wet_ref[0, jnext, at, :]
                e_t = jnp.where(rf > 0, e_prev, e_next) if cos_up else jnp.where(rf < 0, e_prev, e_next)
                e_s = jnp.where(fs > 0, low_ref[0, j, at, :], high_ref[0, j, at, :])
                spatial = (par_ref[0, at, :] * ax) * (wet - e_x) + (par_ref[1, at, :] * ay) * (wet - e_y)
                spectral = (jnp.abs(rf) * acos) * (wet - e_t) + (jnp.abs(fs) * speed) * (wet - e_s)
                out_ref[b // per_share, j, (b % per_share) * ROWS : (b % per_share + 1) * ROWS, :] = (
                    wet - spatial - spectral
                )
            return 0

        lax.fori_loop(0, QUART, body, 0)


def front(speed, dirs, nbr, par, wet, low, high, hs, hn, count, shares, kmin, kmax):
    tiles = nbr.shape[1]
    vm = pltpu.VMEM

    def freq_spec(first):
        return pl.BlockSpec((1, ND, tiles, LANES), lambda i: (first + i, 0, 0, 0))

    def whole(shape):
        return pl.BlockSpec(shape, lambda i: (0,) * len(shape))

    halo_spec = pl.BlockSpec((1,) + hs.shape[1:], lambda i: (i, 0, 0))
    rows = tiles // shares
    elems = count * ND * tiles * LANES
    return pl.pallas_call(
        functools.partial(front_kernel, shares, tiles, kmin, kmax),
        grid=(count,),
        out_shape=jax.ShapeDtypeStruct((shares, count * ND, rows, LANES), jnp.float32),
        in_specs=[
            pl.BlockSpec(memory_space=pltpu.SMEM),
            pl.BlockSpec(memory_space=pltpu.SMEM),
            whole(nbr.shape),
            whole(par.shape),
            freq_spec(wet[1]),
            freq_spec(low[1]),
            freq_spec(high[1]),
            halo_spec,
            halo_spec,
        ],
        out_specs=pl.BlockSpec((shares, ND, rows, LANES), lambda i: (0, i, 0, 0)),
        scratch_shapes=[vm((ND, 2 * tiles + ROWS, LANES), jnp.float32)],
        compiler_params=pltpu.CompilerParams(vmem_limit_bytes=32 << 20),
        cost_estimate=pl.CostEstimate(flops=elems * 150, bytes_accessed=elems * 24, transcendentals=0),
        name="front",
    )(speed, dirs, nbr, par, wet[0], low[0], high[0], hs, hn)


def tail_kernel(nfreq, bins_dev, plan, bins_ref, wts_ref, ftab_ref, dir_ref, wind_ref, mask_ref, *refs):
    nch = len(plan)
    parts = refs[:nch]
    out_hbm = refs[nch]
    mv, base, a0, a1, a2, a3, dw, out_v, in_sem, out_sem = refs[nch + 1 :]
    shares = parts[0].shape[0]
    nbins = nfreq * ND
    loads = []
    for c, (lo, hi) in enumerate(plan):
        for s in range(shares):
            rows = pl.ds(s * bins_dev + lo * ND, (hi - lo) * ND)
            copy = pltpu.make_async_copy(parts[c].at[s], mv.at[rows], in_sem.at[len(loads)])
            copy.start()
            loads.append(copy)
    zero = jnp.zeros((ROWS, LANES), jnp.float32)

    def clear(g, _):
        for acc in (a0, a1, a2, a3):
            acc[g] = zero
        return 0

    lax.fori_loop(0, nbins, clear, 0, unroll=8)
    for j in range(ND):
        dw[j] = wind_ref[0] * dir_ref[0, j] + wind_ref[1] * dir_ref[1, j]
    for copy in loads:
        copy.wait()

    def per_freq(f, steep):
        fr2, fr4, hspeed = ftab_ref[0, f], ftab_ref[1, f], ftab_ref[3, f]

        def per_dir(j, total):
            g = f * ND + j
            b0, b1, b2, b3 = (bins_ref[k, g] for k in range(4))
            wp, wm = wts_ref[0, g], wts_ref[1, g]
            vp, vm = 1.0 - wp, 1.0 - wm
            m = mv[g]
            ep = wp * mv[b0] + vp * mv[b1]
            em = wm * mv[b2] + vm * mv[b3]
            half = fr4 * (m * m * (ep * (1 / 1.25**4) + em * (1 / 0.75**4)) - m * ep * em * (2.0 / 0.9375**4))
            drive = jnp.maximum(0.0, dw[j] - hspeed)
            base[g] = m + 0.15 * (drive * drive) * m - 2.0 * half
            a0[b0] += wp * half
            a1[b1] += vp * half
            a2[b2] += wm * half
            a3[b3] += vm * half
            return total + m

        part = lax.fori_loop(0, ND, per_dir, zero, unroll=4)
        return steep + part * fr2

    steep = lax.fori_loop(0, nfreq, per_freq, zero) * (1.0 / nbins)
    mask = mask_ref[...].astype(jnp.float32)

    def finish_freq(f, _):
        fr = ftab_ref[2, f] * steep

        def finish(j, _):
            g = f * ND + j
            total = base[g] - fr * mv[g] + ((a0[g] + a1[g]) + (a2[g] + a3[g]))
            base[g] = total * mask
            return 0

        return lax.fori_loop(0, ND, finish, 0, unroll=4)

    flat = base.reshape(nbins * ROWS, LANES)
    per = nfreq // PIECES
    copies = []
    for p in range(PIECES):
        lax.fori_loop(p * per, (p + 1) * per, finish_freq, 0)

        def place(t, _):
            g0 = pl.multiple_of((p * per * ND) + t * ROWS, ROWS)
            for c in range(ROWS):
                out_v[pl.ds(g0, ROWS), c * LANES : (c + 1) * LANES] = flat[pl.ds(g0 * ROWS + c, ROWS, stride=ROWS), :]
            return 0

        first, last = p * per * ND, (p + 1) * per * ND
        lax.fori_loop(0, (last - first) // ROWS, place, 0)
        rows = pl.ds(first, last - first)
        copy = pltpu.make_async_copy(out_v.at[rows], out_hbm.at[rows], out_sem.at[p])
        copy.start()
        copies.append(copy)
    for copy in copies:
        copy.wait()


def tail(parts, plan, bins_dev, dia_bins, dia_wts, ftab, dirs, wind, mask):
    nbins = dia_bins.shape[1]
    nfreq = nbins // ND
    anywhere = pl.BlockSpec(memory_space=pl.ANY)
    smem = pl.BlockSpec(memory_space=pltpu.SMEM)
    vmem = pl.BlockSpec(memory_space=pltpu.VMEM)
    shares = parts[0].shape[0]
    points = ROWS * LANES
    field = pltpu.VMEM((nbins, ROWS, LANES), jnp.float32)
    return pl.pallas_call(
        functools.partial(tail_kernel, nfreq, bins_dev, plan),
        out_shape=jax.ShapeDtypeStruct((nbins, points), jnp.float32),
        in_specs=[smem] * 4 + [vmem] * 2 + [anywhere] * len(parts),
        out_specs=anywhere,
        scratch_shapes=[field] * 6
        + [
            pltpu.VMEM((ND, ROWS, LANES), jnp.float32),
            pltpu.VMEM((nbins, points), jnp.float32),
            pltpu.SemaphoreType.DMA((len(parts) * shares,)),
            pltpu.SemaphoreType.DMA((PIECES,)),
        ],
        compiler_params=pltpu.CompilerParams(vmem_limit_bytes=56 << 20),
        cost_estimate=pl.CostEstimate(flops=nbins * points * 60, bytes_accessed=nbins * points * 8, transcendentals=0),
        name="tail",
    )(dia_bins, dia_wts, ftab, dirs, wind, mask, *parts)


def fast_on_device(
    spectrum, wind, sea_mask, neighbours, metric_x, metric_y, refraction, freq_shift, dia_bins, dia_wts
):
    bins_dev, points = spectrum.shape
    nbins = dia_bins.shape[1]
    nfreq = nbins // ND
    nloc = bins_dev // ND
    tiles = points // LANES
    shares = lax.axis_size("bin")
    share = points // shares
    bin_pos = lax.axis_index("bin")
    space_pos = lax.axis_index("space")
    plan = chunk_plan(nloc)

    freqs = np.arange(nfreq, dtype=np.float32)
    speed = jnp.asarray(np.exp(-np.log(1.1) * freqs.astype(np.float64)).astype(np.float32))
    ratio = np.exp(np.log(1.1) * (freqs.astype(np.float64) - (nfreq - 1)))
    ftab = jnp.asarray(
        np.stack([ratio**2, 4.0 * ratio**4, 3.0 * ratio, 0.5 * np.exp(-np.log(1.1) * freqs)]).astype(np.float32)
    )
    theta = 2.0 * np.pi * (np.arange(ND) + 0.5) / ND
    dirs = jnp.asarray(np.stack([np.cos(theta), np.sin(theta)]).astype(np.float32))
    speed_own = lax.dynamic_slice_in_dim(speed, bin_pos * nloc, nloc, 0)

    wet, low_out, high_out, hs, hn = prep(spectrum, sea_mask.reshape(1, points), plan)
    wet = wet.reshape(nloc, ND, tiles, LANES)

    def shift(array, axis, step):
        peers = lax.axis_size(axis)
        pairs = [(i, i + 1) for i in range(peers - 1)]
        if step < 0:
            pairs = [(b, a) for a, b in pairs]
        return lax.ppermute(array, axis, pairs)

    hs = [shift(a, "space", 1) for a in hs]
    hn = [shift(a, "space", -1) for a in hn]
    low_in = shift(low_out, "bin", 1).reshape(1, ND, tiles, LANES)
    high_in = shift(high_out, "bin", -1).reshape(1, ND, tiles, LANES)

    nbr = (neighbours - space_pos * points).reshape(4, tiles, LANES)
    par = jnp.stack([metric_x, metric_y, refraction, freq_shift]).reshape(4, tiles, LANES)
    kmin, kmax = points // 2, points
    parts = []
    for c, (lo, hi) in enumerate(plan):
        low = (low_in, 0) if lo == 0 else (wet, lo - 1)
        high = (high_in, 0) if hi == nloc else (wet, lo + 1)
        moved = front(
            speed_own[lo:hi], dirs, nbr, par, (wet, lo), low, high, hs[c], hn[c], hi - lo, shares, kmin, kmax
        )
        parts.append(lax.all_to_all(moved, "bin", split_axis=0, concat_axis=0, tiled=True))
    wind_part = lax.dynamic_slice_in_dim(wind, bin_pos * share, share, 1).reshape(2, ROWS, LANES)
    mask_part = lax.dynamic_slice_in_dim(sea_mask, bin_pos * share, share, 0).reshape(ROWS, LANES)
    return tail(parts, plan, bins_dev, dia_bins, dia_wts, ftab, dirs, wind_part, mask_part)


def pick_path(spectrum, *others):
    bins_dev, points = spectrum.shape
    fits = bins_dev % ND == 0 and bins_dev // ND >= 3 and points // lax.axis_size("bin") == ROWS * LANES
    return (fast_on_device if fits else on_device)(spectrum, *others)


def solution(mesh):
    return jax.shard_map(
        pick_path,
        mesh=mesh,
        in_specs=(
            P("bin", ("ens", "space")),
            P(None, ("ens", "space")),
            P("space"),
            P(None, "space"),
            P("space"),
            P("space"),
            P("space"),
            P("space"),
            P(),
            P(),
        ),
        out_specs=P(None, ("ens", "space", "bin")),
        check_vma=False,
    )
```

```python
import functools

import jax
import jax.numpy as jnp
import numpy as np
from jax import lax
from jax.experimental import pallas as pl
from jax.experimental.pallas import tpu as pltpu
from jax.sharding import PartitionSpec as P

ND = 36


def extended(array, sides, width):
    for axis, dim in sides:
        peers, length = (lax.axis_size(axis), array.shape[dim])
        up = [(i, (i + 1) % peers) for i in range(peers - 1)]
        down = [(j, i) for i, j in up]
        last = lax.slice_in_dim(array, length - width, length, axis=dim)
        initial = lax.slice_in_dim(array, 0, width, axis=dim)
        before = lax.ppermute(last, axis, up)
        after = lax.ppermute(initial, axis, down)
        array = jnp.concatenate([before, array, after], axis=dim)
    return array


def bin_tables(index, nfreq, ndir):
    freq = (index // ndir).astype(jnp.float32)
    direc = index % ndir
    fratio = jnp.exp(jnp.log(1.1) * (freq - (nfreq - 1)))
    speed = jnp.exp(-jnp.log(1.1) * freq)
    theta = 2.0 * jnp.pi * (direc.astype(jnp.float32) + 0.5) / ndir
    return (fratio, speed, jnp.cos(theta), jnp.sin(theta), direc == 0, direc == ndir - 1)


def spatial_term(wet, padded, local, metric_x, metric_y, speed, cosv, sinv):
    east = jnp.take(padded, local[0], axis=1)
    west = jnp.take(padded, local[1], axis=1)
    north = jnp.take(padded, local[2], axis=1)
    south = jnp.take(padded, local[3], axis=1)
    along_x = metric_x[None, :] * (speed * cosv)[:, None]
    along_y = metric_y[None, :] * (speed * sinv)[:, None]
    flux_x = jnp.abs(along_x) * (wet - jnp.where(along_x > 0, west, east))
    flux_y = jnp.abs(along_y) * (wet - jnp.where(along_y > 0, south, north))
    return flux_x + flux_y


def spectral_term(wet, padded, ndir, first, last, refraction, freq_shift, speed, cosv):
    rows = wet.shape[0]

    def moved_rows(offset):
        return lax.slice_in_dim(padded, ndir + offset, ndir + offset + rows, axis=0)

    prev_dir = jnp.where(first[:, None], moved_rows(ndir - 1), moved_rows(-1))
    next_dir = jnp.where(last[:, None], moved_rows(1 - ndir), moved_rows(1))
    lower = moved_rows(-ndir)
    upper = moved_rows(ndir)
    turning = refraction[None, :] * cosv[:, None]
    shifting = freq_shift[None, :] * speed[:, None]
    flux_t = jnp.abs(turning) * (wet - jnp.where(turning > 0, prev_dir, next_dir))
    flux_s = jnp.abs(shifting) * (wet - jnp.where(shifting > 0, lower, upper))
    return flux_t + flux_s


def source_step(
    moved, wind, maskf, fratio, speed, cosv, sinv, plus_fwd, minus_fwd, plus_back, minus_back
):
    steep = jnp.mean(moved * (fratio * fratio)[:, None], axis=0)
    drive = jnp.maximum(
        0.0,
        wind[0][None, :] * cosv[:, None] + wind[1][None, :] * sinv[:, None] - 0.5 * speed[:, None],
    )
    s_in = 0.3 * drive * drive * moved
    s_ds = -6.0 * fratio[:, None] * steep[None, :] * moved
    e_plus = plus_fwd(moved)
    e_minus = minus_fwd(moved)
    delta = (
        8.0
        * (fratio**4)[:, None]
        * (
            moved * moved * (e_plus / 1.25**4 + e_minus / 0.75**4)
            - 2.0 * moved * e_plus * e_minus / 0.9375**4
        )
    )
    s_nl = -2.0 * delta + plus_back(delta) + minus_back(delta)
    return (moved + 0.5 * (s_in + s_ds + s_nl)) * maskf[None, :]


def pair_matrix(first_bins, second_bins, weight, count):
    columns = jnp.arange(count, dtype=jnp.int32)[None, :]
    return weight[:, None] * (first_bins[:, None] == columns).astype(jnp.float32) + (1.0 - weight)[
        :, None
    ] * (second_bins[:, None] == columns).astype(jnp.float32)


def forward_product(matrix, values):
    return jnp.dot(
        matrix, values, precision=lax.Precision.HIGHEST, preferred_element_type=jnp.float32
    )


def backward_product(matrix, values):
    return lax.dot_general(
        matrix,
        values,
        (((0,), (0,)), ((), ())),
        precision=lax.Precision.HIGHEST,
        preferred_element_type=jnp.float32,
    )


def on_device(
    spectrum,
    wind,
    sea_mask,
    neighbours,
    metric_x,
    metric_y,
    refraction,
    freq_shift,
    dia_bins,
    dia_wts,
):
    bins_dev, points_dev = spectrum.shape
    nbins = dia_bins.shape[1]
    ndir = ND
    nfreq = nbins // ndir
    space_pos = lax.axis_index("space")
    bin_pos = lax.axis_index("bin")
    maskf = sea_mask.astype(jnp.float32)
    wet = spectrum * maskf[None, :]
    padded = extended(wet, (("space", 1),), points_dev)
    base = space_pos * points_dev - points_dev
    local = neighbours - base
    own_bins = bin_pos * bins_dev + jnp.arange(bins_dev, dtype=jnp.int32)
    fratio, speed, cosv, sinv, first, last = bin_tables(own_bins, nfreq, ndir)
    spatial = spatial_term(wet, padded, local, metric_x, metric_y, speed, cosv, sinv)
    share = points_dev // lax.axis_size("bin")
    start = bin_pos * share
    all_bins = jnp.arange(nbins, dtype=jnp.int32)
    fratio_all, speed_all, cos_all, sin_all, first_all, last_all = bin_tables(all_bins, nfreq, ndir)
    bin_pad = extended(wet, (("bin", 0),), ndir)
    spectral = spectral_term(wet, bin_pad, ndir, first, last, refraction, freq_shift, speed, cosv)
    moved_own = wet - spatial - spectral
    moved = lax.all_to_all(moved_own, "bin", split_axis=1, concat_axis=0, tiled=True)
    wind_part = lax.dynamic_slice_in_dim(wind, start, share, 1)
    mask_part = lax.dynamic_slice_in_dim(maskf, start, share, 0)
    plus_matrix = pair_matrix(dia_bins[0], dia_bins[1], dia_wts[0], nbins)
    minus_matrix = pair_matrix(dia_bins[2], dia_bins[3], dia_wts[1], nbins)
    result = source_step(
        moved,
        wind_part,
        mask_part,
        fratio_all,
        speed_all,
        cos_all,
        sin_all,
        lambda v: forward_product(plus_matrix, v),
        lambda v: forward_product(minus_matrix, v),
        lambda v: backward_product(plus_matrix, v),
        lambda v: backward_product(minus_matrix, v),
    )
    return result


LANES = 128
ROWS = 8
EDGE = 16
QUART = ND // 4
PIECES = 3
GROUP = 4


def chunk_plan(nloc):
    mid = nloc // 2
    plan = [(mid, mid + 1)]
    if mid > 1:
        plan.append((1, mid))
    if mid + 1 < nloc - 1:
        plan.append((mid + 1, nloc - 1))
    plan += [(0, 1), (nloc - 1, nloc)]
    return plan


def prep_kernel(nloc, points, plan, spec_hbm, mask_ref, *refs):
    nch = len(plan)
    wet_hbm, low_hbm, high_hbm = refs[0:3]
    hs_hbm = refs[3 : 3 + nch]
    hn_hbm = refs[3 + nch : 3 + 2 * nch]
    spec_v, wet_v, edge_v, in_sem, out_sem = refs[3 + 2 * nch :]
    tiles = points // LANES
    half = ND // 2
    where = {}
    for c, (lo, hi) in enumerate(plan):
        for f in range(lo, hi):
            where[f] = (c, f - lo)
    blocks = [(f, min(f + 2, nloc)) for f in range(0, nloc, 2)]
    first = plan[0][0] // 2
    order = [first] + [b for b in range(len(blocks)) if b != first]
    loads = {}
    for b in order:
        lo, hi = blocks[b]
        rows = pl.ds(lo * ND, (hi - lo) * ND)
        loads[b] = pltpu.make_async_copy(spec_hbm.at[rows], spec_v.at[rows], in_sem.at[b])
        loads[b].start()
    masks = [mask_ref[:, c * LANES : (c + 1) * LANES].astype(jnp.float32) for c in range(tiles)]
    copies = []

    def send(src, dst):
        copy = pltpu.make_async_copy(src, dst, out_sem.at[len(copies)])
        copy.start()
        copies.append(copy)

    for b in order:
        lo, hi = blocks[b]
        loads[b].wait()
        start, rows = lo * ND, (hi - lo) * ND

        def relayout(t, _):
            g0 = pl.multiple_of(start + t * ROWS, ROWS)
            for c in range(tiles):
                tile = spec_v[pl.ds(g0, ROWS), c * LANES : (c + 1) * LANES]
                wet_v[pl.ds(g0 * tiles + c, ROWS, stride=tiles), :] = tile * masks[c]
            return 0

        lax.fori_loop(0, rows // ROWS, relayout, 0)
        rest = rows % ROWS
        if rest:
            g0 = start + rows - rest
            for c in range(tiles):
                tile = spec_v[pl.ds(g0, rest), c * LANES : (c + 1) * LANES]
                wet_v[pl.ds(g0 * tiles + c, rest, stride=tiles), :] = tile * masks[c]
        for f in range(lo, hi):
            c, k = where[f]
            base = f * ND * tiles
            for side, (j0, row) in enumerate(((3 * QUART, tiles - 1), (QUART, 0))):
                at = base + j0 * tiles + row
                edge_v[f, side, ROWS:EDGE, :] = jnp.zeros((EDGE - ROWS, LANES), jnp.float32)
                edge_v[f, side, 0:ROWS, :] = wet_v[pl.ds(at, ROWS, stride=tiles), :]
                edge_v[f, side, ROWS : ROWS + 1, :] = wet_v[pl.ds(at + ROWS * tiles, 1), :]
            send(wet_v.at[pl.ds(base, half * tiles)], hs_hbm[c].at[k, pl.ds(0, half * tiles)])
            send(wet_v.at[pl.ds(base + half * tiles, half * tiles)], hn_hbm[c].at[k, pl.ds(0, half * tiles)])
            send(edge_v.at[f, 0], hs_hbm[c].at[k, pl.ds(half * tiles, EDGE)])
            send(edge_v.at[f, 1], hn_hbm[c].at[k, pl.ds(half * tiles, EDGE)])
            if f == nloc - 1:
                send(wet_v.at[pl.ds(base, ND * tiles)], low_hbm)
            if f == 0:
                send(wet_v.at[pl.ds(base, ND * tiles)], high_hbm)
        span = pl.ds(start * tiles, rows * tiles)
        send(wet_v.at[span], wet_hbm.at[span])
    for copy in copies:
        copy.wait()


def prep(spectrum, mask, plan):
    bins, points = spectrum.shape
    nloc = bins // ND
    tiles = points // LANES
    halo_rows = ND // 2 * tiles + EDGE
    halos = [jax.ShapeDtypeStruct((hi - lo, halo_rows, LANES), jnp.float32) for lo, hi in plan]
    one = jax.ShapeDtypeStruct((ND * tiles, LANES), jnp.float32)
    outs = [jax.ShapeDtypeStruct((bins * tiles, LANES), jnp.float32), one, one] + halos + halos
    nblocks = -(-nloc // 2)
    anywhere = pl.BlockSpec(memory_space=pl.ANY)
    res = pl.pallas_call(
        functools.partial(prep_kernel, nloc, points, plan),
        out_shape=outs,
        in_specs=[anywhere, pl.BlockSpec(memory_space=pltpu.VMEM)],
        out_specs=[anywhere] * len(outs),
        scratch_shapes=[
            pltpu.VMEM((bins, points), jnp.float32),
            pltpu.VMEM((bins * tiles, LANES), jnp.float32),
            pltpu.VMEM((nloc, 2, EDGE, LANES), jnp.float32),
            pltpu.SemaphoreType.DMA((nblocks,)),
            pltpu.SemaphoreType.DMA((4 * nloc + 2 + nblocks,)),
        ],
        compiler_params=pltpu.CompilerParams(vmem_limit_bytes=40 << 20),
        cost_estimate=pl.CostEstimate(flops=bins * points, bytes_accessed=bins * points * 12, transcendentals=0),
        name="prep",
    )(spectrum, mask)
    nch = len(plan)
    return res[0], res[1], res[2], res[3 : 3 + nch], res[3 + nch : 3 + 2 * nch]


def front_kernel(
    shares, tiles, kmin, kmax, tab_ref, dir_ref, nbr_ref, par_ref, wet_ref, low_ref, high_ref, hs_ref, hn_ref, out_ref, ext_ref
):
    speed = tab_ref[pl.program_id(0)]
    half = ND // 2
    span = half * tiles
    south, north = tiles, ROWS
    pitch = 2 * (2 * tiles + ROWS)

    def rows_at(j, row, count=ROWS):
        return pl.ds(j * pitch + 2 * row, count, stride=2)

    def extend(q, _):
        for t in range(0, tiles, ROWS):
            ext_ref[rows_at(q, t), :] = hs_ref[0, pl.ds(pl.multiple_of(q * tiles + t, ROWS), ROWS), :]
            ext_ref[rows_at(q, south + t), :] = wet_ref[0, q, t : t + ROWS, :]
            ext_ref[rows_at(half + q, north + t), :] = wet_ref[0, half + q, t : t + ROWS, :]
            ext_ref[rows_at(half + q, north + tiles + t), :] = hn_ref[
                0, pl.ds(pl.multiple_of(q * tiles + t, ROWS), ROWS), :
            ]
        return 0

    lax.fori_loop(0, half, extend, 0, unroll=2)
    for q in range(QUART):
        ext_ref[pl.ds((QUART + q) * pitch + 2 * (south + tiles), 1), :] = hn_ref[0, span + q : span + q + 1, :]
        ext_ref[pl.ds((3 * QUART + q) * pitch + 2 * (north - 1), 1), :] = hs_ref[0, span + q : span + q + 1, :]

    nblk = tiles // ROWS
    sub = lax.broadcasted_iota(jnp.int32, (ROWS, LANES), 0)
    lanes, rels = {}, {}
    for d in range(4):
        for b in range(nblk):
            src = nbr_ref[d, b * ROWS : (b + 1) * ROWS, :]
            lanes[d, b] = src & (LANES - 1)
            rels[d, b] = (src >> 7) - (sub + b * ROWS)

    def picked(j, own, b, d, offsets):
        out = None
        for r in offsets:
            window = ext_ref[rows_at(j, own + b * ROWS + r), :]
            got = jnp.take_along_axis(window, lanes[d, b], axis=1, mode="promise_in_bounds")
            out = got if out is None else jnp.where(rels[d, b] == r, got, out)
        return out

    per_share = nblk // shares
    for quad in range(4):
        cos_up = quad in (0, 3)
        own, dy, off_y = (
            (south, 3, range(-(kmax // LANES), -(kmin // LANES) + 1))
            if quad < 2
            else (north, 2, range(kmin // LANES, kmax // LANES + 1))
        )
        dx, off_x = (1, (-1, 0)) if cos_up else (0, (0, 1))

        def body(q, _):
            j = quad * QUART + q
            jprev = jnp.where(j == 0, ND - 1, j - 1)
            jnext = jnp.where(j == ND - 1, 0, j + 1)
            acos = jnp.abs(dir_ref[0, j])
            asin = jnp.abs(dir_ref[1, j])
            ax, ay = speed * acos, speed * asin
            for b in range(nblk):
                at = slice(b * ROWS, (b + 1) * ROWS)
                wet = wet_ref[0, j, at, :]
                e_y = picked(j, own, b, dy, off_y)
                e_x = picked(j, own, b, dx, off_x)
                rf, fs = par_ref[2, at, :], par_ref[3, at, :]
                e_prev, e_next = wet_ref[0, jprev, at, :], wet_ref[0, jnext, at, :]
                e_t = jnp.where(rf > 0, e_prev, e_next) if cos_up else jnp.where(rf < 0, e_prev, e_next)
                e_s = jnp.where(fs > 0, low_ref[0, j, at, :], high_ref[0, j, at, :])
                spatial = (par_ref[0, at, :] * ax) * (wet - e_x) + (par_ref[1, at, :] * ay) * (wet - e_y)
                spectral = (jnp.abs(rf) * acos) * (wet - e_t) + (jnp.abs(fs) * speed) * (wet - e_s)
                out_ref[b // per_share, j, (b % per_share) * ROWS : (b % per_share + 1) * ROWS, :] = (
                    wet - spatial - spectral
                )
            return 0

        lax.fori_loop(0, QUART, body, 0)


def front(speed, dirs, nbr, par, wet, low, high, hs, hn, count, shares, kmin, kmax):
    tiles = nbr.shape[1]
    vm = pltpu.VMEM

    def freq_spec(first):
        return pl.BlockSpec((1, ND, tiles, LANES), lambda i: (first + i, 0, 0, 0))

    def whole(shape):
        return pl.BlockSpec(shape, lambda i: (0,) * len(shape))

    halo_spec = pl.BlockSpec((1,) + hs.shape[1:], lambda i: (i, 0, 0))
    rows = tiles // shares
    elems = count * ND * tiles * LANES
    return pl.pallas_call(
        functools.partial(front_kernel, shares, tiles, kmin, kmax),
        grid=(count,),
        out_shape=jax.ShapeDtypeStruct((shares, count * ND, rows, LANES), jnp.float32),
        in_specs=[
            pl.BlockSpec(memory_space=pltpu.SMEM),
            pl.BlockSpec(memory_space=pltpu.SMEM),
            whole(nbr.shape),
            whole(par.shape),
            freq_spec(wet[1]),
            freq_spec(low[1]),
            freq_spec(high[1]),
            halo_spec,
            halo_spec,
        ],
        out_specs=pl.BlockSpec((shares, ND, rows, LANES), lambda i: (0, i, 0, 0)),
        scratch_shapes=[vm((ND * 2 * (2 * tiles + ROWS), LANES), jnp.float32)],
        compiler_params=pltpu.CompilerParams(vmem_limit_bytes=32 << 20),
        cost_estimate=pl.CostEstimate(flops=elems * 150, bytes_accessed=elems * 24, transcendentals=0),
        name="front",
    )(speed, dirs, nbr, par, wet[0], low[0], high[0], hs, hn)


def tail_kernel(nfreq, bins_dev, plan, bins_ref, wts_ref, ftab_ref, frs_ref, dir_ref, wind_ref, mask_ref, *refs):
    nch = len(plan)
    parts = refs[:nch]
    out_hbm = refs[nch]
    mv, base, a0, a1, a2, a3, dw, out_v, in_sem, out_sem = refs[nch + 1 :]
    shares = parts[0].shape[0]
    nbins = nfreq * ND
    loads = []
    for c, (lo, hi) in enumerate(plan):
        for s in range(shares):
            rows = pl.ds(s * bins_dev + lo * ND, (hi - lo) * ND)
            copy = pltpu.make_async_copy(parts[c].at[s], mv.at[rows], in_sem.at[len(loads)])
            copy.start()
            loads.append(copy)
    zero = jnp.zeros((ROWS, LANES), jnp.float32)

    def clear(g, _):
        for acc in (a0, a1, a2, a3):
            acc[g] = zero
        return 0

    lax.fori_loop(0, nbins, clear, 0, unroll=8)
    for j in range(ND):
        dw[j] = wind_ref[0] * dir_ref[0, j] + wind_ref[1] * dir_ref[1, j]
    for copy in loads:
        copy.wait()

    def spread(g, half):
        weights = (wts_ref[0, g], 1.0 - wts_ref[0, g], wts_ref[1, g], 1.0 - wts_ref[1, g])
        spots = [bins_ref[k, g] for k in range(4)]
        accs = (a0, a1, a2, a3)
        old = [acc[b] for acc, b in zip(accs, spots)]
        for acc, b, was, w in zip(accs, spots, old, weights):
            acc[b] = was + w * half

    def per_freq(f, carry):
        fr2, fr4, hspeed = ftab_ref[0, f], ftab_ref[1, f], ftab_ref[2, f]

        def per_group(t, carry):
            total, before = carry
            j0 = t * GROUP
            g0 = f * ND + j0
            own = [mv[g0 + i] for i in range(GROUP)]
            found = [[mv[bins_ref[k, g0 + i]] for k in range(4)] for i in range(GROUP)]
            dws = [dw[j0 + i] for i in range(GROUP)]
            last = jnp.maximum(g0 - GROUP, 0)
            for i in range(GROUP):
                spread(last + i, before[i])
            halves = []
            for i in range(GROUP):
                m, (p0, p1, m0, m1) = own[i], found[i]
                wp, wm = wts_ref[0, g0 + i], wts_ref[1, g0 + i]
                ep = wp * p0 + (1.0 - wp) * p1
                em = wm * m0 + (1.0 - wm) * m1
                mf = fr4 * m
                half = mf * (m * (ep * (1 / 1.25**4) + em * (1 / 0.75**4)) - ep * em * (2.0 / 0.9375**4))
                drive = jnp.maximum(0.0, dws[i] - hspeed)
                base[g0 + i] = m + 0.15 * (drive * drive) * m - 2.0 * half
                halves.append(half)
                total = total + m
            return total, tuple(halves)

        steep, before = carry
        part, before = lax.fori_loop(0, ND // GROUP, per_group, (zero, before))
        return steep + part * fr2, before

    steep, before = lax.fori_loop(0, nfreq, per_freq, (zero, (zero,) * GROUP))
    for i in range(GROUP):
        spread(nbins - GROUP + i, before[i])
    steep = steep * (1.0 / nbins)
    mask = mask_ref[...].astype(jnp.float32)
    flat = base.reshape(nbins * ROWS, LANES)
    per = nbins // PIECES
    copies = []
    for p in range(PIECES):

        def finish(t, _):
            g0 = pl.multiple_of(t * ROWS, ROWS)
            done = []
            for i in range(ROWS):
                g = g0 + i
                mine = base[g] - (frs_ref[g] * steep) * mv[g]
                done.append((mine + ((a0[g] + a1[g]) + (a2[g] + a3[g]))) * mask)
            for i in range(ROWS):
                base[g0 + i] = done[i]
            for c in range(ROWS):
                out_v[pl.ds(g0, ROWS), c * LANES : (c + 1) * LANES] = flat[pl.ds(g0 * ROWS + c, ROWS, stride=ROWS), :]
            return 0

        lax.fori_loop(p * per // ROWS, (p + 1) * per // ROWS, finish, 0)
        rows = pl.ds(p * per, per)
        copy = pltpu.make_async_copy(out_v.at[rows], out_hbm.at[rows], out_sem.at[p])
        copy.start()
        copies.append(copy)
    for copy in copies:
        copy.wait()


def tail(parts, plan, bins_dev, dia_bins, dia_wts, ftab, frs, dirs, wind, mask):
    nbins = dia_bins.shape[1]
    nfreq = nbins // ND
    anywhere = pl.BlockSpec(memory_space=pl.ANY)
    smem = pl.BlockSpec(memory_space=pltpu.SMEM)
    vmem = pl.BlockSpec(memory_space=pltpu.VMEM)
    shares = parts[0].shape[0]
    points = ROWS * LANES
    field = pltpu.VMEM((nbins, ROWS, LANES), jnp.float32)
    return pl.pallas_call(
        functools.partial(tail_kernel, nfreq, bins_dev, plan),
        out_shape=jax.ShapeDtypeStruct((nbins, points), jnp.float32),
        in_specs=[smem] * 5 + [vmem] * 2 + [anywhere] * len(parts),
        out_specs=anywhere,
        scratch_shapes=[field] * 6
        + [
            pltpu.VMEM((ND, ROWS, LANES), jnp.float32),
            pltpu.VMEM((nbins, points), jnp.float32),
            pltpu.SemaphoreType.DMA((len(parts) * shares,)),
            pltpu.SemaphoreType.DMA((PIECES,)),
        ],
        compiler_params=pltpu.CompilerParams(vmem_limit_bytes=56 << 20),
        cost_estimate=pl.CostEstimate(flops=nbins * points * 60, bytes_accessed=nbins * points * 8, transcendentals=0),
        name="tail",
    )(dia_bins, dia_wts, ftab, frs, dirs, wind, mask, *parts)


def fast_on_device(
    spectrum, wind, sea_mask, neighbours, metric_x, metric_y, refraction, freq_shift, dia_bins, dia_wts
):
    bins_dev, points = spectrum.shape
    nbins = dia_bins.shape[1]
    nfreq = nbins // ND
    nloc = bins_dev // ND
    tiles = points // LANES
    shares = lax.axis_size("bin")
    share = points // shares
    bin_pos = lax.axis_index("bin")
    space_pos = lax.axis_index("space")
    plan = chunk_plan(nloc)

    freqs = np.arange(nfreq, dtype=np.float32)
    speed = jnp.asarray(np.exp(-np.log(1.1) * freqs.astype(np.float64)).astype(np.float32))
    ratio = np.exp(np.log(1.1) * (freqs.astype(np.float64) - (nfreq - 1)))
    ftab = jnp.asarray(
        np.stack([ratio**2, 4.0 * ratio**4, 0.5 * np.exp(-np.log(1.1) * freqs)]).astype(np.float32)
    )
    frs = jnp.asarray(np.repeat(3.0 * ratio, ND).astype(np.float32))
    theta = 2.0 * np.pi * (np.arange(ND) + 0.5) / ND
    dirs = jnp.asarray(np.stack([np.cos(theta), np.sin(theta)]).astype(np.float32))
    speed_own = lax.dynamic_slice_in_dim(speed, bin_pos * nloc, nloc, 0)

    wet, low_out, high_out, hs, hn = prep(spectrum, sea_mask.reshape(1, points), plan)
    wet = wet.reshape(nloc, ND, tiles, LANES)

    def shift(array, axis, step):
        peers = lax.axis_size(axis)
        pairs = [(i, i + 1) for i in range(peers - 1)]
        if step < 0:
            pairs = [(b, a) for a, b in pairs]
        return lax.ppermute(array, axis, pairs)

    hs = [shift(a, "space", 1) for a in hs]
    hn = [shift(a, "space", -1) for a in hn]
    low_in = shift(low_out, "bin", 1).reshape(1, ND, tiles, LANES)
    high_in = shift(high_out, "bin", -1).reshape(1, ND, tiles, LANES)

    nbr = (neighbours - space_pos * points).reshape(4, tiles, LANES)
    par = jnp.stack([metric_x, metric_y, refraction, freq_shift]).reshape(4, tiles, LANES)
    kmin, kmax = points // 2, points
    parts = []
    for c, (lo, hi) in enumerate(plan):
        low = (low_in, 0) if lo == 0 else (wet, lo - 1)
        high = (high_in, 0) if hi == nloc else (wet, lo + 1)
        moved = front(
            speed_own[lo:hi], dirs, nbr, par, (wet, lo), low, high, hs[c], hn[c], hi - lo, shares, kmin, kmax
        )
        parts.append(lax.all_to_all(moved, "bin", split_axis=0, concat_axis=0, tiled=True))
    wind_part = lax.dynamic_slice_in_dim(wind, bin_pos * share, share, 1).reshape(2, ROWS, LANES)
    mask_part = lax.dynamic_slice_in_dim(sea_mask, bin_pos * share, share, 0).reshape(ROWS, LANES)
    return tail(parts, plan, bins_dev, dia_bins, dia_wts, ftab, frs, dirs, wind_part, mask_part)


def pick_path(spectrum, *others):
    bins_dev, points = spectrum.shape
    fits = bins_dev % ND == 0 and bins_dev // ND >= 3 and points // lax.axis_size("bin") == ROWS * LANES
    return (fast_on_device if fits else on_device)(spectrum, *others)


def solution(mesh):
    return jax.shard_map(
        pick_path,
        mesh=mesh,
        in_specs=(
            P("bin", ("ens", "space")),
            P(None, ("ens", "space")),
            P("space"),
            P(None, "space"),
            P("space"),
            P("space"),
            P("space"),
            P("space"),
            P(),
            P(),
        ),
        out_specs=P(None, ("ens", "space", "bin")),
        check_vma=False,
    )
```

```python
import functools
import itertools

import jax
import jax.numpy as jnp
import numpy as np
from jax import lax
from jax.experimental import pallas as pl
from jax.experimental.pallas import tpu as pltpu
from jax.sharding import PartitionSpec as P

ND = 36


def extended(array, sides, width):
    for axis, dim in sides:
        peers, length = (lax.axis_size(axis), array.shape[dim])
        up = [(i, (i + 1) % peers) for i in range(peers - 1)]
        down = [(j, i) for i, j in up]
        last = lax.slice_in_dim(array, length - width, length, axis=dim)
        initial = lax.slice_in_dim(array, 0, width, axis=dim)
        before = lax.ppermute(last, axis, up)
        after = lax.ppermute(initial, axis, down)
        array = jnp.concatenate([before, array, after], axis=dim)
    return array


def bin_tables(index, nfreq, ndir):
    freq = (index // ndir).astype(jnp.float32)
    direc = index % ndir
    fratio = jnp.exp(jnp.log(1.1) * (freq - (nfreq - 1)))
    speed = jnp.exp(-jnp.log(1.1) * freq)
    theta = 2.0 * jnp.pi * (direc.astype(jnp.float32) + 0.5) / ndir
    return (fratio, speed, jnp.cos(theta), jnp.sin(theta), direc == 0, direc == ndir - 1)


def spatial_term(wet, padded, local, metric_x, metric_y, speed, cosv, sinv):
    east = jnp.take(padded, local[0], axis=1)
    west = jnp.take(padded, local[1], axis=1)
    north = jnp.take(padded, local[2], axis=1)
    south = jnp.take(padded, local[3], axis=1)
    along_x = metric_x[None, :] * (speed * cosv)[:, None]
    along_y = metric_y[None, :] * (speed * sinv)[:, None]
    flux_x = jnp.abs(along_x) * (wet - jnp.where(along_x > 0, west, east))
    flux_y = jnp.abs(along_y) * (wet - jnp.where(along_y > 0, south, north))
    return flux_x + flux_y


def spectral_term(wet, padded, ndir, first, last, refraction, freq_shift, speed, cosv):
    rows = wet.shape[0]

    def moved_rows(offset):
        return lax.slice_in_dim(padded, ndir + offset, ndir + offset + rows, axis=0)

    prev_dir = jnp.where(first[:, None], moved_rows(ndir - 1), moved_rows(-1))
    next_dir = jnp.where(last[:, None], moved_rows(1 - ndir), moved_rows(1))
    lower = moved_rows(-ndir)
    upper = moved_rows(ndir)
    turning = refraction[None, :] * cosv[:, None]
    shifting = freq_shift[None, :] * speed[:, None]
    flux_t = jnp.abs(turning) * (wet - jnp.where(turning > 0, prev_dir, next_dir))
    flux_s = jnp.abs(shifting) * (wet - jnp.where(shifting > 0, lower, upper))
    return flux_t + flux_s


def source_step(
    moved, wind, maskf, fratio, speed, cosv, sinv, plus_fwd, minus_fwd, plus_back, minus_back
):
    steep = jnp.mean(moved * (fratio * fratio)[:, None], axis=0)
    drive = jnp.maximum(
        0.0,
        wind[0][None, :] * cosv[:, None] + wind[1][None, :] * sinv[:, None] - 0.5 * speed[:, None],
    )
    s_in = 0.3 * drive * drive * moved
    s_ds = -6.0 * fratio[:, None] * steep[None, :] * moved
    e_plus = plus_fwd(moved)
    e_minus = minus_fwd(moved)
    delta = (
        8.0
        * (fratio**4)[:, None]
        * (
            moved * moved * (e_plus / 1.25**4 + e_minus / 0.75**4)
            - 2.0 * moved * e_plus * e_minus / 0.9375**4
        )
    )
    s_nl = -2.0 * delta + plus_back(delta) + minus_back(delta)
    return (moved + 0.5 * (s_in + s_ds + s_nl)) * maskf[None, :]


def pair_matrix(first_bins, second_bins, weight, count):
    columns = jnp.arange(count, dtype=jnp.int32)[None, :]
    return weight[:, None] * (first_bins[:, None] == columns).astype(jnp.float32) + (1.0 - weight)[
        :, None
    ] * (second_bins[:, None] == columns).astype(jnp.float32)


def forward_product(matrix, values):
    return jnp.dot(
        matrix, values, precision=lax.Precision.HIGHEST, preferred_element_type=jnp.float32
    )


def backward_product(matrix, values):
    return lax.dot_general(
        matrix,
        values,
        (((0,), (0,)), ((), ())),
        precision=lax.Precision.HIGHEST,
        preferred_element_type=jnp.float32,
    )


def on_device(
    spectrum,
    wind,
    sea_mask,
    neighbours,
    metric_x,
    metric_y,
    refraction,
    freq_shift,
    dia_bins,
    dia_wts,
):
    bins_dev, points_dev = spectrum.shape
    nbins = dia_bins.shape[1]
    ndir = ND
    nfreq = nbins // ndir
    space_pos = lax.axis_index("space")
    bin_pos = lax.axis_index("bin")
    maskf = sea_mask.astype(jnp.float32)
    wet = spectrum * maskf[None, :]
    padded = extended(wet, (("space", 1),), points_dev)
    base = space_pos * points_dev - points_dev
    local = neighbours - base
    own_bins = bin_pos * bins_dev + jnp.arange(bins_dev, dtype=jnp.int32)
    fratio, speed, cosv, sinv, first, last = bin_tables(own_bins, nfreq, ndir)
    spatial = spatial_term(wet, padded, local, metric_x, metric_y, speed, cosv, sinv)
    share = points_dev // lax.axis_size("bin")
    start = bin_pos * share
    all_bins = jnp.arange(nbins, dtype=jnp.int32)
    fratio_all, speed_all, cos_all, sin_all, first_all, last_all = bin_tables(all_bins, nfreq, ndir)
    bin_pad = extended(wet, (("bin", 0),), ndir)
    spectral = spectral_term(wet, bin_pad, ndir, first, last, refraction, freq_shift, speed, cosv)
    moved_own = wet - spatial - spectral
    moved = lax.all_to_all(moved_own, "bin", split_axis=1, concat_axis=0, tiled=True)
    wind_part = lax.dynamic_slice_in_dim(wind, start, share, 1)
    mask_part = lax.dynamic_slice_in_dim(maskf, start, share, 0)
    plus_matrix = pair_matrix(dia_bins[0], dia_bins[1], dia_wts[0], nbins)
    minus_matrix = pair_matrix(dia_bins[2], dia_bins[3], dia_wts[1], nbins)
    result = source_step(
        moved,
        wind_part,
        mask_part,
        fratio_all,
        speed_all,
        cos_all,
        sin_all,
        lambda v: forward_product(plus_matrix, v),
        lambda v: forward_product(minus_matrix, v),
        lambda v: backward_product(plus_matrix, v),
        lambda v: backward_product(minus_matrix, v),
    )
    return result


LANES = 128
ROWS = 8
EDGE = 16
QUART = ND // 4
PIECES = 3
VMEM_ASK = 60 << 20
GROUP = 4


def chunk_plan(nloc):
    mid = nloc // 2

    def pieces(freqs):
        return [freqs[:1]] + [freqs[i : i + 2] for i in range(1, len(freqs), 2)] if freqs else []

    down = pieces(list(range(mid - 1, 0, -1)))
    up = pieces(list(range(mid + 1, nloc - 1)))
    inner = [c for pair in itertools.zip_longest(down, up) for c in pair if c]
    chunks = [[mid]] + inner + [[0], [nloc - 1]]
    return [(min(c), max(c) + 1) for c in chunks]


def halo_groups(plan):
    return [g for g in (plan[:1], plan[1:3], plan[3:]) if g]


def slots_of(group):
    freqs = [f for lo, hi in group for f in range(lo, hi)]
    return {f: i for i, f in enumerate(freqs)}


def prep_kernel(points, bins, blocks, groups, full, spec_hbm, mask_ref, *refs):
    ngr = len(groups)
    nloc = bins // ND
    hs_hbm, hn_hbm = refs[:ngr], refs[ngr : 2 * ngr]
    if full:
        wet_hbm, low_hbm, high_hbm = refs[2 * ngr : 2 * ngr + 3]
    spec_v, wet_v, edge_v, in_sem, out_sem = refs[-5:]
    tiles = points // LANES
    half = ND // 2
    where = {f: (i, k) for i, group in enumerate(groups) for f, k in slots_of(group).items()}
    loads = []
    spans = []
    for lo, hi in blocks:
        start = lo * ND // ROWS * ROWS
        stop = min(-(-hi * ND // ROWS) * ROWS, bins)
        spans.append((start, stop))
        rows = pl.ds(start, stop - start)
        copy = pltpu.make_async_copy(spec_hbm.at[rows], spec_v.at[rows], in_sem.at[len(loads)])
        copy.start()
        loads.append(copy)
    masks = [mask_ref[:, c * LANES : (c + 1) * LANES].astype(jnp.float32) for c in range(tiles)]
    copies = []

    def send(src, dst):
        copy = pltpu.make_async_copy(src, dst, out_sem.at[len(copies)])
        copy.start()
        copies.append(copy)

    for (lo, hi), (start, stop), load in zip(blocks, spans, loads):
        load.wait()

        def relayout(t, _):
            g0 = pl.multiple_of(start + t * ROWS, ROWS)
            for c in range(tiles):
                tile = spec_v[pl.ds(g0, ROWS), c * LANES : (c + 1) * LANES]
                wet_v[pl.ds(g0 * tiles + c, ROWS, stride=tiles), :] = tile * masks[c]
            return 0

        lax.fori_loop(0, (stop - start) // ROWS, relayout, 0)
        rest = (stop - start) % ROWS
        if rest:
            g0 = stop - rest
            for c in range(tiles):
                tile = spec_v[pl.ds(g0, rest), c * LANES : (c + 1) * LANES]
                wet_v[pl.ds(g0 * tiles + c, rest, stride=tiles), :] = tile * masks[c]
        for f in range(lo, hi):
            base = f * ND * tiles
            if f in where:
                i, k = where[f]
                for side, (j0, row) in enumerate(((3 * QUART, tiles - 1), (QUART, 0))):
                    at = base + j0 * tiles + row
                    edge_v[f, side, ROWS:EDGE, :] = jnp.zeros((EDGE - ROWS, LANES), jnp.float32)
                    edge_v[f, side, 0:ROWS, :] = wet_v[pl.ds(at, ROWS, stride=tiles), :]
                    edge_v[f, side, ROWS : ROWS + 1, :] = wet_v[pl.ds(at + ROWS * tiles, 1), :]
                span = half * tiles
                send(wet_v.at[pl.ds(base, span)], hs_hbm[i].at[k, pl.ds(0, span)])
                send(wet_v.at[pl.ds(base + span, span)], hn_hbm[i].at[k, pl.ds(0, span)])
                send(edge_v.at[f, 0], hs_hbm[i].at[k, pl.ds(span, EDGE)])
                send(edge_v.at[f, 1], hn_hbm[i].at[k, pl.ds(span, EDGE)])
            if full:
                own = pl.ds(base, ND * tiles)
                if f == nloc - 1:
                    send(wet_v.at[own], low_hbm)
                if f == 0:
                    send(wet_v.at[own], high_hbm)
                send(wet_v.at[own], wet_hbm.at[own])
    for copy in copies:
        copy.wait()


def prep(spectrum, mask, blocks, groups, full):
    bins, points = spectrum.shape
    nloc = bins // ND
    tiles = points // LANES
    halo_rows = ND // 2 * tiles + EDGE
    halos = [jax.ShapeDtypeStruct((len(slots_of(g)), halo_rows, LANES), jnp.float32) for g in groups]
    one = jax.ShapeDtypeStruct((ND * tiles, LANES), jnp.float32)
    outs = halos + halos
    if full:
        outs += [jax.ShapeDtypeStruct((bins * tiles, LANES), jnp.float32), one, one]
    anywhere = pl.BlockSpec(memory_space=pl.ANY)
    count = sum(hi - lo for lo, hi in blocks)
    sends = 4 * sum(len(slots_of(g)) for g in groups) + (nloc + 2 if full else 0)
    res = pl.pallas_call(
        functools.partial(prep_kernel, points, bins, blocks, groups, full),
        out_shape=outs,
        in_specs=[anywhere, pl.BlockSpec(memory_space=pltpu.VMEM)],
        out_specs=[anywhere] * len(outs),
        scratch_shapes=[
            pltpu.VMEM((bins, points), jnp.float32),
            pltpu.VMEM((bins * tiles, LANES), jnp.float32),
            pltpu.VMEM((nloc, 2, EDGE, LANES), jnp.float32),
            pltpu.SemaphoreType.DMA((len(blocks),)),
            pltpu.SemaphoreType.DMA((sends,)),
        ],
        compiler_params=pltpu.CompilerParams(vmem_limit_bytes=VMEM_ASK),
        cost_estimate=pl.CostEstimate(flops=0, bytes_accessed=count * 3_000_000, transcendentals=0),
        name="prep",
    )(spectrum, mask)
    ngr = len(groups)
    return res[:ngr], res[ngr : 2 * ngr], res[2 * ngr :]


def front_kernel(
    tiles, kmin, kmax, tab_ref, dir_ref, pos_ref, nbr_ref, par_ref, wet_ref, low_ref, high_ref, hs_ref, hn_ref, *refs
):
    outs, ext_ref = refs[:-1], refs[-1]
    speed = tab_ref[pl.program_id(0)]
    half = ND // 2
    span = half * tiles
    south, north = tiles, ROWS
    pitch = 2 * (2 * tiles + ROWS)

    def rows_at(j, row, count=ROWS):
        return pl.ds(j * pitch + 2 * row, count, stride=2)

    def extend(q, _):
        for t in range(0, tiles, ROWS):
            ext_ref[rows_at(q, t), :] = hs_ref[0, pl.ds(pl.multiple_of(q * tiles + t, ROWS), ROWS), :]
            ext_ref[rows_at(q, south + t), :] = wet_ref[0, q, t : t + ROWS, :]
            ext_ref[rows_at(half + q, north + t), :] = wet_ref[0, half + q, t : t + ROWS, :]
            ext_ref[rows_at(half + q, north + tiles + t), :] = hn_ref[
                0, pl.ds(pl.multiple_of(q * tiles + t, ROWS), ROWS), :
            ]
        return 0

    lax.fori_loop(0, half, extend, 0, unroll=2)
    for q in range(QUART):
        ext_ref[pl.ds((QUART + q) * pitch + 2 * (south + tiles), 1), :] = hn_ref[0, span + q : span + q + 1, :]
        ext_ref[pl.ds((3 * QUART + q) * pitch + 2 * (north - 1), 1), :] = hs_ref[0, span + q : span + q + 1, :]

    shares = len(outs)
    per_share = tiles // shares
    steps = [(d, k) for d in range(shares) for k in range(per_share // ROWS)]
    firsts = {}
    for d, k in steps:
        share = lax.rem(pos_ref[0] + d, shares)
        firsts[d, k] = pl.multiple_of(share * per_share + k * ROWS, ROWS)
    sub = lax.broadcasted_iota(jnp.int32, (ROWS, LANES), 0)
    lanes, rels = {}, {}
    for way in range(4):
        for step in steps:
            src = nbr_ref[way, pl.ds(firsts[step], ROWS), :]
            lanes[way, step] = src & (LANES - 1)
            rels[way, step] = (src >> 7) - (sub + firsts[step])

    def picked(j, own, step, way, offsets):
        out = None
        for r in offsets:
            window = ext_ref[rows_at(j, own + firsts[step] + r), :]
            got = jnp.take_along_axis(window, lanes[way, step], axis=1, mode="promise_in_bounds")
            out = got if out is None else jnp.where(rels[way, step] == r, got, out)
        return out

    for quad in range(4):
        cos_up = quad in (0, 3)
        own, way_y, off_y = (
            (south, 3, range(-(kmax // LANES), -(kmin // LANES) + 1))
            if quad < 2
            else (north, 2, range(kmin // LANES, kmax // LANES + 1))
        )
        way_x, off_x = (1, (-1, 0)) if cos_up else (0, (0, 1))

        def body(q, _):
            j = quad * QUART + q
            jprev = jnp.where(j == 0, ND - 1, j - 1)
            jnext = jnp.where(j == ND - 1, 0, j + 1)
            acos = jnp.abs(dir_ref[0, j])
            asin = jnp.abs(dir_ref[1, j])
            ax, ay = speed * acos, speed * asin
            for step in steps:
                at = pl.ds(firsts[step], ROWS)
                wet = wet_ref[0, j, at, :]
                e_y = picked(j, own, step, way_y, off_y)
                e_x = picked(j, own, step, way_x, off_x)
                rf, fs = par_ref[2, at, :], par_ref[3, at, :]
                e_prev, e_next = wet_ref[0, jprev, at, :], wet_ref[0, jnext, at, :]
                e_t = jnp.where(rf > 0, e_prev, e_next) if cos_up else jnp.where(rf < 0, e_prev, e_next)
                e_s = jnp.where(fs > 0, low_ref[0, j, at, :], high_ref[0, j, at, :])
                spatial = (par_ref[0, at, :] * ax) * (wet - e_x) + (par_ref[1, at, :] * ay) * (wet - e_y)
                spectral = (jnp.abs(rf) * acos) * (wet - e_t) + (jnp.abs(fs) * speed) * (wet - e_s)
                d, k = step
                outs[d][j, k * ROWS : (k + 1) * ROWS, :] = wet - spatial - spectral
            return 0

        lax.fori_loop(0, QUART, body, 0)


def front(speed, dirs, pos, nbr, par, wet, low, high, hs, hn, count, shares, kmin, kmax):
    tiles = nbr.shape[1]
    smem = pl.BlockSpec(memory_space=pltpu.SMEM)

    def freq_spec(first):
        return pl.BlockSpec((1, ND, tiles, LANES), lambda i: (first + i, 0, 0, 0))

    def halo_spec(halo):
        array, first = halo
        return pl.BlockSpec((1,) + array.shape[1:], lambda i: (first + i, 0, 0))

    def whole(shape):
        return pl.BlockSpec(shape, lambda i: (0,) * len(shape))

    rows = tiles // shares
    return pl.pallas_call(
        functools.partial(front_kernel, tiles, kmin, kmax),
        grid=(count,),
        out_shape=[jax.ShapeDtypeStruct((count * ND, rows, LANES), jnp.float32)] * shares,
        in_specs=[
            smem,
            smem,
            smem,
            whole(nbr.shape),
            whole(par.shape),
            freq_spec(wet[1]),
            freq_spec(low[1]),
            freq_spec(high[1]),
            halo_spec(hs),
            halo_spec(hn),
        ],
        out_specs=[pl.BlockSpec((ND, rows, LANES), lambda i: (i, 0, 0))] * shares,
        scratch_shapes=[pltpu.VMEM((ND * 2 * (2 * tiles + ROWS), LANES), jnp.float32)],
        compiler_params=pltpu.CompilerParams(vmem_limit_bytes=VMEM_ASK),
        cost_estimate=pl.CostEstimate(flops=0, bytes_accessed=count * 22_000_000, transcendentals=0),
        name="front",
    )(speed, dirs, pos, nbr, par, wet[0], low[0], high[0], hs[0], hn[0])


def tail_kernel(nfreq, bins_dev, plan, spot_ref, wts_ref, ftab_ref, frs_ref, dir_ref, pos_ref, wind_ref, mask_ref, *refs):
    out_hbm, mv, base, a0, a1, a2, a3, dw, out_v, in_sem, out_sem = refs[-11:]
    parts = refs[:-11]
    nparts = len(parts)
    shares = nparts // len(plan)
    nbins = nfreq * ND
    loads = []
    for c, (lo, hi) in enumerate(plan):
        for d in range(shares):
            source = lax.rem(pos_ref[0] + (shares - d), shares)
            first = pl.multiple_of((source * bins_dev + lo * ND) * ROWS, ROWS)
            rows = pl.ds(first, (hi - lo) * ND * ROWS)
            copy = pltpu.make_async_copy(parts[c * shares + d], mv.at[rows], in_sem.at[len(loads)])
            copy.start()
            loads.append(copy)
    zero = jnp.zeros((ROWS, LANES), jnp.float32)
    accs = (a0, a1, a2, a3)

    def tile(row):
        return pl.ds(pl.multiple_of(row, ROWS), ROWS)

    def clear(g, _):
        for acc in accs:
            acc[tile(g * ROWS), :] = zero
        return 0

    lax.fori_loop(0, nbins, clear, 0, unroll=8)
    for j in range(ND):
        dw[j] = wind_ref[0] * dir_ref[0, j] + wind_ref[1] * dir_ref[1, j]
    for copy in loads:
        copy.wait()

    def spread(g, shares_of):
        for i in range(GROUP):
            spots = [tile(spot_ref[4 * g + 4 * i + k]) for k in range(4)]
            old = [acc[at, :] for acc, at in zip(accs, spots)]
            for acc, at, was, add in zip(accs, spots, old, shares_of[4 * i : 4 * i + 4]):
                acc[at, :] = was + add

    def per_freq(f, carry):
        fr2, fr4, hspeed = ftab_ref[0, f], ftab_ref[1, f], ftab_ref[2, f]

        def per_group(t, carry):
            total, before = carry
            j0 = t * GROUP
            g0 = f * ND + j0
            own = [mv[tile((g0 + i) * ROWS), :] for i in range(GROUP)]
            found = [[mv[tile(spot_ref[4 * g0 + 4 * i + k]), :] for k in range(4)] for i in range(GROUP)]
            spread(jnp.maximum(g0 - GROUP, 0), before)
            shares_of = []
            for i in range(GROUP):
                m, (p0, p1, m0, m1) = own[i], found[i]
                wp, wm = wts_ref[2 * g0 + 2 * i], wts_ref[2 * g0 + 2 * i + 1]
                ep = p1 + wp * (p0 - p1)
                em = m1 + wm * (m0 - m1)
                mf = fr4 * m
                half = mf * (m * (ep * (1 / 1.25**4) + em * (1 / 0.75**4)) - ep * em * (2.0 / 0.9375**4))
                drive = jnp.maximum(0.0, dw[j0 + i] - hspeed)
                base[tile((g0 + i) * ROWS), :] = m + 0.15 * (drive * drive) * m - 2.0 * half
                sp, sm = wp * half, wm * half
                shares_of += [sp, half - sp, sm, half - sm]
                total = total + m
            return total, tuple(shares_of)

        steep, before = carry
        part, before = lax.fori_loop(0, ND // GROUP, per_group, (zero, before))
        return steep + part * fr2, before

    steep, before = lax.fori_loop(0, nfreq, per_freq, (zero, (zero,) * (4 * GROUP)))
    spread(nbins - GROUP, before)
    steep = steep * (1.0 / nbins)
    mask = mask_ref[...].astype(jnp.float32)
    per = nbins // PIECES
    copies = []
    for p in range(PIECES):

        def finish(t, _):
            g0 = t * ROWS
            done = []
            for i in range(ROWS):
                at = tile((g0 + i) * ROWS)
                mine = base[at, :] - (frs_ref[g0 + i] * steep) * mv[at, :]
                done.append((mine + ((a0[at, :] + a1[at, :]) + (a2[at, :] + a3[at, :]))) * mask)
            for i in range(ROWS):
                base[tile((g0 + i) * ROWS), :] = done[i]
            return 0

        def place(t, _):
            g0 = pl.multiple_of(t * ROWS, ROWS)
            for c in range(ROWS):
                out_v[pl.ds(g0, ROWS), c * LANES : (c + 1) * LANES] = base[pl.ds(g0 * ROWS + c, ROWS, stride=ROWS), :]
            return 0

        lax.fori_loop(p * per // ROWS, (p + 1) * per // ROWS, finish, 0)
        lax.fori_loop(p * per // ROWS, (p + 1) * per // ROWS, place, 0, unroll=2)
        rows = pl.ds(p * per, per)
        copy = pltpu.make_async_copy(out_v.at[rows], out_hbm.at[rows], out_sem.at[p])
        copy.start()
        copies.append(copy)
    for copy in copies:
        copy.wait()


def tail(parts, plan, bins_dev, dia_bins, dia_wts, ftab, frs, dirs, pos, wind, mask):
    nbins = dia_bins.shape[1]
    nfreq = nbins // ND
    anywhere = pl.BlockSpec(memory_space=pl.ANY)
    smem = pl.BlockSpec(memory_space=pltpu.SMEM)
    vmem = pl.BlockSpec(memory_space=pltpu.VMEM)
    points = ROWS * LANES
    spots = (dia_bins * ROWS).T.reshape(-1)
    wts = dia_wts.T.reshape(-1)
    field = pltpu.VMEM((nbins * ROWS, LANES), jnp.float32)
    return pl.pallas_call(
        functools.partial(tail_kernel, nfreq, bins_dev, plan),
        out_shape=jax.ShapeDtypeStruct((nbins, points), jnp.float32),
        in_specs=[smem] * 6 + [vmem] * 2 + [anywhere] * len(parts),
        out_specs=anywhere,
        scratch_shapes=[field] * 6
        + [
            pltpu.VMEM((ND, ROWS, LANES), jnp.float32),
            pltpu.VMEM((nbins, points), jnp.float32),
            pltpu.SemaphoreType.DMA((len(parts),)),
            pltpu.SemaphoreType.DMA((PIECES,)),
        ],
        compiler_params=pltpu.CompilerParams(vmem_limit_bytes=VMEM_ASK),
        cost_estimate=pl.CostEstimate(flops=0, bytes_accessed=70_000_000, transcendentals=0),
        name="tail",
    )(spots, wts, ftab, frs, dirs, pos, wind, mask, *parts)


def fast_on_device(
    spectrum, wind, sea_mask, neighbours, metric_x, metric_y, refraction, freq_shift, dia_bins, dia_wts
):
    bins_dev, points = spectrum.shape
    nbins = dia_bins.shape[1]
    nfreq = nbins // ND
    nloc = bins_dev // ND
    tiles = points // LANES
    shares = lax.axis_size("bin")
    share = points // shares
    bin_pos = lax.axis_index("bin")
    space_pos = lax.axis_index("space")
    plan = chunk_plan(nloc)

    freqs = np.arange(nfreq, dtype=np.float32)
    speed = jnp.asarray(np.exp(-np.log(1.1) * freqs.astype(np.float64)).astype(np.float32))
    ratio = np.exp(np.log(1.1) * (freqs.astype(np.float64) - (nfreq - 1)))
    ftab = jnp.asarray(
        np.stack([ratio**2, 4.0 * ratio**4, 0.5 * np.exp(-np.log(1.1) * freqs)]).astype(np.float32)
    )
    frs = jnp.asarray(np.repeat(3.0 * ratio, ND).astype(np.float32))
    theta = 2.0 * np.pi * (np.arange(ND) + 0.5) / ND
    dirs = jnp.asarray(np.stack([np.cos(theta), np.sin(theta)]).astype(np.float32))
    speed_own = lax.dynamic_slice_in_dim(speed, bin_pos * nloc, nloc, 0)

    groups = halo_groups(plan)
    mask_row = sea_mask.reshape(1, points)
    hs, hn, _ = prep(spectrum, mask_row, plan[:1], groups[:1], False)
    whole_blocks = [(f, min(f + 2, nloc)) for f in range(0, nloc, 2)]
    hs_rest, hn_rest, (wet, low_out, high_out) = prep(spectrum, mask_row, whole_blocks, groups[1:], True)
    wet = wet.reshape(nloc, ND, tiles, LANES)

    def line(array, axis, step):
        peers = lax.axis_size(axis)
        pairs = [(i, i + 1) for i in range(peers - 1)]
        if step < 0:
            pairs = [(b, a) for a, b in pairs]
        return lax.ppermute(array, axis, pairs)

    hs = [line(a, "space", 1) for a in list(hs) + list(hs_rest)]
    hn = [line(a, "space", -1) for a in list(hn) + list(hn_rest)]
    low_in = line(low_out, "bin", 1).reshape(1, ND, tiles, LANES)
    high_in = line(high_out, "bin", -1).reshape(1, ND, tiles, LANES)

    nbr = (neighbours - space_pos * points).reshape(4, tiles, LANES)
    par = jnp.stack([metric_x, metric_y, refraction, freq_shift]).reshape(4, tiles, LANES)
    pos = bin_pos.reshape(1)
    kmin, kmax = points // 2, points
    parts = []
    for lo, hi in plan:
        low = (low_in, 0) if lo == 0 else (wet, lo - 1)
        high = (high_in, 0) if hi == nloc else (wet, lo + 1)
        gi, slot = [(i, slots_of(g)[lo]) for i, g in enumerate(groups) if (lo, hi) in g][0]
        blocks = front(
            speed_own[lo:hi], dirs, pos, nbr, par, (wet, lo), low, high, (hs[gi], slot), (hn[gi], slot), hi - lo, shares, kmin, kmax
        )
        for d, block in enumerate(blocks):
            rows = block.reshape(-1, LANES)
            pairs = [(i, (i + d) % shares) for i in range(shares)]
            parts.append(lax.ppermute(rows, "bin", pairs) if d else rows)
    wind_part = lax.dynamic_slice_in_dim(wind, bin_pos * share, share, 1).reshape(2, ROWS, LANES)
    mask_part = lax.dynamic_slice_in_dim(sea_mask, bin_pos * share, share, 0).reshape(ROWS, LANES)
    return tail(parts, plan, bins_dev, dia_bins, dia_wts, ftab, frs, dirs, pos, wind_part, mask_part)


def pick_path(spectrum, *others):
    bins_dev, points = spectrum.shape
    fits = bins_dev % ND == 0 and bins_dev // ND >= 3 and points // lax.axis_size("bin") == ROWS * LANES
    return (fast_on_device if fits else on_device)(spectrum, *others)


def solution(mesh):
    return jax.shard_map(
        pick_path,
        mesh=mesh,
        in_specs=(
            P("bin", ("ens", "space")),
            P(None, ("ens", "space")),
            P("space"),
            P(None, "space"),
            P("space"),
            P("space"),
            P("space"),
            P("space"),
            P(),
            P(),
        ),
        out_specs=P(None, ("ens", "space", "bin")),
        check_vma=False,
    )
```

```python
import functools
import itertools

import jax
import jax.numpy as jnp
import numpy as np
from jax import lax
from jax.experimental import pallas as pl
from jax.experimental.pallas import tpu as pltpu
from jax.sharding import PartitionSpec as P

ND = 36


def extended(array, sides, width):
    for axis, dim in sides:
        peers, length = (lax.axis_size(axis), array.shape[dim])
        up = [(i, (i + 1) % peers) for i in range(peers - 1)]
        down = [(j, i) for i, j in up]
        last = lax.slice_in_dim(array, length - width, length, axis=dim)
        initial = lax.slice_in_dim(array, 0, width, axis=dim)
        before = lax.ppermute(last, axis, up)
        after = lax.ppermute(initial, axis, down)
        array = jnp.concatenate([before, array, after], axis=dim)
    return array


def bin_tables(index, nfreq, ndir):
    freq = (index // ndir).astype(jnp.float32)
    direc = index % ndir
    fratio = jnp.exp(jnp.log(1.1) * (freq - (nfreq - 1)))
    speed = jnp.exp(-jnp.log(1.1) * freq)
    theta = 2.0 * jnp.pi * (direc.astype(jnp.float32) + 0.5) / ndir
    return (fratio, speed, jnp.cos(theta), jnp.sin(theta), direc == 0, direc == ndir - 1)


def spatial_term(wet, padded, local, metric_x, metric_y, speed, cosv, sinv):
    east = jnp.take(padded, local[0], axis=1)
    west = jnp.take(padded, local[1], axis=1)
    north = jnp.take(padded, local[2], axis=1)
    south = jnp.take(padded, local[3], axis=1)
    along_x = metric_x[None, :] * (speed * cosv)[:, None]
    along_y = metric_y[None, :] * (speed * sinv)[:, None]
    flux_x = jnp.abs(along_x) * (wet - jnp.where(along_x > 0, west, east))
    flux_y = jnp.abs(along_y) * (wet - jnp.where(along_y > 0, south, north))
    return flux_x + flux_y


def spectral_term(wet, padded, ndir, first, last, refraction, freq_shift, speed, cosv):
    rows = wet.shape[0]

    def moved_rows(offset):
        return lax.slice_in_dim(padded, ndir + offset, ndir + offset + rows, axis=0)

    prev_dir = jnp.where(first[:, None], moved_rows(ndir - 1), moved_rows(-1))
    next_dir = jnp.where(last[:, None], moved_rows(1 - ndir), moved_rows(1))
    lower = moved_rows(-ndir)
    upper = moved_rows(ndir)
    turning = refraction[None, :] * cosv[:, None]
    shifting = freq_shift[None, :] * speed[:, None]
    flux_t = jnp.abs(turning) * (wet - jnp.where(turning > 0, prev_dir, next_dir))
    flux_s = jnp.abs(shifting) * (wet - jnp.where(shifting > 0, lower, upper))
    return flux_t + flux_s


def source_step(
    moved, wind, maskf, fratio, speed, cosv, sinv, plus_fwd, minus_fwd, plus_back, minus_back
):
    steep = jnp.mean(moved * (fratio * fratio)[:, None], axis=0)
    drive = jnp.maximum(
        0.0,
        wind[0][None, :] * cosv[:, None] + wind[1][None, :] * sinv[:, None] - 0.5 * speed[:, None],
    )
    s_in = 0.3 * drive * drive * moved
    s_ds = -6.0 * fratio[:, None] * steep[None, :] * moved
    e_plus = plus_fwd(moved)
    e_minus = minus_fwd(moved)
    delta = (
        8.0
        * (fratio**4)[:, None]
        * (
            moved * moved * (e_plus / 1.25**4 + e_minus / 0.75**4)
            - 2.0 * moved * e_plus * e_minus / 0.9375**4
        )
    )
    s_nl = -2.0 * delta + plus_back(delta) + minus_back(delta)
    return (moved + 0.5 * (s_in + s_ds + s_nl)) * maskf[None, :]


def pair_matrix(first_bins, second_bins, weight, count):
    columns = jnp.arange(count, dtype=jnp.int32)[None, :]
    return weight[:, None] * (first_bins[:, None] == columns).astype(jnp.float32) + (1.0 - weight)[
        :, None
    ] * (second_bins[:, None] == columns).astype(jnp.float32)


def forward_product(matrix, values):
    return jnp.dot(
        matrix, values, precision=lax.Precision.HIGHEST, preferred_element_type=jnp.float32
    )


def backward_product(matrix, values):
    return lax.dot_general(
        matrix,
        values,
        (((0,), (0,)), ((), ())),
        precision=lax.Precision.HIGHEST,
        preferred_element_type=jnp.float32,
    )


def on_device(
    spectrum,
    wind,
    sea_mask,
    neighbours,
    metric_x,
    metric_y,
    refraction,
    freq_shift,
    dia_bins,
    dia_wts,
):
    bins_dev, points_dev = spectrum.shape
    nbins = dia_bins.shape[1]
    ndir = ND
    nfreq = nbins // ndir
    space_pos = lax.axis_index("space")
    bin_pos = lax.axis_index("bin")
    maskf = sea_mask.astype(jnp.float32)
    wet = spectrum * maskf[None, :]
    padded = extended(wet, (("space", 1),), points_dev)
    base = space_pos * points_dev - points_dev
    local = neighbours - base
    own_bins = bin_pos * bins_dev + jnp.arange(bins_dev, dtype=jnp.int32)
    fratio, speed, cosv, sinv, first, last = bin_tables(own_bins, nfreq, ndir)
    spatial = spatial_term(wet, padded, local, metric_x, metric_y, speed, cosv, sinv)
    share = points_dev // lax.axis_size("bin")
    start = bin_pos * share
    all_bins = jnp.arange(nbins, dtype=jnp.int32)
    fratio_all, speed_all, cos_all, sin_all, first_all, last_all = bin_tables(all_bins, nfreq, ndir)
    bin_pad = extended(wet, (("bin", 0),), ndir)
    spectral = spectral_term(wet, bin_pad, ndir, first, last, refraction, freq_shift, speed, cosv)
    moved_own = wet - spatial - spectral
    moved = lax.all_to_all(moved_own, "bin", split_axis=1, concat_axis=0, tiled=True)
    wind_part = lax.dynamic_slice_in_dim(wind, start, share, 1)
    mask_part = lax.dynamic_slice_in_dim(maskf, start, share, 0)
    plus_matrix = pair_matrix(dia_bins[0], dia_bins[1], dia_wts[0], nbins)
    minus_matrix = pair_matrix(dia_bins[2], dia_bins[3], dia_wts[1], nbins)
    result = source_step(
        moved,
        wind_part,
        mask_part,
        fratio_all,
        speed_all,
        cos_all,
        sin_all,
        lambda v: forward_product(plus_matrix, v),
        lambda v: forward_product(minus_matrix, v),
        lambda v: backward_product(plus_matrix, v),
        lambda v: backward_product(minus_matrix, v),
    )
    return result


LANES = 128
ROWS = 8
EDGE = 16
QUART = ND // 4
PIECES = 3
VMEM_ASK = 60 << 20
GROUP = 4


def chunk_plan(nloc):
    mid = nloc // 2
    return [(mid, 1, 1)] + [(mid - d, 2 * d, 2) for d in range(1, mid + 1)]


def freqs_of(chunk):
    first, step, count = chunk
    return [first + i * step for i in range(count)]


def halo_groups(plan):
    return [g for g in (plan[:2], plan[2:]) if g]


def slots_of(group):
    return {f: i for i, f in enumerate(f for chunk in group for f in freqs_of(chunk))}


def prep_kernel(points, bins, blocks, groups, full, spec_hbm, mask_ref, *refs):
    ngr = len(groups)
    nloc = bins // ND
    hs_hbm, hn_hbm = refs[:ngr], refs[ngr : 2 * ngr]
    if full:
        wet_hbm, low_hbm, high_hbm = refs[2 * ngr : 2 * ngr + 3]
    spec_v, wet_v, edge_v, in_sem, out_sem = refs[-5:]
    tiles = points // LANES
    half = ND // 2
    where = {f: (i, k) for i, group in enumerate(groups) for f, k in slots_of(group).items()}
    loads = []
    spans = []
    for lo, hi in blocks:
        start = lo * ND // ROWS * ROWS
        stop = min(-(-hi * ND // ROWS) * ROWS, bins)
        spans.append((start, stop))
        rows = pl.ds(start, stop - start)
        copy = pltpu.make_async_copy(spec_hbm.at[rows], spec_v.at[rows], in_sem.at[len(loads)])
        copy.start()
        loads.append(copy)
    masks = [mask_ref[:, c * LANES : (c + 1) * LANES].astype(jnp.float32) for c in range(tiles)]
    copies = []

    def send(src, dst):
        copy = pltpu.make_async_copy(src, dst, out_sem.at[len(copies)])
        copy.start()
        copies.append(copy)

    for (lo, hi), (start, stop), load in zip(blocks, spans, loads):
        load.wait()

        def relayout(t, _):
            g0 = pl.multiple_of(start + t * ROWS, ROWS)
            for c in range(tiles):
                tile = spec_v[pl.ds(g0, ROWS), c * LANES : (c + 1) * LANES]
                wet_v[pl.ds(g0 * tiles + c, ROWS, stride=tiles), :] = tile * masks[c]
            return 0

        lax.fori_loop(0, (stop - start) // ROWS, relayout, 0)
        rest = (stop - start) % ROWS
        if rest:
            g0 = stop - rest
            for c in range(tiles):
                tile = spec_v[pl.ds(g0, rest), c * LANES : (c + 1) * LANES]
                wet_v[pl.ds(g0 * tiles + c, rest, stride=tiles), :] = tile * masks[c]
        for f in range(lo, hi):
            base = f * ND * tiles
            if f in where:
                i, k = where[f]
                for side, (j0, row) in enumerate(((3 * QUART, tiles - 1), (QUART, 0))):
                    at = base + j0 * tiles + row
                    edge_v[f, side, ROWS:EDGE, :] = jnp.zeros((EDGE - ROWS, LANES), jnp.float32)
                    edge_v[f, side, 0:ROWS, :] = wet_v[pl.ds(at, ROWS, stride=tiles), :]
                    edge_v[f, side, ROWS : ROWS + 1, :] = wet_v[pl.ds(at + ROWS * tiles, 1), :]
                span = half * tiles
                send(wet_v.at[pl.ds(base, span)], hs_hbm[i].at[k, pl.ds(0, span)])
                send(wet_v.at[pl.ds(base + span, span)], hn_hbm[i].at[k, pl.ds(0, span)])
                send(edge_v.at[f, 0], hs_hbm[i].at[k, pl.ds(span, EDGE)])
                send(edge_v.at[f, 1], hn_hbm[i].at[k, pl.ds(span, EDGE)])
            if full:
                own = pl.ds(base, ND * tiles)
                if f == nloc - 1:
                    send(wet_v.at[own], low_hbm)
                if f == 0:
                    send(wet_v.at[own], high_hbm)
                send(wet_v.at[own], wet_hbm.at[own])
    for copy in copies:
        copy.wait()


def prep(spectrum, mask, blocks, groups, full):
    bins, points = spectrum.shape
    nloc = bins // ND
    tiles = points // LANES
    halo_rows = ND // 2 * tiles + EDGE
    halos = [jax.ShapeDtypeStruct((len(slots_of(g)), halo_rows, LANES), jnp.float32) for g in groups]
    one = jax.ShapeDtypeStruct((ND * tiles, LANES), jnp.float32)
    outs = halos + halos
    if full:
        outs += [jax.ShapeDtypeStruct((bins * tiles, LANES), jnp.float32), one, one]
    anywhere = pl.BlockSpec(memory_space=pl.ANY)
    count = sum(hi - lo for lo, hi in blocks)
    sends = 4 * sum(len(slots_of(g)) for g in groups) + (nloc + 2 if full else 0)
    res = pl.pallas_call(
        functools.partial(prep_kernel, points, bins, blocks, groups, full),
        out_shape=outs,
        in_specs=[anywhere, pl.BlockSpec(memory_space=pltpu.VMEM)],
        out_specs=[anywhere] * len(outs),
        scratch_shapes=[
            pltpu.VMEM((bins, points), jnp.float32),
            pltpu.VMEM((bins * tiles, LANES), jnp.float32),
            pltpu.VMEM((nloc, 2, EDGE, LANES), jnp.float32),
            pltpu.SemaphoreType.DMA((len(blocks),)),
            pltpu.SemaphoreType.DMA((sends,)),
        ],
        compiler_params=pltpu.CompilerParams(vmem_limit_bytes=VMEM_ASK),
        cost_estimate=pl.CostEstimate(flops=0, bytes_accessed=count * 3_000_000, transcendentals=0),
        name="prep",
    )(spectrum, mask)
    ngr = len(groups)
    return res[:ngr], res[ngr : 2 * ngr], res[2 * ngr :]


def front_kernel(
    tiles, shares, kmin, kmax, edge, tab_ref, dir_ref, pos_ref, nbr_ref, par_ref, hs_ref, hn_ref, wet_ref, *refs
):
    near, outs, ext_ref = refs[: -shares - 1], refs[-shares - 1 : -1], refs[-1]
    place = pl.program_id(0)
    speed = tab_ref[place]
    first = place == 0
    half = ND // 2
    span = half * tiles
    south, north = tiles, ROWS
    pitch = 2 * (2 * tiles + ROWS)

    def rows_at(j, row, count=ROWS):
        return pl.ds(j * pitch + 2 * row, count, stride=2)

    def extend(q, _):
        for t in range(0, tiles, ROWS):
            ext_ref[rows_at(q, t), :] = hs_ref[0, pl.ds(pl.multiple_of(q * tiles + t, ROWS), ROWS), :]
            ext_ref[rows_at(q, south + t), :] = wet_ref[0, q, t : t + ROWS, :]
            ext_ref[rows_at(half + q, north + t), :] = wet_ref[0, half + q, t : t + ROWS, :]
            ext_ref[rows_at(half + q, north + tiles + t), :] = hn_ref[
                0, pl.ds(pl.multiple_of(q * tiles + t, ROWS), ROWS), :
            ]
        return 0

    lax.fori_loop(0, half, extend, 0, unroll=2)
    for q in range(QUART):
        ext_ref[pl.ds((QUART + q) * pitch + 2 * (south + tiles), 1), :] = hn_ref[0, span + q : span + q + 1, :]
        ext_ref[pl.ds((3 * QUART + q) * pitch + 2 * (north - 1), 1), :] = hs_ref[0, span + q : span + q + 1, :]

    side = jnp.where(first, 1.0, -1.0)
    per_share = tiles // shares
    steps = [(d, k) for d in range(shares) for k in range(per_share // ROWS)]
    firsts = {}
    for d, k in steps:
        share = lax.rem(pos_ref[0] + d, shares)
        firsts[d, k] = pl.multiple_of(share * per_share + k * ROWS, ROWS)
    sub = lax.broadcasted_iota(jnp.int32, (ROWS, LANES), 0)
    lanes, rels = {}, {}
    for way in range(4):
        for step in steps:
            src = nbr_ref[way, pl.ds(firsts[step], ROWS), :]
            lanes[way, step] = src & (LANES - 1)
            rels[way, step] = (src >> 7) - (sub + firsts[step])

    def picked(j, own, step, way, offsets):
        out = None
        for r in offsets:
            window = ext_ref[rows_at(j, own + firsts[step] + r), :]
            got = jnp.take_along_axis(window, lanes[way, step], axis=1, mode="promise_in_bounds")
            out = got if out is None else jnp.where(rels[way, step] == r, got, out)
        return out

    for quad in range(4):
        cos_up = quad in (0, 3)
        own, way_y, off_y = (
            (south, 3, range(-(kmax // LANES), -(kmin // LANES) + 1))
            if quad < 2
            else (north, 2, range(kmin // LANES, kmax // LANES + 1))
        )
        way_x, off_x = (1, (-1, 0)) if cos_up else (0, (0, 1))

        def body(q, _):
            j = quad * QUART + q
            jprev = jnp.where(j == 0, ND - 1, j - 1)
            jnext = jnp.where(j == ND - 1, 0, j + 1)
            acos = jnp.abs(dir_ref[0, j])
            asin = jnp.abs(dir_ref[1, j])
            ax, ay = speed * acos, speed * asin
            for step in steps:
                at = pl.ds(firsts[step], ROWS)
                wet = wet_ref[0, j, at, :]
                e_y = picked(j, own, step, way_y, off_y)
                e_x = picked(j, own, step, way_x, off_x)
                rf, fs = par_ref[2, at, :], par_ref[3, at, :]
                e_prev, e_next = wet_ref[0, jprev, at, :], wet_ref[0, jnext, at, :]
                e_t = jnp.where(rf > 0, e_prev, e_next) if cos_up else jnp.where(rf < 0, e_prev, e_next)
                if edge:
                    inner, low, high = (ref[0, j, at, :] for ref in near)
                    outer = jnp.where(first, low, high)
                    e_s = jnp.where(fs * side > 0, outer, inner)
                else:
                    e_s = jnp.where(fs > 0, near[0][0, j, at, :], near[1][0, j, at, :])
                spatial = (par_ref[0, at, :] * ax) * (wet - e_x) + (par_ref[1, at, :] * ay) * (wet - e_y)
                spectral = (jnp.abs(rf) * acos) * (wet - e_t) + (jnp.abs(fs) * speed) * (wet - e_s)
                d, k = step
                outs[d][j, k * ROWS : (k + 1) * ROWS, :] = wet - spatial - spectral
            return 0

        lax.fori_loop(0, QUART, body, 0)


def front(speed, dirs, pos, nbr, par, hs, hn, slot, wet, ends, chunk, shares, kmin, kmax):
    first, step, count = chunk
    tiles = nbr.shape[1]
    nloc = wet.shape[0]
    smem = pl.BlockSpec(memory_space=pltpu.SMEM)

    def freq_spec(start, step):
        return pl.BlockSpec((1, ND, tiles, LANES), lambda i: (start + i * step, 0, 0, 0))

    halo_spec = pl.BlockSpec((1,) + hs.shape[1:], lambda i: (slot + i, 0, 0))

    def whole(shape):
        return pl.BlockSpec(shape, lambda i: (0,) * len(shape))

    if ends:
        near, near_specs = (wet,) + ends, [freq_spec(1, nloc - 3), freq_spec(0, 0), freq_spec(0, 0)]
    else:
        near, near_specs = (wet, wet), [freq_spec(first - 1, step), freq_spec(first + 1, step)]
    rows = tiles // shares
    return pl.pallas_call(
        functools.partial(front_kernel, tiles, shares, kmin, kmax, bool(ends)),
        grid=(count,),
        out_shape=[jax.ShapeDtypeStruct((count * ND, rows, LANES), jnp.float32)] * shares,
        in_specs=[smem] * 3
        + [whole(nbr.shape), whole(par.shape), halo_spec, halo_spec, freq_spec(first, step)]
        + near_specs,
        out_specs=[pl.BlockSpec((ND, rows, LANES), lambda i: (i, 0, 0))] * shares,
        scratch_shapes=[pltpu.VMEM((ND * 2 * (2 * tiles + ROWS), LANES), jnp.float32)],
        compiler_params=pltpu.CompilerParams(vmem_limit_bytes=VMEM_ASK),
        cost_estimate=pl.CostEstimate(flops=0, bytes_accessed=count * 22_000_000, transcendentals=0),
        name="front",
    )(speed, dirs, pos, nbr, par, hs, hn, wet, *near)


def tail_kernel(nfreq, bins_dev, plan, spot_ref, wts_ref, ftab_ref, frs_ref, dir_ref, pos_ref, wind_ref, mask_ref, *refs):
    out_hbm, mv, base, a0, a1, a2, a3, dw, out_v, in_sem, out_sem = refs[-11:]
    parts = refs[:-11]
    nparts = len(parts)
    shares = nparts // len(plan)
    nbins = nfreq * ND
    loads = []
    block = ND * ROWS
    for c, chunk in enumerate(plan):
        for d in range(shares):
            source = lax.rem(pos_ref[0] + (shares - d), shares)
            for i, f in enumerate(freqs_of(chunk)):
                rows = pl.ds(pl.multiple_of((source * bins_dev + f * ND) * ROWS, ROWS), block)
                part = parts[c * shares + d].at[pl.ds(i * block, block)]
                copy = pltpu.make_async_copy(part, mv.at[rows], in_sem.at[len(loads)])
                copy.start()
                loads.append(copy)
    zero = jnp.zeros((ROWS, LANES), jnp.float32)
    accs = (a0, a1, a2, a3)

    def tile(row):
        return pl.ds(pl.multiple_of(row, ROWS), ROWS)

    def clear(g, _):
        for acc in accs:
            acc[tile(g * ROWS), :] = zero
        return 0

    lax.fori_loop(0, nbins, clear, 0, unroll=8)
    for j in range(ND):
        dw[j] = wind_ref[0] * dir_ref[0, j] + wind_ref[1] * dir_ref[1, j]
    for copy in loads:
        copy.wait()

    def spread(g, shares_of):
        for i in range(GROUP):
            spots = [tile(spot_ref[4 * g + 4 * i + k]) for k in range(4)]
            old = [acc[at, :] for acc, at in zip(accs, spots)]
            for acc, at, was, add in zip(accs, spots, old, shares_of[4 * i : 4 * i + 4]):
                acc[at, :] = was + add

    def per_freq(f, carry):
        fr2, fr4, hspeed = ftab_ref[0, f], ftab_ref[1, f], ftab_ref[2, f]

        def per_group(t, carry):
            total, before = carry
            j0 = t * GROUP
            g0 = f * ND + j0
            own = [mv[tile((g0 + i) * ROWS), :] for i in range(GROUP)]
            found = [[mv[tile(spot_ref[4 * g0 + 4 * i + k]), :] for k in range(4)] for i in range(GROUP)]
            spread(jnp.maximum(g0 - GROUP, 0), before)
            shares_of = []
            for i in range(GROUP):
                m, (p0, p1, m0, m1) = own[i], found[i]
                wp, wm = wts_ref[2 * g0 + 2 * i], wts_ref[2 * g0 + 2 * i + 1]
                ep = p1 + wp * (p0 - p1)
                em = m1 + wm * (m0 - m1)
                mf = fr4 * m
                half = mf * (m * (ep * (1 / 1.25**4) + em * (1 / 0.75**4)) - ep * em * (2.0 / 0.9375**4))
                drive = jnp.maximum(0.0, dw[j0 + i] - hspeed)
                base[tile((g0 + i) * ROWS), :] = m + 0.15 * (drive * drive) * m - 2.0 * half
                sp, sm = wp * half, wm * half
                shares_of += [sp, half - sp, sm, half - sm]
                total = total + m
            return total, tuple(shares_of)

        steep, before = carry
        part, before = lax.fori_loop(0, ND // GROUP, per_group, (zero, before))
        return steep + part * fr2, before

    steep, before = lax.fori_loop(0, nfreq, per_freq, (zero, (zero,) * (4 * GROUP)))
    spread(nbins - GROUP, before)
    steep = steep * (1.0 / nbins)
    mask = mask_ref[...].astype(jnp.float32)
    per = nbins // PIECES
    copies = []
    for p in range(PIECES):

        def finish(t, _):
            g0 = t * ROWS
            done = []
            for i in range(ROWS):
                at = tile((g0 + i) * ROWS)
                mine = base[at, :] - (frs_ref[g0 + i] * steep) * mv[at, :]
                done.append((mine + ((a0[at, :] + a1[at, :]) + (a2[at, :] + a3[at, :]))) * mask)
            for i in range(ROWS):
                base[tile((g0 + i) * ROWS), :] = done[i]
            return 0

        def place(t, _):
            g0 = pl.multiple_of(t * ROWS, ROWS)
            for c in range(ROWS):
                out_v[pl.ds(g0, ROWS), c * LANES : (c + 1) * LANES] = base[pl.ds(g0 * ROWS + c, ROWS, stride=ROWS), :]
            return 0

        lax.fori_loop(p * per // ROWS, (p + 1) * per // ROWS, finish, 0)
        lax.fori_loop(p * per // ROWS, (p + 1) * per // ROWS, place, 0, unroll=2)
        rows = pl.ds(p * per, per)
        copy = pltpu.make_async_copy(out_v.at[rows], out_hbm.at[rows], out_sem.at[p])
        copy.start()
        copies.append(copy)
    for copy in copies:
        copy.wait()


def tail(parts, plan, bins_dev, dia_bins, dia_wts, ftab, frs, dirs, pos, wind, mask):
    nbins = dia_bins.shape[1]
    nfreq = nbins // ND
    anywhere = pl.BlockSpec(memory_space=pl.ANY)
    smem = pl.BlockSpec(memory_space=pltpu.SMEM)
    vmem = pl.BlockSpec(memory_space=pltpu.VMEM)
    points = ROWS * LANES
    spots = (dia_bins * ROWS).T.reshape(-1)
    wts = dia_wts.T.reshape(-1)
    field = pltpu.VMEM((nbins * ROWS, LANES), jnp.float32)
    return pl.pallas_call(
        functools.partial(tail_kernel, nfreq, bins_dev, plan),
        out_shape=jax.ShapeDtypeStruct((nbins, points), jnp.float32),
        in_specs=[smem] * 6 + [vmem] * 2 + [anywhere] * len(parts),
        out_specs=anywhere,
        scratch_shapes=[field] * 6
        + [
            pltpu.VMEM((ND, ROWS, LANES), jnp.float32),
            pltpu.VMEM((nbins, points), jnp.float32),
            pltpu.SemaphoreType.DMA((nbins // ND,)),
            pltpu.SemaphoreType.DMA((PIECES,)),
        ],
        compiler_params=pltpu.CompilerParams(vmem_limit_bytes=VMEM_ASK),
        cost_estimate=pl.CostEstimate(flops=0, bytes_accessed=70_000_000, transcendentals=0),
        name="tail",
    )(spots, wts, ftab, frs, dirs, pos, wind, mask, *parts)


def fast_on_device(
    spectrum, wind, sea_mask, neighbours, metric_x, metric_y, refraction, freq_shift, dia_bins, dia_wts
):
    bins_dev, points = spectrum.shape
    nbins = dia_bins.shape[1]
    nfreq = nbins // ND
    nloc = bins_dev // ND
    tiles = points // LANES
    shares = lax.axis_size("bin")
    share = points // shares
    bin_pos = lax.axis_index("bin")
    space_pos = lax.axis_index("space")
    plan = chunk_plan(nloc)

    freqs = np.arange(nfreq, dtype=np.float32)
    speed = jnp.asarray(np.exp(-np.log(1.1) * freqs.astype(np.float64)).astype(np.float32))
    ratio = np.exp(np.log(1.1) * (freqs.astype(np.float64) - (nfreq - 1)))
    ftab = jnp.asarray(
        np.stack([ratio**2, 4.0 * ratio**4, 0.5 * np.exp(-np.log(1.1) * freqs)]).astype(np.float32)
    )
    frs = jnp.asarray(np.repeat(3.0 * ratio, ND).astype(np.float32))
    theta = 2.0 * np.pi * (np.arange(ND) + 0.5) / ND
    dirs = jnp.asarray(np.stack([np.cos(theta), np.sin(theta)]).astype(np.float32))
    speed_own = lax.dynamic_slice_in_dim(speed, bin_pos * nloc, nloc, 0)

    groups = halo_groups(plan)
    mid = nloc // 2
    mask_row = sea_mask.reshape(1, points)
    hs, hn, _ = prep(spectrum, mask_row, [(mid - 1, mid + 2)], groups[:1], False)
    after, *_ = lax.optimization_barrier((spectrum, hs[0], hn[0]))
    whole_blocks = [(f, min(f + 2, nloc)) for f in range(0, nloc, 2)]
    hs_rest, hn_rest, (wet, low_out, high_out) = prep(after, mask_row, whole_blocks, groups[1:], True)
    wet = wet.reshape(nloc, ND, tiles, LANES)

    def line(array, axis, step):
        peers = lax.axis_size(axis)
        pairs = [(i, i + 1) for i in range(peers - 1)]
        if step < 0:
            pairs = [(b, a) for a, b in pairs]
        return lax.ppermute(array, axis, pairs)

    sends = list(zip(list(hs) + list(hs_rest), list(hn) + list(hn_rest)))
    halos = []

    def send_halos(sent, *after):
        south, north, *_ = lax.optimization_barrier(sent + after) if after else sent
        halos.append((line(south, "space", 1), line(north, "space", -1)))

    send_halos(sends[0])
    low_in = line(low_out, "bin", 1).reshape(1, ND, tiles, LANES)
    high_in = line(high_out, "bin", -1).reshape(1, ND, tiles, LANES)

    nbr = (neighbours - space_pos * points).reshape(4, tiles, LANES)
    par = jnp.stack([metric_x, metric_y, refraction, freq_shift]).reshape(4, tiles, LANES)
    pos = bin_pos.reshape(1)
    kmin, kmax = points // 2, points
    parts = []
    order = pos
    for c, chunk in enumerate(plan):
        first, step, count = chunk
        gi, slot = [(i, slots_of(g)[first]) for i, g in enumerate(groups) if chunk in g][0]
        ends = (low_in, high_in) if first == 0 else None
        speeds = jnp.stack([speed_own[f] for f in freqs_of(chunk)])
        blocks = front(speeds, dirs, order, nbr, par, *halos[gi], slot, wet, ends, chunk, shares, kmin, kmax)
        if c == 0 and len(sends) > 1:
            send_halos(sends[1], blocks[0], low_in, high_in)
        arrived = []
        for d, block in enumerate(blocks):
            rows = block.reshape(-1, LANES)
            pairs = [(i, (i + d) % shares) for i in range(shares)]
            arrived.append(lax.ppermute(rows, "bin", pairs) if d else rows)
        order, *_ = lax.optimization_barrier((pos, blocks[0]) + tuple(parts[-shares:][1:]))
        parts += arrived
    wind_part = lax.dynamic_slice_in_dim(wind, bin_pos * share, share, 1).reshape(2, ROWS, LANES)
    mask_part = lax.dynamic_slice_in_dim(sea_mask, bin_pos * share, share, 0).reshape(ROWS, LANES)
    return tail(parts, plan, bins_dev, dia_bins, dia_wts, ftab, frs, dirs, pos, wind_part, mask_part)


def pick_path(spectrum, *others):
    bins_dev, points = spectrum.shape
    fits = bins_dev % (2 * ND) == ND and bins_dev > ND and points // lax.axis_size("bin") == ROWS * LANES
    return (fast_on_device if fits else on_device)(spectrum, *others)


def solution(mesh):
    return jax.shard_map(
        pick_path,
        mesh=mesh,
        in_specs=(
            P("bin", ("ens", "space")),
            P(None, ("ens", "space")),
            P("space"),
            P(None, "space"),
            P("space"),
            P("space"),
            P("space"),
            P("space"),
            P(),
            P(),
        ),
        out_specs=P(None, ("ens", "space", "bin")),
        check_vma=False,
    )
```

```python
import functools
import itertools

import jax
import jax.numpy as jnp
import numpy as np
from jax import lax
from jax.experimental import pallas as pl
from jax.experimental.pallas import tpu as pltpu
from jax.sharding import PartitionSpec as P

ND = 36


def extended(array, sides, width):
    for axis, dim in sides:
        peers, length = (lax.axis_size(axis), array.shape[dim])
        up = [(i, (i + 1) % peers) for i in range(peers - 1)]
        down = [(j, i) for i, j in up]
        last = lax.slice_in_dim(array, length - width, length, axis=dim)
        initial = lax.slice_in_dim(array, 0, width, axis=dim)
        before = lax.ppermute(last, axis, up)
        after = lax.ppermute(initial, axis, down)
        array = jnp.concatenate([before, array, after], axis=dim)
    return array


def bin_tables(index, nfreq, ndir):
    freq = (index // ndir).astype(jnp.float32)
    direc = index % ndir
    fratio = jnp.exp(jnp.log(1.1) * (freq - (nfreq - 1)))
    speed = jnp.exp(-jnp.log(1.1) * freq)
    theta = 2.0 * jnp.pi * (direc.astype(jnp.float32) + 0.5) / ndir
    return (fratio, speed, jnp.cos(theta), jnp.sin(theta), direc == 0, direc == ndir - 1)


def spatial_term(wet, padded, local, metric_x, metric_y, speed, cosv, sinv):
    east = jnp.take(padded, local[0], axis=1)
    west = jnp.take(padded, local[1], axis=1)
    north = jnp.take(padded, local[2], axis=1)
    south = jnp.take(padded, local[3], axis=1)
    along_x = metric_x[None, :] * (speed * cosv)[:, None]
    along_y = metric_y[None, :] * (speed * sinv)[:, None]
    flux_x = jnp.abs(along_x) * (wet - jnp.where(along_x > 0, west, east))
    flux_y = jnp.abs(along_y) * (wet - jnp.where(along_y > 0, south, north))
    return flux_x + flux_y


def spectral_term(wet, padded, ndir, first, last, refraction, freq_shift, speed, cosv):
    rows = wet.shape[0]

    def moved_rows(offset):
        return lax.slice_in_dim(padded, ndir + offset, ndir + offset + rows, axis=0)

    prev_dir = jnp.where(first[:, None], moved_rows(ndir - 1), moved_rows(-1))
    next_dir = jnp.where(last[:, None], moved_rows(1 - ndir), moved_rows(1))
    lower = moved_rows(-ndir)
    upper = moved_rows(ndir)
    turning = refraction[None, :] * cosv[:, None]
    shifting = freq_shift[None, :] * speed[:, None]
    flux_t = jnp.abs(turning) * (wet - jnp.where(turning > 0, prev_dir, next_dir))
    flux_s = jnp.abs(shifting) * (wet - jnp.where(shifting > 0, lower, upper))
    return flux_t + flux_s


def source_step(
    moved, wind, maskf, fratio, speed, cosv, sinv, plus_fwd, minus_fwd, plus_back, minus_back
):
    steep = jnp.mean(moved * (fratio * fratio)[:, None], axis=0)
    drive = jnp.maximum(
        0.0,
        wind[0][None, :] * cosv[:, None] + wind[1][None, :] * sinv[:, None] - 0.5 * speed[:, None],
    )
    s_in = 0.3 * drive * drive * moved
    s_ds = -6.0 * fratio[:, None] * steep[None, :] * moved
    e_plus = plus_fwd(moved)
    e_minus = minus_fwd(moved)
    delta = (
        8.0
        * (fratio**4)[:, None]
        * (
            moved * moved * (e_plus / 1.25**4 + e_minus / 0.75**4)
            - 2.0 * moved * e_plus * e_minus / 0.9375**4
        )
    )
    s_nl = -2.0 * delta + plus_back(delta) + minus_back(delta)
    return (moved + 0.5 * (s_in + s_ds + s_nl)) * maskf[None, :]


def pair_matrix(first_bins, second_bins, weight, count):
    columns = jnp.arange(count, dtype=jnp.int32)[None, :]
    return weight[:, None] * (first_bins[:, None] == columns).astype(jnp.float32) + (1.0 - weight)[
        :, None
    ] * (second_bins[:, None] == columns).astype(jnp.float32)


def forward_product(matrix, values):
    return jnp.dot(
        matrix, values, precision=lax.Precision.HIGHEST, preferred_element_type=jnp.float32
    )


def backward_product(matrix, values):
    return lax.dot_general(
        matrix,
        values,
        (((0,), (0,)), ((), ())),
        precision=lax.Precision.HIGHEST,
        preferred_element_type=jnp.float32,
    )


def on_device(
    spectrum,
    wind,
    sea_mask,
    neighbours,
    metric_x,
    metric_y,
    refraction,
    freq_shift,
    dia_bins,
    dia_wts,
):
    bins_dev, points_dev = spectrum.shape
    nbins = dia_bins.shape[1]
    ndir = ND
    nfreq = nbins // ndir
    space_pos = lax.axis_index("space")
    bin_pos = lax.axis_index("bin")
    maskf = sea_mask.astype(jnp.float32)
    wet = spectrum * maskf[None, :]
    padded = extended(wet, (("space", 1),), points_dev)
    base = space_pos * points_dev - points_dev
    local = neighbours - base
    own_bins = bin_pos * bins_dev + jnp.arange(bins_dev, dtype=jnp.int32)
    fratio, speed, cosv, sinv, first, last = bin_tables(own_bins, nfreq, ndir)
    spatial = spatial_term(wet, padded, local, metric_x, metric_y, speed, cosv, sinv)
    share = points_dev // lax.axis_size("bin")
    start = bin_pos * share
    all_bins = jnp.arange(nbins, dtype=jnp.int32)
    fratio_all, speed_all, cos_all, sin_all, first_all, last_all = bin_tables(all_bins, nfreq, ndir)
    bin_pad = extended(wet, (("bin", 0),), ndir)
    spectral = spectral_term(wet, bin_pad, ndir, first, last, refraction, freq_shift, speed, cosv)
    moved_own = wet - spatial - spectral
    moved = lax.all_to_all(moved_own, "bin", split_axis=1, concat_axis=0, tiled=True)
    wind_part = lax.dynamic_slice_in_dim(wind, start, share, 1)
    mask_part = lax.dynamic_slice_in_dim(maskf, start, share, 0)
    plus_matrix = pair_matrix(dia_bins[0], dia_bins[1], dia_wts[0], nbins)
    minus_matrix = pair_matrix(dia_bins[2], dia_bins[3], dia_wts[1], nbins)
    result = source_step(
        moved,
        wind_part,
        mask_part,
        fratio_all,
        speed_all,
        cos_all,
        sin_all,
        lambda v: forward_product(plus_matrix, v),
        lambda v: forward_product(minus_matrix, v),
        lambda v: backward_product(plus_matrix, v),
        lambda v: backward_product(minus_matrix, v),
    )
    return result


LANES = 128
ROWS = 8
EDGE = 16
QUART = ND // 4
PIECES = 3
VMEM_ASK = 60 << 20
GROUP = 4


def chunk_plan(nloc):
    mid = nloc // 2
    return [(mid - d, 2 * d, 2) for d in range(1, mid + 1)] + [(mid, 1, 1)]


def freqs_of(chunk):
    first, step, count = chunk
    return [first + i * step for i in range(count)]


def halo_groups(plan):
    return [g for g in (plan[:2], plan[2:]) if g]


def slots_of(group):
    return {f: i for i, f in enumerate(f for chunk in group for f in freqs_of(chunk))}


def runs_of(freqs):
    runs = []
    for f in sorted(freqs):
        if runs and runs[-1][1] == f:
            runs[-1] = (runs[-1][0], f + 1)
        else:
            runs.append((f, f + 1))
    return runs


def prep_kernel(points, bins, blocks, groups, full, spec_hbm, mask_ref, *refs):
    ngr = len(groups)
    nloc = bins // ND
    hs_hbm, hn_hbm = refs[:ngr], refs[ngr : 2 * ngr]
    if full:
        wet_hbm, low_hbm, high_hbm = refs[2 * ngr : 2 * ngr + 3]
    spec_v, wet_v, edge_v, in_sem, out_sem = refs[-5:]
    tiles = points // LANES
    half = ND // 2
    where = {f: (i, k) for i, group in enumerate(groups) for f, k in slots_of(group).items()}
    loads = []
    spans = []
    for lo, hi in blocks:
        start = lo * ND // ROWS * ROWS
        stop = min(-(-hi * ND // ROWS) * ROWS, bins)
        spans.append((start, stop))
        rows = pl.ds(start, stop - start)
        copy = pltpu.make_async_copy(spec_hbm.at[rows], spec_v.at[rows], in_sem.at[len(loads)])
        copy.start()
        loads.append(copy)
    masks = [mask_ref[:, c * LANES : (c + 1) * LANES].astype(jnp.float32) for c in range(tiles)]
    copies = []

    def send(src, dst):
        copy = pltpu.make_async_copy(src, dst, out_sem.at[len(copies)])
        copy.start()
        copies.append(copy)

    for (lo, hi), (start, stop), load in zip(blocks, spans, loads):
        load.wait()

        def turn(g0, count):
            for c0 in range(0, tiles, ROWS):
                cols = range(c0, c0 + ROWS)
                block = jnp.stack(
                    [spec_v[pl.ds(g0, count), c * LANES : (c + 1) * LANES] * masks[c] for c in cols], axis=0
                )
                block = jnp.swapaxes(block, 0, 1)
                for i in range(count):
                    wet_v[pl.ds(pl.multiple_of((g0 + i) * tiles + c0, ROWS), ROWS), :] = block[i]

        def relayout(t, _):
            turn(pl.multiple_of(start + t * ROWS, ROWS), ROWS)
            return 0

        lax.fori_loop(0, (stop - start) // ROWS, relayout, 0)
        rest = (stop - start) % ROWS
        if rest:
            g0 = stop - rest
            for c in range(tiles):
                tile = spec_v[pl.ds(g0, rest), c * LANES : (c + 1) * LANES]
                wet_v[pl.ds(g0 * tiles + c, rest, stride=tiles), :] = tile * masks[c]
        for f in range(lo, hi):
            base = f * ND * tiles
            if f in where:
                i, k = where[f]
                for side, (j0, row) in enumerate(((3 * QUART, tiles - 1), (QUART, 0))):
                    at = base + j0 * tiles + row
                    edge_v[f, side, ROWS:EDGE, :] = jnp.zeros((EDGE - ROWS, LANES), jnp.float32)
                    edge_v[f, side, 0:ROWS, :] = wet_v[pl.ds(at, ROWS, stride=tiles), :]
                    edge_v[f, side, ROWS : ROWS + 1, :] = wet_v[pl.ds(at + ROWS * tiles, 1), :]
                span = half * tiles
                send(wet_v.at[pl.ds(base, span)], hs_hbm[i].at[k, pl.ds(0, span)])
                send(wet_v.at[pl.ds(base + span, span)], hn_hbm[i].at[k, pl.ds(0, span)])
                send(edge_v.at[f, 0], hs_hbm[i].at[k, pl.ds(span, EDGE)])
                send(edge_v.at[f, 1], hn_hbm[i].at[k, pl.ds(span, EDGE)])
            if full:
                own = pl.ds(base, ND * tiles)
                if f == nloc - 1:
                    send(wet_v.at[own], low_hbm)
                if f == 0:
                    send(wet_v.at[own], high_hbm)
                send(wet_v.at[own], wet_hbm.at[own])
    for copy in copies:
        copy.wait()


def prep(spectrum, mask, blocks, groups, full):
    bins, points = spectrum.shape
    nloc = bins // ND
    tiles = points // LANES
    halo_rows = ND // 2 * tiles + EDGE
    halos = [jax.ShapeDtypeStruct((len(slots_of(g)), halo_rows, LANES), jnp.float32) for g in groups]
    one = jax.ShapeDtypeStruct((ND * tiles, LANES), jnp.float32)
    outs = halos + halos
    if full:
        outs += [jax.ShapeDtypeStruct((bins * tiles, LANES), jnp.float32), one, one]
    anywhere = pl.BlockSpec(memory_space=pl.ANY)
    count = sum(hi - lo for lo, hi in blocks)
    sends = 4 * sum(len(slots_of(g)) for g in groups) + (nloc + 2 if full else 0)
    res = pl.pallas_call(
        functools.partial(prep_kernel, points, bins, blocks, groups, full),
        out_shape=outs,
        in_specs=[anywhere, pl.BlockSpec(memory_space=pltpu.VMEM)],
        out_specs=[anywhere] * len(outs),
        scratch_shapes=[
            pltpu.VMEM((bins, points), jnp.float32),
            pltpu.VMEM((bins * tiles, LANES), jnp.float32),
            pltpu.VMEM((nloc, 2, EDGE, LANES), jnp.float32),
            pltpu.SemaphoreType.DMA((len(blocks),)),
            pltpu.SemaphoreType.DMA((sends,)),
        ],
        compiler_params=pltpu.CompilerParams(vmem_limit_bytes=VMEM_ASK),
        cost_estimate=pl.CostEstimate(flops=0, bytes_accessed=count * 3_000_000, transcendentals=0),
        name="prep",
    )(spectrum, mask)
    ngr = len(groups)
    return res[:ngr], res[ngr : 2 * ngr], res[2 * ngr :]


def front_kernel(
    tiles, shares, kmin, kmax, chunk, edge, tab_ref, dir_ref, pos_ref, nbr_ref, par_ref, hs_ref, hn_ref, wet_ref, *refs
):
    near, outs, ext_ref = refs[: -shares - 1], refs[-shares - 1 : -1], refs[-1]
    place = pl.program_id(0)
    speed = tab_ref[chunk[0] + chunk[1] * place]
    first = place == 0
    half = ND // 2
    span = half * tiles
    south, north = tiles, ROWS
    pitch = 2 * (2 * tiles + ROWS)

    def rows_at(j, row, count=ROWS):
        return pl.ds(j * pitch + 2 * row, count, stride=2)

    def extend(q, _):
        for t in range(0, tiles, ROWS):
            ext_ref[rows_at(q, t), :] = hs_ref[0, pl.ds(pl.multiple_of(q * tiles + t, ROWS), ROWS), :]
            ext_ref[rows_at(q, south + t), :] = wet_ref[0, q, t : t + ROWS, :]
            ext_ref[rows_at(half + q, north + t), :] = wet_ref[0, half + q, t : t + ROWS, :]
            ext_ref[rows_at(half + q, north + tiles + t), :] = hn_ref[
                0, pl.ds(pl.multiple_of(q * tiles + t, ROWS), ROWS), :
            ]
        return 0

    lax.fori_loop(0, half, extend, 0, unroll=2)
    for q in range(QUART):
        ext_ref[pl.ds((QUART + q) * pitch + 2 * (south + tiles), 1), :] = hn_ref[0, span + q : span + q + 1, :]
        ext_ref[pl.ds((3 * QUART + q) * pitch + 2 * (north - 1), 1), :] = hs_ref[0, span + q : span + q + 1, :]

    side = jnp.where(first, 1.0, -1.0)
    per_share = tiles // shares
    steps = [(d, k) for d in range(shares) for k in range(per_share // ROWS)]
    firsts = {}
    for d, k in steps:
        share = lax.rem(pos_ref[0] + d, shares)
        firsts[d, k] = pl.multiple_of(share * per_share + k * ROWS, ROWS)
    sub = lax.broadcasted_iota(jnp.int32, (ROWS, LANES), 0)
    lanes, rels = {}, {}
    for way in range(4):
        for step in steps:
            src = nbr_ref[way, pl.ds(firsts[step], ROWS), :]
            lanes[way, step] = src & (LANES - 1)
            rels[way, step] = (src >> 7) - (sub + firsts[step])

    def picked(j, own, step, way, offsets):
        out = None
        for r in offsets:
            window = ext_ref[rows_at(j, own + firsts[step] + r), :]
            got = jnp.take_along_axis(window, lanes[way, step], axis=1, mode="promise_in_bounds")
            out = got if out is None else jnp.where(rels[way, step] == r, got, out)
        return out

    for quad in range(4):
        cos_up = quad in (0, 3)
        own, way_y, off_y = (
            (south, 3, range(-(kmax // LANES), -(kmin // LANES) + 1))
            if quad < 2
            else (north, 2, range(kmin // LANES, kmax // LANES + 1))
        )
        way_x, off_x = (1, (-1, 0)) if cos_up else (0, (0, 1))

        def body(q, _):
            j = quad * QUART + q
            jprev = jnp.where(j == 0, ND - 1, j - 1)
            jnext = jnp.where(j == ND - 1, 0, j + 1)
            acos = jnp.abs(dir_ref[0, j])
            asin = jnp.abs(dir_ref[1, j])
            ax, ay = speed * acos, speed * asin
            for step in steps:
                at = pl.ds(firsts[step], ROWS)
                wet = wet_ref[0, j, at, :]
                e_y = picked(j, own, step, way_y, off_y)
                e_x = picked(j, own, step, way_x, off_x)
                rf, fs = par_ref[2, at, :], par_ref[3, at, :]
                e_prev, e_next = wet_ref[0, jprev, at, :], wet_ref[0, jnext, at, :]
                e_t = jnp.where(rf > 0, e_prev, e_next) if cos_up else jnp.where(rf < 0, e_prev, e_next)
                if edge:
                    inner, low, high = (ref[0, j, at, :] for ref in near)
                    outer = jnp.where(first, low, high)
                    e_s = jnp.where(fs * side > 0, outer, inner)
                else:
                    e_s = jnp.where(fs > 0, near[0][0, j, at, :], near[1][0, j, at, :])
                spatial = (par_ref[0, at, :] * ax) * (wet - e_x) + (par_ref[1, at, :] * ay) * (wet - e_y)
                spectral = (jnp.abs(rf) * acos) * (wet - e_t) + (jnp.abs(fs) * speed) * (wet - e_s)
                d, k = step
                outs[d][j, k * ROWS : (k + 1) * ROWS, :] = wet - spatial - spectral
            return 0

        lax.fori_loop(0, QUART, body, 0)


def front(speed, dirs, pos, nbr, par, hs, hn, slot, wet, ends, chunk, shares, kmin, kmax):
    first, step, count = chunk
    tiles = nbr.shape[1]
    nloc = wet.shape[0]
    smem = pl.BlockSpec(memory_space=pltpu.SMEM)

    def freq_spec(start, step):
        return pl.BlockSpec((1, ND, tiles, LANES), lambda i: (start + i * step, 0, 0, 0))

    halo_spec = pl.BlockSpec((1,) + hs.shape[1:], lambda i: (slot + i, 0, 0))

    def whole(shape):
        return pl.BlockSpec(shape, lambda i: (0,) * len(shape))

    if ends:
        near, near_specs = (wet,) + ends, [freq_spec(1, nloc - 3), freq_spec(0, 0), freq_spec(0, 0)]
    else:
        near, near_specs = (wet, wet), [freq_spec(first - 1, step), freq_spec(first + 1, step)]
    rows = tiles // shares
    return pl.pallas_call(
        functools.partial(front_kernel, tiles, shares, kmin, kmax, chunk, bool(ends)),
        grid=(count,),
        out_shape=[jax.ShapeDtypeStruct((count * ND, rows, LANES), jnp.float32)] * shares,
        in_specs=[smem] * 3
        + [whole(nbr.shape), whole(par.shape), halo_spec, halo_spec, freq_spec(first, step)]
        + near_specs,
        out_specs=[pl.BlockSpec((ND, rows, LANES), lambda i: (i, 0, 0))] * shares,
        scratch_shapes=[pltpu.VMEM((ND * 2 * (2 * tiles + ROWS), LANES), jnp.float32)],
        compiler_params=pltpu.CompilerParams(vmem_limit_bytes=VMEM_ASK),
        cost_estimate=pl.CostEstimate(flops=0, bytes_accessed=count * 22_000_000, transcendentals=0),
        name="front",
    )(speed, dirs, pos, nbr, par, hs, hn, wet, *near)


def tail_kernel(nfreq, bins_dev, plan, spot_ref, wts_ref, ftab_ref, frs_ref, dir_ref, pos_ref, wind_ref, mask_ref, *refs):
    out_hbm, mv, base, a0, a1, a2, a3, dw, out_v, in_sem, out_sem = refs[-11:]
    parts = refs[:-11]
    nparts = len(parts)
    shares = nparts // len(plan)
    nbins = nfreq * ND
    loads = []
    block = ND * ROWS
    for c, chunk in enumerate(plan):
        for d in range(shares):
            source = lax.rem(pos_ref[0] + (shares - d), shares)
            for i, f in enumerate(freqs_of(chunk)):
                rows = pl.ds(pl.multiple_of((source * bins_dev + f * ND) * ROWS, ROWS), block)
                part = parts[c * shares + d].at[pl.ds(i * block, block)]
                copy = pltpu.make_async_copy(part, mv.at[rows], in_sem.at[len(loads)])
                copy.start()
                loads.append(copy)
    zero = jnp.zeros((ROWS, LANES), jnp.float32)
    accs = (a0, a1, a2, a3)

    def tile(row):
        return pl.ds(pl.multiple_of(row, ROWS), ROWS)

    def clear(g, _):
        for acc in accs:
            acc[tile(g * ROWS), :] = zero
        return 0

    lax.fori_loop(0, nbins, clear, 0, unroll=8)
    for j in range(ND):
        dw[j] = wind_ref[0] * dir_ref[0, j] + wind_ref[1] * dir_ref[1, j]
    for copy in loads:
        copy.wait()

    def spread(g, shares_of):
        for i in range(GROUP):
            spots = [tile(spot_ref[4 * g + 4 * i + k]) for k in range(4)]
            old = [acc[at, :] for acc, at in zip(accs, spots)]
            for acc, at, was, add in zip(accs, spots, old, shares_of[4 * i : 4 * i + 4]):
                acc[at, :] = was + add

    def per_freq(f, carry):
        fr2, fr4, hspeed = ftab_ref[0, f], ftab_ref[1, f], ftab_ref[2, f]

        def per_group(t, carry):
            total, before = carry
            j0 = t * GROUP
            g0 = f * ND + j0
            own = [mv[tile((g0 + i) * ROWS), :] for i in range(GROUP)]
            found = [[mv[tile(spot_ref[4 * g0 + 4 * i + k]), :] for k in range(4)] for i in range(GROUP)]
            spread(jnp.maximum(g0 - GROUP, 0), before)
            shares_of = []
            for i in range(GROUP):
                m, (p0, p1, m0, m1) = own[i], found[i]
                wp, wm = wts_ref[2 * g0 + 2 * i], wts_ref[2 * g0 + 2 * i + 1]
                ep = p1 + wp * (p0 - p1)
                em = m1 + wm * (m0 - m1)
                mf = fr4 * m
                half = mf * (m * (ep * (1 / 1.25**4) + em * (1 / 0.75**4)) - ep * em * (2.0 / 0.9375**4))
                drive = jnp.maximum(0.0, dw[j0 + i] - hspeed)
                base[tile((g0 + i) * ROWS), :] = m + 0.15 * (drive * drive) * m - 2.0 * half
                sp, sm = wp * half, wm * half
                shares_of += [sp, half - sp, sm, half - sm]
                total = total + m
            return total, tuple(shares_of)

        steep, before = carry
        part, before = lax.fori_loop(0, ND // GROUP, per_group, (zero, before), unroll=3)
        return steep + part * fr2, before

    steep, before = lax.fori_loop(0, nfreq, per_freq, (zero, (zero,) * (4 * GROUP)))
    spread(nbins - GROUP, before)
    steep = steep * (1.0 / nbins)
    mask = mask_ref[...].astype(jnp.float32)
    per = nbins // PIECES
    copies = []
    for p in range(PIECES):

        def finish(t, _):
            g0 = t * ROWS
            done = []
            for i in range(ROWS):
                at = tile((g0 + i) * ROWS)
                mine = base[at, :] - (frs_ref[g0 + i] * steep) * mv[at, :]
                done.append((mine + ((a0[at, :] + a1[at, :]) + (a2[at, :] + a3[at, :]))) * mask)
            turned = jnp.swapaxes(jnp.stack(done, axis=0), 0, 1)
            for c in range(ROWS):
                out_v[pl.ds(pl.multiple_of(g0, ROWS), ROWS), c * LANES : (c + 1) * LANES] = turned[c]
            return 0

        lax.fori_loop(p * per // ROWS, (p + 1) * per // ROWS, finish, 0)
        rows = pl.ds(p * per, per)
        copy = pltpu.make_async_copy(out_v.at[rows], out_hbm.at[rows], out_sem.at[p])
        copy.start()
        copies.append(copy)
    for copy in copies:
        copy.wait()


def tail(parts, plan, bins_dev, dia_bins, dia_wts, ftab, frs, dirs, pos, wind, mask):
    nbins = dia_bins.shape[1]
    nfreq = nbins // ND
    anywhere = pl.BlockSpec(memory_space=pl.ANY)
    smem = pl.BlockSpec(memory_space=pltpu.SMEM)
    vmem = pl.BlockSpec(memory_space=pltpu.VMEM)
    points = ROWS * LANES
    spots = (dia_bins * ROWS).T.reshape(-1)
    wts = dia_wts.T.reshape(-1)
    field = pltpu.VMEM((nbins * ROWS, LANES), jnp.float32)
    return pl.pallas_call(
        functools.partial(tail_kernel, nfreq, bins_dev, plan),
        out_shape=jax.ShapeDtypeStruct((nbins, points), jnp.float32),
        in_specs=[smem] * 6 + [vmem] * 2 + [anywhere] * len(parts),
        out_specs=anywhere,
        scratch_shapes=[field] * 6
        + [
            pltpu.VMEM((ND, ROWS, LANES), jnp.float32),
            pltpu.VMEM((nbins, points), jnp.float32),
            pltpu.SemaphoreType.DMA((nbins // ND,)),
            pltpu.SemaphoreType.DMA((PIECES,)),
        ],
        compiler_params=pltpu.CompilerParams(vmem_limit_bytes=VMEM_ASK),
        cost_estimate=pl.CostEstimate(flops=0, bytes_accessed=70_000_000, transcendentals=0),
        name="tail",
    )(spots, wts, ftab, frs, dirs, pos, wind, mask, *parts)


def fast_on_device(
    spectrum, wind, sea_mask, neighbours, metric_x, metric_y, refraction, freq_shift, dia_bins, dia_wts
):
    bins_dev, points = spectrum.shape
    nbins = dia_bins.shape[1]
    nfreq = nbins // ND
    nloc = bins_dev // ND
    tiles = points // LANES
    shares = lax.axis_size("bin")
    share = points // shares
    bin_pos = lax.axis_index("bin")
    space_pos = lax.axis_index("space")
    plan = chunk_plan(nloc)

    freqs = np.arange(nfreq, dtype=np.float32)
    speed = jnp.asarray(np.exp(-np.log(1.1) * freqs.astype(np.float64)).astype(np.float32))
    ratio = np.exp(np.log(1.1) * (freqs.astype(np.float64) - (nfreq - 1)))
    ftab = jnp.asarray(
        np.stack([ratio**2, 4.0 * ratio**4, 0.5 * np.exp(-np.log(1.1) * freqs)]).astype(np.float32)
    )
    frs = jnp.asarray(np.repeat(3.0 * ratio, ND).astype(np.float32))
    theta = 2.0 * np.pi * (np.arange(ND) + 0.5) / ND
    dirs = jnp.asarray(np.stack([np.cos(theta), np.sin(theta)]).astype(np.float32))
    speed_own = lax.dynamic_slice_in_dim(speed, bin_pos * nloc, nloc, 0)

    groups = halo_groups(plan)
    early = runs_of(slots_of(groups[0]))
    mask_row = sea_mask.reshape(1, points)
    hs, hn, _ = prep(spectrum, mask_row, early, groups[:1], False)
    after, *_ = lax.optimization_barrier((spectrum, hs[0], hn[0]))
    whole_blocks = [(f, min(f + 2, nloc)) for f in range(0, nloc, 2)]
    hs_rest, hn_rest, (wet, low_out, high_out) = prep(after, mask_row, whole_blocks, groups[1:], True)
    wet = wet.reshape(nloc, ND, tiles, LANES)

    def line(array, axis, step):
        peers = lax.axis_size(axis)
        pairs = [(i, i + 1) for i in range(peers - 1)]
        if step < 0:
            pairs = [(b, a) for a, b in pairs]
        return lax.ppermute(array, axis, pairs)

    sends = list(zip(list(hs) + list(hs_rest), list(hn) + list(hn_rest)))
    halos = []

    def send_halos(sent, *after):
        south, north, *_ = lax.optimization_barrier(sent + after) if after else sent
        halos.append((line(south, "space", 1), line(north, "space", -1)))

    send_halos(sends[0])
    low_in = line(low_out, "bin", 1).reshape(1, ND, tiles, LANES)
    high_in = line(high_out, "bin", -1).reshape(1, ND, tiles, LANES)

    nbr = (neighbours - space_pos * points).reshape(4, tiles, LANES)
    par = jnp.stack([metric_x, metric_y, refraction, freq_shift]).reshape(4, tiles, LANES)
    pos = bin_pos.reshape(1)
    kmin, kmax = points // 2, points
    parts = []
    order = pos
    for c, chunk in enumerate(plan):
        first, step, count = chunk
        gi, slot = [(i, slots_of(g)[first]) for i, g in enumerate(groups) if chunk in g][0]
        ends = (low_in, high_in) if first == 0 else None
        blocks = front(speed_own, dirs, order, nbr, par, *halos[gi], slot, wet, ends, chunk, shares, kmin, kmax)
        if c == 0 and len(sends) > 1:
            send_halos(sends[1], blocks[0], low_in, high_in)
        arrived = []
        for d, block in enumerate(blocks):
            rows = block.reshape(-1, LANES)
            if d and parts:
                rows, _ = lax.optimization_barrier((rows, parts[d - shares]))
            pairs = [(i, (i + d) % shares) for i in range(shares)]
            arrived.append(lax.ppermute(rows, "bin", pairs) if d else rows)
        order, *_ = lax.optimization_barrier((pos, blocks[0]) + tuple(parts[-shares:][1:]))
        parts += arrived
    wind_part = lax.dynamic_slice_in_dim(wind, bin_pos * share, share, 1).reshape(2, ROWS, LANES)
    mask_part = lax.dynamic_slice_in_dim(sea_mask, bin_pos * share, share, 0).reshape(ROWS, LANES)
    return tail(parts, plan, bins_dev, dia_bins, dia_wts, ftab, frs, dirs, pos, wind_part, mask_part)


def pick_path(spectrum, *others):
    bins_dev, points = spectrum.shape
    fits = bins_dev % (2 * ND) == ND and bins_dev > ND and points // lax.axis_size("bin") == ROWS * LANES
    return (fast_on_device if fits else on_device)(spectrum, *others)


def solution(mesh):
    return jax.shard_map(
        pick_path,
        mesh=mesh,
        in_specs=(
            P("bin", ("ens", "space")),
            P(None, ("ens", "space")),
            P("space"),
            P(None, "space"),
            P("space"),
            P("space"),
            P("space"),
            P("space"),
            P(),
            P(),
        ),
        out_specs=P(None, ("ens", "space", "bin")),
        check_vma=False,
    )
```

```python
import functools
import itertools

import jax
import jax.numpy as jnp
import numpy as np
from jax import lax
from jax.experimental import pallas as pl
from jax.experimental.pallas import tpu as pltpu
from jax.sharding import PartitionSpec as P

ND = 36


def extended(array, sides, width):
    for axis, dim in sides:
        peers, length = (lax.axis_size(axis), array.shape[dim])
        up = [(i, (i + 1) % peers) for i in range(peers - 1)]
        down = [(j, i) for i, j in up]
        last = lax.slice_in_dim(array, length - width, length, axis=dim)
        initial = lax.slice_in_dim(array, 0, width, axis=dim)
        before = lax.ppermute(last, axis, up)
        after = lax.ppermute(initial, axis, down)
        array = jnp.concatenate([before, array, after], axis=dim)
    return array


def bin_tables(index, nfreq, ndir):
    freq = (index // ndir).astype(jnp.float32)
    direc = index % ndir
    fratio = jnp.exp(jnp.log(1.1) * (freq - (nfreq - 1)))
    speed = jnp.exp(-jnp.log(1.1) * freq)
    theta = 2.0 * jnp.pi * (direc.astype(jnp.float32) + 0.5) / ndir
    return (fratio, speed, jnp.cos(theta), jnp.sin(theta), direc == 0, direc == ndir - 1)


def spatial_term(wet, padded, local, metric_x, metric_y, speed, cosv, sinv):
    east = jnp.take(padded, local[0], axis=1)
    west = jnp.take(padded, local[1], axis=1)
    north = jnp.take(padded, local[2], axis=1)
    south = jnp.take(padded, local[3], axis=1)
    along_x = metric_x[None, :] * (speed * cosv)[:, None]
    along_y = metric_y[None, :] * (speed * sinv)[:, None]
    flux_x = jnp.abs(along_x) * (wet - jnp.where(along_x > 0, west, east))
    flux_y = jnp.abs(along_y) * (wet - jnp.where(along_y > 0, south, north))
    return flux_x + flux_y


def spectral_term(wet, padded, ndir, first, last, refraction, freq_shift, speed, cosv):
    rows = wet.shape[0]

    def moved_rows(offset):
        return lax.slice_in_dim(padded, ndir + offset, ndir + offset + rows, axis=0)

    prev_dir = jnp.where(first[:, None], moved_rows(ndir - 1), moved_rows(-1))
    next_dir = jnp.where(last[:, None], moved_rows(1 - ndir), moved_rows(1))
    lower = moved_rows(-ndir)
    upper = moved_rows(ndir)
    turning = refraction[None, :] * cosv[:, None]
    shifting = freq_shift[None, :] * speed[:, None]
    flux_t = jnp.abs(turning) * (wet - jnp.where(turning > 0, prev_dir, next_dir))
    flux_s = jnp.abs(shifting) * (wet - jnp.where(shifting > 0, lower, upper))
    return flux_t + flux_s


def source_step(
    moved, wind, maskf, fratio, speed, cosv, sinv, plus_fwd, minus_fwd, plus_back, minus_back
):
    steep = jnp.mean(moved * (fratio * fratio)[:, None], axis=0)
    drive = jnp.maximum(
        0.0,
        wind[0][None, :] * cosv[:, None] + wind[1][None, :] * sinv[:, None] - 0.5 * speed[:, None],
    )
    s_in = 0.3 * drive * drive * moved
    s_ds = -6.0 * fratio[:, None] * steep[None, :] * moved
    e_plus = plus_fwd(moved)
    e_minus = minus_fwd(moved)
    delta = (
        8.0
        * (fratio**4)[:, None]
        * (
            moved * moved * (e_plus / 1.25**4 + e_minus / 0.75**4)
            - 2.0 * moved * e_plus * e_minus / 0.9375**4
        )
    )
    s_nl = -2.0 * delta + plus_back(delta) + minus_back(delta)
    return (moved + 0.5 * (s_in + s_ds + s_nl)) * maskf[None, :]


def pair_matrix(first_bins, second_bins, weight, count):
    columns = jnp.arange(count, dtype=jnp.int32)[None, :]
    return weight[:, None] * (first_bins[:, None] == columns).astype(jnp.float32) + (1.0 - weight)[
        :, None
    ] * (second_bins[:, None] == columns).astype(jnp.float32)


def forward_product(matrix, values):
    return jnp.dot(
        matrix, values, precision=lax.Precision.HIGHEST, preferred_element_type=jnp.float32
    )


def backward_product(matrix, values):
    return lax.dot_general(
        matrix,
        values,
        (((0,), (0,)), ((), ())),
        precision=lax.Precision.HIGHEST,
        preferred_element_type=jnp.float32,
    )


def on_device(
    spectrum,
    wind,
    sea_mask,
    neighbours,
    metric_x,
    metric_y,
    refraction,
    freq_shift,
    dia_bins,
    dia_wts,
):
    bins_dev, points_dev = spectrum.shape
    nbins = dia_bins.shape[1]
    ndir = ND
    nfreq = nbins // ndir
    space_pos = lax.axis_index("space")
    bin_pos = lax.axis_index("bin")
    maskf = sea_mask.astype(jnp.float32)
    wet = spectrum * maskf[None, :]
    padded = extended(wet, (("space", 1),), points_dev)
    base = space_pos * points_dev - points_dev
    local = neighbours - base
    own_bins = bin_pos * bins_dev + jnp.arange(bins_dev, dtype=jnp.int32)
    fratio, speed, cosv, sinv, first, last = bin_tables(own_bins, nfreq, ndir)
    spatial = spatial_term(wet, padded, local, metric_x, metric_y, speed, cosv, sinv)
    share = points_dev // lax.axis_size("bin")
    start = bin_pos * share
    all_bins = jnp.arange(nbins, dtype=jnp.int32)
    fratio_all, speed_all, cos_all, sin_all, first_all, last_all = bin_tables(all_bins, nfreq, ndir)
    bin_pad = extended(wet, (("bin", 0),), ndir)
    spectral = spectral_term(wet, bin_pad, ndir, first, last, refraction, freq_shift, speed, cosv)
    moved_own = wet - spatial - spectral
    moved = lax.all_to_all(moved_own, "bin", split_axis=1, concat_axis=0, tiled=True)
    wind_part = lax.dynamic_slice_in_dim(wind, start, share, 1)
    mask_part = lax.dynamic_slice_in_dim(maskf, start, share, 0)
    plus_matrix = pair_matrix(dia_bins[0], dia_bins[1], dia_wts[0], nbins)
    minus_matrix = pair_matrix(dia_bins[2], dia_bins[3], dia_wts[1], nbins)
    result = source_step(
        moved,
        wind_part,
        mask_part,
        fratio_all,
        speed_all,
        cos_all,
        sin_all,
        lambda v: forward_product(plus_matrix, v),
        lambda v: forward_product(minus_matrix, v),
        lambda v: backward_product(plus_matrix, v),
        lambda v: backward_product(minus_matrix, v),
    )
    return result


LANES = 128
ROWS = 8
EDGE = 16
QUART = ND // 4
PIECES = 3
VMEM_ASK = 60 << 20
GROUP = 4


def chunk_plan(nloc):
    mid = nloc // 2
    return [(mid - d, 2 * d, 2) for d in range(1, mid + 1)] + [(mid, 1, 1)]


def freqs_of(chunk):
    first, step, count = chunk
    return [first + i * step for i in range(count)]


def halo_groups(plan):
    return [g for g in (plan[:2], plan[2:]) if g]


def slots_of(group):
    return {f: i for i, f in enumerate(f for chunk in group for f in freqs_of(chunk))}


def runs_of(freqs):
    runs = []
    for f in sorted(freqs):
        if runs and runs[-1][1] == f:
            runs[-1] = (runs[-1][0], f + 1)
        else:
            runs.append((f, f + 1))
    return runs


def prep_kernel(points, bins, blocks, groups, full, spec_hbm, mask_ref, *refs):
    ngr = len(groups)
    nloc = bins // ND
    hs_hbm, hn_hbm = refs[:ngr], refs[ngr : 2 * ngr]
    if full:
        wet_hbm, low_hbm, high_hbm = refs[2 * ngr : 2 * ngr + 3]
    spec_v, wet_v, edge_v, in_sem, out_sem = refs[-5:]
    tiles = points // LANES
    half = ND // 2
    where = {f: (i, k) for i, group in enumerate(groups) for f, k in slots_of(group).items()}
    loads = []
    spans = []
    for lo, hi in blocks:
        start = lo * ND // ROWS * ROWS
        stop = min(-(-hi * ND // ROWS) * ROWS, bins)
        spans.append((start, stop))
        rows = pl.ds(start, stop - start)
        copy = pltpu.make_async_copy(spec_hbm.at[rows], spec_v.at[rows], in_sem.at[len(loads)])
        copy.start()
        loads.append(copy)
    masks = [mask_ref[:, c * LANES : (c + 1) * LANES].astype(jnp.float32) for c in range(tiles)]
    copies = []

    def send(src, dst):
        copy = pltpu.make_async_copy(src, dst, out_sem.at[len(copies)])
        copy.start()
        copies.append(copy)

    for (lo, hi), (start, stop), load in zip(blocks, spans, loads):
        load.wait()

        def turn(g0, count):
            for c0 in range(0, tiles, ROWS):
                cols = range(c0, c0 + ROWS)
                block = jnp.stack(
                    [spec_v[pl.ds(g0, count), c * LANES : (c + 1) * LANES] * masks[c] for c in cols], axis=0
                )
                block = jnp.swapaxes(block, 0, 1)
                for i in range(count):
                    wet_v[pl.ds(pl.multiple_of((g0 + i) * tiles + c0, ROWS), ROWS), :] = block[i]

        def relayout(t, _):
            turn(pl.multiple_of(start + t * ROWS, ROWS), ROWS)
            return 0

        lax.fori_loop(0, (stop - start) // ROWS, relayout, 0)
        rest = (stop - start) % ROWS
        if rest:
            g0 = stop - rest
            for c in range(tiles):
                tile = spec_v[pl.ds(g0, rest), c * LANES : (c + 1) * LANES]
                wet_v[pl.ds(g0 * tiles + c, rest, stride=tiles), :] = tile * masks[c]
        for f in range(lo, hi):
            base = f * ND * tiles
            if f in where:
                i, k = where[f]
                for side, (j0, row) in enumerate(((3 * QUART, tiles - 1), (QUART, 0))):
                    at = base + j0 * tiles + row
                    edge_v[f, side, ROWS:EDGE, :] = jnp.zeros((EDGE - ROWS, LANES), jnp.float32)
                    edge_v[f, side, 0:ROWS, :] = wet_v[pl.ds(at, ROWS, stride=tiles), :]
                    edge_v[f, side, ROWS : ROWS + 1, :] = wet_v[pl.ds(at + ROWS * tiles, 1), :]
                span = half * tiles
                send(wet_v.at[pl.ds(base, span)], hs_hbm[i].at[k, pl.ds(0, span)])
                send(wet_v.at[pl.ds(base + span, span)], hn_hbm[i].at[k, pl.ds(0, span)])
                send(edge_v.at[f, 0], hs_hbm[i].at[k, pl.ds(span, EDGE)])
                send(edge_v.at[f, 1], hn_hbm[i].at[k, pl.ds(span, EDGE)])
            if full:
                own = pl.ds(base, ND * tiles)
                if f == nloc - 1:
                    send(wet_v.at[own], low_hbm)
                if f == 0:
                    send(wet_v.at[own], high_hbm)
                send(wet_v.at[own], wet_hbm.at[own])
    for copy in copies:
        copy.wait()


def prep(spectrum, mask, blocks, groups, full):
    bins, points = spectrum.shape
    nloc = bins // ND
    tiles = points // LANES
    halo_rows = ND // 2 * tiles + EDGE
    halos = [jax.ShapeDtypeStruct((len(slots_of(g)), halo_rows, LANES), jnp.float32) for g in groups]
    one = jax.ShapeDtypeStruct((ND * tiles, LANES), jnp.float32)
    outs = halos + halos
    if full:
        outs += [jax.ShapeDtypeStruct((bins * tiles, LANES), jnp.float32), one, one]
    anywhere = pl.BlockSpec(memory_space=pl.ANY)
    count = sum(hi - lo for lo, hi in blocks)
    sends = 4 * sum(len(slots_of(g)) for g in groups) + (nloc + 2 if full else 0)
    res = pl.pallas_call(
        functools.partial(prep_kernel, points, bins, blocks, groups, full),
        out_shape=outs,
        in_specs=[anywhere, pl.BlockSpec(memory_space=pltpu.VMEM)],
        out_specs=[anywhere] * len(outs),
        scratch_shapes=[
            pltpu.VMEM((bins, points), jnp.float32),
            pltpu.VMEM((bins * tiles, LANES), jnp.float32),
            pltpu.VMEM((nloc, 2, EDGE, LANES), jnp.float32),
            pltpu.SemaphoreType.DMA((len(blocks),)),
            pltpu.SemaphoreType.DMA((sends,)),
        ],
        compiler_params=pltpu.CompilerParams(vmem_limit_bytes=VMEM_ASK),
        cost_estimate=pl.CostEstimate(flops=0, bytes_accessed=count * 3_000_000, transcendentals=0),
        name="prep",
    )(spectrum, mask)
    ngr = len(groups)
    return res[:ngr], res[ngr : 2 * ngr], res[2 * ngr :]


def front_kernel(
    tiles, shares, kmin, kmax, chunk, edge, joined, tab_ref, dir_ref, pos_ref, nbr_ref, par_ref, hs_ref, hn_ref, wet_ref, *refs
):
    nout = 1 if joined else shares
    near, outs, ext_ref = refs[: -nout - 1], refs[-nout - 1 : -1], refs[-1]
    if joined:
        outs = [outs[0].at[d] for d in range(shares)]
    place = pl.program_id(0)
    speed = tab_ref[chunk[0] + chunk[1] * place]
    first = place == 0
    half = ND // 2
    span = half * tiles
    south, north = tiles, ROWS
    pitch = 2 * (2 * tiles + ROWS)

    def rows_at(j, row, count=ROWS):
        return pl.ds(j * pitch + 2 * row, count, stride=2)

    def extend(q, _):
        for t in range(0, tiles, ROWS):
            ext_ref[rows_at(q, t), :] = hs_ref[0, pl.ds(pl.multiple_of(q * tiles + t, ROWS), ROWS), :]
            ext_ref[rows_at(q, south + t), :] = wet_ref[0, q, t : t + ROWS, :]
            ext_ref[rows_at(half + q, north + t), :] = wet_ref[0, half + q, t : t + ROWS, :]
            ext_ref[rows_at(half + q, north + tiles + t), :] = hn_ref[
                0, pl.ds(pl.multiple_of(q * tiles + t, ROWS), ROWS), :
            ]
        return 0

    lax.fori_loop(0, half, extend, 0, unroll=2)
    for q in range(QUART):
        ext_ref[pl.ds((QUART + q) * pitch + 2 * (south + tiles), 1), :] = hn_ref[0, span + q : span + q + 1, :]
        ext_ref[pl.ds((3 * QUART + q) * pitch + 2 * (north - 1), 1), :] = hs_ref[0, span + q : span + q + 1, :]

    side = jnp.where(first, 1.0, -1.0)
    per_share = tiles // shares
    steps = [(d, k) for d in range(shares) for k in range(per_share // ROWS)]
    firsts = {}
    for d, k in steps:
        share = d if joined else lax.rem(pos_ref[0] + d, shares)
        row = share * per_share + k * ROWS
        firsts[d, k] = row if joined else pl.multiple_of(row, ROWS)
    sub = lax.broadcasted_iota(jnp.int32, (ROWS, LANES), 0)
    lanes, rels = {}, {}
    for way in range(4):
        for step in steps:
            src = nbr_ref[way, pl.ds(firsts[step], ROWS), :]
            lanes[way, step] = src & (LANES - 1)
            rels[way, step] = (src >> 7) - (sub + firsts[step])

    def picked(j, own, step, way, offsets):
        out = None
        for r in offsets:
            window = ext_ref[rows_at(j, own + firsts[step] + r), :]
            got = jnp.take_along_axis(window, lanes[way, step], axis=1, mode="promise_in_bounds")
            out = got if out is None else jnp.where(rels[way, step] == r, got, out)
        return out

    for quad in range(4):
        cos_up = quad in (0, 3)
        own, way_y, off_y = (
            (south, 3, range(-(kmax // LANES), -(kmin // LANES) + 1))
            if quad < 2
            else (north, 2, range(kmin // LANES, kmax // LANES + 1))
        )
        way_x, off_x = (1, (-1, 0)) if cos_up else (0, (0, 1))

        def body(q, _):
            j = quad * QUART + q
            jprev = jnp.where(j == 0, ND - 1, j - 1)
            jnext = jnp.where(j == ND - 1, 0, j + 1)
            acos = jnp.abs(dir_ref[0, j])
            asin = jnp.abs(dir_ref[1, j])
            ax, ay = speed * acos, speed * asin
            for step in steps:
                at = pl.ds(firsts[step], ROWS)
                wet = wet_ref[0, j, at, :]
                e_y = picked(j, own, step, way_y, off_y)
                e_x = picked(j, own, step, way_x, off_x)
                rf, fs = par_ref[2, at, :], par_ref[3, at, :]
                e_prev, e_next = wet_ref[0, jprev, at, :], wet_ref[0, jnext, at, :]
                e_t = jnp.where(rf > 0, e_prev, e_next) if cos_up else jnp.where(rf < 0, e_prev, e_next)
                if edge:
                    inner, low, high = (ref[0, j, at, :] for ref in near)
                    outer = jnp.where(first, low, high)
                    e_s = jnp.where(fs * side > 0, outer, inner)
                else:
                    e_s = jnp.where(fs > 0, near[0][0, j, at, :], near[1][0, j, at, :])
                spatial = (par_ref[0, at, :] * ax) * (wet - e_x) + (par_ref[1, at, :] * ay) * (wet - e_y)
                spectral = (jnp.abs(rf) * acos) * (wet - e_t) + (jnp.abs(fs) * speed) * (wet - e_s)
                d, k = step
                outs[d][j, k * ROWS : (k + 1) * ROWS, :] = wet - spatial - spectral
            return 0

        lax.fori_loop(0, QUART, body, 0)


def front(speed, dirs, pos, nbr, par, hs, hn, slot, wet, ends, chunk, joined, shares, kmin, kmax):
    first, step, count = chunk
    tiles = nbr.shape[1]
    nloc = wet.shape[0]
    smem = pl.BlockSpec(memory_space=pltpu.SMEM)

    def freq_spec(start, step):
        return pl.BlockSpec((1, ND, tiles, LANES), lambda i: (start + i * step, 0, 0, 0))

    halo_spec = pl.BlockSpec((1,) + hs.shape[1:], lambda i: (slot + i, 0, 0))

    def whole(shape):
        return pl.BlockSpec(shape, lambda i: (0,) * len(shape))

    if ends:
        near, near_specs = (wet,) + ends, [freq_spec(1, nloc - 3), freq_spec(0, 0), freq_spec(0, 0)]
    else:
        near, near_specs = (wet, wet), [freq_spec(first - 1, step), freq_spec(first + 1, step)]
    rows = tiles // shares
    if joined:
        outs = [jax.ShapeDtypeStruct((shares, count * ND, rows, LANES), jnp.float32)]
        out_specs = [pl.BlockSpec((shares, ND, rows, LANES), lambda i: (0, i, 0, 0))]
    else:
        outs = [jax.ShapeDtypeStruct((count * ND, rows, LANES), jnp.float32)] * shares
        out_specs = [pl.BlockSpec((ND, rows, LANES), lambda i: (i, 0, 0))] * shares
    return pl.pallas_call(
        functools.partial(front_kernel, tiles, shares, kmin, kmax, chunk, bool(ends), joined),
        grid=(count,),
        out_shape=outs,
        in_specs=[smem] * 3
        + [whole(nbr.shape), whole(par.shape), halo_spec, halo_spec, freq_spec(first, step)]
        + near_specs,
        out_specs=out_specs,
        scratch_shapes=[pltpu.VMEM((ND * 2 * (2 * tiles + ROWS), LANES), jnp.float32)],
        compiler_params=pltpu.CompilerParams(vmem_limit_bytes=VMEM_ASK),
        cost_estimate=pl.CostEstimate(flops=0, bytes_accessed=count * 22_000_000, transcendentals=0),
        name="front",
    )(speed, dirs, pos, nbr, par, hs, hn, wet, *near)


def tail_kernel(nfreq, bins_dev, plan, spot_ref, wts_ref, ftab_ref, frs_ref, dir_ref, pos_ref, wind_ref, mask_ref, *refs):
    out_hbm, mv, base, a0, a1, a2, a3, dw, out_v, in_sem, out_sem = refs[-11:]
    parts = iter(refs[:-11])
    shares = nfreq * ND // bins_dev
    nbins = nfreq * ND
    loads = []
    block = ND * ROWS
    for chunk, joined in plan:
        whole = next(parts) if joined else None
        for d in range(shares):
            part = whole.at[d] if joined else next(parts)
            source = d if joined else lax.rem(pos_ref[0] + (shares - d), shares)
            for i, f in enumerate(freqs_of(chunk)):
                rows = pl.ds(pl.multiple_of((source * bins_dev + f * ND) * ROWS, ROWS), block)
                copy = pltpu.make_async_copy(part.at[pl.ds(i * block, block)], mv.at[rows], in_sem.at[len(loads)])
                copy.start()
                loads.append(copy)
    zero = jnp.zeros((ROWS, LANES), jnp.float32)
    accs = (a0, a1, a2, a3)

    def tile(row):
        return pl.ds(pl.multiple_of(row, ROWS), ROWS)

    def clear(g, _):
        for acc in accs:
            acc[tile(g * ROWS), :] = zero
        return 0

    lax.fori_loop(0, nbins, clear, 0, unroll=8)
    for j in range(ND):
        dw[j] = wind_ref[0] * dir_ref[0, j] + wind_ref[1] * dir_ref[1, j]
    for copy in loads:
        copy.wait()

    def spread(g, shares_of):
        for i in range(GROUP):
            spots = [tile(spot_ref[4 * g + 4 * i + k]) for k in range(4)]
            old = [acc[at, :] for acc, at in zip(accs, spots)]
            for acc, at, was, add in zip(accs, spots, old, shares_of[4 * i : 4 * i + 4]):
                acc[at, :] = was + add

    def per_freq(f, carry):
        fr2, fr4, hspeed = ftab_ref[0, f], ftab_ref[1, f], ftab_ref[2, f]

        def per_group(t, carry):
            total, before = carry
            j0 = t * GROUP
            g0 = f * ND + j0
            own = [mv[tile((g0 + i) * ROWS), :] for i in range(GROUP)]
            found = [[mv[tile(spot_ref[4 * g0 + 4 * i + k]), :] for k in range(4)] for i in range(GROUP)]
            spread(jnp.maximum(g0 - GROUP, 0), before)
            shares_of = []
            for i in range(GROUP):
                m, (p0, p1, m0, m1) = own[i], found[i]
                wp, wm = wts_ref[2 * g0 + 2 * i], wts_ref[2 * g0 + 2 * i + 1]
                ep = p1 + wp * (p0 - p1)
                em = m1 + wm * (m0 - m1)
                mf = fr4 * m
                half = mf * (m * (ep * (1 / 1.25**4) + em * (1 / 0.75**4)) - ep * em * (2.0 / 0.9375**4))
                drive = jnp.maximum(0.0, dw[j0 + i] - hspeed)
                base[tile((g0 + i) * ROWS), :] = m + 0.15 * (drive * drive) * m - 2.0 * half
                sp, sm = wp * half, wm * half
                shares_of += [sp, half - sp, sm, half - sm]
                total = total + m
            return total, tuple(shares_of)

        steep, before = carry
        part, before = lax.fori_loop(0, ND // GROUP, per_group, (zero, before), unroll=3)
        return steep + part * fr2, before

    steep, before = lax.fori_loop(0, nfreq, per_freq, (zero, (zero,) * (4 * GROUP)))
    spread(nbins - GROUP, before)
    steep = steep * (1.0 / nbins)
    mask = mask_ref[...].astype(jnp.float32)
    per = nbins // PIECES
    copies = []
    for p in range(PIECES):

        def finish(t, _):
            g0 = t * ROWS
            done = []
            for i in range(ROWS):
                at = tile((g0 + i) * ROWS)
                mine = base[at, :] - (frs_ref[g0 + i] * steep) * mv[at, :]
                done.append((mine + ((a0[at, :] + a1[at, :]) + (a2[at, :] + a3[at, :]))) * mask)
            turned = jnp.swapaxes(jnp.stack(done, axis=0), 0, 1)
            for c in range(ROWS):
                out_v[pl.ds(pl.multiple_of(g0, ROWS), ROWS), c * LANES : (c + 1) * LANES] = turned[c]
            return 0

        lax.fori_loop(p * per // ROWS, (p + 1) * per // ROWS, finish, 0)
        rows = pl.ds(p * per, per)
        copy = pltpu.make_async_copy(out_v.at[rows], out_hbm.at[rows], out_sem.at[p])
        copy.start()
        copies.append(copy)
    for copy in copies:
        copy.wait()


def tail(parts, plan, bins_dev, dia_bins, dia_wts, ftab, frs, dirs, pos, wind, mask):
    nbins = dia_bins.shape[1]
    nfreq = nbins // ND
    anywhere = pl.BlockSpec(memory_space=pl.ANY)
    smem = pl.BlockSpec(memory_space=pltpu.SMEM)
    vmem = pl.BlockSpec(memory_space=pltpu.VMEM)
    points = ROWS * LANES
    spots = (dia_bins * ROWS).T.reshape(-1)
    wts = dia_wts.T.reshape(-1)
    field = pltpu.VMEM((nbins * ROWS, LANES), jnp.float32)
    return pl.pallas_call(
        functools.partial(tail_kernel, nfreq, bins_dev, plan),
        out_shape=jax.ShapeDtypeStruct((nbins, points), jnp.float32),
        in_specs=[smem] * 6 + [vmem] * 2 + [anywhere] * len(parts),
        out_specs=anywhere,
        scratch_shapes=[field] * 6
        + [
            pltpu.VMEM((ND, ROWS, LANES), jnp.float32),
            pltpu.VMEM((nbins, points), jnp.float32),
            pltpu.SemaphoreType.DMA((nbins // ND,)),
            pltpu.SemaphoreType.DMA((PIECES,)),
        ],
        compiler_params=pltpu.CompilerParams(vmem_limit_bytes=VMEM_ASK),
        cost_estimate=pl.CostEstimate(flops=0, bytes_accessed=70_000_000, transcendentals=0),
        name="tail",
    )(spots, wts, ftab, frs, dirs, pos, wind, mask, *parts)


def fast_on_device(
    spectrum, wind, sea_mask, neighbours, metric_x, metric_y, refraction, freq_shift, dia_bins, dia_wts
):
    bins_dev, points = spectrum.shape
    nbins = dia_bins.shape[1]
    nfreq = nbins // ND
    nloc = bins_dev // ND
    tiles = points // LANES
    shares = lax.axis_size("bin")
    share = points // shares
    bin_pos = lax.axis_index("bin")
    space_pos = lax.axis_index("space")
    plan = chunk_plan(nloc)

    freqs = np.arange(nfreq, dtype=np.float32)
    speed = jnp.asarray(np.exp(-np.log(1.1) * freqs.astype(np.float64)).astype(np.float32))
    ratio = np.exp(np.log(1.1) * (freqs.astype(np.float64) - (nfreq - 1)))
    ftab = jnp.asarray(
        np.stack([ratio**2, 4.0 * ratio**4, 0.5 * np.exp(-np.log(1.1) * freqs)]).astype(np.float32)
    )
    frs = jnp.asarray(np.repeat(3.0 * ratio, ND).astype(np.float32))
    theta = 2.0 * np.pi * (np.arange(ND) + 0.5) / ND
    dirs = jnp.asarray(np.stack([np.cos(theta), np.sin(theta)]).astype(np.float32))
    speed_own = lax.dynamic_slice_in_dim(speed, bin_pos * nloc, nloc, 0)

    groups = halo_groups(plan)
    early = runs_of(slots_of(groups[0]))
    mask_row = sea_mask.reshape(1, points)
    hs, hn, _ = prep(spectrum, mask_row, early, groups[:1], False)
    after, *_ = lax.optimization_barrier((spectrum, hs[0], hn[0]))
    whole_blocks = [(f, min(f + 2, nloc)) for f in range(0, nloc, 2)]
    hs_rest, hn_rest, (wet, low_out, high_out) = prep(after, mask_row, whole_blocks, groups[1:], True)
    wet = wet.reshape(nloc, ND, tiles, LANES)

    def line(array, axis, step):
        peers = lax.axis_size(axis)
        pairs = [(i, i + 1) for i in range(peers - 1)]
        if step < 0:
            pairs = [(b, a) for a, b in pairs]
        return lax.ppermute(array, axis, pairs)

    halos = []
    for south, north in zip(list(hs) + list(hs_rest), list(hn) + list(hn_rest)):
        if halos:
            south, north, *_ = lax.optimization_barrier((south, north) + halos[-1])
        halos.append((line(south, "space", 1), line(north, "space", -1)))
    low_in = line(low_out, "bin", 1).reshape(1, ND, tiles, LANES)
    high_in = line(high_out, "bin", -1).reshape(1, ND, tiles, LANES)

    nbr = (neighbours - space_pos * points).reshape(4, tiles, LANES)
    par = jnp.stack([metric_x, metric_y, refraction, freq_shift]).reshape(4, tiles, LANES)
    pos = bin_pos.reshape(1)
    kmin, kmax = points // 2, points
    arrived = []
    order = pos
    ways = [c % 2 == 1 for c in range(len(plan))]
    for c, (chunk, joined) in enumerate(zip(plan, ways)):
        first, step, count = chunk
        gi, slot = [(i, slots_of(g)[first]) for i, g in enumerate(groups) if chunk in g][0]
        ends = (low_in, high_in) if first == 0 else None
        blocks = front(speed_own, dirs, order, nbr, par, *halos[gi], slot, wet, ends, chunk, joined, shares, kmin, kmax)
        blocks = [block.reshape(block.shape[: int(joined)] + (-1, LANES)) for block in blocks]
        earlier = (low_in, high_in) + sum(halos, ()) if c == 0 else tuple(arrived[c - 1])
        order, *_ = lax.optimization_barrier((pos, blocks[0]) + earlier)
        if joined:
            arrived.append([lax.all_to_all(blocks[0], "bin", split_axis=0, concat_axis=0, tiled=True)])
        else:
            pairs = [[(i, (i + d) % shares) for i in range(shares)] for d in range(shares)]
            arrived.append([lax.ppermute(rows, "bin", pairs[d]) if d else rows for d, rows in enumerate(blocks)])
    parts = sum(arrived, [])
    wind_part = lax.dynamic_slice_in_dim(wind, bin_pos * share, share, 1).reshape(2, ROWS, LANES)
    mask_part = lax.dynamic_slice_in_dim(sea_mask, bin_pos * share, share, 0).reshape(ROWS, LANES)
    return tail(parts, list(zip(plan, ways)), bins_dev, dia_bins, dia_wts, ftab, frs, dirs, pos, wind_part, mask_part)


def pick_path(spectrum, *others):
    bins_dev, points = spectrum.shape
    fits = bins_dev % (2 * ND) == ND and bins_dev > ND and points // lax.axis_size("bin") == ROWS * LANES
    return (fast_on_device if fits else on_device)(spectrum, *others)


def solution(mesh):
    return jax.shard_map(
        pick_path,
        mesh=mesh,
        in_specs=(
            P("bin", ("ens", "space")),
            P(None, ("ens", "space")),
            P("space"),
            P(None, "space"),
            P("space"),
            P("space"),
            P("space"),
            P("space"),
            P(),
            P(),
        ),
        out_specs=P(None, ("ens", "space", "bin")),
        check_vma=False,
    )
```

```python
import functools
import itertools

import jax
import jax.numpy as jnp
import numpy as np
from jax import lax
from jax.experimental import pallas as pl
from jax.experimental.pallas import tpu as pltpu
from jax.sharding import PartitionSpec as P

ND = 36


def extended(array, sides, width):
    for axis, dim in sides:
        peers, length = (lax.axis_size(axis), array.shape[dim])
        up = [(i, (i + 1) % peers) for i in range(peers - 1)]
        down = [(j, i) for i, j in up]
        last = lax.slice_in_dim(array, length - width, length, axis=dim)
        initial = lax.slice_in_dim(array, 0, width, axis=dim)
        before = lax.ppermute(last, axis, up)
        after = lax.ppermute(initial, axis, down)
        array = jnp.concatenate([before, array, after], axis=dim)
    return array


def bin_tables(index, nfreq, ndir):
    freq = (index // ndir).astype(jnp.float32)
    direc = index % ndir
    fratio = jnp.exp(jnp.log(1.1) * (freq - (nfreq - 1)))
    speed = jnp.exp(-jnp.log(1.1) * freq)
    theta = 2.0 * jnp.pi * (direc.astype(jnp.float32) + 0.5) / ndir
    return (fratio, speed, jnp.cos(theta), jnp.sin(theta), direc == 0, direc == ndir - 1)


def spatial_term(wet, padded, local, metric_x, metric_y, speed, cosv, sinv):
    east = jnp.take(padded, local[0], axis=1)
    west = jnp.take(padded, local[1], axis=1)
    north = jnp.take(padded, local[2], axis=1)
    south = jnp.take(padded, local[3], axis=1)
    along_x = metric_x[None, :] * (speed * cosv)[:, None]
    along_y = metric_y[None, :] * (speed * sinv)[:, None]
    flux_x = jnp.abs(along_x) * (wet - jnp.where(along_x > 0, west, east))
    flux_y = jnp.abs(along_y) * (wet - jnp.where(along_y > 0, south, north))
    return flux_x + flux_y


def spectral_term(wet, padded, ndir, first, last, refraction, freq_shift, speed, cosv):
    rows = wet.shape[0]

    def moved_rows(offset):
        return lax.slice_in_dim(padded, ndir + offset, ndir + offset + rows, axis=0)

    prev_dir = jnp.where(first[:, None], moved_rows(ndir - 1), moved_rows(-1))
    next_dir = jnp.where(last[:, None], moved_rows(1 - ndir), moved_rows(1))
    lower = moved_rows(-ndir)
    upper = moved_rows(ndir)
    turning = refraction[None, :] * cosv[:, None]
    shifting = freq_shift[None, :] * speed[:, None]
    flux_t = jnp.abs(turning) * (wet - jnp.where(turning > 0, prev_dir, next_dir))
    flux_s = jnp.abs(shifting) * (wet - jnp.where(shifting > 0, lower, upper))
    return flux_t + flux_s


def source_step(
    moved, wind, maskf, fratio, speed, cosv, sinv, plus_fwd, minus_fwd, plus_back, minus_back
):
    steep = jnp.mean(moved * (fratio * fratio)[:, None], axis=0)
    drive = jnp.maximum(
        0.0,
        wind[0][None, :] * cosv[:, None] + wind[1][None, :] * sinv[:, None] - 0.5 * speed[:, None],
    )
    s_in = 0.3 * drive * drive * moved
    s_ds = -6.0 * fratio[:, None] * steep[None, :] * moved
    e_plus = plus_fwd(moved)
    e_minus = minus_fwd(moved)
    delta = (
        8.0
        * (fratio**4)[:, None]
        * (
            moved * moved * (e_plus / 1.25**4 + e_minus / 0.75**4)
            - 2.0 * moved * e_plus * e_minus / 0.9375**4
        )
    )
    s_nl = -2.0 * delta + plus_back(delta) + minus_back(delta)
    return (moved + 0.5 * (s_in + s_ds + s_nl)) * maskf[None, :]


def pair_matrix(first_bins, second_bins, weight, count):
    columns = jnp.arange(count, dtype=jnp.int32)[None, :]
    return weight[:, None] * (first_bins[:, None] == columns).astype(jnp.float32) + (1.0 - weight)[
        :, None
    ] * (second_bins[:, None] == columns).astype(jnp.float32)


def forward_product(matrix, values):
    return jnp.dot(
        matrix, values, precision=lax.Precision.HIGHEST, preferred_element_type=jnp.float32
    )


def backward_product(matrix, values):
    return lax.dot_general(
        matrix,
        values,
        (((0,), (0,)), ((), ())),
        precision=lax.Precision.HIGHEST,
        preferred_element_type=jnp.float32,
    )


def on_device(
    spectrum,
    wind,
    sea_mask,
    neighbours,
    metric_x,
    metric_y,
    refraction,
    freq_shift,
    dia_bins,
    dia_wts,
):
    bins_dev, points_dev = spectrum.shape
    nbins = dia_bins.shape[1]
    ndir = ND
    nfreq = nbins // ndir
    space_pos = lax.axis_index("space")
    bin_pos = lax.axis_index("bin")
    maskf = sea_mask.astype(jnp.float32)
    wet = spectrum * maskf[None, :]
    padded = extended(wet, (("space", 1),), points_dev)
    base = space_pos * points_dev - points_dev
    local = neighbours - base
    own_bins = bin_pos * bins_dev + jnp.arange(bins_dev, dtype=jnp.int32)
    fratio, speed, cosv, sinv, first, last = bin_tables(own_bins, nfreq, ndir)
    spatial = spatial_term(wet, padded, local, metric_x, metric_y, speed, cosv, sinv)
    share = points_dev // lax.axis_size("bin")
    start = bin_pos * share
    all_bins = jnp.arange(nbins, dtype=jnp.int32)
    fratio_all, speed_all, cos_all, sin_all, first_all, last_all = bin_tables(all_bins, nfreq, ndir)
    bin_pad = extended(wet, (("bin", 0),), ndir)
    spectral = spectral_term(wet, bin_pad, ndir, first, last, refraction, freq_shift, speed, cosv)
    moved_own = wet - spatial - spectral
    moved = lax.all_to_all(moved_own, "bin", split_axis=1, concat_axis=0, tiled=True)
    wind_part = lax.dynamic_slice_in_dim(wind, start, share, 1)
    mask_part = lax.dynamic_slice_in_dim(maskf, start, share, 0)
    plus_matrix = pair_matrix(dia_bins[0], dia_bins[1], dia_wts[0], nbins)
    minus_matrix = pair_matrix(dia_bins[2], dia_bins[3], dia_wts[1], nbins)
    result = source_step(
        moved,
        wind_part,
        mask_part,
        fratio_all,
        speed_all,
        cos_all,
        sin_all,
        lambda v: forward_product(plus_matrix, v),
        lambda v: forward_product(minus_matrix, v),
        lambda v: backward_product(plus_matrix, v),
        lambda v: backward_product(minus_matrix, v),
    )
    return result


LANES = 128
ROWS = 8
EDGE = 16
QUART = ND // 4
PIECES = 3
VMEM_ASK = 60 << 20
GROUP = 4


def chunk_plan(nloc):
    mid = nloc // 2
    plan = [(mid - d, 2 * d, 2) for d in range(1, mid + 1)]
    if mid > 3:
        plan[2] = (mid - 3, 3, 3)
    else:
        plan.insert(0, (mid, 1, 1))
    return plan


def freqs_of(chunk):
    first, step, count = chunk
    return [first + i * step for i in range(count)]


def halo_groups(plan):
    return [g for g in (plan[:1], plan[1:]) if g]


def slots_of(group):
    return {f: i for i, f in enumerate(f for chunk in group for f in freqs_of(chunk))}


def runs_of(freqs):
    runs = []
    for f in sorted(freqs):
        if runs and runs[-1][1] == f:
            runs[-1] = (runs[-1][0], f + 1)
        else:
            runs.append((f, f + 1))
    return runs


def prep_kernel(points, bins, blocks, groups, full, spec_hbm, mask_ref, *refs):
    ngr = len(groups)
    nloc = bins // ND
    hs_hbm, hn_hbm = refs[:ngr], refs[ngr : 2 * ngr]
    if full:
        wet_hbm, low_hbm, high_hbm = refs[2 * ngr : 2 * ngr + 3]
    spec_v, wet_v, edge_v, in_sem, out_sem = refs[-5:]
    tiles = points // LANES
    half = ND // 2
    where = {f: (i, k) for i, group in enumerate(groups) for f, k in slots_of(group).items()}
    loads = []
    spans = []
    for lo, hi in blocks:
        start = lo * ND // ROWS * ROWS
        stop = min(-(-hi * ND // ROWS) * ROWS, bins)
        spans.append((start, stop))
        rows = pl.ds(start, stop - start)
        copy = pltpu.make_async_copy(spec_hbm.at[rows], spec_v.at[rows], in_sem.at[len(loads)])
        copy.start()
        loads.append(copy)
    masks = [mask_ref[:, c * LANES : (c + 1) * LANES].astype(jnp.float32) for c in range(tiles)]
    copies = []

    def send(src, dst):
        copy = pltpu.make_async_copy(src, dst, out_sem.at[len(copies)])
        copy.start()
        copies.append(copy)

    for (lo, hi), (start, stop), load in zip(blocks, spans, loads):
        load.wait()

        def turn(g0, count):
            for c0 in range(0, tiles, ROWS):
                cols = range(c0, c0 + ROWS)
                block = jnp.stack(
                    [spec_v[pl.ds(g0, count), c * LANES : (c + 1) * LANES] * masks[c] for c in cols], axis=0
                )
                block = jnp.swapaxes(block, 0, 1)
                for i in range(count):
                    wet_v[pl.ds(pl.multiple_of((g0 + i) * tiles + c0, ROWS), ROWS), :] = block[i]

        def relayout(t, _):
            turn(pl.multiple_of(start + t * ROWS, ROWS), ROWS)
            return 0

        lax.fori_loop(0, (stop - start) // ROWS, relayout, 0)
        rest = (stop - start) % ROWS
        if rest:
            g0 = stop - rest
            for c in range(tiles):
                tile = spec_v[pl.ds(g0, rest), c * LANES : (c + 1) * LANES]
                wet_v[pl.ds(g0 * tiles + c, rest, stride=tiles), :] = tile * masks[c]
        for f in range(lo, hi):
            base = f * ND * tiles
            if f in where:
                i, k = where[f]
                for side, (j0, row) in enumerate(((3 * QUART, tiles - 1), (QUART, 0))):
                    at = base + j0 * tiles + row
                    edge_v[f, side, ROWS:EDGE, :] = jnp.zeros((EDGE - ROWS, LANES), jnp.float32)
                    edge_v[f, side, 0:ROWS, :] = wet_v[pl.ds(at, ROWS, stride=tiles), :]
                    edge_v[f, side, ROWS : ROWS + 1, :] = wet_v[pl.ds(at + ROWS * tiles, 1), :]
                span = half * tiles
                send(wet_v.at[pl.ds(base, span)], hs_hbm[i].at[k, pl.ds(0, span)])
                send(wet_v.at[pl.ds(base + span, span)], hn_hbm[i].at[k, pl.ds(0, span)])
                send(edge_v.at[f, 0], hs_hbm[i].at[k, pl.ds(span, EDGE)])
                send(edge_v.at[f, 1], hn_hbm[i].at[k, pl.ds(span, EDGE)])
            if full:
                own = pl.ds(base, ND * tiles)
                if f == nloc - 1:
                    send(wet_v.at[own], low_hbm)
                if f == 0:
                    send(wet_v.at[own], high_hbm)
                send(wet_v.at[own], wet_hbm.at[own])
    for copy in copies:
        copy.wait()


def prep(spectrum, mask, blocks, groups, full):
    bins, points = spectrum.shape
    nloc = bins // ND
    tiles = points // LANES
    halo_rows = ND // 2 * tiles + EDGE
    halos = [jax.ShapeDtypeStruct((len(slots_of(g)), halo_rows, LANES), jnp.float32) for g in groups]
    one = jax.ShapeDtypeStruct((ND * tiles, LANES), jnp.float32)
    outs = halos + halos
    if full:
        outs += [jax.ShapeDtypeStruct((bins * tiles, LANES), jnp.float32), one, one]
    anywhere = pl.BlockSpec(memory_space=pl.ANY)
    count = sum(hi - lo for lo, hi in blocks)
    sends = 4 * sum(len(slots_of(g)) for g in groups) + (nloc + 2 if full else 0)
    res = pl.pallas_call(
        functools.partial(prep_kernel, points, bins, blocks, groups, full),
        out_shape=outs,
        in_specs=[anywhere, pl.BlockSpec(memory_space=pltpu.VMEM)],
        out_specs=[anywhere] * len(outs),
        scratch_shapes=[
            pltpu.VMEM((bins, points), jnp.float32),
            pltpu.VMEM((bins * tiles, LANES), jnp.float32),
            pltpu.VMEM((nloc, 2, EDGE, LANES), jnp.float32),
            pltpu.SemaphoreType.DMA((len(blocks),)),
            pltpu.SemaphoreType.DMA((sends,)),
        ],
        compiler_params=pltpu.CompilerParams(vmem_limit_bytes=VMEM_ASK),
        cost_estimate=pl.CostEstimate(flops=0, bytes_accessed=count * 3_000_000, transcendentals=0),
        name="prep",
    )(spectrum, mask)
    ngr = len(groups)
    return res[:ngr], res[ngr : 2 * ngr], res[2 * ngr :]


def front_kernel(
    tiles, shares, kmin, kmax, chunk, edge, tab_ref, dir_ref, pos_ref, nbr_ref, par_ref, hs_ref, hn_ref, wet_ref, *refs
):
    near, outs, ext_ref = refs[: -shares - 1], refs[-shares - 1 : -1], refs[-1]
    place = pl.program_id(0)
    speed = tab_ref[chunk[0] + chunk[1] * place]
    first = place == 0
    half = ND // 2
    span = half * tiles
    south, north = tiles, ROWS
    pitch = 2 * (2 * tiles + ROWS)

    def rows_at(j, row, count=ROWS):
        return pl.ds(j * pitch + 2 * row, count, stride=2)

    def extend(q, _):
        for t in range(0, tiles, ROWS):
            ext_ref[rows_at(q, t), :] = hs_ref[0, pl.ds(pl.multiple_of(q * tiles + t, ROWS), ROWS), :]
            ext_ref[rows_at(q, south + t), :] = wet_ref[0, q, t : t + ROWS, :]
            ext_ref[rows_at(half + q, north + t), :] = wet_ref[0, half + q, t : t + ROWS, :]
            ext_ref[rows_at(half + q, north + tiles + t), :] = hn_ref[
                0, pl.ds(pl.multiple_of(q * tiles + t, ROWS), ROWS), :
            ]
        return 0

    lax.fori_loop(0, half, extend, 0, unroll=2)
    for q in range(QUART):
        ext_ref[pl.ds((QUART + q) * pitch + 2 * (south + tiles), 1), :] = hn_ref[0, span + q : span + q + 1, :]
        ext_ref[pl.ds((3 * QUART + q) * pitch + 2 * (north - 1), 1), :] = hs_ref[0, span + q : span + q + 1, :]

    side = jnp.where(first, 1.0, -1.0)
    per_share = tiles // shares
    steps = [(d, k) for d in range(shares) for k in range(per_share // ROWS)]
    firsts = {}
    for d, k in steps:
        share = lax.rem(pos_ref[0] + d, shares)
        firsts[d, k] = pl.multiple_of(share * per_share + k * ROWS, ROWS)
    sub = lax.broadcasted_iota(jnp.int32, (ROWS, LANES), 0)
    lanes, rels = {}, {}
    for way in range(4):
        for step in steps:
            src = nbr_ref[way, pl.ds(firsts[step], ROWS), :]
            lanes[way, step] = src & (LANES - 1)
            rels[way, step] = (src >> 7) - (sub + firsts[step])

    def picked(j, own, step, way, offsets):
        out = None
        for r in offsets:
            window = ext_ref[rows_at(j, own + firsts[step] + r), :]
            got = jnp.take_along_axis(window, lanes[way, step], axis=1, mode="promise_in_bounds")
            out = got if out is None else jnp.where(rels[way, step] == r, got, out)
        return out

    for quad in range(4):
        cos_up = quad in (0, 3)
        own, way_y, off_y = (
            (south, 3, range(-(kmax // LANES), -(kmin // LANES) + 1))
            if quad < 2
            else (north, 2, range(kmin // LANES, kmax // LANES + 1))
        )
        way_x, off_x = (1, (-1, 0)) if cos_up else (0, (0, 1))

        def body(q, _):
            j = quad * QUART + q
            jprev = jnp.where(j == 0, ND - 1, j - 1)
            jnext = jnp.where(j == ND - 1, 0, j + 1)
            acos = jnp.abs(dir_ref[0, j])
            asin = jnp.abs(dir_ref[1, j])
            ax, ay = speed * acos, speed * asin
            for step in steps:
                at = pl.ds(firsts[step], ROWS)
                wet = wet_ref[0, j, at, :]
                e_y = picked(j, own, step, way_y, off_y)
                e_x = picked(j, own, step, way_x, off_x)
                rf, fs = par_ref[2, at, :], par_ref[3, at, :]
                e_prev, e_next = wet_ref[0, jprev, at, :], wet_ref[0, jnext, at, :]
                e_t = jnp.where(rf > 0, e_prev, e_next) if cos_up else jnp.where(rf < 0, e_prev, e_next)
                if edge:
                    inner, low, high = (ref[0, j, at, :] for ref in near)
                    outer = jnp.where(first, low, high)
                    e_s = jnp.where(fs * side > 0, outer, inner)
                else:
                    e_s = jnp.where(fs > 0, near[0][0, j, at, :], near[1][0, j, at, :])
                spatial = (par_ref[0, at, :] * ax) * (wet - e_x) + (par_ref[1, at, :] * ay) * (wet - e_y)
                spectral = (jnp.abs(rf) * acos) * (wet - e_t) + (jnp.abs(fs) * speed) * (wet - e_s)
                d, k = step
                outs[d][j, k * ROWS : (k + 1) * ROWS, :] = wet - spatial - spectral
            return 0

        lax.fori_loop(0, QUART, body, 0)


def front(speed, dirs, pos, nbr, par, hs, hn, slot, wet, ends, chunk, shares, kmin, kmax):
    first, step, count = chunk
    tiles = nbr.shape[1]
    nloc = wet.shape[0]
    smem = pl.BlockSpec(memory_space=pltpu.SMEM)

    def freq_spec(start, step):
        return pl.BlockSpec((1, ND, tiles, LANES), lambda i: (start + i * step, 0, 0, 0))

    halo_spec = pl.BlockSpec((1,) + hs.shape[1:], lambda i: (slot + i, 0, 0))

    def whole(shape):
        return pl.BlockSpec(shape, lambda i: (0,) * len(shape))

    if ends:
        near, near_specs = (wet,) + ends, [freq_spec(1, nloc - 3), freq_spec(0, 0), freq_spec(0, 0)]
    else:
        near, near_specs = (wet, wet), [freq_spec(first - 1, step), freq_spec(first + 1, step)]
    rows = tiles // shares
    return pl.pallas_call(
        functools.partial(front_kernel, tiles, shares, kmin, kmax, chunk, bool(ends)),
        grid=(count,),
        out_shape=[jax.ShapeDtypeStruct((count * ND, rows, LANES), jnp.float32)] * shares,
        in_specs=[smem] * 3
        + [whole(nbr.shape), whole(par.shape), halo_spec, halo_spec, freq_spec(first, step)]
        + near_specs,
        out_specs=[pl.BlockSpec((ND, rows, LANES), lambda i: (i, 0, 0))] * shares,
        scratch_shapes=[pltpu.VMEM((ND * 2 * (2 * tiles + ROWS), LANES), jnp.float32)],
        compiler_params=pltpu.CompilerParams(vmem_limit_bytes=VMEM_ASK),
        cost_estimate=pl.CostEstimate(flops=0, bytes_accessed=count * 22_000_000, transcendentals=0),
        name="front",
    )(speed, dirs, pos, nbr, par, hs, hn, wet, *near)


def tail_kernel(nfreq, bins_dev, plan, spot_ref, wts_ref, ftab_ref, frs_ref, dir_ref, pos_ref, wind_ref, mask_ref, *refs):
    out_hbm, mv, base, a0, a1, a2, a3, dw, out_v, in_sem, out_sem = refs[-11:]
    parts = refs[:-11]
    nparts = len(parts)
    shares = nparts // len(plan)
    nbins = nfreq * ND
    loads = []
    block = ND * ROWS
    for c, chunk in enumerate(plan):
        for d in range(shares):
            source = lax.rem(pos_ref[0] + (shares - d), shares)
            for i, f in enumerate(freqs_of(chunk)):
                rows = pl.ds(pl.multiple_of((source * bins_dev + f * ND) * ROWS, ROWS), block)
                part = parts[c * shares + d].at[pl.ds(i * block, block)]
                copy = pltpu.make_async_copy(part, mv.at[rows], in_sem.at[len(loads)])
                copy.start()
                loads.append(copy)
    zero = jnp.zeros((ROWS, LANES), jnp.float32)
    accs = (a0, a1, a2, a3)

    def tile(row):
        return pl.ds(pl.multiple_of(row, ROWS), ROWS)

    def clear(g, _):
        for acc in accs:
            acc[tile(g * ROWS), :] = zero
        return 0

    lax.fori_loop(0, nbins, clear, 0, unroll=8)
    for j in range(ND):
        dw[j] = wind_ref[0] * dir_ref[0, j] + wind_ref[1] * dir_ref[1, j]
    for copy in loads:
        copy.wait()

    def spread(g, shares_of):
        for i in range(GROUP):
            spots = [tile(spot_ref[4 * g + 4 * i + k]) for k in range(4)]
            old = [acc[at, :] for acc, at in zip(accs, spots)]
            for acc, at, was, add in zip(accs, spots, old, shares_of[4 * i : 4 * i + 4]):
                acc[at, :] = was + add

    def per_freq(f, carry):
        fr2, fr4, hspeed = ftab_ref[0, f], ftab_ref[1, f], ftab_ref[2, f]

        def per_group(t, carry):
            total, before = carry
            j0 = t * GROUP
            g0 = f * ND + j0
            own = [mv[tile((g0 + i) * ROWS), :] for i in range(GROUP)]
            found = [[mv[tile(spot_ref[4 * g0 + 4 * i + k]), :] for k in range(4)] for i in range(GROUP)]
            spread(jnp.maximum(g0 - GROUP, 0), before)
            shares_of = []
            for i in range(GROUP):
                m, (p0, p1, m0, m1) = own[i], found[i]
                wp, wm = wts_ref[2 * g0 + 2 * i], wts_ref[2 * g0 + 2 * i + 1]
                ep = p1 + wp * (p0 - p1)
                em = m1 + wm * (m0 - m1)
                mf = fr4 * m
                half = mf * (m * (ep * (1 / 1.25**4) + em * (1 / 0.75**4)) - ep * em * (2.0 / 0.9375**4))
                drive = jnp.maximum(0.0, dw[j0 + i] - hspeed)
                base[tile((g0 + i) * ROWS), :] = m + 0.15 * (drive * drive) * m - 2.0 * half
                sp, sm = wp * half, wm * half
                shares_of += [sp, half - sp, sm, half - sm]
                total = total + m
            return total, tuple(shares_of)

        steep, before = carry
        part, before = lax.fori_loop(0, ND // GROUP, per_group, (zero, before), unroll=3)
        return steep + part * fr2, before

    steep, before = lax.fori_loop(0, nfreq, per_freq, (zero, (zero,) * (4 * GROUP)))
    spread(nbins - GROUP, before)
    steep = steep * (1.0 / nbins)
    mask = mask_ref[...].astype(jnp.float32)
    per = nbins // PIECES
    copies = []
    for p in range(PIECES):

        def finish(t, _):
            g0 = t * ROWS
            done = []
            for i in range(ROWS):
                at = tile((g0 + i) * ROWS)
                mine = base[at, :] - (frs_ref[g0 + i] * steep) * mv[at, :]
                done.append((mine + ((a0[at, :] + a1[at, :]) + (a2[at, :] + a3[at, :]))) * mask)
            turned = jnp.swapaxes(jnp.stack(done, axis=0), 0, 1)
            for c in range(ROWS):
                out_v[pl.ds(pl.multiple_of(g0, ROWS), ROWS), c * LANES : (c + 1) * LANES] = turned[c]
            return 0

        lax.fori_loop(p * per // ROWS, (p + 1) * per // ROWS, finish, 0)
        rows = pl.ds(p * per, per)
        copy = pltpu.make_async_copy(out_v.at[rows], out_hbm.at[rows], out_sem.at[p])
        copy.start()
        copies.append(copy)
    for copy in copies:
        copy.wait()


def tail(parts, plan, bins_dev, dia_bins, dia_wts, ftab, frs, dirs, pos, wind, mask):
    nbins = dia_bins.shape[1]
    nfreq = nbins // ND
    anywhere = pl.BlockSpec(memory_space=pl.ANY)
    smem = pl.BlockSpec(memory_space=pltpu.SMEM)
    vmem = pl.BlockSpec(memory_space=pltpu.VMEM)
    points = ROWS * LANES
    spots = (dia_bins * ROWS).T.reshape(-1)
    wts = dia_wts.T.reshape(-1)
    field = pltpu.VMEM((nbins * ROWS, LANES), jnp.float32)
    return pl.pallas_call(
        functools.partial(tail_kernel, nfreq, bins_dev, plan),
        out_shape=jax.ShapeDtypeStruct((nbins, points), jnp.float32),
        in_specs=[smem] * 6 + [vmem] * 2 + [anywhere] * len(parts),
        out_specs=anywhere,
        scratch_shapes=[field] * 6
        + [
            pltpu.VMEM((ND, ROWS, LANES), jnp.float32),
            pltpu.VMEM((nbins, points), jnp.float32),
            pltpu.SemaphoreType.DMA((nbins // ND,)),
            pltpu.SemaphoreType.DMA((PIECES,)),
        ],
        compiler_params=pltpu.CompilerParams(vmem_limit_bytes=VMEM_ASK),
        cost_estimate=pl.CostEstimate(flops=0, bytes_accessed=70_000_000, transcendentals=0),
        name="tail",
    )(spots, wts, ftab, frs, dirs, pos, wind, mask, *parts)


def fast_on_device(
    spectrum, wind, sea_mask, neighbours, metric_x, metric_y, refraction, freq_shift, dia_bins, dia_wts
):
    bins_dev, points = spectrum.shape
    nbins = dia_bins.shape[1]
    nfreq = nbins // ND
    nloc = bins_dev // ND
    tiles = points // LANES
    shares = lax.axis_size("bin")
    share = points // shares
    bin_pos = lax.axis_index("bin")
    space_pos = lax.axis_index("space")
    plan = chunk_plan(nloc)

    freqs = np.arange(nfreq, dtype=np.float32)
    speed = jnp.asarray(np.exp(-np.log(1.1) * freqs.astype(np.float64)).astype(np.float32))
    ratio = np.exp(np.log(1.1) * (freqs.astype(np.float64) - (nfreq - 1)))
    ftab = jnp.asarray(
        np.stack([ratio**2, 4.0 * ratio**4, 0.5 * np.exp(-np.log(1.1) * freqs)]).astype(np.float32)
    )
    frs = jnp.asarray(np.repeat(3.0 * ratio, ND).astype(np.float32))
    theta = 2.0 * np.pi * (np.arange(ND) + 0.5) / ND
    dirs = jnp.asarray(np.stack([np.cos(theta), np.sin(theta)]).astype(np.float32))
    speed_own = lax.dynamic_slice_in_dim(speed, bin_pos * nloc, nloc, 0)

    groups = halo_groups(plan)
    early = runs_of(slots_of(groups[0]))
    mask_row = sea_mask.reshape(1, points)
    hs, hn, _ = prep(spectrum, mask_row, early, groups[:1], False)
    after, *_ = lax.optimization_barrier((spectrum, hs[0], hn[0]))
    whole_blocks = [(f, min(f + 2, nloc)) for f in range(0, nloc, 2)]
    hs_rest, hn_rest, (wet, low_out, high_out) = prep(after, mask_row, whole_blocks, groups[1:], True)
    wet = wet.reshape(nloc, ND, tiles, LANES)

    def line(array, axis, step):
        peers = lax.axis_size(axis)
        pairs = [(i, i + 1) for i in range(peers - 1)]
        if step < 0:
            pairs = [(b, a) for a, b in pairs]
        return lax.ppermute(array, axis, pairs)

    halos = []
    for south, north in zip(list(hs) + list(hs_rest), list(hn) + list(hn_rest)):
        if halos:
            south, north, *_ = lax.optimization_barrier((south, north) + halos[-1])
        halos.append((line(south, "space", 1), line(north, "space", -1)))
    low_in = line(low_out, "bin", 1).reshape(1, ND, tiles, LANES)
    high_in = line(high_out, "bin", -1).reshape(1, ND, tiles, LANES)

    nbr = (neighbours - space_pos * points).reshape(4, tiles, LANES)
    par = jnp.stack([metric_x, metric_y, refraction, freq_shift]).reshape(4, tiles, LANES)
    pos = bin_pos.reshape(1)
    kmin, kmax = points // 2, points
    parts = []
    order = pos
    for c, chunk in enumerate(plan):
        first, step, count = chunk
        gi, slot = [(i, slots_of(g)[first]) for i, g in enumerate(groups) if chunk in g][0]
        ends = (low_in, high_in) if first == 0 else None
        blocks = front(speed_own, dirs, order, nbr, par, *halos[gi], slot, wet, ends, chunk, shares, kmin, kmax)
        arrived = []
        for d, block in enumerate(blocks):
            rows = block.reshape(-1, LANES)
            if d and parts:
                rows, *_ = lax.optimization_barrier((rows,) + tuple(parts[-shares:][1:]))
            pairs = [(i, (i + d) % shares) for i in range(shares)]
            arrived.append(lax.ppermute(rows, "bin", pairs) if d else rows)
        earlier = tuple(parts[-shares:][1:]) if parts else (low_in, high_in) + sum(halos, ())
        order, *_ = lax.optimization_barrier((pos, blocks[0]) + earlier)
        parts += arrived
    wind_part = lax.dynamic_slice_in_dim(wind, bin_pos * share, share, 1).reshape(2, ROWS, LANES)
    mask_part = lax.dynamic_slice_in_dim(sea_mask, bin_pos * share, share, 0).reshape(ROWS, LANES)
    return tail(parts, plan, bins_dev, dia_bins, dia_wts, ftab, frs, dirs, pos, wind_part, mask_part)


def pick_path(spectrum, *others):
    bins_dev, points = spectrum.shape
    fits = bins_dev % (2 * ND) == ND and bins_dev > ND and points // lax.axis_size("bin") == ROWS * LANES
    return (fast_on_device if fits else on_device)(spectrum, *others)


def solution(mesh):
    return jax.shard_map(
        pick_path,
        mesh=mesh,
        in_specs=(
            P("bin", ("ens", "space")),
            P(None, ("ens", "space")),
            P("space"),
            P(None, "space"),
            P("space"),
            P("space"),
            P("space"),
            P("space"),
            P(),
            P(),
        ),
        out_specs=P(None, ("ens", "space", "bin")),
        check_vma=False,
    )
```

```python
import functools
import itertools

import jax
import jax.numpy as jnp
import numpy as np
from jax import lax
from jax.experimental import pallas as pl
from jax.experimental.pallas import tpu as pltpu
from jax.sharding import PartitionSpec as P

ND = 36


def extended(array, sides, width):
    for axis, dim in sides:
        peers, length = (lax.axis_size(axis), array.shape[dim])
        up = [(i, (i + 1) % peers) for i in range(peers - 1)]
        down = [(j, i) for i, j in up]
        last = lax.slice_in_dim(array, length - width, length, axis=dim)
        initial = lax.slice_in_dim(array, 0, width, axis=dim)
        before = lax.ppermute(last, axis, up)
        after = lax.ppermute(initial, axis, down)
        array = jnp.concatenate([before, array, after], axis=dim)
    return array


def bin_tables(index, nfreq, ndir):
    freq = (index // ndir).astype(jnp.float32)
    direc = index % ndir
    fratio = jnp.exp(jnp.log(1.1) * (freq - (nfreq - 1)))
    speed = jnp.exp(-jnp.log(1.1) * freq)
    theta = 2.0 * jnp.pi * (direc.astype(jnp.float32) + 0.5) / ndir
    return (fratio, speed, jnp.cos(theta), jnp.sin(theta), direc == 0, direc == ndir - 1)


def spatial_term(wet, padded, local, metric_x, metric_y, speed, cosv, sinv):
    east = jnp.take(padded, local[0], axis=1)
    west = jnp.take(padded, local[1], axis=1)
    north = jnp.take(padded, local[2], axis=1)
    south = jnp.take(padded, local[3], axis=1)
    along_x = metric_x[None, :] * (speed * cosv)[:, None]
    along_y = metric_y[None, :] * (speed * sinv)[:, None]
    flux_x = jnp.abs(along_x) * (wet - jnp.where(along_x > 0, west, east))
    flux_y = jnp.abs(along_y) * (wet - jnp.where(along_y > 0, south, north))
    return flux_x + flux_y


def spectral_term(wet, padded, ndir, first, last, refraction, freq_shift, speed, cosv):
    rows = wet.shape[0]

    def moved_rows(offset):
        return lax.slice_in_dim(padded, ndir + offset, ndir + offset + rows, axis=0)

    prev_dir = jnp.where(first[:, None], moved_rows(ndir - 1), moved_rows(-1))
    next_dir = jnp.where(last[:, None], moved_rows(1 - ndir), moved_rows(1))
    lower = moved_rows(-ndir)
    upper = moved_rows(ndir)
    turning = refraction[None, :] * cosv[:, None]
    shifting = freq_shift[None, :] * speed[:, None]
    flux_t = jnp.abs(turning) * (wet - jnp.where(turning > 0, prev_dir, next_dir))
    flux_s = jnp.abs(shifting) * (wet - jnp.where(shifting > 0, lower, upper))
    return flux_t + flux_s


def source_step(
    moved, wind, maskf, fratio, speed, cosv, sinv, plus_fwd, minus_fwd, plus_back, minus_back
):
    steep = jnp.mean(moved * (fratio * fratio)[:, None], axis=0)
    drive = jnp.maximum(
        0.0,
        wind[0][None, :] * cosv[:, None] + wind[1][None, :] * sinv[:, None] - 0.5 * speed[:, None],
    )
    s_in = 0.3 * drive * drive * moved
    s_ds = -6.0 * fratio[:, None] * steep[None, :] * moved
    e_plus = plus_fwd(moved)
    e_minus = minus_fwd(moved)
    delta = (
        8.0
        * (fratio**4)[:, None]
        * (
            moved * moved * (e_plus / 1.25**4 + e_minus / 0.75**4)
            - 2.0 * moved * e_plus * e_minus / 0.9375**4
        )
    )
    s_nl = -2.0 * delta + plus_back(delta) + minus_back(delta)
    return (moved + 0.5 * (s_in + s_ds + s_nl)) * maskf[None, :]


def pair_matrix(first_bins, second_bins, weight, count):
    columns = jnp.arange(count, dtype=jnp.int32)[None, :]
    return weight[:, None] * (first_bins[:, None] == columns).astype(jnp.float32) + (1.0 - weight)[
        :, None
    ] * (second_bins[:, None] == columns).astype(jnp.float32)


def forward_product(matrix, values):
    return jnp.dot(
        matrix, values, precision=lax.Precision.HIGHEST, preferred_element_type=jnp.float32
    )


def backward_product(matrix, values):
    return lax.dot_general(
        matrix,
        values,
        (((0,), (0,)), ((), ())),
        precision=lax.Precision.HIGHEST,
        preferred_element_type=jnp.float32,
    )


def on_device(
    spectrum,
    wind,
    sea_mask,
    neighbours,
    metric_x,
    metric_y,
    refraction,
    freq_shift,
    dia_bins,
    dia_wts,
):
    bins_dev, points_dev = spectrum.shape
    nbins = dia_bins.shape[1]
    ndir = ND
    nfreq = nbins // ndir
    space_pos = lax.axis_index("space")
    bin_pos = lax.axis_index("bin")
    maskf = sea_mask.astype(jnp.float32)
    wet = spectrum * maskf[None, :]
    padded = extended(wet, (("space", 1),), points_dev)
    base = space_pos * points_dev - points_dev
    local = neighbours - base
    own_bins = bin_pos * bins_dev + jnp.arange(bins_dev, dtype=jnp.int32)
    fratio, speed, cosv, sinv, first, last = bin_tables(own_bins, nfreq, ndir)
    spatial = spatial_term(wet, padded, local, metric_x, metric_y, speed, cosv, sinv)
    share = points_dev // lax.axis_size("bin")
    start = bin_pos * share
    all_bins = jnp.arange(nbins, dtype=jnp.int32)
    fratio_all, speed_all, cos_all, sin_all, first_all, last_all = bin_tables(all_bins, nfreq, ndir)
    bin_pad = extended(wet, (("bin", 0),), ndir)
    spectral = spectral_term(wet, bin_pad, ndir, first, last, refraction, freq_shift, speed, cosv)
    moved_own = wet - spatial - spectral
    moved = lax.all_to_all(moved_own, "bin", split_axis=1, concat_axis=0, tiled=True)
    wind_part = lax.dynamic_slice_in_dim(wind, start, share, 1)
    mask_part = lax.dynamic_slice_in_dim(maskf, start, share, 0)
    plus_matrix = pair_matrix(dia_bins[0], dia_bins[1], dia_wts[0], nbins)
    minus_matrix = pair_matrix(dia_bins[2], dia_bins[3], dia_wts[1], nbins)
    result = source_step(
        moved,
        wind_part,
        mask_part,
        fratio_all,
        speed_all,
        cos_all,
        sin_all,
        lambda v: forward_product(plus_matrix, v),
        lambda v: forward_product(minus_matrix, v),
        lambda v: backward_product(plus_matrix, v),
        lambda v: backward_product(minus_matrix, v),
    )
    return result


LANES = 128
ROWS = 8
EDGE = 16
QUART = ND // 4
PIECES = 3
VMEM_ASK = 60 << 20
GROUP = 4


def chunk_plan(nloc):
    mid = nloc // 2
    plan = [(mid - d, 2 * d, 2) for d in range(1, mid + 1)]
    if mid > 3:
        plan[2] = (mid - 3, 3, 3)
    else:
        plan.insert(0, (mid, 1, 1))
    return plan


def freqs_of(chunk):
    first, step, count = chunk
    return [first + i * step for i in range(count)]


def halo_groups(plan):
    return [g for g in (plan[:1], plan[1:]) if g]


def slots_of(group):
    return {f: i for i, f in enumerate(f for chunk in group for f in freqs_of(chunk))}


def prep_kernel(points, bins, blocks, groups, spec_hbm, mask_ref, *refs):
    ngr = len(groups)
    nloc = bins // ND
    hs_hbm, hn_hbm = refs[:ngr], refs[ngr : 2 * ngr]
    wet_hbm, low_hbm, high_hbm = refs[2 * ngr : 2 * ngr + 3]
    spec_v, wet_v, edge_v, in_sem, out_sem = refs[-5:]
    tiles = points // LANES
    half = ND // 2
    where = {f: (i, k) for i, group in enumerate(groups) for f, k in slots_of(group).items()}
    loads = []
    spans = []
    for lo, hi in blocks:
        start = lo * ND // ROWS * ROWS
        stop = min(-(-hi * ND // ROWS) * ROWS, bins)
        spans.append((start, stop))
        rows = pl.ds(start, stop - start)
        copy = pltpu.make_async_copy(spec_hbm.at[rows], spec_v.at[rows], in_sem.at[len(loads)])
        copy.start()
        loads.append(copy)
    masks = [mask_ref[:, c * LANES : (c + 1) * LANES].astype(jnp.float32) for c in range(tiles)]
    copies = []

    def send(src, dst):
        copy = pltpu.make_async_copy(src, dst, out_sem.at[len(copies)])
        copy.start()
        copies.append(copy)

    for (lo, hi), (start, stop), load in zip(blocks, spans, loads):
        load.wait()

        def turn(g0, count):
            for c0 in range(0, tiles, ROWS):
                cols = range(c0, c0 + ROWS)
                block = jnp.stack(
                    [spec_v[pl.ds(g0, count), c * LANES : (c + 1) * LANES] * masks[c] for c in cols], axis=0
                )
                block = jnp.swapaxes(block, 0, 1)
                for i in range(count):
                    wet_v[pl.ds(pl.multiple_of((g0 + i) * tiles + c0, ROWS), ROWS), :] = block[i]

        def relayout(t, _):
            turn(pl.multiple_of(start + t * ROWS, ROWS), ROWS)
            return 0

        lax.fori_loop(0, (stop - start) // ROWS, relayout, 0)
        rest = (stop - start) % ROWS
        if rest:
            g0 = stop - rest
            for c in range(tiles):
                tile = spec_v[pl.ds(g0, rest), c * LANES : (c + 1) * LANES]
                wet_v[pl.ds(g0 * tiles + c, rest, stride=tiles), :] = tile * masks[c]
        for f in range(lo, hi):
            base = f * ND * tiles
            i, k = where[f]
            for side, (j0, row) in enumerate(((3 * QUART, tiles - 1), (QUART, 0))):
                at = base + j0 * tiles + row
                edge_v[f, side, ROWS:EDGE, :] = jnp.zeros((EDGE - ROWS, LANES), jnp.float32)
                edge_v[f, side, 0:ROWS, :] = wet_v[pl.ds(at, ROWS, stride=tiles), :]
                edge_v[f, side, ROWS : ROWS + 1, :] = wet_v[pl.ds(at + ROWS * tiles, 1), :]
            span = half * tiles
            send(wet_v.at[pl.ds(base, span)], hs_hbm[i].at[k, pl.ds(0, span)])
            send(wet_v.at[pl.ds(base + span, span)], hn_hbm[i].at[k, pl.ds(0, span)])
            send(edge_v.at[f, 0], hs_hbm[i].at[k, pl.ds(span, EDGE)])
            send(edge_v.at[f, 1], hn_hbm[i].at[k, pl.ds(span, EDGE)])
            own = pl.ds(base, ND * tiles)
            if f == nloc - 1:
                send(wet_v.at[own], low_hbm)
            if f == 0:
                send(wet_v.at[own], high_hbm)
            send(wet_v.at[own], wet_hbm.at[own])
    for copy in copies:
        copy.wait()


def prep(spectrum, mask, blocks, groups):
    bins, points = spectrum.shape
    nloc = bins // ND
    tiles = points // LANES
    halo_rows = ND // 2 * tiles + EDGE
    halos = [jax.ShapeDtypeStruct((len(slots_of(g)), halo_rows, LANES), jnp.float32) for g in groups]
    one = jax.ShapeDtypeStruct((ND * tiles, LANES), jnp.float32)
    outs = halos + halos + [jax.ShapeDtypeStruct((bins * tiles, LANES), jnp.float32), one, one]
    anywhere = pl.BlockSpec(memory_space=pl.ANY)
    res = pl.pallas_call(
        functools.partial(prep_kernel, points, bins, blocks, groups),
        out_shape=outs,
        in_specs=[anywhere, pl.BlockSpec(memory_space=pltpu.VMEM)],
        out_specs=[anywhere] * len(outs),
        scratch_shapes=[
            pltpu.VMEM((bins, points), jnp.float32),
            pltpu.VMEM((bins * tiles, LANES), jnp.float32),
            pltpu.VMEM((nloc, 2, EDGE, LANES), jnp.float32),
            pltpu.SemaphoreType.DMA((len(blocks),)),
            pltpu.SemaphoreType.DMA((5 * nloc + 2,)),
        ],
        compiler_params=pltpu.CompilerParams(vmem_limit_bytes=VMEM_ASK),
        cost_estimate=pl.CostEstimate(flops=0, bytes_accessed=nloc * 3_000_000, transcendentals=0),
        name="prep",
    )(spectrum, mask)
    ngr = len(groups)
    return res[:ngr], res[ngr : 2 * ngr], *res[2 * ngr :]


def front_kernel(
    tiles, shares, kmin, kmax, chunk, edge, tab_ref, dir_ref, pos_ref, nbr_ref, par_ref, hs_ref, hn_ref, wet_ref, *refs
):
    near, outs, ext_ref = refs[: -shares - 1], refs[-shares - 1 : -1], refs[-1]
    place = pl.program_id(0)
    speed = tab_ref[chunk[0] + chunk[1] * place]
    first = place == 0
    half = ND // 2
    span = half * tiles
    south, north = tiles, ROWS
    pitch = 2 * (2 * tiles + ROWS)

    def rows_at(j, row, count=ROWS):
        return pl.ds(j * pitch + 2 * row, count, stride=2)

    def extend(q, _):
        for t in range(0, tiles, ROWS):
            ext_ref[rows_at(q, t), :] = hs_ref[0, pl.ds(pl.multiple_of(q * tiles + t, ROWS), ROWS), :]
            ext_ref[rows_at(q, south + t), :] = wet_ref[0, q, t : t + ROWS, :]
            ext_ref[rows_at(half + q, north + t), :] = wet_ref[0, half + q, t : t + ROWS, :]
            ext_ref[rows_at(half + q, north + tiles + t), :] = hn_ref[
                0, pl.ds(pl.multiple_of(q * tiles + t, ROWS), ROWS), :
            ]
        return 0

    lax.fori_loop(0, half, extend, 0, unroll=2)
    for q in range(QUART):
        ext_ref[pl.ds((QUART + q) * pitch + 2 * (south + tiles), 1), :] = hn_ref[0, span + q : span + q + 1, :]
        ext_ref[pl.ds((3 * QUART + q) * pitch + 2 * (north - 1), 1), :] = hs_ref[0, span + q : span + q + 1, :]

    side = jnp.where(first, 1.0, -1.0)
    per_share = tiles // shares
    steps = [(d, k) for d in range(shares) for k in range(per_share // ROWS)]
    firsts = {}
    for d, k in steps:
        share = lax.rem(pos_ref[0] + d, shares)
        firsts[d, k] = pl.multiple_of(share * per_share + k * ROWS, ROWS)
    sub = lax.broadcasted_iota(jnp.int32, (ROWS, LANES), 0)
    lanes, rels = {}, {}
    for way in range(4):
        for step in steps:
            src = nbr_ref[way, pl.ds(firsts[step], ROWS), :]
            lanes[way, step] = src & (LANES - 1)
            rels[way, step] = (src >> 7) - (sub + firsts[step])

    def picked(j, own, step, way, offsets):
        out = None
        for r in offsets:
            window = ext_ref[rows_at(j, own + firsts[step] + r), :]
            got = jnp.take_along_axis(window, lanes[way, step], axis=1, mode="promise_in_bounds")
            out = got if out is None else jnp.where(rels[way, step] == r, got, out)
        return out

    for quad in range(4):
        cos_up = quad in (0, 3)
        own, way_y, off_y = (
            (south, 3, range(-(kmax // LANES), -(kmin // LANES) + 1))
            if quad < 2
            else (north, 2, range(kmin // LANES, kmax // LANES + 1))
        )
        way_x, off_x = (1, (-1, 0)) if cos_up else (0, (0, 1))

        def body(q, _):
            j = quad * QUART + q
            jprev = jnp.where(j == 0, ND - 1, j - 1)
            jnext = jnp.where(j == ND - 1, 0, j + 1)
            acos = jnp.abs(dir_ref[0, j])
            asin = jnp.abs(dir_ref[1, j])
            ax, ay = speed * acos, speed * asin
            for step in steps:
                at = pl.ds(firsts[step], ROWS)
                wet = wet_ref[0, j, at, :]
                e_y = picked(j, own, step, way_y, off_y)
                e_x = picked(j, own, step, way_x, off_x)
                rf, fs = par_ref[2, at, :], par_ref[3, at, :]
                e_prev, e_next = wet_ref[0, jprev, at, :], wet_ref[0, jnext, at, :]
                e_t = jnp.where(rf > 0, e_prev, e_next) if cos_up else jnp.where(rf < 0, e_prev, e_next)
                if edge:
                    inner, low, high = (ref[0, j, at, :] for ref in near)
                    outer = jnp.where(first, low, high)
                    e_s = jnp.where(fs * side > 0, outer, inner)
                else:
                    e_s = jnp.where(fs > 0, near[0][0, j, at, :], near[1][0, j, at, :])
                spatial = (par_ref[0, at, :] * ax) * (wet - e_x) + (par_ref[1, at, :] * ay) * (wet - e_y)
                spectral = (jnp.abs(rf) * acos) * (wet - e_t) + (jnp.abs(fs) * speed) * (wet - e_s)
                d, k = step
                outs[d][j, k * ROWS : (k + 1) * ROWS, :] = wet - spatial - spectral
            return 0

        lax.fori_loop(0, QUART, body, 0)


def front(speed, dirs, pos, nbr, par, hs, hn, slot, wet, ends, chunk, shares, kmin, kmax):
    first, step, count = chunk
    tiles = nbr.shape[1]
    nloc = wet.shape[0]
    smem = pl.BlockSpec(memory_space=pltpu.SMEM)

    def freq_spec(start, step):
        return pl.BlockSpec((1, ND, tiles, LANES), lambda i: (start + i * step, 0, 0, 0))

    halo_spec = pl.BlockSpec((1,) + hs.shape[1:], lambda i: (slot + i, 0, 0))

    def whole(shape):
        return pl.BlockSpec(shape, lambda i: (0,) * len(shape))

    if ends:
        near, near_specs = (wet,) + ends, [freq_spec(1, nloc - 3), freq_spec(0, 0), freq_spec(0, 0)]
    else:
        near, near_specs = (wet, wet), [freq_spec(first - 1, step), freq_spec(first + 1, step)]
    rows = tiles // shares
    return pl.pallas_call(
        functools.partial(front_kernel, tiles, shares, kmin, kmax, chunk, bool(ends)),
        grid=(count,),
        out_shape=[jax.ShapeDtypeStruct((count * ND, rows, LANES), jnp.float32)] * shares,
        in_specs=[smem] * 3
        + [whole(nbr.shape), whole(par.shape), halo_spec, halo_spec, freq_spec(first, step)]
        + near_specs,
        out_specs=[pl.BlockSpec((ND, rows, LANES), lambda i: (i, 0, 0))] * shares,
        scratch_shapes=[pltpu.VMEM((ND * 2 * (2 * tiles + ROWS), LANES), jnp.float32)],
        compiler_params=pltpu.CompilerParams(vmem_limit_bytes=VMEM_ASK),
        cost_estimate=pl.CostEstimate(flops=0, bytes_accessed=count * 22_000_000, transcendentals=0),
        name="front",
    )(speed, dirs, pos, nbr, par, hs, hn, wet, *near)


def tail_kernel(nfreq, bins_dev, plan, spot_ref, wts_ref, ftab_ref, frs_ref, dir_ref, pos_ref, wind_ref, mask_ref, *refs):
    out_hbm, mv, base, a0, a1, a2, a3, dw, out_v, in_sem, out_sem = refs[-11:]
    parts = refs[:-11]
    nparts = len(parts)
    shares = nparts // len(plan)
    nbins = nfreq * ND
    loads = []
    for c, chunk in enumerate(plan):
        for d in range(shares):
            source = lax.rem(pos_ref[0] + (shares - d), shares)
            for i, f in enumerate(freqs_of(chunk)):
                rows = pl.ds(source * bins_dev + f * ND, ND)
                part = parts[c * shares + d].at[pl.ds(i * ND, ND)]
                copy = pltpu.make_async_copy(part, mv.at[rows], in_sem.at[len(loads)])
                copy.start()
                loads.append(copy)
    zero = jnp.zeros((ROWS, LANES), jnp.float32)
    accs = (a0, a1, a2, a3)

    def clear(g, _):
        for acc in accs:
            acc[g] = zero
        return 0

    lax.fori_loop(0, nbins, clear, 0, unroll=8)
    for j in range(ND):
        dw[j] = wind_ref[0] * dir_ref[0, j] + wind_ref[1] * dir_ref[1, j]
    for copy in loads:
        copy.wait()

    def per_freq(f, steep):
        fr2, fr4, hspeed = ftab_ref[0, f], ftab_ref[1, f], ftab_ref[2, f]

        def per_group(t, total):
            j0 = t * GROUP
            g0 = f * ND + j0
            spots = [[spot_ref[4 * g0 + 4 * i + k] for k in range(4)] for i in range(GROUP)]
            own = [mv[g0 + i] for i in range(GROUP)]
            found = [[mv[b] for b in spots[i]] for i in range(GROUP)]
            adds = []
            for i in range(GROUP):
                m, (p0, p1, m0, m1) = own[i], found[i]
                wp, wm = wts_ref[2 * g0 + 2 * i], wts_ref[2 * g0 + 2 * i + 1]
                ep = p1 + wp * (p0 - p1)
                em = m1 + wm * (m0 - m1)
                mf = fr4 * m
                half = mf * (m * (ep * (1 / 1.25**4) + em * (1 / 0.75**4)) - ep * em * (2.0 / 0.9375**4))
                drive = jnp.maximum(0.0, dw[j0 + i] - hspeed)
                base[g0 + i] = m + 0.15 * (drive * drive) * m - 2.0 * half
                sp, sm = wp * half, wm * half
                adds.append((sp, half - sp, sm, half - sm))
                total = total + m
            for i in range(GROUP):
                old = [acc[b] for acc, b in zip(accs, spots[i])]
                for acc, b, was, add in zip(accs, spots[i], old, adds[i]):
                    acc[b] = was + add
            return total

        return steep + lax.fori_loop(0, ND // GROUP, per_group, zero, unroll=3) * fr2

    steep = lax.fori_loop(0, nfreq, per_freq, zero)
    steep = steep * (1.0 / nbins)
    mask = mask_ref[...].astype(jnp.float32)
    per = nbins // PIECES
    copies = []
    for p in range(PIECES):

        def finish(t, _):
            g0 = t * ROWS
            done = []
            for i in range(ROWS):
                g = g0 + i
                mine = base[g] - (frs_ref[g] * steep) * mv[g]
                done.append((mine + ((a0[g] + a1[g]) + (a2[g] + a3[g]))) * mask)
            turned = jnp.swapaxes(jnp.stack(done, axis=0), 0, 1)
            for c in range(ROWS):
                out_v[pl.ds(pl.multiple_of(g0, ROWS), ROWS), c * LANES : (c + 1) * LANES] = turned[c]
            return 0

        lax.fori_loop(p * per // ROWS, (p + 1) * per // ROWS, finish, 0)
        rows = pl.ds(p * per, per)
        copy = pltpu.make_async_copy(out_v.at[rows], out_hbm.at[rows], out_sem.at[p])
        copy.start()
        copies.append(copy)
    for copy in copies:
        copy.wait()


def tail(parts, plan, bins_dev, dia_bins, dia_wts, ftab, frs, dirs, pos, wind, mask):
    nbins = dia_bins.shape[1]
    nfreq = nbins // ND
    anywhere = pl.BlockSpec(memory_space=pl.ANY)
    smem = pl.BlockSpec(memory_space=pltpu.SMEM)
    vmem = pl.BlockSpec(memory_space=pltpu.VMEM)
    points = ROWS * LANES
    spots = dia_bins.T.reshape(-1)
    wts = dia_wts.T.reshape(-1)
    field = pltpu.VMEM((nbins, ROWS, LANES), jnp.float32)
    return pl.pallas_call(
        functools.partial(tail_kernel, nfreq, bins_dev, plan),
        out_shape=jax.ShapeDtypeStruct((nbins, points), jnp.float32),
        in_specs=[smem] * 6 + [vmem] * 2 + [anywhere] * len(parts),
        out_specs=anywhere,
        scratch_shapes=[field] * 6
        + [
            pltpu.VMEM((ND, ROWS, LANES), jnp.float32),
            pltpu.VMEM((nbins, points), jnp.float32),
            pltpu.SemaphoreType.DMA((nbins // ND,)),
            pltpu.SemaphoreType.DMA((PIECES,)),
        ],
        compiler_params=pltpu.CompilerParams(vmem_limit_bytes=VMEM_ASK),
        cost_estimate=pl.CostEstimate(flops=0, bytes_accessed=70_000_000, transcendentals=0),
        name="tail",
    )(spots, wts, ftab, frs, dirs, pos, wind, mask, *parts)


def fast_on_device(
    spectrum, wind, sea_mask, neighbours, metric_x, metric_y, refraction, freq_shift, dia_bins, dia_wts
):
    bins_dev, points = spectrum.shape
    nbins = dia_bins.shape[1]
    nfreq = nbins // ND
    nloc = bins_dev // ND
    tiles = points // LANES
    shares = lax.axis_size("bin")
    share = points // shares
    bin_pos = lax.axis_index("bin")
    space_pos = lax.axis_index("space")
    plan = chunk_plan(nloc)

    freqs = np.arange(nfreq, dtype=np.float32)
    speed = jnp.asarray(np.exp(-np.log(1.1) * freqs.astype(np.float64)).astype(np.float32))
    ratio = np.exp(np.log(1.1) * (freqs.astype(np.float64) - (nfreq - 1)))
    ftab = jnp.asarray(
        np.stack([ratio**2, 4.0 * ratio**4, 0.5 * np.exp(-np.log(1.1) * freqs)]).astype(np.float32)
    )
    frs = jnp.asarray(np.repeat(3.0 * ratio, ND).astype(np.float32))
    theta = 2.0 * np.pi * (np.arange(ND) + 0.5) / ND
    dirs = jnp.asarray(np.stack([np.cos(theta), np.sin(theta)]).astype(np.float32))
    speed_own = lax.dynamic_slice_in_dim(speed, bin_pos * nloc, nloc, 0)

    groups = halo_groups(plan)
    blocks = [(f, min(f + 2, nloc)) for f in range(0, nloc, 2)]
    hs, hn, wet, low_out, high_out = prep(spectrum, sea_mask.reshape(1, points), blocks, groups)
    wet = wet.reshape(nloc, ND, tiles, LANES)

    def line(array, axis, step):
        peers = lax.axis_size(axis)
        pairs = [(i, i + 1) for i in range(peers - 1)]
        if step < 0:
            pairs = [(b, a) for a, b in pairs]
        return lax.ppermute(array, axis, pairs)

    halos = []
    for south, north in zip(hs, hn):
        halos.append((line(south, "space", 1), line(north, "space", -1)))
    low_in = line(low_out, "bin", 1).reshape(1, ND, tiles, LANES)
    high_in = line(high_out, "bin", -1).reshape(1, ND, tiles, LANES)

    nbr = (neighbours - space_pos * points).reshape(4, tiles, LANES)
    par = jnp.stack([metric_x, metric_y, refraction, freq_shift]).reshape(4, tiles, LANES)
    pos = bin_pos.reshape(1)
    kmin, kmax = points // 2, points
    parts = []
    order = pos
    for c, chunk in enumerate(plan):
        first, step, count = chunk
        gi, slot = [(i, slots_of(g)[first]) for i, g in enumerate(groups) if chunk in g][0]
        ends = (low_in, high_in) if first == 0 else None
        blocks = front(speed_own, dirs, order, nbr, par, *halos[gi], slot, wet, ends, chunk, shares, kmin, kmax)
        arrived = []
        for d, block in enumerate(blocks):
            rows = block
            if d and parts:
                rows, *_ = lax.optimization_barrier((rows,) + tuple(parts[-shares:][1:]))
            pairs = [(i, (i + d) % shares) for i in range(shares)]
            arrived.append(lax.ppermute(rows, "bin", pairs) if d else rows)
        earlier = tuple(parts[-shares:][1:]) if parts else (low_in, high_in) + sum(halos, ())
        order, *_ = lax.optimization_barrier((pos, blocks[0]) + earlier)
        parts += arrived
    wind_part = lax.dynamic_slice_in_dim(wind, bin_pos * share, share, 1).reshape(2, ROWS, LANES)
    mask_part = lax.dynamic_slice_in_dim(sea_mask, bin_pos * share, share, 0).reshape(ROWS, LANES)
    return tail(parts, plan, bins_dev, dia_bins, dia_wts, ftab, frs, dirs, pos, wind_part, mask_part)


def pick_path(spectrum, *others):
    bins_dev, points = spectrum.shape
    fits = bins_dev % (2 * ND) == ND and bins_dev > ND and points // lax.axis_size("bin") == ROWS * LANES
    return (fast_on_device if fits else on_device)(spectrum, *others)


def solution(mesh):
    return jax.shard_map(
        pick_path,
        mesh=mesh,
        in_specs=(
            P("bin", ("ens", "space")),
            P(None, ("ens", "space")),
            P("space"),
            P(None, "space"),
            P("space"),
            P("space"),
            P("space"),
            P("space"),
            P(),
            P(),
        ),
        out_specs=P(None, ("ens", "space", "bin")),
        check_vma=False,
    )
```

```python
import functools
import itertools

import jax
import jax.numpy as jnp
import numpy as np
from jax import lax
from jax.experimental import pallas as pl
from jax.experimental.pallas import tpu as pltpu
from jax.sharding import PartitionSpec as P

ND = 36


def extended(array, sides, width):
    for axis, dim in sides:
        peers, length = (lax.axis_size(axis), array.shape[dim])
        up = [(i, (i + 1) % peers) for i in range(peers - 1)]
        down = [(j, i) for i, j in up]
        last = lax.slice_in_dim(array, length - width, length, axis=dim)
        initial = lax.slice_in_dim(array, 0, width, axis=dim)
        before = lax.ppermute(last, axis, up)
        after = lax.ppermute(initial, axis, down)
        array = jnp.concatenate([before, array, after], axis=dim)
    return array


def bin_tables(index, nfreq, ndir):
    freq = (index // ndir).astype(jnp.float32)
    direc = index % ndir
    fratio = jnp.exp(jnp.log(1.1) * (freq - (nfreq - 1)))
    speed = jnp.exp(-jnp.log(1.1) * freq)
    theta = 2.0 * jnp.pi * (direc.astype(jnp.float32) + 0.5) / ndir
    return (fratio, speed, jnp.cos(theta), jnp.sin(theta), direc == 0, direc == ndir - 1)


def spatial_term(wet, padded, local, metric_x, metric_y, speed, cosv, sinv):
    east = jnp.take(padded, local[0], axis=1)
    west = jnp.take(padded, local[1], axis=1)
    north = jnp.take(padded, local[2], axis=1)
    south = jnp.take(padded, local[3], axis=1)
    along_x = metric_x[None, :] * (speed * cosv)[:, None]
    along_y = metric_y[None, :] * (speed * sinv)[:, None]
    flux_x = jnp.abs(along_x) * (wet - jnp.where(along_x > 0, west, east))
    flux_y = jnp.abs(along_y) * (wet - jnp.where(along_y > 0, south, north))
    return flux_x + flux_y


def spectral_term(wet, padded, ndir, first, last, refraction, freq_shift, speed, cosv):
    rows = wet.shape[0]

    def moved_rows(offset):
        return lax.slice_in_dim(padded, ndir + offset, ndir + offset + rows, axis=0)

    prev_dir = jnp.where(first[:, None], moved_rows(ndir - 1), moved_rows(-1))
    next_dir = jnp.where(last[:, None], moved_rows(1 - ndir), moved_rows(1))
    lower = moved_rows(-ndir)
    upper = moved_rows(ndir)
    turning = refraction[None, :] * cosv[:, None]
    shifting = freq_shift[None, :] * speed[:, None]
    flux_t = jnp.abs(turning) * (wet - jnp.where(turning > 0, prev_dir, next_dir))
    flux_s = jnp.abs(shifting) * (wet - jnp.where(shifting > 0, lower, upper))
    return flux_t + flux_s


def source_step(
    moved, wind, maskf, fratio, speed, cosv, sinv, plus_fwd, minus_fwd, plus_back, minus_back
):
    steep = jnp.mean(moved * (fratio * fratio)[:, None], axis=0)
    drive = jnp.maximum(
        0.0,
        wind[0][None, :] * cosv[:, None] + wind[1][None, :] * sinv[:, None] - 0.5 * speed[:, None],
    )
    s_in = 0.3 * drive * drive * moved
    s_ds = -6.0 * fratio[:, None] * steep[None, :] * moved
    e_plus = plus_fwd(moved)
    e_minus = minus_fwd(moved)
    delta = (
        8.0
        * (fratio**4)[:, None]
        * (
            moved * moved * (e_plus / 1.25**4 + e_minus / 0.75**4)
            - 2.0 * moved * e_plus * e_minus / 0.9375**4
        )
    )
    s_nl = -2.0 * delta + plus_back(delta) + minus_back(delta)
    return (moved + 0.5 * (s_in + s_ds + s_nl)) * maskf[None, :]


def pair_matrix(first_bins, second_bins, weight, count):
    columns = jnp.arange(count, dtype=jnp.int32)[None, :]
    return weight[:, None] * (first_bins[:, None] == columns).astype(jnp.float32) + (1.0 - weight)[
        :, None
    ] * (second_bins[:, None] == columns).astype(jnp.float32)


def forward_product(matrix, values):
    return jnp.dot(
        matrix, values, precision=lax.Precision.HIGHEST, preferred_element_type=jnp.float32
    )


def backward_product(matrix, values):
    return lax.dot_general(
        matrix,
        values,
        (((0,), (0,)), ((), ())),
        precision=lax.Precision.HIGHEST,
        preferred_element_type=jnp.float32,
    )


def on_device(
    spectrum,
    wind,
    sea_mask,
    neighbours,
    metric_x,
    metric_y,
    refraction,
    freq_shift,
    dia_bins,
    dia_wts,
):
    bins_dev, points_dev = spectrum.shape
    nbins = dia_bins.shape[1]
    ndir = ND
    nfreq = nbins // ndir
    space_pos = lax.axis_index("space")
    bin_pos = lax.axis_index("bin")
    maskf = sea_mask.astype(jnp.float32)
    wet = spectrum * maskf[None, :]
    padded = extended(wet, (("space", 1),), points_dev)
    base = space_pos * points_dev - points_dev
    local = neighbours - base
    own_bins = bin_pos * bins_dev + jnp.arange(bins_dev, dtype=jnp.int32)
    fratio, speed, cosv, sinv, first, last = bin_tables(own_bins, nfreq, ndir)
    spatial = spatial_term(wet, padded, local, metric_x, metric_y, speed, cosv, sinv)
    share = points_dev // lax.axis_size("bin")
    start = bin_pos * share
    all_bins = jnp.arange(nbins, dtype=jnp.int32)
    fratio_all, speed_all, cos_all, sin_all, first_all, last_all = bin_tables(all_bins, nfreq, ndir)
    bin_pad = extended(wet, (("bin", 0),), ndir)
    spectral = spectral_term(wet, bin_pad, ndir, first, last, refraction, freq_shift, speed, cosv)
    moved_own = wet - spatial - spectral
    moved = lax.all_to_all(moved_own, "bin", split_axis=1, concat_axis=0, tiled=True)
    wind_part = lax.dynamic_slice_in_dim(wind, start, share, 1)
    mask_part = lax.dynamic_slice_in_dim(maskf, start, share, 0)
    plus_matrix = pair_matrix(dia_bins[0], dia_bins[1], dia_wts[0], nbins)
    minus_matrix = pair_matrix(dia_bins[2], dia_bins[3], dia_wts[1], nbins)
    result = source_step(
        moved,
        wind_part,
        mask_part,
        fratio_all,
        speed_all,
        cos_all,
        sin_all,
        lambda v: forward_product(plus_matrix, v),
        lambda v: forward_product(minus_matrix, v),
        lambda v: backward_product(plus_matrix, v),
        lambda v: backward_product(minus_matrix, v),
    )
    return result


LANES = 128
ROWS = 8
EDGE = 16
QUART = ND // 4
PIECES = 6
VMEM_ASK = 60 << 20
GROUP = 4


def chunk_plan(nloc):
    mid = nloc // 2
    plan = [(mid - d, 2 * d, 2) for d in range(1, mid + 1)]
    if mid > 3:
        plan[2] = (mid - 3, 3, 3)
    else:
        plan.insert(0, (mid, 1, 1))
    return plan


def freqs_of(chunk):
    first, step, count = chunk
    return [first + i * step for i in range(count)]


def halo_groups(plan):
    return [g for g in (plan[:1], plan[1:]) if g]


def slots_of(group):
    return {f: i for i, f in enumerate(f for chunk in group for f in freqs_of(chunk))}


def prep_kernel(points, bins, blocks, groups, spec_hbm, mask_ref, *refs):
    ngr = len(groups)
    nloc = bins // ND
    hs_hbm, hn_hbm = refs[:ngr], refs[ngr : 2 * ngr]
    wet_hbm, low_hbm, high_hbm = refs[2 * ngr : 2 * ngr + 3]
    spec_v, wet_v, edge_v, in_sem, out_sem = refs[-5:]
    tiles = points // LANES
    half = ND // 2
    where = {f: (i, k) for i, group in enumerate(groups) for f, k in slots_of(group).items()}
    loads = []
    spans = []
    for lo, hi in blocks:
        start = lo * ND // ROWS * ROWS
        stop = min(-(-hi * ND // ROWS) * ROWS, bins)
        spans.append((start, stop))
        rows = pl.ds(start, stop - start)
        copy = pltpu.make_async_copy(spec_hbm.at[rows], spec_v.at[rows], in_sem.at[len(loads)])
        copy.start()
        loads.append(copy)
    masks = [mask_ref[:, c * LANES : (c + 1) * LANES].astype(jnp.float32) for c in range(tiles)]
    copies = []

    def send(src, dst):
        copy = pltpu.make_async_copy(src, dst, out_sem.at[len(copies)])
        copy.start()
        copies.append(copy)

    for (lo, hi), (start, stop), load in zip(blocks, spans, loads):
        load.wait()

        def turn(g0, count):
            for c0 in range(0, tiles, ROWS):
                cols = range(c0, c0 + ROWS)
                block = jnp.stack(
                    [spec_v[pl.ds(g0, count), c * LANES : (c + 1) * LANES] * masks[c] for c in cols], axis=0
                )
                block = jnp.swapaxes(block, 0, 1)
                for i in range(count):
                    wet_v[pl.ds(pl.multiple_of((g0 + i) * tiles + c0, ROWS), ROWS), :] = block[i]

        def relayout(t, _):
            turn(pl.multiple_of(start + t * ROWS, ROWS), ROWS)
            return 0

        lax.fori_loop(0, (stop - start) // ROWS, relayout, 0)
        rest = (stop - start) % ROWS
        if rest:
            g0 = stop - rest
            for c in range(tiles):
                tile = spec_v[pl.ds(g0, rest), c * LANES : (c + 1) * LANES]
                wet_v[pl.ds(g0 * tiles + c, rest, stride=tiles), :] = tile * masks[c]
        for f in range(lo, hi):
            base = f * ND * tiles
            i, k = where[f]
            for side, (j0, row) in enumerate(((3 * QUART, tiles - 1), (QUART, 0))):
                at = base + j0 * tiles + row
                edge_v[f, side, ROWS:EDGE, :] = jnp.zeros((EDGE - ROWS, LANES), jnp.float32)
                edge_v[f, side, 0:ROWS, :] = wet_v[pl.ds(at, ROWS, stride=tiles), :]
                edge_v[f, side, ROWS : ROWS + 1, :] = wet_v[pl.ds(at + ROWS * tiles, 1), :]
            span = half * tiles
            send(wet_v.at[pl.ds(base, span)], hs_hbm[i].at[k, pl.ds(0, span)])
            send(wet_v.at[pl.ds(base + span, span)], hn_hbm[i].at[k, pl.ds(0, span)])
            send(edge_v.at[f, 0], hs_hbm[i].at[k, pl.ds(span, EDGE)])
            send(edge_v.at[f, 1], hn_hbm[i].at[k, pl.ds(span, EDGE)])
            own = pl.ds(base, ND * tiles)
            if f == nloc - 1:
                send(wet_v.at[own], low_hbm)
            if f == 0:
                send(wet_v.at[own], high_hbm)
            send(wet_v.at[own], wet_hbm.at[own])
    for copy in copies:
        copy.wait()


def prep(spectrum, mask, blocks, groups):
    bins, points = spectrum.shape
    nloc = bins // ND
    tiles = points // LANES
    halo_rows = ND // 2 * tiles + EDGE
    halos = [jax.ShapeDtypeStruct((len(slots_of(g)), halo_rows, LANES), jnp.float32) for g in groups]
    one = jax.ShapeDtypeStruct((ND * tiles, LANES), jnp.float32)
    outs = halos + halos + [jax.ShapeDtypeStruct((bins * tiles, LANES), jnp.float32), one, one]
    anywhere = pl.BlockSpec(memory_space=pl.ANY)
    res = pl.pallas_call(
        functools.partial(prep_kernel, points, bins, blocks, groups),
        out_shape=outs,
        in_specs=[anywhere, pl.BlockSpec(memory_space=pltpu.VMEM)],
        out_specs=[anywhere] * len(outs),
        scratch_shapes=[
            pltpu.VMEM((bins, points), jnp.float32),
            pltpu.VMEM((bins * tiles, LANES), jnp.float32),
            pltpu.VMEM((nloc, 2, EDGE, LANES), jnp.float32),
            pltpu.SemaphoreType.DMA((len(blocks),)),
            pltpu.SemaphoreType.DMA((5 * nloc + 2,)),
        ],
        compiler_params=pltpu.CompilerParams(vmem_limit_bytes=VMEM_ASK),
        cost_estimate=pl.CostEstimate(flops=0, bytes_accessed=nloc * 3_000_000, transcendentals=0),
        name="prep",
    )(spectrum, mask)
    ngr = len(groups)
    return res[:ngr], res[ngr : 2 * ngr], *res[2 * ngr :]


def front_kernel(
    tiles, shares, kmin, kmax, chunk, edge, tab_ref, dir_ref, pos_ref, nbr_ref, par_ref, hs_ref, hn_ref, wet_ref, *refs
):
    near, outs, ext_ref = refs[: -shares - 1], refs[-shares - 1 : -1], refs[-1]
    place = pl.program_id(0)
    speed = tab_ref[chunk[0] + chunk[1] * place]
    first = place == 0
    half = ND // 2
    span = half * tiles
    south, north = tiles, ROWS
    pitch = 2 * (2 * tiles + ROWS)

    def rows_at(j, row, count=ROWS):
        return pl.ds(j * pitch + 2 * row, count, stride=2)

    def extend(q, _):
        for t in range(0, tiles, ROWS):
            ext_ref[rows_at(q, t), :] = hs_ref[0, pl.ds(pl.multiple_of(q * tiles + t, ROWS), ROWS), :]
            ext_ref[rows_at(q, south + t), :] = wet_ref[0, q, t : t + ROWS, :]
            ext_ref[rows_at(half + q, north + t), :] = wet_ref[0, half + q, t : t + ROWS, :]
            ext_ref[rows_at(half + q, north + tiles + t), :] = hn_ref[
                0, pl.ds(pl.multiple_of(q * tiles + t, ROWS), ROWS), :
            ]
        return 0

    lax.fori_loop(0, half, extend, 0, unroll=2)
    for q in range(QUART):
        ext_ref[pl.ds((QUART + q) * pitch + 2 * (south + tiles), 1), :] = hn_ref[0, span + q : span + q + 1, :]
        ext_ref[pl.ds((3 * QUART + q) * pitch + 2 * (north - 1), 1), :] = hs_ref[0, span + q : span + q + 1, :]

    side = jnp.where(first, 1.0, -1.0)
    per_share = tiles // shares
    steps = [(d, k) for d in range(shares) for k in range(per_share // ROWS)]
    firsts = {}
    for d, k in steps:
        share = lax.rem(pos_ref[0] + d, shares)
        firsts[d, k] = pl.multiple_of(share * per_share + k * ROWS, ROWS)
    sub = lax.broadcasted_iota(jnp.int32, (ROWS, LANES), 0)
    lanes, rels = {}, {}
    for way in range(4):
        for step in steps:
            src = nbr_ref[way, pl.ds(firsts[step], ROWS), :]
            lanes[way, step] = src & (LANES - 1)
            rels[way, step] = (src >> 7) - (sub + firsts[step])

    def picked(j, own, step, way, offsets):
        out = None
        for r in offsets:
            window = ext_ref[rows_at(j, own + firsts[step] + r), :]
            got = jnp.take_along_axis(window, lanes[way, step], axis=1, mode="promise_in_bounds")
            out = got if out is None else jnp.where(rels[way, step] == r, got, out)
        return out

    for quad in range(4):
        cos_up = quad in (0, 3)
        own, way_y, off_y = (
            (south, 3, range(-(kmax // LANES), -(kmin // LANES) + 1))
            if quad < 2
            else (north, 2, range(kmin // LANES, kmax // LANES + 1))
        )
        way_x, off_x = (1, (-1, 0)) if cos_up else (0, (0, 1))

        def body(q, _):
            j = quad * QUART + q
            jprev = jnp.where(j == 0, ND - 1, j - 1)
            jnext = jnp.where(j == ND - 1, 0, j + 1)
            acos = jnp.abs(dir_ref[0, j])
            asin = jnp.abs(dir_ref[1, j])
            ax, ay = speed * acos, speed * asin
            for step in steps:
                at = pl.ds(firsts[step], ROWS)
                wet = wet_ref[0, j, at, :]
                e_y = picked(j, own, step, way_y, off_y)
                e_x = picked(j, own, step, way_x, off_x)
                rf, fs = par_ref[2, at, :], par_ref[3, at, :]
                e_prev, e_next = wet_ref[0, jprev, at, :], wet_ref[0, jnext, at, :]
                e_t = jnp.where(rf > 0, e_prev, e_next) if cos_up else jnp.where(rf < 0, e_prev, e_next)
                if edge:
                    inner, low, high = (ref[0, j, at, :] for ref in near)
                    outer = jnp.where(first, low, high)
                    e_s = jnp.where(fs * side > 0, outer, inner)
                else:
                    e_s = jnp.where(fs > 0, near[0][0, j, at, :], near[1][0, j, at, :])
                spatial = (par_ref[0, at, :] * ax) * (wet - e_x) + (par_ref[1, at, :] * ay) * (wet - e_y)
                spectral = (jnp.abs(rf) * acos) * (wet - e_t) + (jnp.abs(fs) * speed) * (wet - e_s)
                d, k = step
                outs[d][j, k * ROWS : (k + 1) * ROWS, :] = wet - spatial - spectral
            return 0

        lax.fori_loop(0, QUART, body, 0)


def front(speed, dirs, pos, nbr, par, hs, hn, slot, wet, ends, chunk, shares, kmin, kmax):
    first, step, count = chunk
    tiles = nbr.shape[1]
    nloc = wet.shape[0]
    smem = pl.BlockSpec(memory_space=pltpu.SMEM)

    def freq_spec(start, step):
        return pl.BlockSpec((1, ND, tiles, LANES), lambda i: (start + i * step, 0, 0, 0))

    halo_spec = pl.BlockSpec((1,) + hs.shape[1:], lambda i: (slot + i, 0, 0))

    def whole(shape):
        return pl.BlockSpec(shape, lambda i: (0,) * len(shape))

    if ends:
        near, near_specs = (wet,) + ends, [freq_spec(1, nloc - 3), freq_spec(0, 0), freq_spec(0, 0)]
    else:
        near, near_specs = (wet, wet), [freq_spec(first - 1, step), freq_spec(first + 1, step)]
    rows = tiles // shares
    return pl.pallas_call(
        functools.partial(front_kernel, tiles, shares, kmin, kmax, chunk, bool(ends)),
        grid=(count,),
        out_shape=[jax.ShapeDtypeStruct((count * ND, rows, LANES), jnp.float32)] * shares,
        in_specs=[smem] * 3
        + [whole(nbr.shape), whole(par.shape), halo_spec, halo_spec, freq_spec(first, step)]
        + near_specs,
        out_specs=[pl.BlockSpec((ND, rows, LANES), lambda i: (i, 0, 0))] * shares,
        scratch_shapes=[pltpu.VMEM((ND * 2 * (2 * tiles + ROWS), LANES), jnp.float32)],
        compiler_params=pltpu.CompilerParams(vmem_limit_bytes=VMEM_ASK),
        cost_estimate=pl.CostEstimate(flops=0, bytes_accessed=count * 22_000_000, transcendentals=0),
        name="front",
    )(speed, dirs, pos, nbr, par, hs, hn, wet, *near)


def tail_kernel(nfreq, bins_dev, plan, spot_ref, wts_ref, ftab_ref, frs_ref, dir_ref, pos_ref, wind_ref, mask_ref, *refs):
    out_hbm, mv, base, a0, a1, a2, a3, dw, out_v, in_sem, out_sem = refs[-11:]
    parts = refs[:-11]
    nparts = len(parts)
    shares = nparts // len(plan)
    nbins = nfreq * ND
    loads = []
    for c, chunk in enumerate(plan):
        for d in range(shares):
            source = lax.rem(pos_ref[0] + (shares - d), shares)
            for i, f in enumerate(freqs_of(chunk)):
                rows = pl.ds(source * bins_dev + f * ND, ND)
                part = parts[c * shares + d].at[pl.ds(i * ND, ND)]
                copy = pltpu.make_async_copy(part, mv.at[rows], in_sem.at[len(loads)])
                copy.start()
                loads.append(copy)
    zero = jnp.zeros((ROWS, LANES), jnp.float32)
    accs = (a0, a1, a2, a3)

    def clear(g, _):
        for acc in accs:
            acc[g] = zero
        return 0

    lax.fori_loop(0, nbins, clear, 0, unroll=8)
    for j in range(ND):
        dw[j] = wind_ref[0] * dir_ref[0, j] + wind_ref[1] * dir_ref[1, j]
    for copy in loads:
        copy.wait()

    def per_freq(f, steep):
        fr2, fr4, hspeed = ftab_ref[0, f], ftab_ref[1, f], ftab_ref[2, f]

        def per_group(t, total):
            j0 = t * GROUP
            g0 = f * ND + j0
            spots = [[spot_ref[4 * g0 + 4 * i + k] for k in range(4)] for i in range(GROUP)]
            own = [mv[g0 + i] for i in range(GROUP)]
            found = [[mv[b] for b in spots[i]] for i in range(GROUP)]
            adds = []
            for i in range(GROUP):
                m, (p0, p1, m0, m1) = own[i], found[i]
                wp, wm = wts_ref[2 * g0 + 2 * i], wts_ref[2 * g0 + 2 * i + 1]
                ep = p1 + wp * (p0 - p1)
                em = m1 + wm * (m0 - m1)
                mf = fr4 * m
                half = mf * (m * (ep * (1 / 1.25**4) + em * (1 / 0.75**4)) - ep * em * (2.0 / 0.9375**4))
                drive = jnp.maximum(0.0, dw[j0 + i] - hspeed)
                base[g0 + i] = m + 0.15 * (drive * drive) * m - 2.0 * half
                sp, sm = wp * half, wm * half
                adds.append((sp, half - sp, sm, half - sm))
                total = total + m
            for i in range(GROUP):
                old = [acc[b] for acc, b in zip(accs, spots[i])]
                for acc, b, was, add in zip(accs, spots[i], old, adds[i]):
                    acc[b] = was + add
            return total

        return steep + lax.fori_loop(0, ND // GROUP, per_group, zero, unroll=3) * fr2

    steep = lax.fori_loop(0, nfreq, per_freq, zero)
    steep = steep * (1.0 / nbins)
    mask = mask_ref[...].astype(jnp.float32)
    per = nbins // PIECES
    copies = []
    for p in range(PIECES):

        def finish(t, _):
            g0 = t * ROWS
            done = []
            for i in range(ROWS):
                g = g0 + i
                mine = base[g] - (frs_ref[g] * steep) * mv[g]
                done.append((mine + ((a0[g] + a1[g]) + (a2[g] + a3[g]))) * mask)
            turned = jnp.swapaxes(jnp.stack(done, axis=0), 0, 1)
            for c in range(ROWS):
                out_v[pl.ds(pl.multiple_of(g0, ROWS), ROWS), c * LANES : (c + 1) * LANES] = turned[c]
            return 0

        lax.fori_loop(p * per // ROWS, (p + 1) * per // ROWS, finish, 0)
        rows = pl.ds(p * per, per)
        copy = pltpu.make_async_copy(out_v.at[rows], out_hbm.at[rows], out_sem.at[p])
        copy.start()
        copies.append(copy)
    for copy in copies:
        copy.wait()


def tail(parts, plan, bins_dev, dia_bins, dia_wts, ftab, frs, dirs, pos, wind, mask):
    nbins = dia_bins.shape[1]
    nfreq = nbins // ND
    anywhere = pl.BlockSpec(memory_space=pl.ANY)
    smem = pl.BlockSpec(memory_space=pltpu.SMEM)
    vmem = pl.BlockSpec(memory_space=pltpu.VMEM)
    points = ROWS * LANES
    spots = dia_bins.T.reshape(-1)
    wts = dia_wts.T.reshape(-1)
    field = pltpu.VMEM((nbins, ROWS, LANES), jnp.float32)
    return pl.pallas_call(
        functools.partial(tail_kernel, nfreq, bins_dev, plan),
        out_shape=jax.ShapeDtypeStruct((nbins, points), jnp.float32),
        in_specs=[smem] * 6 + [vmem] * 2 + [anywhere] * len(parts),
        out_specs=anywhere,
        scratch_shapes=[field] * 6
        + [
            pltpu.VMEM((ND, ROWS, LANES), jnp.float32),
            pltpu.VMEM((nbins, points), jnp.float32),
            pltpu.SemaphoreType.DMA((nbins // ND,)),
            pltpu.SemaphoreType.DMA((PIECES,)),
        ],
        compiler_params=pltpu.CompilerParams(vmem_limit_bytes=VMEM_ASK),
        cost_estimate=pl.CostEstimate(flops=0, bytes_accessed=70_000_000, transcendentals=0),
        name="tail",
    )(spots, wts, ftab, frs, dirs, pos, wind, mask, *parts)


def fast_on_device(
    spectrum, wind, sea_mask, neighbours, metric_x, metric_y, refraction, freq_shift, dia_bins, dia_wts
):
    bins_dev, points = spectrum.shape
    nbins = dia_bins.shape[1]
    nfreq = nbins // ND
    nloc = bins_dev // ND
    tiles = points // LANES
    shares = lax.axis_size("bin")
    share = points // shares
    bin_pos = lax.axis_index("bin")
    space_pos = lax.axis_index("space")
    plan = chunk_plan(nloc)

    freqs = np.arange(nfreq, dtype=np.float32)
    speed = jnp.asarray(np.exp(-np.log(1.1) * freqs.astype(np.float64)).astype(np.float32))
    ratio = np.exp(np.log(1.1) * (freqs.astype(np.float64) - (nfreq - 1)))
    ftab = jnp.asarray(
        np.stack([ratio**2, 4.0 * ratio**4, 0.5 * np.exp(-np.log(1.1) * freqs)]).astype(np.float32)
    )
    frs = jnp.asarray(np.repeat(3.0 * ratio, ND).astype(np.float32))
    theta = 2.0 * np.pi * (np.arange(ND) + 0.5) / ND
    dirs = jnp.asarray(np.stack([np.cos(theta), np.sin(theta)]).astype(np.float32))
    speed_own = lax.dynamic_slice_in_dim(speed, bin_pos * nloc, nloc, 0)

    groups = halo_groups(plan)
    blocks = [(f, min(f + 2, nloc)) for f in range(0, nloc, 2)]
    hs, hn, wet, low_out, high_out = prep(spectrum, sea_mask.reshape(1, points), blocks, groups)
    wet = wet.reshape(nloc, ND, tiles, LANES)

    def line(array, axis, step):
        peers = lax.axis_size(axis)
        pairs = [(i, i + 1) for i in range(peers - 1)]
        if step < 0:
            pairs = [(b, a) for a, b in pairs]
        return lax.ppermute(array, axis, pairs)

    low_in = line(low_out, "bin", 1).reshape(1, ND, tiles, LANES)
    high_in = line(high_out, "bin", -1).reshape(1, ND, tiles, LANES)
    halos = []
    for south, north in zip(hs, hn):
        if halos:
            south, north, *_ = lax.optimization_barrier((south, north, low_in, high_in) + halos[-1])
        halos.append((line(south, "space", 1), line(north, "space", -1)))

    nbr = (neighbours - space_pos * points).reshape(4, tiles, LANES)
    par = jnp.stack([metric_x, metric_y, refraction, freq_shift]).reshape(4, tiles, LANES)
    pos = bin_pos.reshape(1)
    kmin, kmax = points // 2, points
    parts = []
    order = pos
    for c, chunk in enumerate(plan):
        first, step, count = chunk
        gi, slot = [(i, slots_of(g)[first]) for i, g in enumerate(groups) if chunk in g][0]
        ends = (low_in, high_in) if first == 0 else None
        blocks = front(speed_own, dirs, order, nbr, par, *halos[gi], slot, wet, ends, chunk, shares, kmin, kmax)
        arrived = []
        for d, block in enumerate(blocks):
            rows = block
            if d and parts:
                before = parts[-shares:][1:] if c < len(plan) - 1 else [parts[d - shares]]
                rows, *_ = lax.optimization_barrier((rows, *before))
            pairs = [(i, (i + d) % shares) for i in range(shares)]
            arrived.append(lax.ppermute(rows, "bin", pairs) if d else rows)
        earlier = tuple(parts[-shares:][1:]) if parts else (low_in, high_in) + sum(halos, ())
        order, *_ = lax.optimization_barrier((pos, blocks[0]) + earlier)
        parts += arrived
    wind_part = lax.dynamic_slice_in_dim(wind, bin_pos * share, share, 1).reshape(2, ROWS, LANES)
    mask_part = lax.dynamic_slice_in_dim(sea_mask, bin_pos * share, share, 0).reshape(ROWS, LANES)
    return tail(parts, plan, bins_dev, dia_bins, dia_wts, ftab, frs, dirs, pos, wind_part, mask_part)


def pick_path(spectrum, *others):
    bins_dev, points = spectrum.shape
    fits = bins_dev % (2 * ND) == ND and bins_dev > ND and points // lax.axis_size("bin") == ROWS * LANES
    return (fast_on_device if fits else on_device)(spectrum, *others)


def solution(mesh):
    return jax.shard_map(
        pick_path,
        mesh=mesh,
        in_specs=(
            P("bin", ("ens", "space")),
            P(None, ("ens", "space")),
            P("space"),
            P(None, "space"),
            P("space"),
            P("space"),
            P("space"),
            P("space"),
            P(),
            P(),
        ),
        out_specs=P(None, ("ens", "space", "bin")),
        check_vma=False,
    )
```

```python
import functools
import itertools

import jax
import jax.numpy as jnp
import numpy as np
from jax import lax
from jax.experimental import pallas as pl
from jax.experimental.pallas import tpu as pltpu
from jax.sharding import PartitionSpec as P

ND = 36


def extended(array, sides, width):
    for axis, dim in sides:
        peers, length = (lax.axis_size(axis), array.shape[dim])
        up = [(i, (i + 1) % peers) for i in range(peers - 1)]
        down = [(j, i) for i, j in up]
        last = lax.slice_in_dim(array, length - width, length, axis=dim)
        initial = lax.slice_in_dim(array, 0, width, axis=dim)
        before = lax.ppermute(last, axis, up)
        after = lax.ppermute(initial, axis, down)
        array = jnp.concatenate([before, array, after], axis=dim)
    return array


def bin_tables(index, nfreq, ndir):
    freq = (index // ndir).astype(jnp.float32)
    direc = index % ndir
    fratio = jnp.exp(jnp.log(1.1) * (freq - (nfreq - 1)))
    speed = jnp.exp(-jnp.log(1.1) * freq)
    theta = 2.0 * jnp.pi * (direc.astype(jnp.float32) + 0.5) / ndir
    return (fratio, speed, jnp.cos(theta), jnp.sin(theta), direc == 0, direc == ndir - 1)


def spatial_term(wet, padded, local, metric_x, metric_y, speed, cosv, sinv):
    east = jnp.take(padded, local[0], axis=1)
    west = jnp.take(padded, local[1], axis=1)
    north = jnp.take(padded, local[2], axis=1)
    south = jnp.take(padded, local[3], axis=1)
    along_x = metric_x[None, :] * (speed * cosv)[:, None]
    along_y = metric_y[None, :] * (speed * sinv)[:, None]
    flux_x = jnp.abs(along_x) * (wet - jnp.where(along_x > 0, west, east))
    flux_y = jnp.abs(along_y) * (wet - jnp.where(along_y > 0, south, north))
    return flux_x + flux_y


def spectral_term(wet, padded, ndir, first, last, refraction, freq_shift, speed, cosv):
    rows = wet.shape[0]

    def moved_rows(offset):
        return lax.slice_in_dim(padded, ndir + offset, ndir + offset + rows, axis=0)

    prev_dir = jnp.where(first[:, None], moved_rows(ndir - 1), moved_rows(-1))
    next_dir = jnp.where(last[:, None], moved_rows(1 - ndir), moved_rows(1))
    lower = moved_rows(-ndir)
    upper = moved_rows(ndir)
    turning = refraction[None, :] * cosv[:, None]
    shifting = freq_shift[None, :] * speed[:, None]
    flux_t = jnp.abs(turning) * (wet - jnp.where(turning > 0, prev_dir, next_dir))
    flux_s = jnp.abs(shifting) * (wet - jnp.where(shifting > 0, lower, upper))
    return flux_t + flux_s


def source_step(
    moved, wind, maskf, fratio, speed, cosv, sinv, plus_fwd, minus_fwd, plus_back, minus_back
):
    steep = jnp.mean(moved * (fratio * fratio)[:, None], axis=0)
    drive = jnp.maximum(
        0.0,
        wind[0][None, :] * cosv[:, None] + wind[1][None, :] * sinv[:, None] - 0.5 * speed[:, None],
    )
    s_in = 0.3 * drive * drive * moved
    s_ds = -6.0 * fratio[:, None] * steep[None, :] * moved
    e_plus = plus_fwd(moved)
    e_minus = minus_fwd(moved)
    delta = (
        8.0
        * (fratio**4)[:, None]
        * (
            moved * moved * (e_plus / 1.25**4 + e_minus / 0.75**4)
            - 2.0 * moved * e_plus * e_minus / 0.9375**4
        )
    )
    s_nl = -2.0 * delta + plus_back(delta) + minus_back(delta)
    return (moved + 0.5 * (s_in + s_ds + s_nl)) * maskf[None, :]


def pair_matrix(first_bins, second_bins, weight, count):
    columns = jnp.arange(count, dtype=jnp.int32)[None, :]
    return weight[:, None] * (first_bins[:, None] == columns).astype(jnp.float32) + (1.0 - weight)[
        :, None
    ] * (second_bins[:, None] == columns).astype(jnp.float32)


def forward_product(matrix, values):
    return jnp.dot(
        matrix, values, precision=lax.Precision.HIGHEST, preferred_element_type=jnp.float32
    )


def backward_product(matrix, values):
    return lax.dot_general(
        matrix,
        values,
        (((0,), (0,)), ((), ())),
        precision=lax.Precision.HIGHEST,
        preferred_element_type=jnp.float32,
    )


def on_device(
    spectrum,
    wind,
    sea_mask,
    neighbours,
    metric_x,
    metric_y,
    refraction,
    freq_shift,
    dia_bins,
    dia_wts,
):
    bins_dev, points_dev = spectrum.shape
    nbins = dia_bins.shape[1]
    ndir = ND
    nfreq = nbins // ndir
    space_pos = lax.axis_index("space")
    bin_pos = lax.axis_index("bin")
    maskf = sea_mask.astype(jnp.float32)
    wet = spectrum * maskf[None, :]
    padded = extended(wet, (("space", 1),), points_dev)
    base = space_pos * points_dev - points_dev
    local = neighbours - base
    own_bins = bin_pos * bins_dev + jnp.arange(bins_dev, dtype=jnp.int32)
    fratio, speed, cosv, sinv, first, last = bin_tables(own_bins, nfreq, ndir)
    spatial = spatial_term(wet, padded, local, metric_x, metric_y, speed, cosv, sinv)
    share = points_dev // lax.axis_size("bin")
    start = bin_pos * share
    all_bins = jnp.arange(nbins, dtype=jnp.int32)
    fratio_all, speed_all, cos_all, sin_all, first_all, last_all = bin_tables(all_bins, nfreq, ndir)
    bin_pad = extended(wet, (("bin", 0),), ndir)
    spectral = spectral_term(wet, bin_pad, ndir, first, last, refraction, freq_shift, speed, cosv)
    moved_own = wet - spatial - spectral
    moved = lax.all_to_all(moved_own, "bin", split_axis=1, concat_axis=0, tiled=True)
    wind_part = lax.dynamic_slice_in_dim(wind, start, share, 1)
    mask_part = lax.dynamic_slice_in_dim(maskf, start, share, 0)
    plus_matrix = pair_matrix(dia_bins[0], dia_bins[1], dia_wts[0], nbins)
    minus_matrix = pair_matrix(dia_bins[2], dia_bins[3], dia_wts[1], nbins)
    result = source_step(
        moved,
        wind_part,
        mask_part,
        fratio_all,
        speed_all,
        cos_all,
        sin_all,
        lambda v: forward_product(plus_matrix, v),
        lambda v: forward_product(minus_matrix, v),
        lambda v: backward_product(plus_matrix, v),
        lambda v: backward_product(minus_matrix, v),
    )
    return result


LANES = 128
ROWS = 8
EDGE = 16
QUART = ND // 4
PIECES = 6
VMEM_ASK = 60 << 20
GROUP = 4


def chunk_plan(nloc):
    mid = nloc // 2
    plan = [(mid - d, 2 * d, 2) for d in range(1, mid + 1)]
    if mid > 3:
        plan[2] = (mid - 3, 3, 3)
    else:
        plan.insert(0, (mid, 1, 1))
    return plan


def freqs_of(chunk):
    first, step, count = chunk
    return [first + i * step for i in range(count)]


def halo_groups(plan):
    return [g for g in (plan[:2], plan[2:]) if g]


def slots_of(group):
    return {f: i for i, f in enumerate(f for chunk in group for f in freqs_of(chunk))}


def prep_kernel(points, bins, blocks, groups, spec_hbm, mask_ref, *refs):
    ngr = len(groups)
    nloc = bins // ND
    hs_hbm, hn_hbm = refs[:ngr], refs[ngr : 2 * ngr]
    wet_hbm, low_hbm, high_hbm = refs[2 * ngr : 2 * ngr + 3]
    spec_v, wet_v, edge_v, in_sem, out_sem = refs[-5:]
    tiles = points // LANES
    half = ND // 2
    where = {f: (i, k) for i, group in enumerate(groups) for f, k in slots_of(group).items()}
    loads = []
    spans = []
    for lo, hi in blocks:
        start = lo * ND // ROWS * ROWS
        stop = min(-(-hi * ND // ROWS) * ROWS, bins)
        spans.append((start, stop))
        rows = pl.ds(start, stop - start)
        copy = pltpu.make_async_copy(spec_hbm.at[rows], spec_v.at[rows], in_sem.at[len(loads)])
        copy.start()
        loads.append(copy)
    masks = [mask_ref[:, c * LANES : (c + 1) * LANES].astype(jnp.float32) for c in range(tiles)]
    copies = []

    def send(src, dst):
        copy = pltpu.make_async_copy(src, dst, out_sem.at[len(copies)])
        copy.start()
        copies.append(copy)

    for (lo, hi), (start, stop), load in zip(blocks, spans, loads):
        load.wait()

        def turn(g0, count):
            for c0 in range(0, tiles, ROWS):
                cols = range(c0, c0 + ROWS)
                block = jnp.stack(
                    [spec_v[pl.ds(g0, count), c * LANES : (c + 1) * LANES] * masks[c] for c in cols], axis=0
                )
                block = jnp.swapaxes(block, 0, 1)
                for i in range(count):
                    wet_v[pl.ds(pl.multiple_of((g0 + i) * tiles + c0, ROWS), ROWS), :] = block[i]

        def relayout(t, _):
            turn(pl.multiple_of(start + t * ROWS, ROWS), ROWS)
            return 0

        lax.fori_loop(0, (stop - start) // ROWS, relayout, 0)
        rest = (stop - start) % ROWS
        if rest:
            g0 = stop - rest
            for c in range(tiles):
                tile = spec_v[pl.ds(g0, rest), c * LANES : (c + 1) * LANES]
                wet_v[pl.ds(g0 * tiles + c, rest, stride=tiles), :] = tile * masks[c]
        for f in range(lo, hi):
            base = f * ND * tiles
            i, k = where[f]
            for side, (j0, row) in enumerate(((3 * QUART, tiles - 1), (QUART, 0))):
                at = base + j0 * tiles + row
                edge_v[f, side, ROWS:EDGE, :] = jnp.zeros((EDGE - ROWS, LANES), jnp.float32)
                edge_v[f, side, 0:ROWS, :] = wet_v[pl.ds(at, ROWS, stride=tiles), :]
                edge_v[f, side, ROWS : ROWS + 1, :] = wet_v[pl.ds(at + ROWS * tiles, 1), :]
            span = half * tiles
            send(wet_v.at[pl.ds(base, span)], hs_hbm[i].at[k, pl.ds(0, span)])
            send(wet_v.at[pl.ds(base + span, span)], hn_hbm[i].at[k, pl.ds(0, span)])
            send(edge_v.at[f, 0], hs_hbm[i].at[k, pl.ds(span, EDGE)])
            send(edge_v.at[f, 1], hn_hbm[i].at[k, pl.ds(span, EDGE)])
            own = pl.ds(base, ND * tiles)
            if f == nloc - 1:
                send(wet_v.at[own], low_hbm)
            if f == 0:
                send(wet_v.at[own], high_hbm)
            send(wet_v.at[own], wet_hbm.at[own])
    for copy in copies:
        copy.wait()


def prep(spectrum, mask, blocks, groups):
    bins, points = spectrum.shape
    nloc = bins // ND
    tiles = points // LANES
    halo_rows = ND // 2 * tiles + EDGE
    halos = [jax.ShapeDtypeStruct((len(slots_of(g)), halo_rows, LANES), jnp.float32) for g in groups]
    one = jax.ShapeDtypeStruct((ND * tiles, LANES), jnp.float32)
    outs = halos + halos + [jax.ShapeDtypeStruct((bins * tiles, LANES), jnp.float32), one, one]
    anywhere = pl.BlockSpec(memory_space=pl.ANY)
    res = pl.pallas_call(
        functools.partial(prep_kernel, points, bins, blocks, groups),
        out_shape=outs,
        in_specs=[anywhere, pl.BlockSpec(memory_space=pltpu.VMEM)],
        out_specs=[anywhere] * len(outs),
        scratch_shapes=[
            pltpu.VMEM((bins, points), jnp.float32),
            pltpu.VMEM((bins * tiles, LANES), jnp.float32),
            pltpu.VMEM((nloc, 2, EDGE, LANES), jnp.float32),
            pltpu.SemaphoreType.DMA((len(blocks),)),
            pltpu.SemaphoreType.DMA((5 * nloc + 2,)),
        ],
        compiler_params=pltpu.CompilerParams(vmem_limit_bytes=VMEM_ASK),
        cost_estimate=pl.CostEstimate(flops=0, bytes_accessed=nloc * 3_000_000, transcendentals=0),
        name="prep",
    )(spectrum, mask)
    ngr = len(groups)
    return res[:ngr], res[ngr : 2 * ngr], *res[2 * ngr :]


def front_kernel(
    tiles, shares, kmin, kmax, chunk, edge, tab_ref, dir_ref, pos_ref, nbr_ref, par_ref, hs_ref, hn_ref, wet_ref, *refs
):
    near, outs, ext_ref = refs[: -shares - 1], refs[-shares - 1 : -1], refs[-1]
    place = pl.program_id(0)
    speed = tab_ref[chunk[0] + chunk[1] * place]
    first = place == 0
    half = ND // 2
    span = half * tiles
    south, north = tiles, ROWS
    pitch = 2 * (2 * tiles + ROWS)

    def rows_at(j, row, count=ROWS):
        return pl.ds(j * pitch + 2 * row, count, stride=2)

    def extend(q, _):
        for t in range(0, tiles, ROWS):
            ext_ref[rows_at(q, t), :] = hs_ref[0, pl.ds(pl.multiple_of(q * tiles + t, ROWS), ROWS), :]
            ext_ref[rows_at(q, south + t), :] = wet_ref[0, q, t : t + ROWS, :]
            ext_ref[rows_at(half + q, north + t), :] = wet_ref[0, half + q, t : t + ROWS, :]
            ext_ref[rows_at(half + q, north + tiles + t), :] = hn_ref[
                0, pl.ds(pl.multiple_of(q * tiles + t, ROWS), ROWS), :
            ]
        return 0

    lax.fori_loop(0, half, extend, 0, unroll=2)
    for q in range(QUART):
        ext_ref[pl.ds((QUART + q) * pitch + 2 * (south + tiles), 1), :] = hn_ref[0, span + q : span + q + 1, :]
        ext_ref[pl.ds((3 * QUART + q) * pitch + 2 * (north - 1), 1), :] = hs_ref[0, span + q : span + q + 1, :]

    side = jnp.where(first, 1.0, -1.0)
    per_share = tiles // shares
    steps = [(d, k) for d in range(shares) for k in range(per_share // ROWS)]
    firsts = {}
    for d, k in steps:
        share = lax.rem(pos_ref[0] + d, shares)
        firsts[d, k] = pl.multiple_of(share * per_share + k * ROWS, ROWS)
    sub = lax.broadcasted_iota(jnp.int32, (ROWS, LANES), 0)
    lanes, rels = {}, {}
    for way in range(4):
        for step in steps:
            src = nbr_ref[way, pl.ds(firsts[step], ROWS), :]
            lanes[way, step] = src & (LANES - 1)
            rels[way, step] = (src >> 7) - (sub + firsts[step])

    def picked(j, own, step, way, offsets):
        out = None
        for r in offsets:
            window = ext_ref[rows_at(j, own + firsts[step] + r), :]
            got = jnp.take_along_axis(window, lanes[way, step], axis=1, mode="promise_in_bounds")
            out = got if out is None else jnp.where(rels[way, step] == r, got, out)
        return out

    for quad in range(4):
        cos_up = quad in (0, 3)
        own, way_y, off_y = (
            (south, 3, range(-(kmax // LANES), -(kmin // LANES) + 1))
            if quad < 2
            else (north, 2, range(kmin // LANES, kmax // LANES + 1))
        )
        way_x, off_x = (1, (-1, 0)) if cos_up else (0, (0, 1))

        def body(q, _):
            j = quad * QUART + q
            jprev = jnp.where(j == 0, ND - 1, j - 1)
            jnext = jnp.where(j == ND - 1, 0, j + 1)
            acos = jnp.abs(dir_ref[0, j])
            asin = jnp.abs(dir_ref[1, j])
            ax, ay = speed * acos, speed * asin
            for step in steps:
                at = pl.ds(firsts[step], ROWS)
                wet = wet_ref[0, j, at, :]
                e_y = picked(j, own, step, way_y, off_y)
                e_x = picked(j, own, step, way_x, off_x)
                rf, fs = par_ref[2, at, :], par_ref[3, at, :]
                e_prev, e_next = wet_ref[0, jprev, at, :], wet_ref[0, jnext, at, :]
                e_t = jnp.where(rf > 0, e_prev, e_next) if cos_up else jnp.where(rf < 0, e_prev, e_next)
                if edge:
                    inner, low, high = (ref[0, j, at, :] for ref in near)
                    outer = jnp.where(first, low, high)
                    e_s = jnp.where(fs * side > 0, outer, inner)
                else:
                    e_s = jnp.where(fs > 0, near[0][0, j, at, :], near[1][0, j, at, :])
                spatial = (par_ref[0, at, :] * ax) * (wet - e_x) + (par_ref[1, at, :] * ay) * (wet - e_y)
                spectral = (jnp.abs(rf) * acos) * (wet - e_t) + (jnp.abs(fs) * speed) * (wet - e_s)
                d, k = step
                outs[d][j, k * ROWS : (k + 1) * ROWS, :] = wet - spatial - spectral
            return 0

        lax.fori_loop(0, QUART, body, 0)


def front(speed, dirs, pos, nbr, par, hs, hn, slot, wet, ends, chunk, shares, kmin, kmax):
    first, step, count = chunk
    tiles = nbr.shape[1]
    nloc = wet.shape[0]
    smem = pl.BlockSpec(memory_space=pltpu.SMEM)

    def freq_spec(start, step):
        return pl.BlockSpec((1, ND, tiles, LANES), lambda i: (start + i * step, 0, 0, 0))

    halo_spec = pl.BlockSpec((1,) + hs.shape[1:], lambda i: (slot + i, 0, 0))

    def whole(shape):
        return pl.BlockSpec(shape, lambda i: (0,) * len(shape))

    if ends:
        near, near_specs = (wet,) + ends, [freq_spec(1, nloc - 3), freq_spec(0, 0), freq_spec(0, 0)]
    else:
        near, near_specs = (wet, wet), [freq_spec(first - 1, step), freq_spec(first + 1, step)]
    rows = tiles // shares
    return pl.pallas_call(
        functools.partial(front_kernel, tiles, shares, kmin, kmax, chunk, bool(ends)),
        grid=(count,),
        out_shape=[jax.ShapeDtypeStruct((count * ND, rows, LANES), jnp.float32)] * shares,
        in_specs=[smem] * 3
        + [whole(nbr.shape), whole(par.shape), halo_spec, halo_spec, freq_spec(first, step)]
        + near_specs,
        out_specs=[pl.BlockSpec((ND, rows, LANES), lambda i: (i, 0, 0))] * shares,
        scratch_shapes=[pltpu.VMEM((ND * 2 * (2 * tiles + ROWS), LANES), jnp.float32)],
        compiler_params=pltpu.CompilerParams(vmem_limit_bytes=VMEM_ASK),
        cost_estimate=pl.CostEstimate(flops=0, bytes_accessed=count * 22_000_000, transcendentals=0),
        name="front",
    )(speed, dirs, pos, nbr, par, hs, hn, wet, *near)


def tail_kernel(nfreq, bins_dev, plan, spot_ref, wts_ref, ftab_ref, frs_ref, dir_ref, pos_ref, wind_ref, mask_ref, *refs):
    out_hbm, mv, base, a0, a1, a2, a3, dw, out_v, in_sem, out_sem = refs[-11:]
    parts = refs[:-11]
    nparts = len(parts)
    shares = nparts // len(plan)
    nbins = nfreq * ND
    loads = []
    for c, chunk in enumerate(plan):
        for d in range(shares):
            source = lax.rem(pos_ref[0] + (shares - d), shares)
            for i, f in enumerate(freqs_of(chunk)):
                rows = pl.ds(source * bins_dev + f * ND, ND)
                part = parts[c * shares + d].at[pl.ds(i * ND, ND)]
                copy = pltpu.make_async_copy(part, mv.at[rows], in_sem.at[len(loads)])
                copy.start()
                loads.append(copy)
    zero = jnp.zeros((ROWS, LANES), jnp.float32)
    accs = (a0, a1, a2, a3)

    def clear(g, _):
        for acc in accs:
            acc[g] = zero
        return 0

    lax.fori_loop(0, nbins, clear, 0, unroll=8)
    for j in range(ND):
        dw[j] = wind_ref[0] * dir_ref[0, j] + wind_ref[1] * dir_ref[1, j]
    for copy in loads:
        copy.wait()

    def per_freq(f, steep):
        fr2, fr4, hspeed = ftab_ref[0, f], ftab_ref[1, f], ftab_ref[2, f]

        def per_group(t, total):
            j0 = t * GROUP
            g0 = f * ND + j0
            spots = [[spot_ref[4 * g0 + 4 * i + k] for k in range(4)] for i in range(GROUP)]
            own = [mv[g0 + i] for i in range(GROUP)]
            found = [[mv[b] for b in spots[i]] for i in range(GROUP)]
            adds = []
            for i in range(GROUP):
                m, (p0, p1, m0, m1) = own[i], found[i]
                wp, wm = wts_ref[2 * g0 + 2 * i], wts_ref[2 * g0 + 2 * i + 1]
                ep = p1 + wp * (p0 - p1)
                em = m1 + wm * (m0 - m1)
                mf = fr4 * m
                half = mf * (m * (ep * (1 / 1.25**4) + em * (1 / 0.75**4)) - ep * em * (2.0 / 0.9375**4))
                drive = jnp.maximum(0.0, dw[j0 + i] - hspeed)
                base[g0 + i] = m + 0.15 * (drive * drive) * m - 2.0 * half
                sp, sm = wp * half, wm * half
                adds.append((sp, half - sp, sm, half - sm))
                total = total + m
            for i in range(0, GROUP, 2):
                for acc, b0, b1, x0, x1 in zip(accs, spots[i], spots[i + 1], adds[i], adds[i + 1]):
                    old0, old1 = acc[b0], acc[b1]
                    acc[b0] = old0 + x0
                    acc[b1] = old1 + (x1 + jnp.where(b0 == b1, x0, zero))
            return total

        return steep + lax.fori_loop(0, ND // GROUP, per_group, zero, unroll=3) * fr2

    steep = lax.fori_loop(0, nfreq, per_freq, zero)
    steep = steep * (1.0 / nbins)
    mask = mask_ref[...].astype(jnp.float32)
    per = nbins // PIECES
    copies = []
    for p in range(PIECES):

        def finish(t, _):
            g0 = t * ROWS
            done = []
            for i in range(ROWS):
                g = g0 + i
                mine = base[g] - (frs_ref[g] * steep) * mv[g]
                done.append((mine + ((a0[g] + a1[g]) + (a2[g] + a3[g]))) * mask)
            turned = jnp.swapaxes(jnp.stack(done, axis=0), 0, 1)
            for c in range(ROWS):
                out_v[pl.ds(pl.multiple_of(g0, ROWS), ROWS), c * LANES : (c + 1) * LANES] = turned[c]
            return 0

        lax.fori_loop(p * per // ROWS, (p + 1) * per // ROWS, finish, 0)
        rows = pl.ds(p * per, per)
        copy = pltpu.make_async_copy(out_v.at[rows], out_hbm.at[rows], out_sem.at[p])
        copy.start()
        copies.append(copy)
    for copy in copies:
        copy.wait()


def tail(parts, plan, bins_dev, dia_bins, dia_wts, ftab, frs, dirs, pos, wind, mask):
    nbins = dia_bins.shape[1]
    nfreq = nbins // ND
    anywhere = pl.BlockSpec(memory_space=pl.ANY)
    smem = pl.BlockSpec(memory_space=pltpu.SMEM)
    vmem = pl.BlockSpec(memory_space=pltpu.VMEM)
    points = ROWS * LANES
    spots = dia_bins.T.reshape(-1)
    wts = dia_wts.T.reshape(-1)
    field = pltpu.VMEM((nbins, ROWS, LANES), jnp.float32)
    return pl.pallas_call(
        functools.partial(tail_kernel, nfreq, bins_dev, plan),
        out_shape=jax.ShapeDtypeStruct((nbins, points), jnp.float32),
        in_specs=[smem] * 6 + [vmem] * 2 + [anywhere] * len(parts),
        out_specs=anywhere,
        scratch_shapes=[field] * 6
        + [
            pltpu.VMEM((ND, ROWS, LANES), jnp.float32),
            pltpu.VMEM((nbins, points), jnp.float32),
            pltpu.SemaphoreType.DMA((nbins // ND,)),
            pltpu.SemaphoreType.DMA((PIECES,)),
        ],
        compiler_params=pltpu.CompilerParams(vmem_limit_bytes=VMEM_ASK),
        cost_estimate=pl.CostEstimate(flops=0, bytes_accessed=70_000_000, transcendentals=0),
        name="tail",
    )(spots, wts, ftab, frs, dirs, pos, wind, mask, *parts)


def fast_on_device(
    spectrum, wind, sea_mask, neighbours, metric_x, metric_y, refraction, freq_shift, dia_bins, dia_wts
):
    bins_dev, points = spectrum.shape
    nbins = dia_bins.shape[1]
    nfreq = nbins // ND
    nloc = bins_dev // ND
    tiles = points // LANES
    shares = lax.axis_size("bin")
    share = points // shares
    bin_pos = lax.axis_index("bin")
    space_pos = lax.axis_index("space")
    plan = chunk_plan(nloc)

    freqs = np.arange(nfreq, dtype=np.float32)
    speed = jnp.asarray(np.exp(-np.log(1.1) * freqs.astype(np.float64)).astype(np.float32))
    ratio = np.exp(np.log(1.1) * (freqs.astype(np.float64) - (nfreq - 1)))
    ftab = jnp.asarray(
        np.stack([ratio**2, 4.0 * ratio**4, 0.5 * np.exp(-np.log(1.1) * freqs)]).astype(np.float32)
    )
    frs = jnp.asarray(np.repeat(3.0 * ratio, ND).astype(np.float32))
    theta = 2.0 * np.pi * (np.arange(ND) + 0.5) / ND
    dirs = jnp.asarray(np.stack([np.cos(theta), np.sin(theta)]).astype(np.float32))
    speed_own = lax.dynamic_slice_in_dim(speed, bin_pos * nloc, nloc, 0)

    groups = halo_groups(plan)
    blocks = [(f, min(f + 2, nloc)) for f in range(0, nloc, 2)]
    hs, hn, wet, low_out, high_out = prep(spectrum, sea_mask.reshape(1, points), blocks, groups)
    wet = wet.reshape(nloc, ND, tiles, LANES)

    def line(array, axis, step):
        peers = lax.axis_size(axis)
        pairs = [(i, i + 1) for i in range(peers - 1)]
        if step < 0:
            pairs = [(b, a) for a, b in pairs]
        return lax.ppermute(array, axis, pairs)

    low_in = line(low_out, "bin", 1).reshape(1, ND, tiles, LANES)
    high_in = line(high_out, "bin", -1).reshape(1, ND, tiles, LANES)
    halos = []

    def send_halos(south, north):
        halos.append((line(south, "space", 1), line(north, "space", -1)))

    send_halos(hs[0], hn[0])

    nbr = (neighbours - space_pos * points).reshape(4, tiles, LANES)
    par = jnp.stack([metric_x, metric_y, refraction, freq_shift]).reshape(4, tiles, LANES)
    pos = bin_pos.reshape(1)
    kmin, kmax = points // 2, points
    parts = []
    order = pos
    for c, chunk in enumerate(plan):
        first, step, count = chunk
        gi, slot = [(i, slots_of(g)[first]) for i, g in enumerate(groups) if chunk in g][0]
        ends = (low_in, high_in) if first == 0 else None
        blocks = front(speed_own, dirs, order, nbr, par, *halos[gi], slot, wet, ends, chunk, shares, kmin, kmax)
        arrived = []
        for d, block in enumerate(blocks):
            rows = block
            if d and parts:
                before = parts[-shares:][1:] if c < len(plan) - 1 else [parts[d - shares]]
                rows, *_ = lax.optimization_barrier((rows, *before))
            pairs = [(i, (i + d) % shares) for i in range(shares)]
            arrived.append(lax.ppermute(rows, "bin", pairs) if d else rows)
        if c == 0 and len(hs) > 1:
            send_halos(*lax.optimization_barrier((hs[1], hn[1], low_in, high_in, blocks[0]))[:2])
        earlier = tuple(parts[-shares:][1:]) if parts else (low_in, high_in)
        order, *_ = lax.optimization_barrier((pos, blocks[0]) + earlier)
        parts += arrived
    wind_part = lax.dynamic_slice_in_dim(wind, bin_pos * share, share, 1).reshape(2, ROWS, LANES)
    mask_part = lax.dynamic_slice_in_dim(sea_mask, bin_pos * share, share, 0).reshape(ROWS, LANES)
    return tail(parts, plan, bins_dev, dia_bins, dia_wts, ftab, frs, dirs, pos, wind_part, mask_part)


def pick_path(spectrum, *others):
    bins_dev, points = spectrum.shape
    fits = bins_dev % (2 * ND) == ND and bins_dev > ND and points // lax.axis_size("bin") == ROWS * LANES
    return (fast_on_device if fits else on_device)(spectrum, *others)


def solution(mesh):
    return jax.shard_map(
        pick_path,
        mesh=mesh,
        in_specs=(
            P("bin", ("ens", "space")),
            P(None, ("ens", "space")),
            P("space"),
            P(None, "space"),
            P("space"),
            P("space"),
            P("space"),
            P("space"),
            P(),
            P(),
        ),
        out_specs=P(None, ("ens", "space", "bin")),
        check_vma=False,
    )
```

```python
import functools
import itertools

import jax
import jax.numpy as jnp
import numpy as np
from jax import lax
from jax.experimental import pallas as pl
from jax.experimental.pallas import tpu as pltpu
from jax.sharding import PartitionSpec as P

ND = 36


def extended(array, sides, width):
    for axis, dim in sides:
        peers, length = (lax.axis_size(axis), array.shape[dim])
        up = [(i, (i + 1) % peers) for i in range(peers - 1)]
        down = [(j, i) for i, j in up]
        last = lax.slice_in_dim(array, length - width, length, axis=dim)
        initial = lax.slice_in_dim(array, 0, width, axis=dim)
        before = lax.ppermute(last, axis, up)
        after = lax.ppermute(initial, axis, down)
        array = jnp.concatenate([before, array, after], axis=dim)
    return array


def bin_tables(index, nfreq, ndir):
    freq = (index // ndir).astype(jnp.float32)
    direc = index % ndir
    fratio = jnp.exp(jnp.log(1.1) * (freq - (nfreq - 1)))
    speed = jnp.exp(-jnp.log(1.1) * freq)
    theta = 2.0 * jnp.pi * (direc.astype(jnp.float32) + 0.5) / ndir
    return (fratio, speed, jnp.cos(theta), jnp.sin(theta), direc == 0, direc == ndir - 1)


def spatial_term(wet, padded, local, metric_x, metric_y, speed, cosv, sinv):
    east = jnp.take(padded, local[0], axis=1)
    west = jnp.take(padded, local[1], axis=1)
    north = jnp.take(padded, local[2], axis=1)
    south = jnp.take(padded, local[3], axis=1)
    along_x = metric_x[None, :] * (speed * cosv)[:, None]
    along_y = metric_y[None, :] * (speed * sinv)[:, None]
    flux_x = jnp.abs(along_x) * (wet - jnp.where(along_x > 0, west, east))
    flux_y = jnp.abs(along_y) * (wet - jnp.where(along_y > 0, south, north))
    return flux_x + flux_y


def spectral_term(wet, padded, ndir, first, last, refraction, freq_shift, speed, cosv):
    rows = wet.shape[0]

    def moved_rows(offset):
        return lax.slice_in_dim(padded, ndir + offset, ndir + offset + rows, axis=0)

    prev_dir = jnp.where(first[:, None], moved_rows(ndir - 1), moved_rows(-1))
    next_dir = jnp.where(last[:, None], moved_rows(1 - ndir), moved_rows(1))
    lower = moved_rows(-ndir)
    upper = moved_rows(ndir)
    turning = refraction[None, :] * cosv[:, None]
    shifting = freq_shift[None, :] * speed[:, None]
    flux_t = jnp.abs(turning) * (wet - jnp.where(turning > 0, prev_dir, next_dir))
    flux_s = jnp.abs(shifting) * (wet - jnp.where(shifting > 0, lower, upper))
    return flux_t + flux_s


def source_step(
    moved, wind, maskf, fratio, speed, cosv, sinv, plus_fwd, minus_fwd, plus_back, minus_back
):
    steep = jnp.mean(moved * (fratio * fratio)[:, None], axis=0)
    drive = jnp.maximum(
        0.0,
        wind[0][None, :] * cosv[:, None] + wind[1][None, :] * sinv[:, None] - 0.5 * speed[:, None],
    )
    s_in = 0.3 * drive * drive * moved
    s_ds = -6.0 * fratio[:, None] * steep[None, :] * moved
    e_plus = plus_fwd(moved)
    e_minus = minus_fwd(moved)
    delta = (
        8.0
        * (fratio**4)[:, None]
        * (
            moved * moved * (e_plus / 1.25**4 + e_minus / 0.75**4)
            - 2.0 * moved * e_plus * e_minus / 0.9375**4
        )
    )
    s_nl = -2.0 * delta + plus_back(delta) + minus_back(delta)
    return (moved + 0.5 * (s_in + s_ds + s_nl)) * maskf[None, :]


def pair_matrix(first_bins, second_bins, weight, count):
    columns = jnp.arange(count, dtype=jnp.int32)[None, :]
    return weight[:, None] * (first_bins[:, None] == columns).astype(jnp.float32) + (1.0 - weight)[
        :, None
    ] * (second_bins[:, None] == columns).astype(jnp.float32)


def forward_product(matrix, values):
    return jnp.dot(
        matrix, values, precision=lax.Precision.HIGHEST, preferred_element_type=jnp.float32
    )


def backward_product(matrix, values):
    return lax.dot_general(
        matrix,
        values,
        (((0,), (0,)), ((), ())),
        precision=lax.Precision.HIGHEST,
        preferred_element_type=jnp.float32,
    )


def on_device(
    spectrum,
    wind,
    sea_mask,
    neighbours,
    metric_x,
    metric_y,
    refraction,
    freq_shift,
    dia_bins,
    dia_wts,
):
    bins_dev, points_dev = spectrum.shape
    nbins = dia_bins.shape[1]
    ndir = ND
    nfreq = nbins // ndir
    space_pos = lax.axis_index("space")
    bin_pos = lax.axis_index("bin")
    maskf = sea_mask.astype(jnp.float32)
    wet = spectrum * maskf[None, :]
    padded = extended(wet, (("space", 1),), points_dev)
    base = space_pos * points_dev - points_dev
    local = neighbours - base
    own_bins = bin_pos * bins_dev + jnp.arange(bins_dev, dtype=jnp.int32)
    fratio, speed, cosv, sinv, first, last = bin_tables(own_bins, nfreq, ndir)
    spatial = spatial_term(wet, padded, local, metric_x, metric_y, speed, cosv, sinv)
    share = points_dev // lax.axis_size("bin")
    start = bin_pos * share
    all_bins = jnp.arange(nbins, dtype=jnp.int32)
    fratio_all, speed_all, cos_all, sin_all, first_all, last_all = bin_tables(all_bins, nfreq, ndir)
    bin_pad = extended(wet, (("bin", 0),), ndir)
    spectral = spectral_term(wet, bin_pad, ndir, first, last, refraction, freq_shift, speed, cosv)
    moved_own = wet - spatial - spectral
    moved = lax.all_to_all(moved_own, "bin", split_axis=1, concat_axis=0, tiled=True)
    wind_part = lax.dynamic_slice_in_dim(wind, start, share, 1)
    mask_part = lax.dynamic_slice_in_dim(maskf, start, share, 0)
    plus_matrix = pair_matrix(dia_bins[0], dia_bins[1], dia_wts[0], nbins)
    minus_matrix = pair_matrix(dia_bins[2], dia_bins[3], dia_wts[1], nbins)
    result = source_step(
        moved,
        wind_part,
        mask_part,
        fratio_all,
        speed_all,
        cos_all,
        sin_all,
        lambda v: forward_product(plus_matrix, v),
        lambda v: forward_product(minus_matrix, v),
        lambda v: backward_product(plus_matrix, v),
        lambda v: backward_product(minus_matrix, v),
    )
    return result


LANES = 128
ROWS = 8
EDGE = 16
QUART = ND // 4
PIECES = 6
VMEM_ASK = 60 << 20
GROUP = 4


def chunk_plan(nloc):
    mid = nloc // 2
    plan = [(mid - d, 2 * d, 2) for d in range(1, mid + 1)]
    if mid > 3:
        plan[2] = (mid - 3, 3, 3)
    else:
        plan.insert(0, (mid, 1, 1))
    return plan


def freqs_of(chunk):
    first, step, count = chunk
    return [first + i * step for i in range(count)]


def halo_groups(plan):
    return [g for g in (plan[:1], plan[1:]) if g]


def slots_of(group):
    return {f: i for i, f in enumerate(f for chunk in group for f in freqs_of(chunk))}


def runs_of(freqs):
    runs = []
    for f in sorted(freqs):
        if runs and runs[-1][1] == f:
            runs[-1] = (runs[-1][0], f + 1)
        else:
            runs.append((f, f + 1))
    return runs


def prep_kernel(points, bins, blocks, groups, full, spec_hbm, mask_ref, *refs):
    ngr = len(groups)
    nloc = bins // ND
    hs_hbm, hn_hbm = refs[:ngr], refs[ngr : 2 * ngr]
    if full:
        wet_hbm, low_hbm, high_hbm = refs[2 * ngr : 2 * ngr + 3]
    spec_v, wet_v, edge_v, in_sem, out_sem = refs[-5:]
    tiles = points // LANES
    half = ND // 2
    where = {f: (i, k) for i, group in enumerate(groups) for f, k in slots_of(group).items()}
    loads = []
    spans = []
    for lo, hi in blocks:
        start = lo * ND // ROWS * ROWS
        stop = min(-(-hi * ND // ROWS) * ROWS, bins)
        spans.append((start, stop))
        rows = pl.ds(start, stop - start)
        copy = pltpu.make_async_copy(spec_hbm.at[rows], spec_v.at[rows], in_sem.at[len(loads)])
        copy.start()
        loads.append(copy)
    masks = [mask_ref[:, c * LANES : (c + 1) * LANES].astype(jnp.float32) for c in range(tiles)]
    copies = []

    def send(src, dst):
        copy = pltpu.make_async_copy(src, dst, out_sem.at[len(copies)])
        copy.start()
        copies.append(copy)

    for (lo, hi), (start, stop), load in zip(blocks, spans, loads):
        load.wait()

        def turn(g0, count):
            for c0 in range(0, tiles, ROWS):
                cols = range(c0, c0 + ROWS)
                block = jnp.stack(
                    [spec_v[pl.ds(g0, count), c * LANES : (c + 1) * LANES] * masks[c] for c in cols], axis=0
                )
                block = jnp.swapaxes(block, 0, 1)
                for i in range(count):
                    wet_v[pl.ds(pl.multiple_of((g0 + i) * tiles + c0, ROWS), ROWS), :] = block[i]

        def relayout(t, _):
            turn(pl.multiple_of(start + t * ROWS, ROWS), ROWS)
            return 0

        lax.fori_loop(0, (stop - start) // ROWS, relayout, 0)
        rest = (stop - start) % ROWS
        if rest:
            g0 = stop - rest
            for c in range(tiles):
                tile = spec_v[pl.ds(g0, rest), c * LANES : (c + 1) * LANES]
                wet_v[pl.ds(g0 * tiles + c, rest, stride=tiles), :] = tile * masks[c]
        for f in range(lo, hi):
            base = f * ND * tiles
            if f in where:
                i, k = where[f]
                for side, (j0, row) in enumerate(((3 * QUART, tiles - 1), (QUART, 0))):
                    at = base + j0 * tiles + row
                    edge_v[f, side, ROWS:EDGE, :] = jnp.zeros((EDGE - ROWS, LANES), jnp.float32)
                    edge_v[f, side, 0:ROWS, :] = wet_v[pl.ds(at, ROWS, stride=tiles), :]
                    edge_v[f, side, ROWS : ROWS + 1, :] = wet_v[pl.ds(at + ROWS * tiles, 1), :]
                span = half * tiles
                send(wet_v.at[pl.ds(base, span)], hs_hbm[i].at[k, pl.ds(0, span)])
                send(wet_v.at[pl.ds(base + span, span)], hn_hbm[i].at[k, pl.ds(0, span)])
                send(edge_v.at[f, 0], hs_hbm[i].at[k, pl.ds(span, EDGE)])
                send(edge_v.at[f, 1], hn_hbm[i].at[k, pl.ds(span, EDGE)])
            if full:
                own = pl.ds(base, ND * tiles)
                if f == nloc - 1:
                    send(wet_v.at[own], low_hbm)
                if f == 0:
                    send(wet_v.at[own], high_hbm)
                send(wet_v.at[own], wet_hbm.at[own])
    for copy in copies:
        copy.wait()


def prep(spectrum, mask, blocks, groups, full):
    bins, points = spectrum.shape
    nloc = bins // ND
    tiles = points // LANES
    halo_rows = ND // 2 * tiles + EDGE
    halos = [jax.ShapeDtypeStruct((len(slots_of(g)), halo_rows, LANES), jnp.float32) for g in groups]
    one = jax.ShapeDtypeStruct((ND * tiles, LANES), jnp.float32)
    outs = halos + halos
    if full:
        outs += [jax.ShapeDtypeStruct((bins * tiles, LANES), jnp.float32), one, one]
    anywhere = pl.BlockSpec(memory_space=pl.ANY)
    count = sum(hi - lo for lo, hi in blocks)
    sends = 4 * sum(len(slots_of(g)) for g in groups) + (nloc + 2 if full else 0)
    res = pl.pallas_call(
        functools.partial(prep_kernel, points, bins, blocks, groups, full),
        out_shape=outs,
        in_specs=[anywhere, pl.BlockSpec(memory_space=pltpu.VMEM)],
        out_specs=[anywhere] * len(outs),
        scratch_shapes=[
            pltpu.VMEM((bins, points), jnp.float32),
            pltpu.VMEM((bins * tiles, LANES), jnp.float32),
            pltpu.VMEM((nloc, 2, EDGE, LANES), jnp.float32),
            pltpu.SemaphoreType.DMA((len(blocks),)),
            pltpu.SemaphoreType.DMA((sends,)),
        ],
        compiler_params=pltpu.CompilerParams(vmem_limit_bytes=VMEM_ASK),
        cost_estimate=pl.CostEstimate(flops=0, bytes_accessed=count * 3_000_000, transcendentals=0),
        name="prep",
    )(spectrum, mask)
    ngr = len(groups)
    return res[:ngr], res[ngr : 2 * ngr], res[2 * ngr :]


def front_kernel(
    tiles, shares, kmin, kmax, chunk, edge, tab_ref, dir_ref, pos_ref, nbr_ref, par_ref, hs_ref, hn_ref, wet_ref, *refs
):
    near, outs, ext_ref = refs[: -shares - 1], refs[-shares - 1 : -1], refs[-1]
    place = pl.program_id(0)
    speed = tab_ref[chunk[0] + chunk[1] * place]
    first = place == 0
    half = ND // 2
    span = half * tiles
    south, north = tiles, ROWS
    pitch = 2 * (2 * tiles + ROWS)

    def rows_at(j, row, count=ROWS):
        return pl.ds(j * pitch + 2 * row, count, stride=2)

    def extend(q, _):
        for t in range(0, tiles, ROWS):
            ext_ref[rows_at(q, t), :] = hs_ref[0, pl.ds(pl.multiple_of(q * tiles + t, ROWS), ROWS), :]
            ext_ref[rows_at(q, south + t), :] = wet_ref[0, q, t : t + ROWS, :]
            ext_ref[rows_at(half + q, north + t), :] = wet_ref[0, half + q, t : t + ROWS, :]
            ext_ref[rows_at(half + q, north + tiles + t), :] = hn_ref[
                0, pl.ds(pl.multiple_of(q * tiles + t, ROWS), ROWS), :
            ]
        return 0

    lax.fori_loop(0, half, extend, 0, unroll=2)
    for q in range(QUART):
        ext_ref[pl.ds((QUART + q) * pitch + 2 * (south + tiles), 1), :] = hn_ref[0, span + q : span + q + 1, :]
        ext_ref[pl.ds((3 * QUART + q) * pitch + 2 * (north - 1), 1), :] = hs_ref[0, span + q : span + q + 1, :]

    side = jnp.where(first, 1.0, -1.0)
    per_share = tiles // shares
    steps = [(d, k) for d in range(shares) for k in range(per_share // ROWS)]
    firsts = {}
    for d, k in steps:
        share = lax.rem(pos_ref[0] + d, shares)
        firsts[d, k] = pl.multiple_of(share * per_share + k * ROWS, ROWS)
    sub = lax.broadcasted_iota(jnp.int32, (ROWS, LANES), 0)
    lanes, rels = {}, {}
    for way in range(4):
        for step in steps:
            src = nbr_ref[way, pl.ds(firsts[step], ROWS), :]
            lanes[way, step] = src & (LANES - 1)
            rels[way, step] = (src >> 7) - (sub + firsts[step])

    def picked(j, own, step, way, offsets):
        out = None
        for r in offsets:
            window = ext_ref[rows_at(j, own + firsts[step] + r), :]
            got = jnp.take_along_axis(window, lanes[way, step], axis=1, mode="promise_in_bounds")
            out = got if out is None else jnp.where(rels[way, step] == r, got, out)
        return out

    for quad in range(4):
        cos_up = quad in (0, 3)
        own, way_y, off_y = (
            (south, 3, range(-(kmax // LANES), -(kmin // LANES) + 1))
            if quad < 2
            else (north, 2, range(kmin // LANES, kmax // LANES + 1))
        )
        way_x, off_x = (1, (-1, 0)) if cos_up else (0, (0, 1))

        def body(q, _):
            j = quad * QUART + q
            jprev = jnp.where(j == 0, ND - 1, j - 1)
            jnext = jnp.where(j == ND - 1, 0, j + 1)
            acos = jnp.abs(dir_ref[0, j])
            asin = jnp.abs(dir_ref[1, j])
            ax, ay = speed * acos, speed * asin
            for step in steps:
                at = pl.ds(firsts[step], ROWS)
                wet = wet_ref[0, j, at, :]
                e_y = picked(j, own, step, way_y, off_y)
                e_x = picked(j, own, step, way_x, off_x)
                rf, fs = par_ref[2, at, :], par_ref[3, at, :]
                e_prev, e_next = wet_ref[0, jprev, at, :], wet_ref[0, jnext, at, :]
                e_t = jnp.where(rf > 0, e_prev, e_next) if cos_up else jnp.where(rf < 0, e_prev, e_next)
                if edge:
                    inner, low, high = (ref[0, j, at, :] for ref in near)
                    outer = jnp.where(first, low, high)
                    e_s = jnp.where(fs * side > 0, outer, inner)
                else:
                    e_s = jnp.where(fs > 0, near[0][0, j, at, :], near[1][0, j, at, :])
                spatial = (par_ref[0, at, :] * ax) * (wet - e_x) + (par_ref[1, at, :] * ay) * (wet - e_y)
                spectral = (jnp.abs(rf) * acos) * (wet - e_t) + (jnp.abs(fs) * speed) * (wet - e_s)
                d, k = step
                outs[d][j, k * ROWS : (k + 1) * ROWS, :] = wet - spatial - spectral
            return 0

        lax.fori_loop(0, QUART, body, 0, unroll=3)


def front(speed, dirs, pos, nbr, par, hs, hn, slot, wet, ends, chunk, shares, kmin, kmax):
    first, step, count = chunk
    tiles = nbr.shape[1]
    nloc = wet.shape[0]
    smem = pl.BlockSpec(memory_space=pltpu.SMEM)

    def freq_spec(start, step):
        return pl.BlockSpec((1, ND, tiles, LANES), lambda i: (start + i * step, 0, 0, 0))

    halo_spec = pl.BlockSpec((1,) + hs.shape[1:], lambda i: (slot + i, 0, 0))

    def whole(shape):
        return pl.BlockSpec(shape, lambda i: (0,) * len(shape))

    if ends:
        near, near_specs = (wet,) + ends, [freq_spec(1, nloc - 3), freq_spec(0, 0), freq_spec(0, 0)]
    else:
        near, near_specs = (wet, wet), [freq_spec(first - 1, step), freq_spec(first + 1, step)]
    rows = tiles // shares
    return pl.pallas_call(
        functools.partial(front_kernel, tiles, shares, kmin, kmax, chunk, bool(ends)),
        grid=(count,),
        out_shape=[jax.ShapeDtypeStruct((count * ND, rows, LANES), jnp.float32)] * shares,
        in_specs=[smem] * 3
        + [whole(nbr.shape), whole(par.shape), halo_spec, halo_spec, freq_spec(first, step)]
        + near_specs,
        out_specs=[pl.BlockSpec((ND, rows, LANES), lambda i: (i, 0, 0))] * shares,
        scratch_shapes=[pltpu.VMEM((ND * 2 * (2 * tiles + ROWS), LANES), jnp.float32)],
        compiler_params=pltpu.CompilerParams(vmem_limit_bytes=VMEM_ASK),
        cost_estimate=pl.CostEstimate(flops=0, bytes_accessed=count * 22_000_000, transcendentals=0),
        name="front",
    )(speed, dirs, pos, nbr, par, hs, hn, wet, *near)


def tail_kernel(nfreq, bins_dev, plan, spot_ref, wts_ref, ftab_ref, frs_ref, dir_ref, pos_ref, wind_ref, mask_ref, *refs):
    out_hbm, mv, base, a0, a1, a2, a3, dw, out_v, in_sem, out_sem = refs[-11:]
    parts = refs[:-11]
    nparts = len(parts)
    shares = nparts // len(plan)
    nbins = nfreq * ND
    loads = []
    for c, chunk in enumerate(plan):
        for d in range(shares):
            source = lax.rem(pos_ref[0] + (shares - d), shares)
            for i, f in enumerate(freqs_of(chunk)):
                rows = pl.ds(source * bins_dev + f * ND, ND)
                part = parts[c * shares + d].at[pl.ds(i * ND, ND)]
                copy = pltpu.make_async_copy(part, mv.at[rows], in_sem.at[len(loads)])
                copy.start()
                loads.append(copy)
    zero = jnp.zeros((ROWS, LANES), jnp.float32)
    accs = (a0, a1, a2, a3)

    def clear(g, _):
        for acc in accs:
            acc[g] = zero
        return 0

    lax.fori_loop(0, nbins, clear, 0, unroll=8)
    for j in range(ND):
        dw[j] = wind_ref[0] * dir_ref[0, j] + wind_ref[1] * dir_ref[1, j]
    for copy in loads:
        copy.wait()

    def per_freq(f, steep):
        fr2, fr4, hspeed = ftab_ref[0, f], ftab_ref[1, f], ftab_ref[2, f]

        def per_group(t, total):
            j0 = t * GROUP
            g0 = f * ND + j0
            spots = [[spot_ref[4 * g0 + 4 * i + k] for k in range(4)] for i in range(GROUP)]
            own = [mv[g0 + i] for i in range(GROUP)]
            found = [[mv[b] for b in spots[i]] for i in range(GROUP)]
            adds = []
            for i in range(GROUP):
                m, (p0, p1, m0, m1) = own[i], found[i]
                wp, wm = wts_ref[2 * g0 + 2 * i], wts_ref[2 * g0 + 2 * i + 1]
                ep = p1 + wp * (p0 - p1)
                em = m1 + wm * (m0 - m1)
                mf = fr4 * m
                half = mf * (m * (ep * (1 / 1.25**4) + em * (1 / 0.75**4)) - ep * em * (2.0 / 0.9375**4))
                drive = jnp.maximum(0.0, dw[j0 + i] - hspeed)
                base[g0 + i] = m + 0.15 * (drive * drive) * m - 2.0 * half
                sp, sm = wp * half, wm * half
                adds.append((sp, half - sp, sm, half - sm))
                total = total + m
            for i in range(0, GROUP, 2):
                for acc, b0, b1, x0, x1 in zip(accs, spots[i], spots[i + 1], adds[i], adds[i + 1]):
                    old0, old1 = acc[b0], acc[b1]
                    acc[b0] = old0 + x0
                    acc[b1] = old1 + (x1 + jnp.where(b0 == b1, x0, zero))
            return total

        return steep + lax.fori_loop(0, ND // GROUP, per_group, zero, unroll=3) * fr2

    steep = lax.fori_loop(0, nfreq, per_freq, zero)
    steep = steep * (1.0 / nbins)
    mask = mask_ref[...].astype(jnp.float32)
    per = nbins // PIECES
    copies = []
    for p in range(PIECES):

        def finish(t, _):
            g0 = t * ROWS
            done = []
            for i in range(ROWS):
                g = g0 + i
                mine = base[g] - (frs_ref[g] * steep) * mv[g]
                done.append((mine + ((a0[g] + a1[g]) + (a2[g] + a3[g]))) * mask)
            turned = jnp.swapaxes(jnp.stack(done, axis=0), 0, 1)
            for c in range(ROWS):
                out_v[pl.ds(pl.multiple_of(g0, ROWS), ROWS), c * LANES : (c + 1) * LANES] = turned[c]
            return 0

        lax.fori_loop(p * per // ROWS, (p + 1) * per // ROWS, finish, 0, unroll=3)
        rows = pl.ds(p * per, per)
        copy = pltpu.make_async_copy(out_v.at[rows], out_hbm.at[rows], out_sem.at[p])
        copy.start()
        copies.append(copy)
    for copy in copies:
        copy.wait()


def tail(parts, plan, bins_dev, dia_bins, dia_wts, ftab, frs, dirs, pos, wind, mask):
    nbins = dia_bins.shape[1]
    nfreq = nbins // ND
    anywhere = pl.BlockSpec(memory_space=pl.ANY)
    smem = pl.BlockSpec(memory_space=pltpu.SMEM)
    vmem = pl.BlockSpec(memory_space=pltpu.VMEM)
    points = ROWS * LANES
    spots = dia_bins.T.reshape(-1)
    wts = dia_wts.T.reshape(-1)
    field = pltpu.VMEM((nbins, ROWS, LANES), jnp.float32)
    return pl.pallas_call(
        functools.partial(tail_kernel, nfreq, bins_dev, plan),
        out_shape=jax.ShapeDtypeStruct((nbins, points), jnp.float32),
        in_specs=[smem] * 6 + [vmem] * 2 + [anywhere] * len(parts),
        out_specs=anywhere,
        scratch_shapes=[field] * 6
        + [
            pltpu.VMEM((ND, ROWS, LANES), jnp.float32),
            pltpu.VMEM((nbins, points), jnp.float32),
            pltpu.SemaphoreType.DMA((nbins // ND,)),
            pltpu.SemaphoreType.DMA((PIECES,)),
        ],
        compiler_params=pltpu.CompilerParams(vmem_limit_bytes=VMEM_ASK),
        cost_estimate=pl.CostEstimate(flops=0, bytes_accessed=70_000_000, transcendentals=0),
        name="tail",
    )(spots, wts, ftab, frs, dirs, pos, wind, mask, *parts)


def fast_on_device(
    spectrum, wind, sea_mask, neighbours, metric_x, metric_y, refraction, freq_shift, dia_bins, dia_wts
):
    bins_dev, points = spectrum.shape
    nbins = dia_bins.shape[1]
    nfreq = nbins // ND
    nloc = bins_dev // ND
    tiles = points // LANES
    shares = lax.axis_size("bin")
    share = points // shares
    bin_pos = lax.axis_index("bin")
    space_pos = lax.axis_index("space")
    plan = chunk_plan(nloc)

    freqs = np.arange(nfreq, dtype=np.float32)
    speed = jnp.asarray(np.exp(-np.log(1.1) * freqs.astype(np.float64)).astype(np.float32))
    ratio = np.exp(np.log(1.1) * (freqs.astype(np.float64) - (nfreq - 1)))
    ftab = jnp.asarray(
        np.stack([ratio**2, 4.0 * ratio**4, 0.5 * np.exp(-np.log(1.1) * freqs)]).astype(np.float32)
    )
    frs = jnp.asarray(np.repeat(3.0 * ratio, ND).astype(np.float32))
    theta = 2.0 * np.pi * (np.arange(ND) + 0.5) / ND
    dirs = jnp.asarray(np.stack([np.cos(theta), np.sin(theta)]).astype(np.float32))
    speed_own = lax.dynamic_slice_in_dim(speed, bin_pos * nloc, nloc, 0)

    groups = halo_groups(plan)
    early = runs_of(slots_of(groups[0]))
    mask_row = sea_mask.reshape(1, points)
    hs, hn, _ = prep(spectrum, mask_row, early, groups[:1], False)
    after, *_ = lax.optimization_barrier((spectrum, hs[0], hn[0]))
    whole_blocks = [(f, min(f + 2, nloc)) for f in range(0, nloc, 2)]
    hs_rest, hn_rest, (wet, low_out, high_out) = prep(after, mask_row, whole_blocks, groups[1:], True)
    wet = wet.reshape(nloc, ND, tiles, LANES)

    def line(array, axis, step):
        peers = lax.axis_size(axis)
        pairs = [(i, i + 1) for i in range(peers - 1)]
        if step < 0:
            pairs = [(b, a) for a, b in pairs]
        return lax.ppermute(array, axis, pairs)

    halos = []
    for south, north in zip(list(hs) + list(hs_rest), list(hn) + list(hn_rest)):
        if halos:
            south, north, *_ = lax.optimization_barrier((south, north) + halos[-1])
        halos.append((line(south, "space", 1), line(north, "space", -1)))
    low_in = line(low_out, "bin", 1).reshape(1, ND, tiles, LANES)
    high_in = line(high_out, "bin", -1).reshape(1, ND, tiles, LANES)

    nbr = (neighbours - space_pos * points).reshape(4, tiles, LANES)
    par = jnp.stack([metric_x, metric_y, refraction, freq_shift]).reshape(4, tiles, LANES)
    pos = bin_pos.reshape(1)
    kmin, kmax = points // 2, points
    parts = []
    order = pos
    for c, chunk in enumerate(plan):
        first, step, count = chunk
        gi, slot = [(i, slots_of(g)[first]) for i, g in enumerate(groups) if chunk in g][0]
        ends = (low_in, high_in) if first == 0 else None
        blocks = front(speed_own, dirs, order, nbr, par, *halos[gi], slot, wet, ends, chunk, shares, kmin, kmax)
        arrived = []
        for d, block in enumerate(blocks):
            rows = block
            if d and parts:
                before = parts[-shares:][1:] if c < len(plan) - 1 else [parts[d - shares]]
                rows, *_ = lax.optimization_barrier((rows, *before))
            pairs = [(i, (i + d) % shares) for i in range(shares)]
            arrived.append(lax.ppermute(rows, "bin", pairs) if d else rows)
        earlier = tuple(parts[-shares:][1:]) if parts else (low_in, high_in) + sum(halos, ())
        order, *_ = lax.optimization_barrier((pos, blocks[0]) + earlier)
        parts += arrived
    wind_part = lax.dynamic_slice_in_dim(wind, bin_pos * share, share, 1).reshape(2, ROWS, LANES)
    mask_part = lax.dynamic_slice_in_dim(sea_mask, bin_pos * share, share, 0).reshape(ROWS, LANES)
    return tail(parts, plan, bins_dev, dia_bins, dia_wts, ftab, frs, dirs, pos, wind_part, mask_part)


def pick_path(spectrum, *others):
    bins_dev, points = spectrum.shape
    fits = bins_dev % (2 * ND) == ND and bins_dev > ND and points // lax.axis_size("bin") == ROWS * LANES
    return (fast_on_device if fits else on_device)(spectrum, *others)


def solution(mesh):
    return jax.shard_map(
        pick_path,
        mesh=mesh,
        in_specs=(
            P("bin", ("ens", "space")),
            P(None, ("ens", "space")),
            P("space"),
            P(None, "space"),
            P("space"),
            P("space"),
            P("space"),
            P("space"),
            P(),
            P(),
        ),
        out_specs=P(None, ("ens", "space", "bin")),
        check_vma=False,
    )
```

```python
import functools
import itertools

import jax
import jax.numpy as jnp
import numpy as np
from jax import lax
from jax.experimental import pallas as pl
from jax.experimental.pallas import tpu as pltpu
from jax.sharding import PartitionSpec as P

ND = 36


def extended(array, sides, width):
    for axis, dim in sides:
        peers, length = (lax.axis_size(axis), array.shape[dim])
        up = [(i, (i + 1) % peers) for i in range(peers - 1)]
        down = [(j, i) for i, j in up]
        last = lax.slice_in_dim(array, length - width, length, axis=dim)
        initial = lax.slice_in_dim(array, 0, width, axis=dim)
        before = lax.ppermute(last, axis, up)
        after = lax.ppermute(initial, axis, down)
        array = jnp.concatenate([before, array, after], axis=dim)
    return array


def bin_tables(index, nfreq, ndir):
    freq = (index // ndir).astype(jnp.float32)
    direc = index % ndir
    fratio = jnp.exp(jnp.log(1.1) * (freq - (nfreq - 1)))
    speed = jnp.exp(-jnp.log(1.1) * freq)
    theta = 2.0 * jnp.pi * (direc.astype(jnp.float32) + 0.5) / ndir
    return (fratio, speed, jnp.cos(theta), jnp.sin(theta), direc == 0, direc == ndir - 1)


def spatial_term(wet, padded, local, metric_x, metric_y, speed, cosv, sinv):
    east = jnp.take(padded, local[0], axis=1)
    west = jnp.take(padded, local[1], axis=1)
    north = jnp.take(padded, local[2], axis=1)
    south = jnp.take(padded, local[3], axis=1)
    along_x = metric_x[None, :] * (speed * cosv)[:, None]
    along_y = metric_y[None, :] * (speed * sinv)[:, None]
    flux_x = jnp.abs(along_x) * (wet - jnp.where(along_x > 0, west, east))
    flux_y = jnp.abs(along_y) * (wet - jnp.where(along_y > 0, south, north))
    return flux_x + flux_y


def spectral_term(wet, padded, ndir, first, last, refraction, freq_shift, speed, cosv):
    rows = wet.shape[0]

    def moved_rows(offset):
        return lax.slice_in_dim(padded, ndir + offset, ndir + offset + rows, axis=0)

    prev_dir = jnp.where(first[:, None], moved_rows(ndir - 1), moved_rows(-1))
    next_dir = jnp.where(last[:, None], moved_rows(1 - ndir), moved_rows(1))
    lower = moved_rows(-ndir)
    upper = moved_rows(ndir)
    turning = refraction[None, :] * cosv[:, None]
    shifting = freq_shift[None, :] * speed[:, None]
    flux_t = jnp.abs(turning) * (wet - jnp.where(turning > 0, prev_dir, next_dir))
    flux_s = jnp.abs(shifting) * (wet - jnp.where(shifting > 0, lower, upper))
    return flux_t + flux_s


def source_step(
    moved, wind, maskf, fratio, speed, cosv, sinv, plus_fwd, minus_fwd, plus_back, minus_back
):
    steep = jnp.mean(moved * (fratio * fratio)[:, None], axis=0)
    drive = jnp.maximum(
        0.0,
        wind[0][None, :] * cosv[:, None] + wind[1][None, :] * sinv[:, None] - 0.5 * speed[:, None],
    )
    s_in = 0.3 * drive * drive * moved
    s_ds = -6.0 * fratio[:, None] * steep[None, :] * moved
    e_plus = plus_fwd(moved)
    e_minus = minus_fwd(moved)
    delta = (
        8.0
        * (fratio**4)[:, None]
        * (
            moved * moved * (e_plus / 1.25**4 + e_minus / 0.75**4)
            - 2.0 * moved * e_plus * e_minus / 0.9375**4
        )
    )
    s_nl = -2.0 * delta + plus_back(delta) + minus_back(delta)
    return (moved + 0.5 * (s_in + s_ds + s_nl)) * maskf[None, :]


def pair_matrix(first_bins, second_bins, weight, count):
    columns = jnp.arange(count, dtype=jnp.int32)[None, :]
    return weight[:, None] * (first_bins[:, None] == columns).astype(jnp.float32) + (1.0 - weight)[
        :, None
    ] * (second_bins[:, None] == columns).astype(jnp.float32)


def forward_product(matrix, values):
    return jnp.dot(
        matrix, values, precision=lax.Precision.HIGHEST, preferred_element_type=jnp.float32
    )


def backward_product(matrix, values):
    return lax.dot_general(
        matrix,
        values,
        (((0,), (0,)), ((), ())),
        precision=lax.Precision.HIGHEST,
        preferred_element_type=jnp.float32,
    )


def on_device(
    spectrum,
    wind,
    sea_mask,
    neighbours,
    metric_x,
    metric_y,
    refraction,
    freq_shift,
    dia_bins,
    dia_wts,
):
    bins_dev, points_dev = spectrum.shape
    nbins = dia_bins.shape[1]
    ndir = ND
    nfreq = nbins // ndir
    space_pos = lax.axis_index("space")
    bin_pos = lax.axis_index("bin")
    maskf = sea_mask.astype(jnp.float32)
    wet = spectrum * maskf[None, :]
    padded = extended(wet, (("space", 1),), points_dev)
    base = space_pos * points_dev - points_dev
    local = neighbours - base
    own_bins = bin_pos * bins_dev + jnp.arange(bins_dev, dtype=jnp.int32)
    fratio, speed, cosv, sinv, first, last = bin_tables(own_bins, nfreq, ndir)
    spatial = spatial_term(wet, padded, local, metric_x, metric_y, speed, cosv, sinv)
    share = points_dev // lax.axis_size("bin")
    start = bin_pos * share
    all_bins = jnp.arange(nbins, dtype=jnp.int32)
    fratio_all, speed_all, cos_all, sin_all, first_all, last_all = bin_tables(all_bins, nfreq, ndir)
    bin_pad = extended(wet, (("bin", 0),), ndir)
    spectral = spectral_term(wet, bin_pad, ndir, first, last, refraction, freq_shift, speed, cosv)
    moved_own = wet - spatial - spectral
    moved = lax.all_to_all(moved_own, "bin", split_axis=1, concat_axis=0, tiled=True)
    wind_part = lax.dynamic_slice_in_dim(wind, start, share, 1)
    mask_part = lax.dynamic_slice_in_dim(maskf, start, share, 0)
    plus_matrix = pair_matrix(dia_bins[0], dia_bins[1], dia_wts[0], nbins)
    minus_matrix = pair_matrix(dia_bins[2], dia_bins[3], dia_wts[1], nbins)
    result = source_step(
        moved,
        wind_part,
        mask_part,
        fratio_all,
        speed_all,
        cos_all,
        sin_all,
        lambda v: forward_product(plus_matrix, v),
        lambda v: forward_product(minus_matrix, v),
        lambda v: backward_product(plus_matrix, v),
        lambda v: backward_product(minus_matrix, v),
    )
    return result


LANES = 128
ROWS = 8
EDGE = 16
QUART = ND // 4
APART = 3
PIECES = 6
VMEM_ASK = 60 << 20
GROUP = 4


def chunk_plan(nloc):
    mid = nloc // 2
    plan = [(mid - d, 2 * d, 2) for d in range(1, mid + 1)]
    if mid > 3:
        plan[2] = (mid - 3, 3, 3)
    else:
        plan.insert(0, (mid, 1, 1))
    return plan


def freqs_of(chunk):
    first, step, count = chunk
    return [first + i * step for i in range(count)]


def halo_groups(plan):
    return [g for g in (plan[:1], plan[1:2], plan[2:]) if g]


def slots_of(group):
    return {f: i for i, f in enumerate(f for chunk in group for f in freqs_of(chunk))}


def runs_of(freqs):
    runs = []
    for f in sorted(freqs):
        if runs and runs[-1][1] == f:
            runs[-1] = (runs[-1][0], f + 1)
        else:
            runs.append((f, f + 1))
    return runs


def prep_kernel(points, bins, blocks, groups, full, spec_hbm, mask_ref, *refs):
    ngr = len(groups)
    nloc = bins // ND
    hs_hbm, hn_hbm = refs[:ngr], refs[ngr : 2 * ngr]
    if full:
        wet_hbm, low_hbm, high_hbm = refs[2 * ngr : 2 * ngr + 3]
    spec_v, wet_v, edge_v, in_sem, out_sem = refs[-5:]
    tiles = points // LANES
    half = ND // 2
    where = {f: (i, k) for i, group in enumerate(groups) for f, k in slots_of(group).items()}
    loads = []
    spans = []
    for lo, hi in blocks:
        start = lo * ND // ROWS * ROWS
        stop = min(-(-hi * ND // ROWS) * ROWS, bins)
        spans.append((start, stop))
        rows = pl.ds(start, stop - start)
        copy = pltpu.make_async_copy(spec_hbm.at[rows], spec_v.at[rows], in_sem.at[len(loads)])
        copy.start()
        loads.append(copy)
    masks = [mask_ref[:, c * LANES : (c + 1) * LANES].astype(jnp.float32) for c in range(tiles)]
    copies = []

    def send(src, dst):
        copy = pltpu.make_async_copy(src, dst, out_sem.at[len(copies)])
        copy.start()
        copies.append(copy)

    for (lo, hi), (start, stop), load in zip(blocks, spans, loads):
        load.wait()

        def turn(g0, count):
            for c0 in range(0, tiles, ROWS):
                cols = range(c0, c0 + ROWS)
                block = jnp.stack(
                    [spec_v[pl.ds(g0, count), c * LANES : (c + 1) * LANES] * masks[c] for c in cols], axis=0
                )
                block = jnp.swapaxes(block, 0, 1)
                for i in range(count):
                    wet_v[pl.ds(pl.multiple_of((g0 + i) * tiles + c0, ROWS), ROWS), :] = block[i]

        def relayout(t, _):
            turn(pl.multiple_of(start + t * ROWS, ROWS), ROWS)
            return 0

        lax.fori_loop(0, (stop - start) // ROWS, relayout, 0)
        rest = (stop - start) % ROWS
        if rest:
            g0 = stop - rest
            for c in range(tiles):
                tile = spec_v[pl.ds(g0, rest), c * LANES : (c + 1) * LANES]
                wet_v[pl.ds(g0 * tiles + c, rest, stride=tiles), :] = tile * masks[c]
        for f in range(lo, hi):
            base = f * ND * tiles
            if f in where:
                i, k = where[f]
                for side, (j0, row) in enumerate(((3 * QUART, tiles - 1), (QUART, 0))):
                    at = base + j0 * tiles + row
                    edge_v[f, side, ROWS:EDGE, :] = jnp.zeros((EDGE - ROWS, LANES), jnp.float32)
                    edge_v[f, side, 0:ROWS, :] = wet_v[pl.ds(at, ROWS, stride=tiles), :]
                    edge_v[f, side, ROWS : ROWS + 1, :] = wet_v[pl.ds(at + ROWS * tiles, 1), :]
                span = half * tiles
                send(wet_v.at[pl.ds(base, span)], hs_hbm[i].at[k, pl.ds(0, span)])
                send(wet_v.at[pl.ds(base + span, span)], hn_hbm[i].at[k, pl.ds(0, span)])
                send(edge_v.at[f, 0], hs_hbm[i].at[k, pl.ds(span, EDGE)])
                send(edge_v.at[f, 1], hn_hbm[i].at[k, pl.ds(span, EDGE)])
            if full:
                own = pl.ds(base, ND * tiles)
                if f == nloc - 1:
                    send(wet_v.at[own], low_hbm)
                if f == 0:
                    send(wet_v.at[own], high_hbm)
                send(wet_v.at[own], wet_hbm.at[own])
    for copy in copies:
        copy.wait()


def prep(spectrum, mask, blocks, groups, full):
    bins, points = spectrum.shape
    nloc = bins // ND
    tiles = points // LANES
    halo_rows = ND // 2 * tiles + EDGE
    halos = [jax.ShapeDtypeStruct((len(slots_of(g)), halo_rows, LANES), jnp.float32) for g in groups]
    one = jax.ShapeDtypeStruct((ND * tiles, LANES), jnp.float32)
    outs = halos + halos
    if full:
        outs += [jax.ShapeDtypeStruct((bins * tiles, LANES), jnp.float32), one, one]
    anywhere = pl.BlockSpec(memory_space=pl.ANY)
    count = sum(hi - lo for lo, hi in blocks)
    sends = 4 * sum(len(slots_of(g)) for g in groups) + (nloc + 2 if full else 0)
    res = pl.pallas_call(
        functools.partial(prep_kernel, points, bins, blocks, groups, full),
        out_shape=outs,
        in_specs=[anywhere, pl.BlockSpec(memory_space=pltpu.VMEM)],
        out_specs=[anywhere] * len(outs),
        scratch_shapes=[
            pltpu.VMEM((bins, points), jnp.float32),
            pltpu.VMEM((bins * tiles, LANES), jnp.float32),
            pltpu.VMEM((nloc, 2, EDGE, LANES), jnp.float32),
            pltpu.SemaphoreType.DMA((len(blocks),)),
            pltpu.SemaphoreType.DMA((sends,)),
        ],
        compiler_params=pltpu.CompilerParams(vmem_limit_bytes=VMEM_ASK),
        cost_estimate=pl.CostEstimate(flops=0, bytes_accessed=count * 3_000_000, transcendentals=0),
        name="prep",
    )(spectrum, mask)
    ngr = len(groups)
    return res[:ngr], res[ngr : 2 * ngr], res[2 * ngr :]


def front_kernel(
    tiles, shares, nloc, kmin, kmax, chunk, edge, joined, tab_ref, dir_ref, pos_ref, nbr_ref, mx_ref, my_ref, rf_ref, fs_ref, hs_ref, hn_ref, wet_ref, *refs
):
    nout = 1 if joined else shares
    near, outs, ext_ref = refs[: -nout - 1], refs[-nout - 1 : -1], refs[-1]
    if joined:
        outs = [outs[0].at[d] for d in range(shares)]
    place = pl.program_id(0)
    speed = tab_ref[pos_ref[0] * nloc + chunk[0] + chunk[1] * place]
    first = place == 0
    half = ND // 2
    span = half * tiles
    south, north = tiles, ROWS
    pitch = APART * (2 * tiles + ROWS)

    def rows_at(j, row, count=ROWS):
        return pl.ds(j * pitch + APART * row, count, stride=APART)

    def extend(q, _):
        for t in range(0, tiles, ROWS):
            ext_ref[rows_at(q, t), :] = hs_ref[0, pl.ds(pl.multiple_of(q * tiles + t, ROWS), ROWS), :]
            ext_ref[rows_at(q, south + t), :] = wet_ref[0, q, t : t + ROWS, :]
            ext_ref[rows_at(half + q, north + t), :] = wet_ref[0, half + q, t : t + ROWS, :]
            ext_ref[rows_at(half + q, north + tiles + t), :] = hn_ref[
                0, pl.ds(pl.multiple_of(q * tiles + t, ROWS), ROWS), :
            ]
        return 0

    lax.fori_loop(0, half, extend, 0, unroll=2)
    for q in range(QUART):
        ext_ref[pl.ds((QUART + q) * pitch + APART * (south + tiles), 1), :] = hn_ref[0, span + q : span + q + 1, :]
        ext_ref[pl.ds((3 * QUART + q) * pitch + APART * (north - 1), 1), :] = hs_ref[0, span + q : span + q + 1, :]

    side = jnp.where(first, 1.0, -1.0)
    per_share = tiles // shares
    steps = [(d, k) for d in range(shares) for k in range(per_share // ROWS)]
    firsts = {}
    for d, k in steps:
        row = (d if joined else lax.rem(pos_ref[0] + d, shares)) * per_share + k * ROWS
        firsts[d, k] = row if joined else pl.multiple_of(row, ROWS)
    sub = lax.broadcasted_iota(jnp.int32, (ROWS, LANES), 0)
    lanes, rels = {}, {}
    for way in range(4):
        for step in steps:
            src = nbr_ref[way, pl.ds(firsts[step], ROWS), :]
            lanes[way, step] = src & (LANES - 1)
            rels[way, step] = (src >> 7) - (sub + firsts[step])

    def picked(j, own, step, way, offsets):
        out = None
        for r in offsets:
            window = ext_ref[rows_at(j, own + firsts[step] + r), :]
            got = jnp.take_along_axis(window, lanes[way, step], axis=1, mode="promise_in_bounds")
            out = got if out is None else jnp.where(rels[way, step] == r, got, out)
        return out

    for quad in range(4):
        cos_up = quad in (0, 3)
        own, way_y, off_y = (
            (south, 3, range(-(kmax // LANES), -(kmin // LANES) + 1))
            if quad < 2
            else (north, 2, range(kmin // LANES, kmax // LANES + 1))
        )
        way_x, off_x = (1, (-1, 0)) if cos_up else (0, (0, 1))

        def body(q, _):
            j = quad * QUART + q
            jprev = jnp.where(j == 0, ND - 1, j - 1)
            jnext = jnp.where(j == ND - 1, 0, j + 1)
            acos = jnp.abs(dir_ref[0, j])
            asin = jnp.abs(dir_ref[1, j])
            ax, ay = speed * acos, speed * asin
            for step in steps:
                at = pl.ds(firsts[step], ROWS)
                wet = wet_ref[0, j, at, :]
                e_y = picked(j, own, step, way_y, off_y)
                e_x = picked(j, own, step, way_x, off_x)
                rf, fs = rf_ref[at, :], fs_ref[at, :]
                e_prev, e_next = wet_ref[0, jprev, at, :], wet_ref[0, jnext, at, :]
                e_t = jnp.where(rf > 0, e_prev, e_next) if cos_up else jnp.where(rf < 0, e_prev, e_next)
                if edge:
                    inner, low, high = (ref[0, j, at, :] for ref in near)
                    outer = jnp.where(first, low, high)
                    e_s = jnp.where(fs * side > 0, outer, inner)
                else:
                    e_s = jnp.where(fs > 0, near[0][0, j, at, :], near[1][0, j, at, :])
                spatial = (mx_ref[at, :] * ax) * (wet - e_x) + (my_ref[at, :] * ay) * (wet - e_y)
                spectral = (jnp.abs(rf) * acos) * (wet - e_t) + (jnp.abs(fs) * speed) * (wet - e_s)
                d, k = step
                outs[d][j, k * ROWS : (k + 1) * ROWS, :] = wet - spatial - spectral
            return 0

        lax.fori_loop(0, QUART, body, 0, unroll=3)


def front(speed, dirs, pos, nbr, par, hs, hn, slot, wet, ends, chunk, joined, shares, kmin, kmax):
    first, step, count = chunk
    tiles = nbr.shape[1]
    nloc = wet.shape[0]
    smem = pl.BlockSpec(memory_space=pltpu.SMEM)

    def freq_spec(start, step):
        return pl.BlockSpec((1, ND, tiles, LANES), lambda i: (start + i * step, 0, 0, 0))

    halo_spec = pl.BlockSpec((1,) + hs.shape[1:], lambda i: (slot + i, 0, 0))

    def whole(shape):
        return pl.BlockSpec(shape, lambda i: (0,) * len(shape))

    if ends:
        near, near_specs = (wet,) + ends, [freq_spec(1, nloc - 3), freq_spec(0, 0), freq_spec(0, 0)]
    else:
        near, near_specs = (wet, wet), [freq_spec(first - 1, step), freq_spec(first + 1, step)]
    rows = tiles // shares
    if joined:
        outs = [jax.ShapeDtypeStruct((shares, count * ND, rows, LANES), jnp.float32)]
        out_specs = [pl.BlockSpec((shares, ND, rows, LANES), lambda i: (0, i, 0, 0))]
    else:
        outs = [jax.ShapeDtypeStruct((count * ND, rows, LANES), jnp.float32)] * shares
        out_specs = [pl.BlockSpec((ND, rows, LANES), lambda i: (i, 0, 0))] * shares
    return pl.pallas_call(
        functools.partial(front_kernel, tiles, shares, nloc, kmin, kmax, chunk, bool(ends), joined),
        grid=(count,),
        out_shape=outs,
        in_specs=[smem] * 3
        + [whole(nbr.shape)] + [whole(p.shape) for p in par] + [halo_spec, halo_spec, freq_spec(first, step)]
        + near_specs,
        out_specs=out_specs,
        scratch_shapes=[pltpu.VMEM((ND * APART * (2 * tiles + ROWS), LANES), jnp.float32)],
        compiler_params=pltpu.CompilerParams(vmem_limit_bytes=VMEM_ASK),
        cost_estimate=pl.CostEstimate(flops=0, bytes_accessed=count * 22_000_000, transcendentals=0),
        name="front",
    )(speed, dirs, pos, nbr, *par, hs, hn, wet, *near)


def tail_kernel(nfreq, bins_dev, plan, spot_ref, wts_ref, ftab_ref, frs_ref, dir_ref, pos_ref, wind_ref, mask_ref, *refs):
    out_hbm, mv, base, a0, a1, a2, a3, dw, out_v, in_sem, out_sem = refs[-11:]
    parts = iter(refs[:-11])
    shares = nfreq * ND // bins_dev
    nbins = nfreq * ND
    loads = []
    for c, chunk in enumerate(plan):
        joined = c == 0
        whole = next(parts) if joined else None
        for d in range(shares):
            part = whole.at[d] if joined else next(parts)
            source = d if joined else lax.rem(pos_ref[0] + (shares - d), shares)
            for i, f in enumerate(freqs_of(chunk)):
                rows = pl.ds(source * bins_dev + f * ND, ND)
                copy = pltpu.make_async_copy(part.at[pl.ds(i * ND, ND)], mv.at[rows], in_sem.at[len(loads)])
                copy.start()
                loads.append(copy)
    zero = jnp.zeros((ROWS, LANES), jnp.float32)
    accs = (a0, a1, a2, a3)

    def clear(g, _):
        for acc in accs:
            acc[g] = zero
        return 0

    lax.fori_loop(0, nbins, clear, 0, unroll=8)
    for j in range(ND):
        dw[j] = wind_ref[0] * dir_ref[0, j] + wind_ref[1] * dir_ref[1, j]
    for copy in loads:
        copy.wait()

    def per_freq(f, steep):
        fr2, fr4, hspeed = ftab_ref[0, f], ftab_ref[1, f], ftab_ref[2, f]

        def per_group(t, total):
            j0 = t * GROUP
            g0 = f * ND + j0
            spots = [[spot_ref[4 * g0 + 4 * i + k] for k in range(4)] for i in range(GROUP)]
            own = [mv[g0 + i] for i in range(GROUP)]
            found = [[mv[b] for b in spots[i]] for i in range(GROUP)]
            adds = []
            for i in range(GROUP):
                m, (p0, p1, m0, m1) = own[i], found[i]
                wp, wm = wts_ref[2 * g0 + 2 * i], wts_ref[2 * g0 + 2 * i + 1]
                ep = p1 + wp * (p0 - p1)
                em = m1 + wm * (m0 - m1)
                mf = fr4 * m
                half = mf * (m * (ep * (1 / 1.25**4) + em * (1 / 0.75**4)) - ep * em * (2.0 / 0.9375**4))
                drive = jnp.maximum(0.0, dw[j0 + i] - hspeed)
                base[g0 + i] = m + 0.15 * (drive * drive) * m - 2.0 * half
                sp, sm = wp * half, wm * half
                adds.append((sp, half - sp, sm, half - sm))
                total = total + m
            for i in range(0, GROUP, 2):
                for acc, b0, b1, x0, x1 in zip(accs, spots[i], spots[i + 1], adds[i], adds[i + 1]):
                    old0, old1 = acc[b0], acc[b1]
                    acc[b0] = old0 + x0
                    acc[b1] = old1 + (x1 + jnp.where(b0 == b1, x0, zero))
            return total

        return steep + lax.fori_loop(0, ND // GROUP, per_group, zero, unroll=3) * fr2

    steep = lax.fori_loop(0, nfreq, per_freq, zero)
    steep = steep * (1.0 / nbins)
    mask = mask_ref[...].astype(jnp.float32)
    per = nbins // PIECES
    copies = []
    for p in range(PIECES):

        def finish(t, _):
            g0 = t * ROWS
            done = []
            for i in range(ROWS):
                g = g0 + i
                mine = base[g] - (frs_ref[g] * steep) * mv[g]
                done.append((mine + ((a0[g] + a1[g]) + (a2[g] + a3[g]))) * mask)
            turned = jnp.swapaxes(jnp.stack(done, axis=0), 0, 1)
            for c in range(ROWS):
                out_v[pl.ds(pl.multiple_of(g0, ROWS), ROWS), c * LANES : (c + 1) * LANES] = turned[c]
            return 0

        lax.fori_loop(p * per // ROWS, (p + 1) * per // ROWS, finish, 0, unroll=3)
        rows = pl.ds(p * per, per)
        copy = pltpu.make_async_copy(out_v.at[rows], out_hbm.at[rows], out_sem.at[p])
        copy.start()
        copies.append(copy)
    for copy in copies:
        copy.wait()


def tail(parts, plan, bins_dev, dia_bins, dia_wts, ftab, frs, dirs, pos, wind, mask):
    nbins = dia_bins.shape[1]
    nfreq = nbins // ND
    anywhere = pl.BlockSpec(memory_space=pl.ANY)
    smem = pl.BlockSpec(memory_space=pltpu.SMEM)
    vmem = pl.BlockSpec(memory_space=pltpu.VMEM)
    points = ROWS * LANES
    spots = dia_bins.T.reshape(-1)
    wts = dia_wts.T.reshape(-1)
    field = pltpu.VMEM((nbins, ROWS, LANES), jnp.float32)
    return pl.pallas_call(
        functools.partial(tail_kernel, nfreq, bins_dev, plan),
        out_shape=jax.ShapeDtypeStruct((nbins, points), jnp.float32),
        in_specs=[smem] * 6 + [vmem] * 2 + [anywhere] * len(parts),
        out_specs=anywhere,
        scratch_shapes=[field] * 6
        + [
            pltpu.VMEM((ND, ROWS, LANES), jnp.float32),
            pltpu.VMEM((nbins, points), jnp.float32),
            pltpu.SemaphoreType.DMA((nbins // ND,)),
            pltpu.SemaphoreType.DMA((PIECES,)),
        ],
        compiler_params=pltpu.CompilerParams(vmem_limit_bytes=VMEM_ASK),
        cost_estimate=pl.CostEstimate(flops=0, bytes_accessed=70_000_000, transcendentals=0),
        name="tail",
    )(spots, wts, ftab, frs, dirs, pos, wind, mask, *parts)


def fast_on_device(
    spectrum, wind, sea_mask, neighbours, metric_x, metric_y, refraction, freq_shift, dia_bins, dia_wts
):
    bins_dev, points = spectrum.shape
    nbins = dia_bins.shape[1]
    nfreq = nbins // ND
    nloc = bins_dev // ND
    tiles = points // LANES
    shares = lax.axis_size("bin")
    share = points // shares
    bin_pos = lax.axis_index("bin")
    space_pos = lax.axis_index("space")
    plan = chunk_plan(nloc)

    freqs = np.arange(nfreq, dtype=np.float32)
    speed = jnp.asarray(np.exp(-np.log(1.1) * freqs.astype(np.float64)).astype(np.float32))
    ratio = np.exp(np.log(1.1) * (freqs.astype(np.float64) - (nfreq - 1)))
    ftab = jnp.asarray(
        np.stack([ratio**2, 4.0 * ratio**4, 0.5 * np.exp(-np.log(1.1) * freqs)]).astype(np.float32)
    )
    frs = jnp.asarray(np.repeat(3.0 * ratio, ND).astype(np.float32))
    theta = 2.0 * np.pi * (np.arange(ND) + 0.5) / ND
    dirs = jnp.asarray(np.stack([np.cos(theta), np.sin(theta)]).astype(np.float32))

    groups = halo_groups(plan)
    early = runs_of(slots_of(groups[0]))
    mask_row = sea_mask.reshape(1, points)
    hs, hn, _ = prep(spectrum, mask_row, early, groups[:1], False)
    after, *_ = lax.optimization_barrier((spectrum, hs[0], hn[0]))
    whole_blocks = [(f, min(f + 2, nloc)) for f in range(0, nloc, 2)]
    hs_rest, hn_rest, (wet, low_out, high_out) = prep(after, mask_row, whole_blocks, groups[1:], True)
    wet = wet.reshape(nloc, ND, tiles, LANES)

    def line(array, axis, step):
        peers = lax.axis_size(axis)
        pairs = [(i, i + 1) for i in range(peers - 1)]
        if step < 0:
            pairs = [(b, a) for a, b in pairs]
        return lax.ppermute(array, axis, pairs)

    sends = list(zip(list(hs) + list(hs_rest), list(hn) + list(hn_rest)))
    halos = []

    def send_halos(*after):
        if len(halos) < len(sends):
            south, north = sends[len(halos)]
            if after:
                south, north, *_ = lax.optimization_barrier((south, north) + after)
            halos.append((line(south, "space", 1), line(north, "space", -1)))

    send_halos()
    low_in = line(low_out, "bin", 1).reshape(1, ND, tiles, LANES)
    high_in = line(high_out, "bin", -1).reshape(1, ND, tiles, LANES)

    nbr = (neighbours - space_pos * points).reshape(4, tiles, LANES)
    par = [p.reshape(tiles, LANES) for p in (metric_x, metric_y, refraction, freq_shift)]
    pos = bin_pos.reshape(1)
    kmin, kmax = points // 2, points
    arrived = []
    order = pos
    for c, chunk in enumerate(plan):
        first, step, count = chunk
        joined = c == 0
        gi, slot = [(i, slots_of(g)[first]) for i, g in enumerate(groups) if chunk in g][0]
        ends = (low_in, high_in) if first == 0 else None
        blocks = front(speed, dirs, order, nbr, par, *halos[gi], slot, wet, ends, chunk, joined, shares, kmin, kmax)
        if c == 0:
            send_halos(low_in, high_in, blocks[0])
            send_halos(*halos[-1])
        earlier = arrived[-1] if arrived else [low_in, high_in]
        order, *_ = lax.optimization_barrier((pos, blocks[0], *earlier))
        if joined:
            arrived.append([lax.all_to_all(blocks[0], "bin", split_axis=0, concat_axis=0, tiled=True)])
            continue
        here = [blocks[0]]
        for d in range(1, shares):
            rows = blocks[d]
            if c > 1:
                before = arrived[-1] if c < len(plan) - 1 else [arrived[-1][d]]
                rows, *_ = lax.optimization_barrier((rows, *before))
            here.append(lax.ppermute(rows, "bin", [(i, (i + d) % shares) for i in range(shares)]))
        arrived.append(here)
    parts = sum(arrived, [])
    wind_part = lax.dynamic_slice_in_dim(wind, bin_pos * share, share, 1).reshape(2, ROWS, LANES)
    mask_part = lax.dynamic_slice_in_dim(sea_mask, bin_pos * share, share, 0).reshape(ROWS, LANES)
    return tail(parts, plan, bins_dev, dia_bins, dia_wts, ftab, frs, dirs, pos, wind_part, mask_part)


def pick_path(spectrum, *others):
    bins_dev, points = spectrum.shape
    fits = bins_dev % (2 * ND) == ND and bins_dev > ND and points // lax.axis_size("bin") == ROWS * LANES
    return (fast_on_device if fits else on_device)(spectrum, *others)


def solution(mesh):
    return jax.shard_map(
        pick_path,
        mesh=mesh,
        in_specs=(
            P("bin", ("ens", "space")),
            P(None, ("ens", "space")),
            P("space"),
            P(None, "space"),
            P("space"),
            P("space"),
            P("space"),
            P("space"),
            P(),
            P(),
        ),
        out_specs=P(None, ("ens", "space", "bin")),
        check_vma=False,
    )
```

```python
import functools
import itertools

import jax
import jax.numpy as jnp
import numpy as np
from jax import lax
from jax.experimental import pallas as pl
from jax.experimental.pallas import tpu as pltpu
from jax.sharding import PartitionSpec as P

ND = 36


def extended(array, sides, width):
    for axis, dim in sides:
        peers, length = (lax.axis_size(axis), array.shape[dim])
        up = [(i, (i + 1) % peers) for i in range(peers - 1)]
        down = [(j, i) for i, j in up]
        last = lax.slice_in_dim(array, length - width, length, axis=dim)
        initial = lax.slice_in_dim(array, 0, width, axis=dim)
        before = lax.ppermute(last, axis, up)
        after = lax.ppermute(initial, axis, down)
        array = jnp.concatenate([before, array, after], axis=dim)
    return array


def bin_tables(index, nfreq, ndir):
    freq = (index // ndir).astype(jnp.float32)
    direc = index % ndir
    fratio = jnp.exp(jnp.log(1.1) * (freq - (nfreq - 1)))
    speed = jnp.exp(-jnp.log(1.1) * freq)
    theta = 2.0 * jnp.pi * (direc.astype(jnp.float32) + 0.5) / ndir
    return (fratio, speed, jnp.cos(theta), jnp.sin(theta), direc == 0, direc == ndir - 1)


def spatial_term(wet, padded, local, metric_x, metric_y, speed, cosv, sinv):
    east = jnp.take(padded, local[0], axis=1)
    west = jnp.take(padded, local[1], axis=1)
    north = jnp.take(padded, local[2], axis=1)
    south = jnp.take(padded, local[3], axis=1)
    along_x = metric_x[None, :] * (speed * cosv)[:, None]
    along_y = metric_y[None, :] * (speed * sinv)[:, None]
    flux_x = jnp.abs(along_x) * (wet - jnp.where(along_x > 0, west, east))
    flux_y = jnp.abs(along_y) * (wet - jnp.where(along_y > 0, south, north))
    return flux_x + flux_y


def spectral_term(wet, padded, ndir, first, last, refraction, freq_shift, speed, cosv):
    rows = wet.shape[0]

    def moved_rows(offset):
        return lax.slice_in_dim(padded, ndir + offset, ndir + offset + rows, axis=0)

    prev_dir = jnp.where(first[:, None], moved_rows(ndir - 1), moved_rows(-1))
    next_dir = jnp.where(last[:, None], moved_rows(1 - ndir), moved_rows(1))
    lower = moved_rows(-ndir)
    upper = moved_rows(ndir)
    turning = refraction[None, :] * cosv[:, None]
    shifting = freq_shift[None, :] * speed[:, None]
    flux_t = jnp.abs(turning) * (wet - jnp.where(turning > 0, prev_dir, next_dir))
    flux_s = jnp.abs(shifting) * (wet - jnp.where(shifting > 0, lower, upper))
    return flux_t + flux_s


def source_step(
    moved, wind, maskf, fratio, speed, cosv, sinv, plus_fwd, minus_fwd, plus_back, minus_back
):
    steep = jnp.mean(moved * (fratio * fratio)[:, None], axis=0)
    drive = jnp.maximum(
        0.0,
        wind[0][None, :] * cosv[:, None] + wind[1][None, :] * sinv[:, None] - 0.5 * speed[:, None],
    )
    s_in = 0.3 * drive * drive * moved
    s_ds = -6.0 * fratio[:, None] * steep[None, :] * moved
    e_plus = plus_fwd(moved)
    e_minus = minus_fwd(moved)
    delta = (
        8.0
        * (fratio**4)[:, None]
        * (
            moved * moved * (e_plus / 1.25**4 + e_minus / 0.75**4)
            - 2.0 * moved * e_plus * e_minus / 0.9375**4
        )
    )
    s_nl = -2.0 * delta + plus_back(delta) + minus_back(delta)
    return (moved + 0.5 * (s_in + s_ds + s_nl)) * maskf[None, :]


def pair_matrix(first_bins, second_bins, weight, count):
    columns = jnp.arange(count, dtype=jnp.int32)[None, :]
    return weight[:, None] * (first_bins[:, None] == columns).astype(jnp.float32) + (1.0 - weight)[
        :, None
    ] * (second_bins[:, None] == columns).astype(jnp.float32)


def forward_product(matrix, values):
    return jnp.dot(
        matrix, values, precision=lax.Precision.HIGHEST, preferred_element_type=jnp.float32
    )


def backward_product(matrix, values):
    return lax.dot_general(
        matrix,
        values,
        (((0,), (0,)), ((), ())),
        precision=lax.Precision.HIGHEST,
        preferred_element_type=jnp.float32,
    )


def on_device(
    spectrum,
    wind,
    sea_mask,
    neighbours,
    metric_x,
    metric_y,
    refraction,
    freq_shift,
    dia_bins,
    dia_wts,
):
    bins_dev, points_dev = spectrum.shape
    nbins = dia_bins.shape[1]
    ndir = ND
    nfreq = nbins // ndir
    space_pos = lax.axis_index("space")
    bin_pos = lax.axis_index("bin")
    maskf = sea_mask.astype(jnp.float32)
    wet = spectrum * maskf[None, :]
    padded = extended(wet, (("space", 1),), points_dev)
    base = space_pos * points_dev - points_dev
    local = neighbours - base
    own_bins = bin_pos * bins_dev + jnp.arange(bins_dev, dtype=jnp.int32)
    fratio, speed, cosv, sinv, first, last = bin_tables(own_bins, nfreq, ndir)
    spatial = spatial_term(wet, padded, local, metric_x, metric_y, speed, cosv, sinv)
    share = points_dev // lax.axis_size("bin")
    start = bin_pos * share
    all_bins = jnp.arange(nbins, dtype=jnp.int32)
    fratio_all, speed_all, cos_all, sin_all, first_all, last_all = bin_tables(all_bins, nfreq, ndir)
    bin_pad = extended(wet, (("bin", 0),), ndir)
    spectral = spectral_term(wet, bin_pad, ndir, first, last, refraction, freq_shift, speed, cosv)
    moved_own = wet - spatial - spectral
    moved = lax.all_to_all(moved_own, "bin", split_axis=1, concat_axis=0, tiled=True)
    wind_part = lax.dynamic_slice_in_dim(wind, start, share, 1)
    mask_part = lax.dynamic_slice_in_dim(maskf, start, share, 0)
    plus_matrix = pair_matrix(dia_bins[0], dia_bins[1], dia_wts[0], nbins)
    minus_matrix = pair_matrix(dia_bins[2], dia_bins[3], dia_wts[1], nbins)
    result = source_step(
        moved,
        wind_part,
        mask_part,
        fratio_all,
        speed_all,
        cos_all,
        sin_all,
        lambda v: forward_product(plus_matrix, v),
        lambda v: forward_product(minus_matrix, v),
        lambda v: backward_product(plus_matrix, v),
        lambda v: backward_product(minus_matrix, v),
    )
    return result


LANES = 128
ROWS = 8
EDGE = 16
QUART = ND // 4
APART = 3
PIECES = 6
VMEM_ASK = 60 << 20
GROUP = 4


def chunk_plan(nloc):
    mid = nloc // 2
    plan = [(mid - d, 2 * d, 2) for d in range(1, mid + 1)]
    if mid > 3:
        plan[2] = (mid - 3, 3, 3)
    else:
        plan.insert(0, (mid, 1, 1))
    return plan


def freqs_of(chunk):
    first, step, count = chunk
    return [first + i * step for i in range(count)]


def halo_groups(plan):
    return [g for g in (plan[:1], plan[1:2], plan[2:]) if g]


def slots_of(group):
    return {f: i for i, f in enumerate(f for chunk in group for f in freqs_of(chunk))}


def runs_of(freqs):
    runs = []
    for f in sorted(freqs):
        if runs and runs[-1][1] == f:
            runs[-1] = (runs[-1][0], f + 1)
        else:
            runs.append((f, f + 1))
    return runs


def prep_kernel(points, bins, blocks, groups, full, spec_hbm, mask_ref, *refs):
    ngr = len(groups)
    nloc = bins // ND
    hs_hbm, hn_hbm = refs[:ngr], refs[ngr : 2 * ngr]
    if full:
        wet_hbm, low_hbm, high_hbm = refs[2 * ngr : 2 * ngr + 3]
    spec_v, wet_v, edge_v, in_sem, out_sem = refs[-5:]
    tiles = points // LANES
    half = ND // 2
    where = {f: (i, k) for i, group in enumerate(groups) for f, k in slots_of(group).items()}
    loads = []
    spans = []
    for lo, hi in blocks:
        start = lo * ND // ROWS * ROWS
        stop = min(-(-hi * ND // ROWS) * ROWS, bins)
        spans.append((start, stop))
        rows = pl.ds(start, stop - start)
        copy = pltpu.make_async_copy(spec_hbm.at[rows], spec_v.at[rows], in_sem.at[len(loads)])
        copy.start()
        loads.append(copy)
    masks = [mask_ref[:, c * LANES : (c + 1) * LANES].astype(jnp.float32) for c in range(tiles)]
    copies = []

    def send(src, dst):
        copy = pltpu.make_async_copy(src, dst, out_sem.at[len(copies)])
        copy.start()
        copies.append(copy)

    for (lo, hi), (start, stop), load in zip(blocks, spans, loads):
        load.wait()

        def turn(g0, count):
            for c0 in range(0, tiles, ROWS):
                cols = range(c0, c0 + ROWS)
                block = jnp.stack(
                    [spec_v[pl.ds(g0, count), c * LANES : (c + 1) * LANES] * masks[c] for c in cols], axis=0
                )
                block = jnp.swapaxes(block, 0, 1)
                for i in range(count):
                    wet_v[pl.ds(pl.multiple_of((g0 + i) * tiles + c0, ROWS), ROWS), :] = block[i]

        def relayout(t, _):
            turn(pl.multiple_of(start + t * ROWS, ROWS), ROWS)
            return 0

        lax.fori_loop(0, (stop - start) // ROWS, relayout, 0)
        rest = (stop - start) % ROWS
        if rest:
            g0 = stop - rest
            for c in range(tiles):
                tile = spec_v[pl.ds(g0, rest), c * LANES : (c + 1) * LANES]
                wet_v[pl.ds(g0 * tiles + c, rest, stride=tiles), :] = tile * masks[c]
        for f in range(lo, hi):
            base = f * ND * tiles
            if f in where:
                i, k = where[f]
                for side, (j0, row) in enumerate(((3 * QUART, tiles - 1), (QUART, 0))):
                    at = base + j0 * tiles + row
                    edge_v[f, side, ROWS:EDGE, :] = jnp.zeros((EDGE - ROWS, LANES), jnp.float32)
                    edge_v[f, side, 0:ROWS, :] = wet_v[pl.ds(at, ROWS, stride=tiles), :]
                    edge_v[f, side, ROWS : ROWS + 1, :] = wet_v[pl.ds(at + ROWS * tiles, 1), :]
                span = half * tiles
                send(wet_v.at[pl.ds(base, span)], hs_hbm[i].at[k, pl.ds(0, span)])
                send(wet_v.at[pl.ds(base + span, span)], hn_hbm[i].at[k, pl.ds(0, span)])
                send(edge_v.at[f, 0], hs_hbm[i].at[k, pl.ds(span, EDGE)])
                send(edge_v.at[f, 1], hn_hbm[i].at[k, pl.ds(span, EDGE)])
            if full:
                own = pl.ds(base, ND * tiles)
                if f == nloc - 1:
                    send(wet_v.at[own], low_hbm)
                if f == 0:
                    send(wet_v.at[own], high_hbm)
                send(wet_v.at[own], wet_hbm.at[own])
    for copy in copies:
        copy.wait()


def prep(spectrum, mask, blocks, groups, full):
    bins, points = spectrum.shape
    nloc = bins // ND
    tiles = points // LANES
    halo_rows = ND // 2 * tiles + EDGE
    halos = [jax.ShapeDtypeStruct((len(slots_of(g)), halo_rows, LANES), jnp.float32) for g in groups]
    one = jax.ShapeDtypeStruct((ND * tiles, LANES), jnp.float32)
    outs = halos + halos
    if full:
        outs += [jax.ShapeDtypeStruct((bins * tiles, LANES), jnp.float32), one, one]
    anywhere = pl.BlockSpec(memory_space=pl.ANY)
    count = sum(hi - lo for lo, hi in blocks)
    sends = 4 * sum(len(slots_of(g)) for g in groups) + (nloc + 2 if full else 0)
    res = pl.pallas_call(
        functools.partial(prep_kernel, points, bins, blocks, groups, full),
        out_shape=outs,
        in_specs=[anywhere, pl.BlockSpec(memory_space=pltpu.VMEM)],
        out_specs=[anywhere] * len(outs),
        scratch_shapes=[
            pltpu.VMEM((bins, points), jnp.float32),
            pltpu.VMEM((bins * tiles, LANES), jnp.float32),
            pltpu.VMEM((nloc, 2, EDGE, LANES), jnp.float32),
            pltpu.SemaphoreType.DMA((len(blocks),)),
            pltpu.SemaphoreType.DMA((sends,)),
        ],
        compiler_params=pltpu.CompilerParams(vmem_limit_bytes=VMEM_ASK),
        cost_estimate=pl.CostEstimate(flops=0, bytes_accessed=count * 3_000_000, transcendentals=0),
        name="prep",
    )(spectrum, mask)
    ngr = len(groups)
    return res[:ngr], res[ngr : 2 * ngr], res[2 * ngr :]


def front_kernel(
    tiles, shares, nloc, kmin, kmax, chunk, edge, joined, tab_ref, dir_ref, pos_ref, nbr_ref, mx_ref, my_ref, rf_ref, fs_ref, hs_ref, hn_ref, wet_ref, *refs
):
    nout = 1 if joined else shares
    near, outs, ext_ref = refs[: -nout - 1], refs[-nout - 1 : -1], refs[-1]
    if joined:
        outs = [outs[0].at[d] for d in range(shares)]
    place = pl.program_id(0)
    speed = tab_ref[pos_ref[0] * nloc + chunk[0] + chunk[1] * place]
    first = place == 0
    half = ND // 2
    span = half * tiles
    south, north = tiles, ROWS
    pitch = APART * (2 * tiles + ROWS)

    def rows_at(j, row, count=ROWS):
        return pl.ds(j * pitch + APART * row, count, stride=APART)

    def extend(q, _):
        for t in range(0, tiles, ROWS):
            ext_ref[rows_at(q, t), :] = hs_ref[0, pl.ds(pl.multiple_of(q * tiles + t, ROWS), ROWS), :]
            ext_ref[rows_at(q, south + t), :] = wet_ref[0, q, t : t + ROWS, :]
            ext_ref[rows_at(half + q, north + t), :] = wet_ref[0, half + q, t : t + ROWS, :]
            ext_ref[rows_at(half + q, north + tiles + t), :] = hn_ref[
                0, pl.ds(pl.multiple_of(q * tiles + t, ROWS), ROWS), :
            ]
        return 0

    lax.fori_loop(0, half, extend, 0, unroll=2)
    for q in range(QUART):
        ext_ref[pl.ds((QUART + q) * pitch + APART * (south + tiles), 1), :] = hn_ref[0, span + q : span + q + 1, :]
        ext_ref[pl.ds((3 * QUART + q) * pitch + APART * (north - 1), 1), :] = hs_ref[0, span + q : span + q + 1, :]

    side = jnp.where(first, 1.0, -1.0)
    per_share = tiles // shares
    steps = [(d, k) for d in range(shares) for k in range(per_share // ROWS)]
    firsts = {}
    for d, k in steps:
        row = (d if joined else lax.rem(pos_ref[0] + d, shares)) * per_share + k * ROWS
        firsts[d, k] = row if joined else pl.multiple_of(row, ROWS)
    sub = lax.broadcasted_iota(jnp.int32, (ROWS, LANES), 0)
    lanes, rels = {}, {}
    for way in range(4):
        for step in steps:
            src = nbr_ref[way, pl.ds(firsts[step], ROWS), :]
            lanes[way, step] = src & (LANES - 1)
            rels[way, step] = (src >> 7) - (sub + firsts[step])

    def picked(j, own, step, way, offsets):
        out = None
        for r in offsets:
            window = ext_ref[rows_at(j, own + firsts[step] + r), :]
            got = jnp.take_along_axis(window, lanes[way, step], axis=1, mode="promise_in_bounds")
            out = got if out is None else jnp.where(rels[way, step] == r, got, out)
        return out

    for quad in range(4):
        cos_up = quad in (0, 3)
        own, way_y, off_y = (
            (south, 3, range(-(kmax // LANES), -(kmin // LANES) + 1))
            if quad < 2
            else (north, 2, range(kmin // LANES, kmax // LANES + 1))
        )
        way_x, off_x = (1, (-1, 0)) if cos_up else (0, (0, 1))

        def body(q, _):
            j = quad * QUART + q
            jprev = jnp.where(j == 0, ND - 1, j - 1)
            jnext = jnp.where(j == ND - 1, 0, j + 1)
            acos = jnp.abs(dir_ref[0, j])
            asin = jnp.abs(dir_ref[1, j])
            ax, ay = speed * acos, speed * asin
            for step in steps:
                at = pl.ds(firsts[step], ROWS)
                wet = wet_ref[0, j, at, :]
                e_y = picked(j, own, step, way_y, off_y)
                e_x = picked(j, own, step, way_x, off_x)
                rf, fs = rf_ref[at, :], fs_ref[at, :]
                e_prev, e_next = wet_ref[0, jprev, at, :], wet_ref[0, jnext, at, :]
                e_t = jnp.where(rf > 0, e_prev, e_next) if cos_up else jnp.where(rf < 0, e_prev, e_next)
                if edge:
                    inner, low, high = (ref[0, j, at, :] for ref in near)
                    outer = jnp.where(first, low, high)
                    e_s = jnp.where(fs * side > 0, outer, inner)
                else:
                    e_s = jnp.where(fs > 0, near[0][0, j, at, :], near[1][0, j, at, :])
                spatial = (mx_ref[at, :] * ax) * (wet - e_x) + (my_ref[at, :] * ay) * (wet - e_y)
                spectral = (jnp.abs(rf) * acos) * (wet - e_t) + (jnp.abs(fs) * speed) * (wet - e_s)
                d, k = step
                outs[d][j, k * ROWS : (k + 1) * ROWS, :] = wet - spatial - spectral
            return 0

        lax.fori_loop(0, QUART, body, 0, unroll=3)


def front(speed, dirs, pos, nbr, par, hs, hn, slot, wet, ends, chunk, joined, shares, kmin, kmax):
    first, step, count = chunk
    tiles = nbr.shape[1]
    nloc = wet.shape[0]
    smem = pl.BlockSpec(memory_space=pltpu.SMEM)

    def freq_spec(start, step):
        return pl.BlockSpec((1, ND, tiles, LANES), lambda i: (start + i * step, 0, 0, 0))

    halo_spec = pl.BlockSpec((1,) + hs.shape[1:], lambda i: (slot + i, 0, 0))

    def whole(shape):
        return pl.BlockSpec(shape, lambda i: (0,) * len(shape))

    if ends:
        near, near_specs = (wet,) + ends, [freq_spec(1, nloc - 3), freq_spec(0, 0), freq_spec(0, 0)]
    else:
        near, near_specs = (wet, wet), [freq_spec(first - 1, step), freq_spec(first + 1, step)]
    rows = tiles // shares
    if joined:
        outs = [jax.ShapeDtypeStruct((shares, count * ND, rows, LANES), jnp.float32)]
        out_specs = [pl.BlockSpec((shares, ND, rows, LANES), lambda i: (0, i, 0, 0))]
    else:
        outs = [jax.ShapeDtypeStruct((count * ND, rows, LANES), jnp.float32)] * shares
        out_specs = [pl.BlockSpec((ND, rows, LANES), lambda i: (i, 0, 0))] * shares
    return pl.pallas_call(
        functools.partial(front_kernel, tiles, shares, nloc, kmin, kmax, chunk, bool(ends), joined),
        grid=(count,),
        out_shape=outs,
        in_specs=[smem] * 3
        + [whole(nbr.shape)] + [whole(p.shape) for p in par] + [halo_spec, halo_spec, freq_spec(first, step)]
        + near_specs,
        out_specs=out_specs,
        scratch_shapes=[pltpu.VMEM((ND * APART * (2 * tiles + ROWS), LANES), jnp.float32)],
        compiler_params=pltpu.CompilerParams(vmem_limit_bytes=VMEM_ASK),
        cost_estimate=pl.CostEstimate(flops=0, bytes_accessed=count * 22_000_000, transcendentals=0),
        name="front",
    )(speed, dirs, pos, nbr, *par, hs, hn, wet, *near)


def tail_kernel(nfreq, bins_dev, plan, spot_ref, wts_ref, ftab_ref, frs_ref, dir_ref, pos_ref, wind_ref, mask_ref, *refs):
    out_hbm, mv, base, a0, a1, a2, a3, dw, out_v, in_sem, out_sem = refs[-11:]
    parts = iter(refs[:-11])
    shares = nfreq * ND // bins_dev
    nbins = nfreq * ND
    loads = []
    for c, chunk in enumerate(plan):
        joined = c == 0
        whole = next(parts) if joined else None
        for d in range(shares):
            part = whole.at[d] if joined else next(parts)
            source = d if joined else lax.rem(pos_ref[0] + (shares - d), shares)
            for i, f in enumerate(freqs_of(chunk)):
                rows = pl.ds(source * bins_dev + f * ND, ND)
                copy = pltpu.make_async_copy(part.at[pl.ds(i * ND, ND)], mv.at[rows], in_sem.at[len(loads)])
                copy.start()
                loads.append(copy)
    zero = jnp.zeros((ROWS, LANES), jnp.float32)
    accs = (a0, a1, a2, a3)

    def clear(g, _):
        for acc in accs:
            acc[g] = zero
        return 0

    lax.fori_loop(0, nbins, clear, 0, unroll=8)
    for j in range(ND):
        dw[j] = wind_ref[0] * dir_ref[0, j] + wind_ref[1] * dir_ref[1, j]
    for copy in loads:
        copy.wait()

    def per_freq(f, steep):
        fr2, fr4, hspeed = ftab_ref[0, f], ftab_ref[1, f], ftab_ref[2, f]

        def per_group(t, total):
            j0 = t * GROUP
            g0 = f * ND + j0
            spots = [[spot_ref[4 * g0 + 4 * i + k] for k in range(4)] for i in range(GROUP)]
            own = [mv[g0 + i] for i in range(GROUP)]
            found = [[mv[b] for b in spots[i]] for i in range(GROUP)]
            adds = []
            for i in range(GROUP):
                m, (p0, p1, m0, m1) = own[i], found[i]
                wp, wm = wts_ref[2 * g0 + 2 * i], wts_ref[2 * g0 + 2 * i + 1]
                ep = p1 + wp * (p0 - p1)
                em = m1 + wm * (m0 - m1)
                mf = fr4 * m
                half = mf * (m * (ep * (1 / 1.25**4) + em * (1 / 0.75**4)) - ep * em * (2.0 / 0.9375**4))
                drive = jnp.maximum(0.0, dw[j0 + i] - hspeed)
                base[g0 + i] = m + 0.15 * (drive * drive) * m - 2.0 * half
                sp, sm = wp * half, wm * half
                adds.append((sp, half - sp, sm, half - sm))
                total = total + m
            for i in range(0, GROUP, 2):
                for acc, b0, b1, x0, x1 in zip(accs, spots[i], spots[i + 1], adds[i], adds[i + 1]):
                    old0, old1 = acc[b0], acc[b1]
                    acc[b0] = old0 + x0
                    acc[b1] = old1 + (x1 + jnp.where(b0 == b1, x0, zero))
            return total

        return steep + lax.fori_loop(0, ND // GROUP, per_group, zero, unroll=3) * fr2

    steep = lax.fori_loop(0, nfreq, per_freq, zero)
    steep = steep * (1.0 / nbins)
    mask = mask_ref[...].astype(jnp.float32)
    per = nbins // PIECES
    copies = []
    for p in range(PIECES):

        def finish(t, _):
            g0 = t * ROWS
            done = []
            for i in range(ROWS):
                g = g0 + i
                mine = base[g] - (frs_ref[g] * steep) * mv[g]
                done.append((mine + ((a0[g] + a1[g]) + (a2[g] + a3[g]))) * mask)
            turned = jnp.swapaxes(jnp.stack(done, axis=0), 0, 1)
            for c in range(ROWS):
                out_v[pl.ds(pl.multiple_of(g0, ROWS), ROWS), c * LANES : (c + 1) * LANES] = turned[c]
            return 0

        lax.fori_loop(p * per // ROWS, (p + 1) * per // ROWS, finish, 0, unroll=3)
        rows = pl.ds(p * per, per)
        copy = pltpu.make_async_copy(out_v.at[rows], out_hbm.at[rows], out_sem.at[p])
        copy.start()
        copies.append(copy)
    for copy in copies:
        copy.wait()


def tail(parts, plan, bins_dev, dia_bins, dia_wts, ftab, frs, dirs, pos, wind, mask):
    nbins = dia_bins.shape[1]
    nfreq = nbins // ND
    anywhere = pl.BlockSpec(memory_space=pl.ANY)
    smem = pl.BlockSpec(memory_space=pltpu.SMEM)
    vmem = pl.BlockSpec(memory_space=pltpu.VMEM)
    points = ROWS * LANES
    spots = dia_bins.T.reshape(-1)
    wts = dia_wts.T.reshape(-1)
    field = pltpu.VMEM((nbins, ROWS, LANES), jnp.float32)
    return pl.pallas_call(
        functools.partial(tail_kernel, nfreq, bins_dev, plan),
        out_shape=jax.ShapeDtypeStruct((nbins, points), jnp.float32),
        in_specs=[smem] * 6 + [vmem] * 2 + [anywhere] * len(parts),
        out_specs=anywhere,
        scratch_shapes=[field] * 6
        + [
            pltpu.VMEM((ND, ROWS, LANES), jnp.float32),
            pltpu.VMEM((nbins, points), jnp.float32),
            pltpu.SemaphoreType.DMA((nbins // ND,)),
            pltpu.SemaphoreType.DMA((PIECES,)),
        ],
        compiler_params=pltpu.CompilerParams(vmem_limit_bytes=VMEM_ASK),
        cost_estimate=pl.CostEstimate(flops=0, bytes_accessed=70_000_000, transcendentals=0),
        name="tail",
    )(spots, wts, ftab, frs, dirs, pos, wind, mask, *parts)


def fast_on_device(
    spectrum, wind, sea_mask, neighbours, metric_x, metric_y, refraction, freq_shift, dia_bins, dia_wts
):
    bins_dev, points = spectrum.shape
    nbins = dia_bins.shape[1]
    nfreq = nbins // ND
    nloc = bins_dev // ND
    tiles = points // LANES
    shares = lax.axis_size("bin")
    share = points // shares
    bin_pos = lax.axis_index("bin")
    space_pos = lax.axis_index("space")
    plan = chunk_plan(nloc)

    freqs = np.arange(nfreq, dtype=np.float32)
    speed = jnp.asarray(np.exp(-np.log(1.1) * freqs.astype(np.float64)).astype(np.float32))
    ratio = np.exp(np.log(1.1) * (freqs.astype(np.float64) - (nfreq - 1)))
    ftab = jnp.asarray(
        np.stack([ratio**2, 4.0 * ratio**4, 0.5 * np.exp(-np.log(1.1) * freqs)]).astype(np.float32)
    )
    frs = jnp.asarray(np.repeat(3.0 * ratio, ND).astype(np.float32))
    theta = 2.0 * np.pi * (np.arange(ND) + 0.5) / ND
    dirs = jnp.asarray(np.stack([np.cos(theta), np.sin(theta)]).astype(np.float32))

    groups = halo_groups(plan)
    early = runs_of(slots_of(groups[0]))
    mask_row = sea_mask.reshape(1, points)
    hs, hn, _ = prep(spectrum, mask_row, early, groups[:1], False)
    after, *_ = lax.optimization_barrier((spectrum, hs[0], hn[0]))
    whole_blocks = [(f, min(f + 2, nloc)) for f in range(0, nloc, 2)]
    hs_rest, hn_rest, (wet, low_out, high_out) = prep(after, mask_row, whole_blocks, groups[1:], True)
    wet = wet.reshape(nloc, ND, tiles, LANES)

    def line(array, axis, step):
        peers = lax.axis_size(axis)
        pairs = [(i, i + 1) for i in range(peers - 1)]
        if step < 0:
            pairs = [(b, a) for a, b in pairs]
        return lax.ppermute(array, axis, pairs)

    sends = list(zip(list(hs) + list(hs_rest), list(hn) + list(hn_rest)))
    halos = []

    def send_halos(*after):
        if len(halos) < len(sends):
            south, north = sends[len(halos)]
            if after:
                south, north, *_ = lax.optimization_barrier((south, north) + after)
            halos.append((line(south, "space", 1), line(north, "space", -1)))

    send_halos()
    send_halos()
    low_in = line(low_out, "bin", 1).reshape(1, ND, tiles, LANES)
    high_in = line(high_out, "bin", -1).reshape(1, ND, tiles, LANES)

    nbr = (neighbours - space_pos * points).reshape(4, tiles, LANES)
    par = [p.reshape(tiles, LANES) for p in (metric_x, metric_y, refraction, freq_shift)]
    pos = bin_pos.reshape(1)
    kmin, kmax = points // 2, points
    arrived = []
    order = pos
    for c, chunk in enumerate(plan):
        first, step, count = chunk
        joined = c == 0
        gi, slot = [(i, slots_of(g)[first]) for i, g in enumerate(groups) if chunk in g][0]
        ends = (low_in, high_in) if first == 0 else None
        blocks = front(speed, dirs, order, nbr, par, *halos[gi], slot, wet, ends, chunk, joined, shares, kmin, kmax)
        if c == 0:
            send_halos(low_in, high_in, blocks[0])
        earlier = arrived[-1] if arrived else [low_in, high_in]
        order, *_ = lax.optimization_barrier((pos, blocks[0], *earlier))
        if joined:
            arrived.append([lax.all_to_all(blocks[0], "bin", split_axis=0, concat_axis=0, tiled=True)])
            continue
        here = [blocks[0]]
        for d in range(1, shares):
            rows = blocks[d]
            if c > 1:
                before = arrived[-1] if c < len(plan) - 1 else [arrived[-1][d]]
                rows, *_ = lax.optimization_barrier((rows, *before))
            here.append(lax.ppermute(rows, "bin", [(i, (i + d) % shares) for i in range(shares)]))
        arrived.append(here)
    parts = sum(arrived, [])
    wind_part = lax.dynamic_slice_in_dim(wind, bin_pos * share, share, 1).reshape(2, ROWS, LANES)
    mask_part = lax.dynamic_slice_in_dim(sea_mask, bin_pos * share, share, 0).reshape(ROWS, LANES)
    return tail(parts, plan, bins_dev, dia_bins, dia_wts, ftab, frs, dirs, pos, wind_part, mask_part)


def pick_path(spectrum, *others):
    bins_dev, points = spectrum.shape
    fits = bins_dev % (2 * ND) == ND and bins_dev > ND and points // lax.axis_size("bin") == ROWS * LANES
    return (fast_on_device if fits else on_device)(spectrum, *others)


def solution(mesh):
    return jax.shard_map(
        pick_path,
        mesh=mesh,
        in_specs=(
            P("bin", ("ens", "space")),
            P(None, ("ens", "space")),
            P("space"),
            P(None, "space"),
            P("space"),
            P("space"),
            P("space"),
            P("space"),
            P(),
            P(),
        ),
        out_specs=P(None, ("ens", "space", "bin")),
        check_vma=False,
    )
```

```python
import functools
import itertools

import jax
import jax.numpy as jnp
import numpy as np
from jax import lax
from jax.experimental import pallas as pl
from jax.experimental.pallas import tpu as pltpu
from jax.sharding import PartitionSpec as P

ND = 36


def extended(array, sides, width):
    for axis, dim in sides:
        peers, length = (lax.axis_size(axis), array.shape[dim])
        up = [(i, (i + 1) % peers) for i in range(peers - 1)]
        down = [(j, i) for i, j in up]
        last = lax.slice_in_dim(array, length - width, length, axis=dim)
        initial = lax.slice_in_dim(array, 0, width, axis=dim)
        before = lax.ppermute(last, axis, up)
        after = lax.ppermute(initial, axis, down)
        array = jnp.concatenate([before, array, after], axis=dim)
    return array


def bin_tables(index, nfreq, ndir):
    freq = (index // ndir).astype(jnp.float32)
    direc = index % ndir
    fratio = jnp.exp(jnp.log(1.1) * (freq - (nfreq - 1)))
    speed = jnp.exp(-jnp.log(1.1) * freq)
    theta = 2.0 * jnp.pi * (direc.astype(jnp.float32) + 0.5) / ndir
    return (fratio, speed, jnp.cos(theta), jnp.sin(theta), direc == 0, direc == ndir - 1)


def spatial_term(wet, padded, local, metric_x, metric_y, speed, cosv, sinv):
    east = jnp.take(padded, local[0], axis=1)
    west = jnp.take(padded, local[1], axis=1)
    north = jnp.take(padded, local[2], axis=1)
    south = jnp.take(padded, local[3], axis=1)
    along_x = metric_x[None, :] * (speed * cosv)[:, None]
    along_y = metric_y[None, :] * (speed * sinv)[:, None]
    flux_x = jnp.abs(along_x) * (wet - jnp.where(along_x > 0, west, east))
    flux_y = jnp.abs(along_y) * (wet - jnp.where(along_y > 0, south, north))
    return flux_x + flux_y


def spectral_term(wet, padded, ndir, first, last, refraction, freq_shift, speed, cosv):
    rows = wet.shape[0]

    def moved_rows(offset):
        return lax.slice_in_dim(padded, ndir + offset, ndir + offset + rows, axis=0)

    prev_dir = jnp.where(first[:, None], moved_rows(ndir - 1), moved_rows(-1))
    next_dir = jnp.where(last[:, None], moved_rows(1 - ndir), moved_rows(1))
    lower = moved_rows(-ndir)
    upper = moved_rows(ndir)
    turning = refraction[None, :] * cosv[:, None]
    shifting = freq_shift[None, :] * speed[:, None]
    flux_t = jnp.abs(turning) * (wet - jnp.where(turning > 0, prev_dir, next_dir))
    flux_s = jnp.abs(shifting) * (wet - jnp.where(shifting > 0, lower, upper))
    return flux_t + flux_s


def source_step(
    moved, wind, maskf, fratio, speed, cosv, sinv, plus_fwd, minus_fwd, plus_back, minus_back
):
    steep = jnp.mean(moved * (fratio * fratio)[:, None], axis=0)
    drive = jnp.maximum(
        0.0,
        wind[0][None, :] * cosv[:, None] + wind[1][None, :] * sinv[:, None] - 0.5 * speed[:, None],
    )
    s_in = 0.3 * drive * drive * moved
    s_ds = -6.0 * fratio[:, None] * steep[None, :] * moved
    e_plus = plus_fwd(moved)
    e_minus = minus_fwd(moved)
    delta = (
        8.0
        * (fratio**4)[:, None]
        * (
            moved * moved * (e_plus / 1.25**4 + e_minus / 0.75**4)
            - 2.0 * moved * e_plus * e_minus / 0.9375**4
        )
    )
    s_nl = -2.0 * delta + plus_back(delta) + minus_back(delta)
    return (moved + 0.5 * (s_in + s_ds + s_nl)) * maskf[None, :]


def pair_matrix(first_bins, second_bins, weight, count):
    columns = jnp.arange(count, dtype=jnp.int32)[None, :]
    return weight[:, None] * (first_bins[:, None] == columns).astype(jnp.float32) + (1.0 - weight)[
        :, None
    ] * (second_bins[:, None] == columns).astype(jnp.float32)


def forward_product(matrix, values):
    return jnp.dot(
        matrix, values, precision=lax.Precision.HIGHEST, preferred_element_type=jnp.float32
    )


def backward_product(matrix, values):
    return lax.dot_general(
        matrix,
        values,
        (((0,), (0,)), ((), ())),
        precision=lax.Precision.HIGHEST,
        preferred_element_type=jnp.float32,
    )


def on_device(
    spectrum,
    wind,
    sea_mask,
    neighbours,
    metric_x,
    metric_y,
    refraction,
    freq_shift,
    dia_bins,
    dia_wts,
):
    bins_dev, points_dev = spectrum.shape
    nbins = dia_bins.shape[1]
    ndir = ND
    nfreq = nbins // ndir
    space_pos = lax.axis_index("space")
    bin_pos = lax.axis_index("bin")
    maskf = sea_mask.astype(jnp.float32)
    wet = spectrum * maskf[None, :]
    padded = extended(wet, (("space", 1),), points_dev)
    base = space_pos * points_dev - points_dev
    local = neighbours - base
    own_bins = bin_pos * bins_dev + jnp.arange(bins_dev, dtype=jnp.int32)
    fratio, speed, cosv, sinv, first, last = bin_tables(own_bins, nfreq, ndir)
    spatial = spatial_term(wet, padded, local, metric_x, metric_y, speed, cosv, sinv)
    share = points_dev // lax.axis_size("bin")
    start = bin_pos * share
    all_bins = jnp.arange(nbins, dtype=jnp.int32)
    fratio_all, speed_all, cos_all, sin_all, first_all, last_all = bin_tables(all_bins, nfreq, ndir)
    bin_pad = extended(wet, (("bin", 0),), ndir)
    spectral = spectral_term(wet, bin_pad, ndir, first, last, refraction, freq_shift, speed, cosv)
    moved_own = wet - spatial - spectral
    moved = lax.all_to_all(moved_own, "bin", split_axis=1, concat_axis=0, tiled=True)
    wind_part = lax.dynamic_slice_in_dim(wind, start, share, 1)
    mask_part = lax.dynamic_slice_in_dim(maskf, start, share, 0)
    plus_matrix = pair_matrix(dia_bins[0], dia_bins[1], dia_wts[0], nbins)
    minus_matrix = pair_matrix(dia_bins[2], dia_bins[3], dia_wts[1], nbins)
    result = source_step(
        moved,
        wind_part,
        mask_part,
        fratio_all,
        speed_all,
        cos_all,
        sin_all,
        lambda v: forward_product(plus_matrix, v),
        lambda v: forward_product(minus_matrix, v),
        lambda v: backward_product(plus_matrix, v),
        lambda v: backward_product(minus_matrix, v),
    )
    return result


LANES = 128
ROWS = 8
EDGE = 16
QUART = ND // 4
APART = 3
PIECES = 6
VMEM_ASK = 60 << 20
GROUP = 4


def chunk_plan(nloc):
    mid = nloc // 2
    plan = [(mid - d, 2 * d, 2) for d in range(1, mid + 1)]
    if mid > 3:
        plan[2] = (mid - 3, 3, 3)
    else:
        plan.insert(0, (mid, 1, 1))
    return plan


def freqs_of(chunk):
    first, step, count = chunk
    return [first + i * step for i in range(count)]


def halo_groups(plan):
    return [g for g in (plan[:1], plan[1:]) if g]


def slots_of(group):
    return {f: i for i, f in enumerate(f for chunk in group for f in freqs_of(chunk))}


def runs_of(freqs):
    runs = []
    for f in sorted(freqs):
        if runs and runs[-1][1] == f:
            runs[-1] = (runs[-1][0], f + 1)
        else:
            runs.append((f, f + 1))
    return runs


def prep_kernel(points, bins, blocks, groups, full, spec_hbm, mask_ref, *refs):
    ngr = len(groups)
    nloc = bins // ND
    hs_hbm, hn_hbm = refs[:ngr], refs[ngr : 2 * ngr]
    if full:
        wet_hbm, low_hbm, high_hbm = refs[2 * ngr : 2 * ngr + 3]
    spec_v, wet_v, edge_v, in_sem, out_sem = refs[-5:]
    tiles = points // LANES
    half = ND // 2
    where = {f: (i, k) for i, group in enumerate(groups) for f, k in slots_of(group).items()}
    loads = []
    spans = []
    for lo, hi in blocks:
        start = lo * ND // ROWS * ROWS
        stop = min(-(-hi * ND // ROWS) * ROWS, bins)
        spans.append((start, stop))
        rows = pl.ds(start, stop - start)
        copy = pltpu.make_async_copy(spec_hbm.at[rows], spec_v.at[rows], in_sem.at[len(loads)])
        copy.start()
        loads.append(copy)
    masks = [mask_ref[:, c * LANES : (c + 1) * LANES].astype(jnp.float32) for c in range(tiles)]
    copies = []

    def send(src, dst):
        copy = pltpu.make_async_copy(src, dst, out_sem.at[len(copies)])
        copy.start()
        copies.append(copy)

    for (lo, hi), (start, stop), load in zip(blocks, spans, loads):
        load.wait()

        def turn(g0, count):
            for c0 in range(0, tiles, ROWS):
                cols = range(c0, c0 + ROWS)
                block = jnp.stack(
                    [spec_v[pl.ds(g0, count), c * LANES : (c + 1) * LANES] * masks[c] for c in cols], axis=0
                )
                block = jnp.swapaxes(block, 0, 1)
                for i in range(count):
                    wet_v[pl.ds(pl.multiple_of((g0 + i) * tiles + c0, ROWS), ROWS), :] = block[i]

        def relayout(t, _):
            turn(pl.multiple_of(start + t * ROWS, ROWS), ROWS)
            return 0

        lax.fori_loop(0, (stop - start) // ROWS, relayout, 0)
        rest = (stop - start) % ROWS
        if rest:
            g0 = stop - rest
            for c in range(tiles):
                tile = spec_v[pl.ds(g0, rest), c * LANES : (c + 1) * LANES]
                wet_v[pl.ds(g0 * tiles + c, rest, stride=tiles), :] = tile * masks[c]
        for f in range(lo, hi):
            base = f * ND * tiles
            if f in where:
                i, k = where[f]
                for side, (j0, row) in enumerate(((3 * QUART, tiles - 1), (QUART, 0))):
                    at = base + j0 * tiles + row
                    edge_v[f, side, ROWS:EDGE, :] = jnp.zeros((EDGE - ROWS, LANES), jnp.float32)
                    edge_v[f, side, 0:ROWS, :] = wet_v[pl.ds(at, ROWS, stride=tiles), :]
                    edge_v[f, side, ROWS : ROWS + 1, :] = wet_v[pl.ds(at + ROWS * tiles, 1), :]
                span = half * tiles
                send(wet_v.at[pl.ds(base, span)], hs_hbm[i].at[k, pl.ds(0, span)])
                send(wet_v.at[pl.ds(base + span, span)], hn_hbm[i].at[k, pl.ds(0, span)])
                send(edge_v.at[f, 0], hs_hbm[i].at[k, pl.ds(span, EDGE)])
                send(edge_v.at[f, 1], hn_hbm[i].at[k, pl.ds(span, EDGE)])
            if full:
                own = pl.ds(base, ND * tiles)
                if f == nloc - 1:
                    send(wet_v.at[own], low_hbm)
                if f == 0:
                    send(wet_v.at[own], high_hbm)
                send(wet_v.at[own], wet_hbm.at[own])
    for copy in copies:
        copy.wait()


def prep(spectrum, mask, blocks, groups, full):
    bins, points = spectrum.shape
    nloc = bins // ND
    tiles = points // LANES
    halo_rows = ND // 2 * tiles + EDGE
    halos = [jax.ShapeDtypeStruct((len(slots_of(g)), halo_rows, LANES), jnp.float32) for g in groups]
    one = jax.ShapeDtypeStruct((ND * tiles, LANES), jnp.float32)
    outs = halos + halos
    if full:
        outs += [jax.ShapeDtypeStruct((bins * tiles, LANES), jnp.float32), one, one]
    anywhere = pl.BlockSpec(memory_space=pl.ANY)
    count = sum(hi - lo for lo, hi in blocks)
    sends = 4 * sum(len(slots_of(g)) for g in groups) + (nloc + 2 if full else 0)
    res = pl.pallas_call(
        functools.partial(prep_kernel, points, bins, blocks, groups, full),
        out_shape=outs,
        in_specs=[anywhere, pl.BlockSpec(memory_space=pltpu.VMEM)],
        out_specs=[anywhere] * len(outs),
        scratch_shapes=[
            pltpu.VMEM((bins, points), jnp.float32),
            pltpu.VMEM((bins * tiles, LANES), jnp.float32),
            pltpu.VMEM((nloc, 2, EDGE, LANES), jnp.float32),
            pltpu.SemaphoreType.DMA((len(blocks),)),
            pltpu.SemaphoreType.DMA((sends,)),
        ],
        compiler_params=pltpu.CompilerParams(vmem_limit_bytes=VMEM_ASK),
        cost_estimate=pl.CostEstimate(flops=0, bytes_accessed=count * 3_000_000, transcendentals=0),
        name="prep",
    )(spectrum, mask)
    ngr = len(groups)
    return res[:ngr], res[ngr : 2 * ngr], res[2 * ngr :]


def front_kernel(
    tiles, shares, nloc, kmin, kmax, chunk, edge, joined, tab_ref, dir_ref, pos_ref, nbr_ref, mx_ref, my_ref, rf_ref, fs_ref, hs_ref, hn_ref, wet_ref, *refs
):
    nout = 1 if joined else shares
    near, outs, ext_ref = refs[: -nout - 1], refs[-nout - 1 : -1], refs[-1]
    if joined:
        outs = [outs[0].at[d] for d in range(shares)]
    place = pl.program_id(0)
    speed = tab_ref[pos_ref[0] * nloc + chunk[0] + chunk[1] * place]
    first = place == 0
    half = ND // 2
    span = half * tiles
    south, north = tiles, ROWS
    pitch = APART * (2 * tiles + ROWS)

    def rows_at(j, row, count=ROWS):
        return pl.ds(j * pitch + APART * row, count, stride=APART)

    def extend(q, _):
        for t in range(0, tiles, ROWS):
            ext_ref[rows_at(q, t), :] = hs_ref[0, pl.ds(pl.multiple_of(q * tiles + t, ROWS), ROWS), :]
            ext_ref[rows_at(q, south + t), :] = wet_ref[0, q, t : t + ROWS, :]
            ext_ref[rows_at(half + q, north + t), :] = wet_ref[0, half + q, t : t + ROWS, :]
            ext_ref[rows_at(half + q, north + tiles + t), :] = hn_ref[
                0, pl.ds(pl.multiple_of(q * tiles + t, ROWS), ROWS), :
            ]
        return 0

    lax.fori_loop(0, half, extend, 0, unroll=2)
    for q in range(QUART):
        ext_ref[pl.ds((QUART + q) * pitch + APART * (south + tiles), 1), :] = hn_ref[0, span + q : span + q + 1, :]
        ext_ref[pl.ds((3 * QUART + q) * pitch + APART * (north - 1), 1), :] = hs_ref[0, span + q : span + q + 1, :]

    side = jnp.where(first, 1.0, -1.0)
    per_share = tiles // shares
    steps = [(d, k) for d in range(shares) for k in range(per_share // ROWS)]
    firsts = {}
    for d, k in steps:
        row = (d if joined else lax.rem(pos_ref[0] + d, shares)) * per_share + k * ROWS
        firsts[d, k] = row if joined else pl.multiple_of(row, ROWS)
    sub = lax.broadcasted_iota(jnp.int32, (ROWS, LANES), 0)
    lanes, rels = {}, {}
    for way in range(4):
        for step in steps:
            src = nbr_ref[way, pl.ds(firsts[step], ROWS), :]
            lanes[way, step] = src & (LANES - 1)
            rels[way, step] = (src >> 7) - (sub + firsts[step])

    def picked(j, own, step, way, offsets):
        out = None
        for r in offsets:
            window = ext_ref[rows_at(j, own + firsts[step] + r), :]
            got = jnp.take_along_axis(window, lanes[way, step], axis=1, mode="promise_in_bounds")
            out = got if out is None else jnp.where(rels[way, step] == r, got, out)
        return out

    for quad in range(4):
        cos_up = quad in (0, 3)
        own, way_y, off_y = (
            (south, 3, range(-(kmax // LANES), -(kmin // LANES) + 1))
            if quad < 2
            else (north, 2, range(kmin // LANES, kmax // LANES + 1))
        )
        way_x, off_x = (1, (-1, 0)) if cos_up else (0, (0, 1))

        def body(q, _):
            j = quad * QUART + q
            jprev = jnp.where(j == 0, ND - 1, j - 1)
            jnext = jnp.where(j == ND - 1, 0, j + 1)
            acos = jnp.abs(dir_ref[0, j])
            asin = jnp.abs(dir_ref[1, j])
            ax, ay = speed * acos, speed * asin
            for step in steps:
                at = pl.ds(firsts[step], ROWS)
                wet = wet_ref[0, j, at, :]
                e_y = picked(j, own, step, way_y, off_y)
                e_x = picked(j, own, step, way_x, off_x)
                rf, fs = rf_ref[at, :], fs_ref[at, :]
                e_prev, e_next = wet_ref[0, jprev, at, :], wet_ref[0, jnext, at, :]
                e_t = jnp.where(rf > 0, e_prev, e_next) if cos_up else jnp.where(rf < 0, e_prev, e_next)
                if edge:
                    inner, low, high = (ref[0, j, at, :] for ref in near)
                    outer = jnp.where(first, low, high)
                    e_s = jnp.where(fs * side > 0, outer, inner)
                else:
                    e_s = jnp.where(fs > 0, near[0][0, j, at, :], near[1][0, j, at, :])
                spatial = (mx_ref[at, :] * ax) * (wet - e_x) + (my_ref[at, :] * ay) * (wet - e_y)
                spectral = (jnp.abs(rf) * acos) * (wet - e_t) + (jnp.abs(fs) * speed) * (wet - e_s)
                d, k = step
                outs[d][j, k * ROWS : (k + 1) * ROWS, :] = wet - spatial - spectral
            return 0

        lax.fori_loop(0, QUART, body, 0, unroll=3)


def front(speed, dirs, pos, nbr, par, hs, hn, slot, wet, ends, chunk, joined, shares, kmin, kmax):
    first, step, count = chunk
    tiles = nbr.shape[1]
    nloc = wet.shape[0]
    smem = pl.BlockSpec(memory_space=pltpu.SMEM)

    def freq_spec(start, step):
        return pl.BlockSpec((1, ND, tiles, LANES), lambda i: (start + i * step, 0, 0, 0))

    halo_spec = pl.BlockSpec((1,) + hs.shape[1:], lambda i: (slot + i, 0, 0))

    def whole(shape):
        return pl.BlockSpec(shape, lambda i: (0,) * len(shape))

    if ends:
        near, near_specs = (wet,) + ends, [freq_spec(1, nloc - 3), freq_spec(0, 0), freq_spec(0, 0)]
    else:
        near, near_specs = (wet, wet), [freq_spec(first - 1, step), freq_spec(first + 1, step)]
    rows = tiles // shares
    if joined:
        outs = [jax.ShapeDtypeStruct((shares, count * ND, rows, LANES), jnp.float32)]
        out_specs = [pl.BlockSpec((shares, ND, rows, LANES), lambda i: (0, i, 0, 0))]
    else:
        outs = [jax.ShapeDtypeStruct((count * ND, rows, LANES), jnp.float32)] * shares
        out_specs = [pl.BlockSpec((ND, rows, LANES), lambda i: (i, 0, 0))] * shares
    return pl.pallas_call(
        functools.partial(front_kernel, tiles, shares, nloc, kmin, kmax, chunk, bool(ends), joined),
        grid=(count,),
        out_shape=outs,
        in_specs=[smem] * 3
        + [whole(nbr.shape)] + [whole(p.shape) for p in par] + [halo_spec, halo_spec, freq_spec(first, step)]
        + near_specs,
        out_specs=out_specs,
        scratch_shapes=[pltpu.VMEM((ND * APART * (2 * tiles + ROWS), LANES), jnp.float32)],
        compiler_params=pltpu.CompilerParams(vmem_limit_bytes=VMEM_ASK),
        cost_estimate=pl.CostEstimate(flops=0, bytes_accessed=count * 22_000_000, transcendentals=0),
        name="front",
    )(speed, dirs, pos, nbr, *par, hs, hn, wet, *near)


def tail_kernel(nfreq, bins_dev, plan, spot_ref, wts_ref, ftab_ref, frs_ref, dir_ref, pos_ref, wind_ref, mask_ref, *refs):
    out_hbm, mv, base, a0, a1, a2, a3, dw, out_v, in_sem, out_sem = refs[-11:]
    parts = iter(refs[:-11])
    shares = nfreq * ND // bins_dev
    nbins = nfreq * ND
    loads = []
    for c, chunk in enumerate(plan):
        joined = c == 0
        whole = next(parts) if joined else None
        for d in range(shares):
            part = whole.at[d] if joined else next(parts)
            source = d if joined else lax.rem(pos_ref[0] + (shares - d), shares)
            for i, f in enumerate(freqs_of(chunk)):
                rows = pl.ds(source * bins_dev + f * ND, ND)
                copy = pltpu.make_async_copy(part.at[pl.ds(i * ND, ND)], mv.at[rows], in_sem.at[len(loads)])
                copy.start()
                loads.append(copy)
    zero = jnp.zeros((ROWS, LANES), jnp.float32)
    accs = (a0, a1, a2, a3)

    def clear(g, _):
        for acc in accs:
            acc[g] = zero
        return 0

    lax.fori_loop(0, nbins, clear, 0, unroll=8)
    for j in range(ND):
        dw[j] = wind_ref[0] * dir_ref[0, j] + wind_ref[1] * dir_ref[1, j]
    for copy in loads:
        copy.wait()

    def per_freq(f, steep):
        fr2, fr4, hspeed = ftab_ref[0, f], ftab_ref[1, f], ftab_ref[2, f]

        def per_group(t, total):
            j0 = t * GROUP
            g0 = f * ND + j0
            spots = [[spot_ref[4 * g0 + 4 * i + k] for k in range(4)] for i in range(GROUP)]
            own = [mv[g0 + i] for i in range(GROUP)]
            found = [[mv[b] for b in spots[i]] for i in range(GROUP)]
            adds = []
            for i in range(GROUP):
                m, (p0, p1, m0, m1) = own[i], found[i]
                wp, wm = wts_ref[2 * g0 + 2 * i], wts_ref[2 * g0 + 2 * i + 1]
                ep = p1 + wp * (p0 - p1)
                em = m1 + wm * (m0 - m1)
                mf = fr4 * m
                half = mf * (m * (ep * (1 / 1.25**4) + em * (1 / 0.75**4)) - ep * em * (2.0 / 0.9375**4))
                drive = jnp.maximum(0.0, dw[j0 + i] - hspeed)
                base[g0 + i] = m + 0.15 * (drive * drive) * m - 2.0 * half
                sp, sm = wp * half, wm * half
                adds.append((sp, half - sp, sm, half - sm))
                total = total + m
            for i in range(0, GROUP, 2):
                for acc, b0, b1, x0, x1 in zip(accs, spots[i], spots[i + 1], adds[i], adds[i + 1]):
                    old0, old1 = acc[b0], acc[b1]
                    acc[b0] = old0 + x0
                    acc[b1] = old1 + (x1 + jnp.where(b0 == b1, x0, zero))
            return total

        return steep + lax.fori_loop(0, ND // GROUP, per_group, zero, unroll=3) * fr2

    steep = lax.fori_loop(0, nfreq, per_freq, zero)
    steep = steep * (1.0 / nbins)
    mask = mask_ref[...].astype(jnp.float32)
    per = nbins // PIECES
    copies = []
    for p in range(PIECES):

        def finish(t, _):
            g0 = t * ROWS
            done = []
            for i in range(ROWS):
                g = g0 + i
                mine = base[g] - (frs_ref[g] * steep) * mv[g]
                done.append((mine + ((a0[g] + a1[g]) + (a2[g] + a3[g]))) * mask)
            turned = jnp.swapaxes(jnp.stack(done, axis=0), 0, 1)
            for c in range(ROWS):
                out_v[pl.ds(pl.multiple_of(g0, ROWS), ROWS), c * LANES : (c + 1) * LANES] = turned[c]
            return 0

        lax.fori_loop(p * per // ROWS, (p + 1) * per // ROWS, finish, 0, unroll=3)
        rows = pl.ds(p * per, per)
        copy = pltpu.make_async_copy(out_v.at[rows], out_hbm.at[rows], out_sem.at[p])
        copy.start()
        copies.append(copy)
    for copy in copies:
        copy.wait()


def tail(parts, plan, bins_dev, dia_bins, dia_wts, ftab, frs, dirs, pos, wind, mask):
    nbins = dia_bins.shape[1]
    nfreq = nbins // ND
    anywhere = pl.BlockSpec(memory_space=pl.ANY)
    smem = pl.BlockSpec(memory_space=pltpu.SMEM)
    vmem = pl.BlockSpec(memory_space=pltpu.VMEM)
    points = ROWS * LANES
    spots = dia_bins.T.reshape(-1)
    wts = dia_wts.T.reshape(-1)
    field = pltpu.VMEM((nbins, ROWS, LANES), jnp.float32)
    return pl.pallas_call(
        functools.partial(tail_kernel, nfreq, bins_dev, plan),
        out_shape=jax.ShapeDtypeStruct((nbins, points), jnp.float32),
        in_specs=[smem] * 6 + [vmem] * 2 + [anywhere] * len(parts),
        out_specs=anywhere,
        scratch_shapes=[field] * 6
        + [
            pltpu.VMEM((ND, ROWS, LANES), jnp.float32),
            pltpu.VMEM((nbins, points), jnp.float32),
            pltpu.SemaphoreType.DMA((nbins // ND,)),
            pltpu.SemaphoreType.DMA((PIECES,)),
        ],
        compiler_params=pltpu.CompilerParams(vmem_limit_bytes=VMEM_ASK),
        cost_estimate=pl.CostEstimate(flops=0, bytes_accessed=70_000_000, transcendentals=0),
        name="tail",
    )(spots, wts, ftab, frs, dirs, pos, wind, mask, *parts)


def fast_on_device(
    spectrum, wind, sea_mask, neighbours, metric_x, metric_y, refraction, freq_shift, dia_bins, dia_wts
):
    bins_dev, points = spectrum.shape
    nbins = dia_bins.shape[1]
    nfreq = nbins // ND
    nloc = bins_dev // ND
    tiles = points // LANES
    shares = lax.axis_size("bin")
    share = points // shares
    bin_pos = lax.axis_index("bin")
    space_pos = lax.axis_index("space")
    plan = chunk_plan(nloc)

    freqs = np.arange(nfreq, dtype=np.float32)
    speed = jnp.asarray(np.exp(-np.log(1.1) * freqs.astype(np.float64)).astype(np.float32))
    ratio = np.exp(np.log(1.1) * (freqs.astype(np.float64) - (nfreq - 1)))
    ftab = jnp.asarray(
        np.stack([ratio**2, 4.0 * ratio**4, 0.5 * np.exp(-np.log(1.1) * freqs)]).astype(np.float32)
    )
    frs = jnp.asarray(np.repeat(3.0 * ratio, ND).astype(np.float32))
    theta = 2.0 * np.pi * (np.arange(ND) + 0.5) / ND
    dirs = jnp.asarray(np.stack([np.cos(theta), np.sin(theta)]).astype(np.float32))

    groups = halo_groups(plan)
    early = runs_of(slots_of(groups[0]))
    mask_row = sea_mask.reshape(1, points)
    hs, hn, _ = prep(spectrum, mask_row, early, groups[:1], False)
    after, *_ = lax.optimization_barrier((spectrum, hs[0], hn[0]))
    whole_blocks = [(f, min(f + 2, nloc)) for f in range(0, nloc, 2)]
    hs_rest, hn_rest, (wet, low_out, high_out) = prep(after, mask_row, whole_blocks, groups[1:], True)
    wet = wet.reshape(nloc, ND, tiles, LANES)

    def line(array, axis, step):
        peers = lax.axis_size(axis)
        pairs = [(i, i + 1) for i in range(peers - 1)]
        if step < 0:
            pairs = [(b, a) for a, b in pairs]
        return lax.ppermute(array, axis, pairs)

    sends = list(zip(list(hs) + list(hs_rest), list(hn) + list(hn_rest)))
    halos = []

    def send_halos(*after):
        if len(halos) < len(sends):
            south, north = sends[len(halos)]
            if after:
                south, north, *_ = lax.optimization_barrier((south, north) + after)
            halos.append((line(south, "space", 1), line(north, "space", -1)))

    send_halos()
    send_halos(*halos[0])
    low_in = line(low_out, "bin", 1).reshape(1, ND, tiles, LANES)
    high_in = line(high_out, "bin", -1).reshape(1, ND, tiles, LANES)

    nbr = (neighbours - space_pos * points).reshape(4, tiles, LANES)
    par = [p.reshape(tiles, LANES) for p in (metric_x, metric_y, refraction, freq_shift)]
    pos = bin_pos.reshape(1)
    kmin, kmax = points // 2, points
    arrived = []
    order = pos
    for c, chunk in enumerate(plan):
        first, step, count = chunk
        joined = c == 0
        gi, slot = [(i, slots_of(g)[first]) for i, g in enumerate(groups) if chunk in g][0]
        ends = (low_in, high_in) if first == 0 else None
        blocks = front(speed, dirs, order, nbr, par, *halos[gi], slot, wet, ends, chunk, joined, shares, kmin, kmax)
        earlier = [low_in, high_in, *sum(halos, ())] if c == 0 else arrived[0] if c == 1 else []
        order, *_ = lax.optimization_barrier((pos, blocks[0], *earlier))
        if joined:
            arrived.append([lax.all_to_all(blocks[0], "bin", split_axis=0, concat_axis=0, tiled=True)])
            continue
        here = [blocks[0]]
        for d in range(1, shares):
            rows = blocks[d]
            if c > 1:
                rows, _ = lax.optimization_barrier((rows, arrived[-1][d]))
            here.append(lax.ppermute(rows, "bin", [(i, (i + d) % shares) for i in range(shares)]))
        arrived.append(here)
    parts = sum(arrived, [])
    wind_part = lax.dynamic_slice_in_dim(wind, bin_pos * share, share, 1).reshape(2, ROWS, LANES)
    mask_part = lax.dynamic_slice_in_dim(sea_mask, bin_pos * share, share, 0).reshape(ROWS, LANES)
    return tail(parts, plan, bins_dev, dia_bins, dia_wts, ftab, frs, dirs, pos, wind_part, mask_part)


def pick_path(spectrum, *others):
    bins_dev, points = spectrum.shape
    fits = bins_dev % (2 * ND) == ND and bins_dev > ND and points // lax.axis_size("bin") == ROWS * LANES
    return (fast_on_device if fits else on_device)(spectrum, *others)


def solution(mesh):
    return jax.shard_map(
        pick_path,
        mesh=mesh,
        in_specs=(
            P("bin", ("ens", "space")),
            P(None, ("ens", "space")),
            P("space"),
            P(None, "space"),
            P("space"),
            P("space"),
            P("space"),
            P("space"),
            P(),
            P(),
        ),
        out_specs=P(None, ("ens", "space", "bin")),
        check_vma=False,
    )
```

```python
import functools
import itertools

import jax
import jax.numpy as jnp
import numpy as np
from jax import lax
from jax.experimental import pallas as pl
from jax.experimental.pallas import tpu as pltpu
from jax.sharding import PartitionSpec as P

ND = 36


def extended(array, sides, width):
    for axis, dim in sides:
        peers, length = (lax.axis_size(axis), array.shape[dim])
        up = [(i, (i + 1) % peers) for i in range(peers - 1)]
        down = [(j, i) for i, j in up]
        last = lax.slice_in_dim(array, length - width, length, axis=dim)
        initial = lax.slice_in_dim(array, 0, width, axis=dim)
        before = lax.ppermute(last, axis, up)
        after = lax.ppermute(initial, axis, down)
        array = jnp.concatenate([before, array, after], axis=dim)
    return array


def bin_tables(index, nfreq, ndir):
    freq = (index // ndir).astype(jnp.float32)
    direc = index % ndir
    fratio = jnp.exp(jnp.log(1.1) * (freq - (nfreq - 1)))
    speed = jnp.exp(-jnp.log(1.1) * freq)
    theta = 2.0 * jnp.pi * (direc.astype(jnp.float32) + 0.5) / ndir
    return (fratio, speed, jnp.cos(theta), jnp.sin(theta), direc == 0, direc == ndir - 1)


def spatial_term(wet, padded, local, metric_x, metric_y, speed, cosv, sinv):
    east = jnp.take(padded, local[0], axis=1)
    west = jnp.take(padded, local[1], axis=1)
    north = jnp.take(padded, local[2], axis=1)
    south = jnp.take(padded, local[3], axis=1)
    along_x = metric_x[None, :] * (speed * cosv)[:, None]
    along_y = metric_y[None, :] * (speed * sinv)[:, None]
    flux_x = jnp.abs(along_x) * (wet - jnp.where(along_x > 0, west, east))
    flux_y = jnp.abs(along_y) * (wet - jnp.where(along_y > 0, south, north))
    return flux_x + flux_y


def spectral_term(wet, padded, ndir, first, last, refraction, freq_shift, speed, cosv):
    rows = wet.shape[0]

    def moved_rows(offset):
        return lax.slice_in_dim(padded, ndir + offset, ndir + offset + rows, axis=0)

    prev_dir = jnp.where(first[:, None], moved_rows(ndir - 1), moved_rows(-1))
    next_dir = jnp.where(last[:, None], moved_rows(1 - ndir), moved_rows(1))
    lower = moved_rows(-ndir)
    upper = moved_rows(ndir)
    turning = refraction[None, :] * cosv[:, None]
    shifting = freq_shift[None, :] * speed[:, None]
    flux_t = jnp.abs(turning) * (wet - jnp.where(turning > 0, prev_dir, next_dir))
    flux_s = jnp.abs(shifting) * (wet - jnp.where(shifting > 0, lower, upper))
    return flux_t + flux_s


def source_step(
    moved, wind, maskf, fratio, speed, cosv, sinv, plus_fwd, minus_fwd, plus_back, minus_back
):
    steep = jnp.mean(moved * (fratio * fratio)[:, None], axis=0)
    drive = jnp.maximum(
        0.0,
        wind[0][None, :] * cosv[:, None] + wind[1][None, :] * sinv[:, None] - 0.5 * speed[:, None],
    )
    s_in = 0.3 * drive * drive * moved
    s_ds = -6.0 * fratio[:, None] * steep[None, :] * moved
    e_plus = plus_fwd(moved)
    e_minus = minus_fwd(moved)
    delta = (
        8.0
        * (fratio**4)[:, None]
        * (
            moved * moved * (e_plus / 1.25**4 + e_minus / 0.75**4)
            - 2.0 * moved * e_plus * e_minus / 0.9375**4
        )
    )
    s_nl = -2.0 * delta + plus_back(delta) + minus_back(delta)
    return (moved + 0.5 * (s_in + s_ds + s_nl)) * maskf[None, :]


def pair_matrix(first_bins, second_bins, weight, count):
    columns = jnp.arange(count, dtype=jnp.int32)[None, :]
    return weight[:, None] * (first_bins[:, None] == columns).astype(jnp.float32) + (1.0 - weight)[
        :, None
    ] * (second_bins[:, None] == columns).astype(jnp.float32)


def forward_product(matrix, values):
    return jnp.dot(
        matrix, values, precision=lax.Precision.HIGHEST, preferred_element_type=jnp.float32
    )


def backward_product(matrix, values):
    return lax.dot_general(
        matrix,
        values,
        (((0,), (0,)), ((), ())),
        precision=lax.Precision.HIGHEST,
        preferred_element_type=jnp.float32,
    )


def on_device(
    spectrum,
    wind,
    sea_mask,
    neighbours,
    metric_x,
    metric_y,
    refraction,
    freq_shift,
    dia_bins,
    dia_wts,
):
    bins_dev, points_dev = spectrum.shape
    nbins = dia_bins.shape[1]
    ndir = ND
    nfreq = nbins // ndir
    space_pos = lax.axis_index("space")
    bin_pos = lax.axis_index("bin")
    maskf = sea_mask.astype(jnp.float32)
    wet = spectrum * maskf[None, :]
    padded = extended(wet, (("space", 1),), points_dev)
    base = space_pos * points_dev - points_dev
    local = neighbours - base
    own_bins = bin_pos * bins_dev + jnp.arange(bins_dev, dtype=jnp.int32)
    fratio, speed, cosv, sinv, first, last = bin_tables(own_bins, nfreq, ndir)
    spatial = spatial_term(wet, padded, local, metric_x, metric_y, speed, cosv, sinv)
    share = points_dev // lax.axis_size("bin")
    start = bin_pos * share
    all_bins = jnp.arange(nbins, dtype=jnp.int32)
    fratio_all, speed_all, cos_all, sin_all, first_all, last_all = bin_tables(all_bins, nfreq, ndir)
    bin_pad = extended(wet, (("bin", 0),), ndir)
    spectral = spectral_term(wet, bin_pad, ndir, first, last, refraction, freq_shift, speed, cosv)
    moved_own = wet - spatial - spectral
    moved = lax.all_to_all(moved_own, "bin", split_axis=1, concat_axis=0, tiled=True)
    wind_part = lax.dynamic_slice_in_dim(wind, start, share, 1)
    mask_part = lax.dynamic_slice_in_dim(maskf, start, share, 0)
    plus_matrix = pair_matrix(dia_bins[0], dia_bins[1], dia_wts[0], nbins)
    minus_matrix = pair_matrix(dia_bins[2], dia_bins[3], dia_wts[1], nbins)
    result = source_step(
        moved,
        wind_part,
        mask_part,
        fratio_all,
        speed_all,
        cos_all,
        sin_all,
        lambda v: forward_product(plus_matrix, v),
        lambda v: forward_product(minus_matrix, v),
        lambda v: backward_product(plus_matrix, v),
        lambda v: backward_product(minus_matrix, v),
    )
    return result


LANES = 128
ROWS = 8
EDGE = 16
QUART = ND // 4
APART = 3
PIECES = 6
VMEM_ASK = 60 << 20
GROUP = 4


def chunk_plan(nloc):
    mid = nloc // 2
    plan = [(mid - d, 2 * d, 2) for d in range(1, mid + 1)]
    if mid > 3:
        plan[2] = (mid - 3, 3, 3)
    else:
        plan.insert(0, (mid, 1, 1))
    return plan


def freqs_of(chunk):
    first, step, count = chunk
    return [first + i * step for i in range(count)]


def halo_groups(plan):
    return [g for g in (plan[:1], plan[1:]) if g]


def slots_of(group):
    return {f: i for i, f in enumerate(f for chunk in group for f in freqs_of(chunk))}


def runs_of(freqs):
    runs = []
    for f in sorted(freqs):
        if runs and runs[-1][1] == f:
            runs[-1] = (runs[-1][0], f + 1)
        else:
            runs.append((f, f + 1))
    return runs


def prep_kernel(points, bins, blocks, groups, full, spec_hbm, mask_ref, *refs):
    ngr = len(groups)
    nloc = bins // ND
    hs_hbm, hn_hbm = refs[:ngr], refs[ngr : 2 * ngr]
    if full:
        wet_hbm, low_hbm, high_hbm = refs[2 * ngr : 2 * ngr + 3]
    spec_v, wet_v, edge_v, in_sem, out_sem = refs[-5:]
    tiles = points // LANES
    half = ND // 2
    where = {f: (i, k) for i, group in enumerate(groups) for f, k in slots_of(group).items()}
    loads = []
    spans = []
    for lo, hi in blocks:
        start = lo * ND // ROWS * ROWS
        stop = min(-(-hi * ND // ROWS) * ROWS, bins)
        spans.append((start, stop))
        rows = pl.ds(start, stop - start)
        copy = pltpu.make_async_copy(spec_hbm.at[rows], spec_v.at[rows], in_sem.at[len(loads)])
        copy.start()
        loads.append(copy)
    masks = [mask_ref[:, c * LANES : (c + 1) * LANES].astype(jnp.float32) for c in range(tiles)]
    copies = []

    def send(src, dst):
        copy = pltpu.make_async_copy(src, dst, out_sem.at[len(copies)])
        copy.start()
        copies.append(copy)

    for (lo, hi), (start, stop), load in zip(blocks, spans, loads):
        load.wait()

        def turn(g0, count):
            for c0 in range(0, tiles, ROWS):
                cols = range(c0, c0 + ROWS)
                block = jnp.stack(
                    [spec_v[pl.ds(g0, count), c * LANES : (c + 1) * LANES] * masks[c] for c in cols], axis=0
                )
                block = jnp.swapaxes(block, 0, 1)
                for i in range(count):
                    wet_v[pl.ds(pl.multiple_of((g0 + i) * tiles + c0, ROWS), ROWS), :] = block[i]

        def relayout(t, _):
            turn(pl.multiple_of(start + t * ROWS, ROWS), ROWS)
            return 0

        lax.fori_loop(0, (stop - start) // ROWS, relayout, 0)
        rest = (stop - start) % ROWS
        if rest:
            g0 = stop - rest
            for c in range(tiles):
                tile = spec_v[pl.ds(g0, rest), c * LANES : (c + 1) * LANES]
                wet_v[pl.ds(g0 * tiles + c, rest, stride=tiles), :] = tile * masks[c]
        for f in range(lo, hi):
            base = f * ND * tiles
            if f in where:
                i, k = where[f]
                for side, (j0, row) in enumerate(((3 * QUART, tiles - 1), (QUART, 0))):
                    at = base + j0 * tiles + row
                    edge_v[f, side, ROWS:EDGE, :] = jnp.zeros((EDGE - ROWS, LANES), jnp.float32)
                    edge_v[f, side, 0:ROWS, :] = wet_v[pl.ds(at, ROWS, stride=tiles), :]
                    edge_v[f, side, ROWS : ROWS + 1, :] = wet_v[pl.ds(at + ROWS * tiles, 1), :]
                span = half * tiles
                send(wet_v.at[pl.ds(base, span)], hs_hbm[i].at[k, pl.ds(0, span)])
                send(wet_v.at[pl.ds(base + span, span)], hn_hbm[i].at[k, pl.ds(0, span)])
                send(edge_v.at[f, 0], hs_hbm[i].at[k, pl.ds(span, EDGE)])
                send(edge_v.at[f, 1], hn_hbm[i].at[k, pl.ds(span, EDGE)])
            if full:
                own = pl.ds(base, ND * tiles)
                if f == nloc - 1:
                    send(wet_v.at[own], low_hbm)
                if f == 0:
                    send(wet_v.at[own], high_hbm)
                send(wet_v.at[own], wet_hbm.at[own])
    for copy in copies:
        copy.wait()


def prep(spectrum, mask, blocks, groups, full):
    bins, points = spectrum.shape
    nloc = bins // ND
    tiles = points // LANES
    halo_rows = ND // 2 * tiles + EDGE
    halos = [jax.ShapeDtypeStruct((len(slots_of(g)), halo_rows, LANES), jnp.float32) for g in groups]
    one = jax.ShapeDtypeStruct((ND * tiles, LANES), jnp.float32)
    outs = halos + halos
    if full:
        outs += [jax.ShapeDtypeStruct((bins * tiles, LANES), jnp.float32), one, one]
    anywhere = pl.BlockSpec(memory_space=pl.ANY)
    count = sum(hi - lo for lo, hi in blocks)
    sends = 4 * sum(len(slots_of(g)) for g in groups) + (nloc + 2 if full else 0)
    res = pl.pallas_call(
        functools.partial(prep_kernel, points, bins, blocks, groups, full),
        out_shape=outs,
        in_specs=[anywhere, pl.BlockSpec(memory_space=pltpu.VMEM)],
        out_specs=[anywhere] * len(outs),
        scratch_shapes=[
            pltpu.VMEM((bins, points), jnp.float32),
            pltpu.VMEM((bins * tiles, LANES), jnp.float32),
            pltpu.VMEM((nloc, 2, EDGE, LANES), jnp.float32),
            pltpu.SemaphoreType.DMA((len(blocks),)),
            pltpu.SemaphoreType.DMA((sends,)),
        ],
        compiler_params=pltpu.CompilerParams(vmem_limit_bytes=VMEM_ASK),
        cost_estimate=pl.CostEstimate(flops=0, bytes_accessed=count * 3_000_000, transcendentals=0),
        name="prep",
    )(spectrum, mask)
    ngr = len(groups)
    return res[:ngr], res[ngr : 2 * ngr], res[2 * ngr :]


def front_kernel(
    tiles, shares, nloc, kmin, kmax, chunk, edge, joined, tab_ref, dir_ref, pos_ref, nbr_ref, mx_ref, my_ref, rf_ref, fs_ref, hs_ref, hn_ref, wet_ref, *refs
):
    nout = 1 if joined else shares
    near, outs, ext_ref = refs[: -nout - 1], refs[-nout - 1 : -1], refs[-1]
    if joined:
        outs = [outs[0].at[d] for d in range(shares)]
    place = pl.program_id(0)
    speed = tab_ref[pos_ref[0] * nloc + chunk[0] + chunk[1] * place]
    first = place == 0
    half = ND // 2
    span = half * tiles
    south, north = tiles, ROWS
    pitch = APART * (2 * tiles + ROWS)

    def rows_at(j, row, count=ROWS):
        return pl.ds(j * pitch + APART * row, count, stride=APART)

    def extend(q, _):
        for t in range(0, tiles, ROWS):
            ext_ref[rows_at(q, t), :] = hs_ref[0, pl.ds(pl.multiple_of(q * tiles + t, ROWS), ROWS), :]
            ext_ref[rows_at(q, south + t), :] = wet_ref[0, q, t : t + ROWS, :]
            ext_ref[rows_at(half + q, north + t), :] = wet_ref[0, half + q, t : t + ROWS, :]
            ext_ref[rows_at(half + q, north + tiles + t), :] = hn_ref[
                0, pl.ds(pl.multiple_of(q * tiles + t, ROWS), ROWS), :
            ]
        return 0

    lax.fori_loop(0, half, extend, 0, unroll=2)
    for q in range(QUART):
        ext_ref[pl.ds((QUART + q) * pitch + APART * (south + tiles), 1), :] = hn_ref[0, span + q : span + q + 1, :]
        ext_ref[pl.ds((3 * QUART + q) * pitch + APART * (north - 1), 1), :] = hs_ref[0, span + q : span + q + 1, :]

    side = jnp.where(first, 1.0, -1.0)
    per_share = tiles // shares
    steps = [(d, k) for d in range(shares) for k in range(per_share // ROWS)]
    firsts = {}
    for d, k in steps:
        row = (d if joined else lax.rem(pos_ref[0] + d, shares)) * per_share + k * ROWS
        firsts[d, k] = row if joined else pl.multiple_of(row, ROWS)
    sub = lax.broadcasted_iota(jnp.int32, (ROWS, LANES), 0)
    lanes, rels = {}, {}
    for way in range(4):
        for step in steps:
            src = nbr_ref[way, pl.ds(firsts[step], ROWS), :]
            lanes[way, step] = src & (LANES - 1)
            rels[way, step] = (src >> 7) - (sub + firsts[step])

    def picked(j, own, step, way, offsets):
        out = None
        for r in offsets:
            window = ext_ref[rows_at(j, own + firsts[step] + r), :]
            got = jnp.take_along_axis(window, lanes[way, step], axis=1, mode="promise_in_bounds")
            out = got if out is None else jnp.where(rels[way, step] == r, got, out)
        return out

    for quad in range(4):
        cos_up = quad in (0, 3)
        own, way_y, off_y = (
            (south, 3, range(-(kmax // LANES), -(kmin // LANES) + 1))
            if quad < 2
            else (north, 2, range(kmin // LANES, kmax // LANES + 1))
        )
        way_x, off_x = (1, (-1, 0)) if cos_up else (0, (0, 1))

        def body(q, _):
            j = quad * QUART + q
            jprev = jnp.where(j == 0, ND - 1, j - 1)
            jnext = jnp.where(j == ND - 1, 0, j + 1)
            acos = jnp.abs(dir_ref[0, j])
            asin = jnp.abs(dir_ref[1, j])
            ax, ay = speed * acos, speed * asin
            for step in steps:
                at = pl.ds(firsts[step], ROWS)
                wet = wet_ref[0, j, at, :]
                e_y = picked(j, own, step, way_y, off_y)
                e_x = picked(j, own, step, way_x, off_x)
                rf, fs = rf_ref[at, :], fs_ref[at, :]
                e_prev, e_next = wet_ref[0, jprev, at, :], wet_ref[0, jnext, at, :]
                e_t = jnp.where(rf > 0, e_prev, e_next) if cos_up else jnp.where(rf < 0, e_prev, e_next)
                if edge:
                    inner, low, high = (ref[0, j, at, :] for ref in near)
                    outer = jnp.where(first, low, high)
                    e_s = jnp.where(fs * side > 0, outer, inner)
                else:
                    e_s = jnp.where(fs > 0, near[0][0, j, at, :], near[1][0, j, at, :])
                spatial = (mx_ref[at, :] * ax) * (wet - e_x) + (my_ref[at, :] * ay) * (wet - e_y)
                spectral = (jnp.abs(rf) * acos) * (wet - e_t) + (jnp.abs(fs) * speed) * (wet - e_s)
                d, k = step
                outs[d][j, k * ROWS : (k + 1) * ROWS, :] = wet - spatial - spectral
            return 0

        lax.fori_loop(0, QUART, body, 0, unroll=3)


def front(speed, dirs, pos, nbr, par, hs, hn, slot, wet, ends, chunk, joined, shares, kmin, kmax):
    first, step, count = chunk
    tiles = nbr.shape[1]
    nloc = wet.shape[0]
    smem = pl.BlockSpec(memory_space=pltpu.SMEM)

    def freq_spec(start, step):
        return pl.BlockSpec((1, ND, tiles, LANES), lambda i: (start + i * step, 0, 0, 0))

    halo_spec = pl.BlockSpec((1,) + hs.shape[1:], lambda i: (slot + i, 0, 0))

    def whole(shape):
        return pl.BlockSpec(shape, lambda i: (0,) * len(shape))

    if ends:
        near, near_specs = (wet,) + ends, [freq_spec(1, nloc - 3), freq_spec(0, 0), freq_spec(0, 0)]
    else:
        near, near_specs = (wet, wet), [freq_spec(first - 1, step), freq_spec(first + 1, step)]
    rows = tiles // shares
    if joined:
        outs = [jax.ShapeDtypeStruct((shares, count * ND, rows, LANES), jnp.float32)]
        out_specs = [pl.BlockSpec((shares, ND, rows, LANES), lambda i: (0, i, 0, 0))]
    else:
        outs = [jax.ShapeDtypeStruct((count * ND, rows, LANES), jnp.float32)] * shares
        out_specs = [pl.BlockSpec((ND, rows, LANES), lambda i: (i, 0, 0))] * shares
    return pl.pallas_call(
        functools.partial(front_kernel, tiles, shares, nloc, kmin, kmax, chunk, bool(ends), joined),
        grid=(count,),
        out_shape=outs,
        in_specs=[smem] * 3
        + [whole(nbr.shape)] + [whole(p.shape) for p in par] + [halo_spec, halo_spec, freq_spec(first, step)]
        + near_specs,
        out_specs=out_specs,
        scratch_shapes=[pltpu.VMEM((ND * APART * (2 * tiles + ROWS), LANES), jnp.float32)],
        compiler_params=pltpu.CompilerParams(vmem_limit_bytes=VMEM_ASK),
        cost_estimate=pl.CostEstimate(flops=0, bytes_accessed=count * 22_000_000, transcendentals=0),
        name="front",
    )(speed, dirs, pos, nbr, *par, hs, hn, wet, *near)


def tail_kernel(nfreq, bins_dev, plan, spot_ref, wts_ref, ftab_ref, frs_ref, dir_ref, pos_ref, wind_ref, mask_ref, *refs):
    out_hbm, mv, base, a0, a1, a2, a3, dw, out_v, in_sem, out_sem = refs[-11:]
    parts = iter(refs[:-11])
    shares = nfreq * ND // bins_dev
    nbins = nfreq * ND
    loads = []
    for c, chunk in enumerate(plan):
        joined = c == 0
        whole = next(parts) if joined else None
        for d in range(shares):
            part = whole.at[d] if joined else next(parts)
            source = d if joined else lax.rem(pos_ref[0] + (shares - d), shares)
            for i, f in enumerate(freqs_of(chunk)):
                rows = pl.ds(source * bins_dev + f * ND, ND)
                copy = pltpu.make_async_copy(part.at[pl.ds(i * ND, ND)], mv.at[rows], in_sem.at[len(loads)])
                copy.start()
                loads.append(copy)
    zero = jnp.zeros((ROWS, LANES), jnp.float32)
    accs = (a0, a1, a2, a3)

    def clear(g, _):
        for acc in accs:
            acc[g] = zero
        return 0

    lax.fori_loop(0, nbins, clear, 0, unroll=8)
    for j in range(ND):
        dw[j] = wind_ref[0] * dir_ref[0, j] + wind_ref[1] * dir_ref[1, j]
    for copy in loads:
        copy.wait()

    def per_freq(f, steep):
        fr2, fr4, hspeed = ftab_ref[0, f], ftab_ref[1, f], ftab_ref[2, f]

        def per_group(t, total):
            j0 = t * GROUP
            g0 = f * ND + j0
            spots = [[spot_ref[4 * g0 + 4 * i + k] for k in range(4)] for i in range(GROUP)]
            own = [mv[g0 + i] for i in range(GROUP)]
            found = [[mv[b] for b in spots[i]] for i in range(GROUP)]
            adds = []
            for i in range(GROUP):
                m, (p0, p1, m0, m1) = own[i], found[i]
                wp, wm = wts_ref[2 * g0 + 2 * i], wts_ref[2 * g0 + 2 * i + 1]
                ep = p1 + wp * (p0 - p1)
                em = m1 + wm * (m0 - m1)
                mf = fr4 * m
                half = mf * (m * (ep * (1 / 1.25**4) + em * (1 / 0.75**4)) - ep * em * (2.0 / 0.9375**4))
                drive = jnp.maximum(0.0, dw[j0 + i] - hspeed)
                base[g0 + i] = m + 0.15 * (drive * drive) * m - 2.0 * half
                sp, sm = wp * half, wm * half
                adds.append((sp, half - sp, sm, half - sm))
                total = total + m
            for i in range(0, GROUP, 2):
                for acc, b0, b1, x0, x1 in zip(accs, spots[i], spots[i + 1], adds[i], adds[i + 1]):
                    old0, old1 = acc[b0], acc[b1]
                    acc[b0] = old0 + x0
                    acc[b1] = old1 + (x1 + jnp.where(b0 == b1, x0, zero))
            return total

        return steep + lax.fori_loop(0, ND // GROUP, per_group, zero, unroll=3) * fr2

    steep = lax.fori_loop(0, nfreq, per_freq, zero)
    steep = steep * (1.0 / nbins)
    mask = mask_ref[...].astype(jnp.float32)
    per = nbins // PIECES
    copies = []
    for p in range(PIECES):

        def finish(t, _):
            g0 = t * ROWS
            done = []
            for i in range(ROWS):
                g = g0 + i
                mine = base[g] - (frs_ref[g] * steep) * mv[g]
                done.append((mine + ((a0[g] + a1[g]) + (a2[g] + a3[g]))) * mask)
            turned = jnp.swapaxes(jnp.stack(done, axis=0), 0, 1)
            for c in range(ROWS):
                out_v[pl.ds(pl.multiple_of(g0, ROWS), ROWS), c * LANES : (c + 1) * LANES] = turned[c]
            return 0

        lax.fori_loop(p * per // ROWS, (p + 1) * per // ROWS, finish, 0, unroll=3)
        rows = pl.ds(p * per, per)
        copy = pltpu.make_async_copy(out_v.at[rows], out_hbm.at[rows], out_sem.at[p])
        copy.start()
        copies.append(copy)
    for copy in copies:
        copy.wait()


def tail(parts, plan, bins_dev, dia_bins, dia_wts, ftab, frs, dirs, pos, wind, mask):
    nbins = dia_bins.shape[1]
    nfreq = nbins // ND
    anywhere = pl.BlockSpec(memory_space=pl.ANY)
    smem = pl.BlockSpec(memory_space=pltpu.SMEM)
    vmem = pl.BlockSpec(memory_space=pltpu.VMEM)
    points = ROWS * LANES
    spots = dia_bins.T.reshape(-1)
    wts = dia_wts.T.reshape(-1)
    field = pltpu.VMEM((nbins, ROWS, LANES), jnp.float32)
    return pl.pallas_call(
        functools.partial(tail_kernel, nfreq, bins_dev, plan),
        out_shape=jax.ShapeDtypeStruct((nbins, points), jnp.float32),
        in_specs=[smem] * 6 + [vmem] * 2 + [anywhere] * len(parts),
        out_specs=anywhere,
        scratch_shapes=[field] * 6
        + [
            pltpu.VMEM((ND, ROWS, LANES), jnp.float32),
            pltpu.VMEM((nbins, points), jnp.float32),
            pltpu.SemaphoreType.DMA((nbins // ND,)),
            pltpu.SemaphoreType.DMA((PIECES,)),
        ],
        compiler_params=pltpu.CompilerParams(vmem_limit_bytes=VMEM_ASK),
        cost_estimate=pl.CostEstimate(flops=0, bytes_accessed=70_000_000, transcendentals=0),
        name="tail",
    )(spots, wts, ftab, frs, dirs, pos, wind, mask, *parts)


def fast_on_device(
    spectrum, wind, sea_mask, neighbours, metric_x, metric_y, refraction, freq_shift, dia_bins, dia_wts
):
    bins_dev, points = spectrum.shape
    nbins = dia_bins.shape[1]
    nfreq = nbins // ND
    nloc = bins_dev // ND
    tiles = points // LANES
    shares = lax.axis_size("bin")
    share = points // shares
    bin_pos = lax.axis_index("bin")
    space_pos = lax.axis_index("space")
    plan = chunk_plan(nloc)

    freqs = np.arange(nfreq, dtype=np.float32)
    speed = jnp.asarray(np.exp(-np.log(1.1) * freqs.astype(np.float64)).astype(np.float32))
    ratio = np.exp(np.log(1.1) * (freqs.astype(np.float64) - (nfreq - 1)))
    ftab = jnp.asarray(
        np.stack([ratio**2, 4.0 * ratio**4, 0.5 * np.exp(-np.log(1.1) * freqs)]).astype(np.float32)
    )
    frs = jnp.asarray(np.repeat(3.0 * ratio, ND).astype(np.float32))
    theta = 2.0 * np.pi * (np.arange(ND) + 0.5) / ND
    dirs = jnp.asarray(np.stack([np.cos(theta), np.sin(theta)]).astype(np.float32))

    groups = halo_groups(plan)
    early = runs_of(slots_of(groups[0]))
    mask_row = sea_mask.reshape(1, points)
    hs, hn, _ = prep(spectrum, mask_row, early, groups[:1], False)
    after, *_ = lax.optimization_barrier((spectrum, hs[0], hn[0]))
    whole_blocks = [(f, min(f + 2, nloc)) for f in range(0, nloc, 2)]
    hs_rest, hn_rest, (wet, low_out, high_out) = prep(after, mask_row, whole_blocks, groups[1:], True)
    wet = wet.reshape(nloc, ND, tiles, LANES)

    def line(array, axis, step):
        peers = lax.axis_size(axis)
        pairs = [(i, i + 1) for i in range(peers - 1)]
        if step < 0:
            pairs = [(b, a) for a, b in pairs]
        return lax.ppermute(array, axis, pairs)

    sends = list(zip(list(hs) + list(hs_rest), list(hn) + list(hn_rest)))
    halos = []

    def send_halos(*after):
        if len(halos) < len(sends):
            south, north = sends[len(halos)]
            if after:
                south, north, *_ = lax.optimization_barrier((south, north) + after)
            halos.append((line(south, "space", 1), line(north, "space", -1)))

    send_halos()
    send_halos(*halos[0])
    low_in = line(low_out, "bin", 1).reshape(1, ND, tiles, LANES)
    high_in = line(high_out, "bin", -1).reshape(1, ND, tiles, LANES)

    nbr = (neighbours - space_pos * points).reshape(4, tiles, LANES)
    par = [p.reshape(tiles, LANES) for p in (metric_x, metric_y, refraction, freq_shift)]
    pos = bin_pos.reshape(1)
    kmin, kmax = points // 2, points
    arrived = []
    order = pos
    for c, chunk in enumerate(plan):
        first, step, count = chunk
        joined = c == 0
        gi, slot = [(i, slots_of(g)[first]) for i, g in enumerate(groups) if chunk in g][0]
        ends = (low_in, high_in) if first == 0 else None
        blocks = front(speed, dirs, order, nbr, par, *halos[gi], slot, wet, ends, chunk, joined, shares, kmin, kmax)
        earlier = sum(halos, ()) if c == 0 else arrived[0] if c == 1 else []
        order, *_ = lax.optimization_barrier((pos, blocks[0], *earlier))
        if joined:
            arrived.append([lax.all_to_all(blocks[0], "bin", split_axis=0, concat_axis=0, tiled=True)])
            continue
        here = [blocks[0]]
        for d in range(1, shares):
            rows = blocks[d]
            if c > 1:
                rows, _ = lax.optimization_barrier((rows, arrived[-1][d]))
            here.append(lax.ppermute(rows, "bin", [(i, (i + d) % shares) for i in range(shares)]))
        arrived.append(here)
    parts = sum(arrived, [])
    wind_part = lax.dynamic_slice_in_dim(wind, bin_pos * share, share, 1).reshape(2, ROWS, LANES)
    mask_part = lax.dynamic_slice_in_dim(sea_mask, bin_pos * share, share, 0).reshape(ROWS, LANES)
    return tail(parts, plan, bins_dev, dia_bins, dia_wts, ftab, frs, dirs, pos, wind_part, mask_part)


def pick_path(spectrum, *others):
    bins_dev, points = spectrum.shape
    fits = bins_dev % (2 * ND) == ND and bins_dev > ND and points // lax.axis_size("bin") == ROWS * LANES
    return (fast_on_device if fits else on_device)(spectrum, *others)


def solution(mesh):
    return jax.shard_map(
        pick_path,
        mesh=mesh,
        in_specs=(
            P("bin", ("ens", "space")),
            P(None, ("ens", "space")),
            P("space"),
            P(None, "space"),
            P("space"),
            P("space"),
            P("space"),
            P("space"),
            P(),
            P(),
        ),
        out_specs=P(None, ("ens", "space", "bin")),
        check_vma=False,
    )
```

```python
import functools
import itertools

import jax
import jax.numpy as jnp
import numpy as np
from jax import lax
from jax.experimental import pallas as pl
from jax.experimental.pallas import tpu as pltpu
from jax.sharding import PartitionSpec as P

ND = 36


def extended(array, sides, width):
    for axis, dim in sides:
        peers, length = (lax.axis_size(axis), array.shape[dim])
        up = [(i, (i + 1) % peers) for i in range(peers - 1)]
        down = [(j, i) for i, j in up]
        last = lax.slice_in_dim(array, length - width, length, axis=dim)
        initial = lax.slice_in_dim(array, 0, width, axis=dim)
        before = lax.ppermute(last, axis, up)
        after = lax.ppermute(initial, axis, down)
        array = jnp.concatenate([before, array, after], axis=dim)
    return array


def bin_tables(index, nfreq, ndir):
    freq = (index // ndir).astype(jnp.float32)
    direc = index % ndir
    fratio = jnp.exp(jnp.log(1.1) * (freq - (nfreq - 1)))
    speed = jnp.exp(-jnp.log(1.1) * freq)
    theta = 2.0 * jnp.pi * (direc.astype(jnp.float32) + 0.5) / ndir
    return (fratio, speed, jnp.cos(theta), jnp.sin(theta), direc == 0, direc == ndir - 1)


def spatial_term(wet, padded, local, metric_x, metric_y, speed, cosv, sinv):
    east = jnp.take(padded, local[0], axis=1)
    west = jnp.take(padded, local[1], axis=1)
    north = jnp.take(padded, local[2], axis=1)
    south = jnp.take(padded, local[3], axis=1)
    along_x = metric_x[None, :] * (speed * cosv)[:, None]
    along_y = metric_y[None, :] * (speed * sinv)[:, None]
    flux_x = jnp.abs(along_x) * (wet - jnp.where(along_x > 0, west, east))
    flux_y = jnp.abs(along_y) * (wet - jnp.where(along_y > 0, south, north))
    return flux_x + flux_y


def spectral_term(wet, padded, ndir, first, last, refraction, freq_shift, speed, cosv):
    rows = wet.shape[0]

    def moved_rows(offset):
        return lax.slice_in_dim(padded, ndir + offset, ndir + offset + rows, axis=0)

    prev_dir = jnp.where(first[:, None], moved_rows(ndir - 1), moved_rows(-1))
    next_dir = jnp.where(last[:, None], moved_rows(1 - ndir), moved_rows(1))
    lower = moved_rows(-ndir)
    upper = moved_rows(ndir)
    turning = refraction[None, :] * cosv[:, None]
    shifting = freq_shift[None, :] * speed[:, None]
    flux_t = jnp.abs(turning) * (wet - jnp.where(turning > 0, prev_dir, next_dir))
    flux_s = jnp.abs(shifting) * (wet - jnp.where(shifting > 0, lower, upper))
    return flux_t + flux_s


def source_step(
    moved, wind, maskf, fratio, speed, cosv, sinv, plus_fwd, minus_fwd, plus_back, minus_back
):
    steep = jnp.mean(moved * (fratio * fratio)[:, None], axis=0)
    drive = jnp.maximum(
        0.0,
        wind[0][None, :] * cosv[:, None] + wind[1][None, :] * sinv[:, None] - 0.5 * speed[:, None],
    )
    s_in = 0.3 * drive * drive * moved
    s_ds = -6.0 * fratio[:, None] * steep[None, :] * moved
    e_plus = plus_fwd(moved)
    e_minus = minus_fwd(moved)
    delta = (
        8.0
        * (fratio**4)[:, None]
        * (
            moved * moved * (e_plus / 1.25**4 + e_minus / 0.75**4)
            - 2.0 * moved * e_plus * e_minus / 0.9375**4
        )
    )
    s_nl = -2.0 * delta + plus_back(delta) + minus_back(delta)
    return (moved + 0.5 * (s_in + s_ds + s_nl)) * maskf[None, :]


def pair_matrix(first_bins, second_bins, weight, count):
    columns = jnp.arange(count, dtype=jnp.int32)[None, :]
    return weight[:, None] * (first_bins[:, None] == columns).astype(jnp.float32) + (1.0 - weight)[
        :, None
    ] * (second_bins[:, None] == columns).astype(jnp.float32)


def forward_product(matrix, values):
    return jnp.dot(
        matrix, values, precision=lax.Precision.HIGHEST, preferred_element_type=jnp.float32
    )


def backward_product(matrix, values):
    return lax.dot_general(
        matrix,
        values,
        (((0,), (0,)), ((), ())),
        precision=lax.Precision.HIGHEST,
        preferred_element_type=jnp.float32,
    )


def on_device(
    spectrum,
    wind,
    sea_mask,
    neighbours,
    metric_x,
    metric_y,
    refraction,
    freq_shift,
    dia_bins,
    dia_wts,
):
    bins_dev, points_dev = spectrum.shape
    nbins = dia_bins.shape[1]
    ndir = ND
    nfreq = nbins // ndir
    space_pos = lax.axis_index("space")
    bin_pos = lax.axis_index("bin")
    maskf = sea_mask.astype(jnp.float32)
    wet = spectrum * maskf[None, :]
    padded = extended(wet, (("space", 1),), points_dev)
    base = space_pos * points_dev - points_dev
    local = neighbours - base
    own_bins = bin_pos * bins_dev + jnp.arange(bins_dev, dtype=jnp.int32)
    fratio, speed, cosv, sinv, first, last = bin_tables(own_bins, nfreq, ndir)
    spatial = spatial_term(wet, padded, local, metric_x, metric_y, speed, cosv, sinv)
    share = points_dev // lax.axis_size("bin")
    start = bin_pos * share
    all_bins = jnp.arange(nbins, dtype=jnp.int32)
    fratio_all, speed_all, cos_all, sin_all, first_all, last_all = bin_tables(all_bins, nfreq, ndir)
    bin_pad = extended(wet, (("bin", 0),), ndir)
    spectral = spectral_term(wet, bin_pad, ndir, first, last, refraction, freq_shift, speed, cosv)
    moved_own = wet - spatial - spectral
    moved = lax.all_to_all(moved_own, "bin", split_axis=1, concat_axis=0, tiled=True)
    wind_part = lax.dynamic_slice_in_dim(wind, start, share, 1)
    mask_part = lax.dynamic_slice_in_dim(maskf, start, share, 0)
    plus_matrix = pair_matrix(dia_bins[0], dia_bins[1], dia_wts[0], nbins)
    minus_matrix = pair_matrix(dia_bins[2], dia_bins[3], dia_wts[1], nbins)
    result = source_step(
        moved,
        wind_part,
        mask_part,
        fratio_all,
        speed_all,
        cos_all,
        sin_all,
        lambda v: forward_product(plus_matrix, v),
        lambda v: forward_product(minus_matrix, v),
        lambda v: backward_product(plus_matrix, v),
        lambda v: backward_product(minus_matrix, v),
    )
    return result


LANES = 128
ROWS = 8
EDGE = 16
QUART = ND // 4
APART = 3
PIECES = 6
VMEM_ASK = 60 << 20
GROUP = 4


def chunk_plan(nloc):
    mid = nloc // 2
    plan = [(mid - d, 2 * d, 2) for d in range(1, mid + 1)]
    if mid > 3:
        plan[2] = (mid - 3, 3, 3)
    else:
        plan.insert(0, (mid, 1, 1))
    return plan


def freqs_of(chunk):
    first, step, count = chunk
    return [first + i * step for i in range(count)]


def halo_groups(plan):
    return [g for g in (plan[:1], plan[1:]) if g]


def slots_of(group):
    return {f: i for i, f in enumerate(f for chunk in group for f in freqs_of(chunk))}


def runs_of(freqs):
    runs = []
    for f in sorted(freqs):
        if runs and runs[-1][1] == f:
            runs[-1] = (runs[-1][0], f + 1)
        else:
            runs.append((f, f + 1))
    return runs


def prep_kernel(points, bins, blocks, groups, full, spec_hbm, mask_ref, *refs):
    ngr = len(groups)
    nloc = bins // ND
    hs_hbm, hn_hbm = refs[:ngr], refs[ngr : 2 * ngr]
    if full:
        wet_hbm, low_hbm, high_hbm = refs[2 * ngr : 2 * ngr + 3]
    spec_v, wet_v, edge_v, in_sem, out_sem = refs[-5:]
    tiles = points // LANES
    half = ND // 2
    where = {f: (i, k) for i, group in enumerate(groups) for f, k in slots_of(group).items()}
    loads = []
    spans = []
    for lo, hi in blocks:
        start = lo * ND // ROWS * ROWS
        stop = min(-(-hi * ND // ROWS) * ROWS, bins)
        spans.append((start, stop))
        rows = pl.ds(start, stop - start)
        copy = pltpu.make_async_copy(spec_hbm.at[rows], spec_v.at[rows], in_sem.at[len(loads)])
        copy.start()
        loads.append(copy)
    masks = [mask_ref[:, c * LANES : (c + 1) * LANES].astype(jnp.float32) for c in range(tiles)]
    copies = []

    def send(src, dst):
        copy = pltpu.make_async_copy(src, dst, out_sem.at[len(copies)])
        copy.start()
        copies.append(copy)

    for (lo, hi), (start, stop), load in zip(blocks, spans, loads):
        load.wait()

        def turn(g0, count):
            for c0 in range(0, tiles, ROWS):
                cols = range(c0, c0 + ROWS)
                block = jnp.stack(
                    [spec_v[pl.ds(g0, count), c * LANES : (c + 1) * LANES] * masks[c] for c in cols], axis=0
                )
                block = jnp.swapaxes(block, 0, 1)
                for i in range(count):
                    wet_v[pl.ds(pl.multiple_of((g0 + i) * tiles + c0, ROWS), ROWS), :] = block[i]

        def relayout(t, _):
            turn(pl.multiple_of(start + t * ROWS, ROWS), ROWS)
            return 0

        lax.fori_loop(0, (stop - start) // ROWS, relayout, 0)
        rest = (stop - start) % ROWS
        if rest:
            g0 = stop - rest
            for c in range(tiles):
                tile = spec_v[pl.ds(g0, rest), c * LANES : (c + 1) * LANES]
                wet_v[pl.ds(g0 * tiles + c, rest, stride=tiles), :] = tile * masks[c]
        for f in range(lo, hi):
            base = f * ND * tiles
            if f in where:
                i, k = where[f]
                for side, (j0, row) in enumerate(((3 * QUART, tiles - 1), (QUART, 0))):
                    at = base + j0 * tiles + row
                    edge_v[f, side, ROWS:EDGE, :] = jnp.zeros((EDGE - ROWS, LANES), jnp.float32)
                    edge_v[f, side, 0:ROWS, :] = wet_v[pl.ds(at, ROWS, stride=tiles), :]
                    edge_v[f, side, ROWS : ROWS + 1, :] = wet_v[pl.ds(at + ROWS * tiles, 1), :]
                span = half * tiles
                send(wet_v.at[pl.ds(base, span)], hs_hbm[i].at[k, pl.ds(0, span)])
                send(wet_v.at[pl.ds(base + span, span)], hn_hbm[i].at[k, pl.ds(0, span)])
                send(edge_v.at[f, 0], hs_hbm[i].at[k, pl.ds(span, EDGE)])
                send(edge_v.at[f, 1], hn_hbm[i].at[k, pl.ds(span, EDGE)])
            if full:
                own = pl.ds(base, ND * tiles)
                if f == nloc - 1:
                    send(wet_v.at[own], low_hbm)
                if f == 0:
                    send(wet_v.at[own], high_hbm)
                send(wet_v.at[own], wet_hbm.at[own])
    for copy in copies:
        copy.wait()


def prep(spectrum, mask, blocks, groups, full):
    bins, points = spectrum.shape
    nloc = bins // ND
    tiles = points // LANES
    halo_rows = ND // 2 * tiles + EDGE
    halos = [jax.ShapeDtypeStruct((len(slots_of(g)), halo_rows, LANES), jnp.float32) for g in groups]
    one = jax.ShapeDtypeStruct((ND * tiles, LANES), jnp.float32)
    outs = halos + halos
    if full:
        outs += [jax.ShapeDtypeStruct((bins * tiles, LANES), jnp.float32), one, one]
    anywhere = pl.BlockSpec(memory_space=pl.ANY)
    count = sum(hi - lo for lo, hi in blocks)
    sends = 4 * sum(len(slots_of(g)) for g in groups) + (nloc + 2 if full else 0)
    res = pl.pallas_call(
        functools.partial(prep_kernel, points, bins, blocks, groups, full),
        out_shape=outs,
        in_specs=[anywhere, pl.BlockSpec(memory_space=pltpu.VMEM)],
        out_specs=[anywhere] * len(outs),
        scratch_shapes=[
            pltpu.VMEM((bins, points), jnp.float32),
            pltpu.VMEM((bins * tiles, LANES), jnp.float32),
            pltpu.VMEM((nloc, 2, EDGE, LANES), jnp.float32),
            pltpu.SemaphoreType.DMA((len(blocks),)),
            pltpu.SemaphoreType.DMA((sends,)),
        ],
        compiler_params=pltpu.CompilerParams(vmem_limit_bytes=VMEM_ASK),
        cost_estimate=pl.CostEstimate(flops=0, bytes_accessed=count * 3_000_000, transcendentals=0),
        name="prep",
    )(spectrum, mask)
    ngr = len(groups)
    return res[:ngr], res[ngr : 2 * ngr], res[2 * ngr :]


def front_kernel(
    tiles, shares, nloc, kmin, kmax, chunk, edge, joined, tab_ref, dir_ref, pos_ref, nbr_ref, mx_ref, my_ref, rf_ref, fs_ref, hs_ref, hn_ref, wet_ref, *refs
):
    nout = 1 if joined else shares
    near, outs, ext_ref = refs[: -nout - 1], refs[-nout - 1 : -1], refs[-1]
    if joined:
        outs = [outs[0].at[d] for d in range(shares)]
    place = pl.program_id(0)
    speed = tab_ref[pos_ref[0] * nloc + chunk[0] + chunk[1] * place]
    first = place == 0
    half = ND // 2
    span = half * tiles
    south, north = tiles, ROWS
    pitch = APART * (2 * tiles + ROWS)

    def rows_at(j, row, count=ROWS):
        return pl.ds(j * pitch + APART * row, count, stride=APART)

    def extend(q, _):
        for t in range(0, tiles, ROWS):
            ext_ref[rows_at(q, t), :] = hs_ref[0, pl.ds(pl.multiple_of(q * tiles + t, ROWS), ROWS), :]
            ext_ref[rows_at(q, south + t), :] = wet_ref[0, q, t : t + ROWS, :]
            ext_ref[rows_at(half + q, north + t), :] = wet_ref[0, half + q, t : t + ROWS, :]
            ext_ref[rows_at(half + q, north + tiles + t), :] = hn_ref[
                0, pl.ds(pl.multiple_of(q * tiles + t, ROWS), ROWS), :
            ]
        return 0

    lax.fori_loop(0, half, extend, 0, unroll=2)
    for q in range(QUART):
        ext_ref[pl.ds((QUART + q) * pitch + APART * (south + tiles), 1), :] = hn_ref[0, span + q : span + q + 1, :]
        ext_ref[pl.ds((3 * QUART + q) * pitch + APART * (north - 1), 1), :] = hs_ref[0, span + q : span + q + 1, :]

    side = jnp.where(first, 1.0, -1.0)
    per_share = tiles // shares
    steps = [(d, k) for d in range(shares) for k in range(per_share // ROWS)]
    firsts = {}
    for d, k in steps:
        row = (d if joined else lax.rem(pos_ref[0] + d, shares)) * per_share + k * ROWS
        firsts[d, k] = row if joined else pl.multiple_of(row, ROWS)
    sub = lax.broadcasted_iota(jnp.int32, (ROWS, LANES), 0)
    lanes, rels = {}, {}
    for way in range(4):
        for step in steps:
            src = nbr_ref[way, pl.ds(firsts[step], ROWS), :]
            lanes[way, step] = src & (LANES - 1)
            rels[way, step] = (src >> 7) - (sub + firsts[step])

    def picked(j, own, step, way, offsets):
        out = None
        for r in offsets:
            window = ext_ref[rows_at(j, own + firsts[step] + r), :]
            got = jnp.take_along_axis(window, lanes[way, step], axis=1, mode="promise_in_bounds")
            out = got if out is None else jnp.where(rels[way, step] == r, got, out)
        return out

    for quad in range(4):
        cos_up = quad in (0, 3)
        own, way_y, off_y = (
            (south, 3, range(-(kmax // LANES), -(kmin // LANES) + 1))
            if quad < 2
            else (north, 2, range(kmin // LANES, kmax // LANES + 1))
        )
        way_x, off_x = (1, (-1, 0)) if cos_up else (0, (0, 1))

        def body(q, _):
            j = quad * QUART + q
            jprev = jnp.where(j == 0, ND - 1, j - 1)
            jnext = jnp.where(j == ND - 1, 0, j + 1)
            acos = jnp.abs(dir_ref[0, j])
            asin = jnp.abs(dir_ref[1, j])
            ax, ay = speed * acos, speed * asin
            for step in steps:
                at = pl.ds(firsts[step], ROWS)
                wet = wet_ref[0, j, at, :]
                e_y = picked(j, own, step, way_y, off_y)
                e_x = picked(j, own, step, way_x, off_x)
                rf, fs = rf_ref[at, :], fs_ref[at, :]
                e_prev, e_next = wet_ref[0, jprev, at, :], wet_ref[0, jnext, at, :]
                e_t = jnp.where(rf > 0, e_prev, e_next) if cos_up else jnp.where(rf < 0, e_prev, e_next)
                if edge:
                    inner, low, high = (ref[0, j, at, :] for ref in near)
                    outer = jnp.where(first, low, high)
                    e_s = jnp.where(fs * side > 0, outer, inner)
                else:
                    e_s = jnp.where(fs > 0, near[0][0, j, at, :], near[1][0, j, at, :])
                spatial = (mx_ref[at, :] * ax) * (wet - e_x) + (my_ref[at, :] * ay) * (wet - e_y)
                spectral = (jnp.abs(rf) * acos) * (wet - e_t) + (jnp.abs(fs) * speed) * (wet - e_s)
                d, k = step
                outs[d][j, k * ROWS : (k + 1) * ROWS, :] = wet - spatial - spectral
            return 0

        lax.fori_loop(0, QUART, body, 0, unroll=3)


def front(speed, dirs, pos, nbr, par, hs, hn, slot, wet, ends, chunk, joined, shares, kmin, kmax):
    first, step, count = chunk
    tiles = nbr.shape[1]
    nloc = wet.shape[0]
    smem = pl.BlockSpec(memory_space=pltpu.SMEM)

    def freq_spec(start, step):
        return pl.BlockSpec((1, ND, tiles, LANES), lambda i: (start + i * step, 0, 0, 0))

    halo_spec = pl.BlockSpec((1,) + hs.shape[1:], lambda i: (slot + i, 0, 0))

    def whole(shape):
        return pl.BlockSpec(shape, lambda i: (0,) * len(shape))

    if ends:
        near, near_specs = (wet,) + ends, [freq_spec(1, nloc - 3), freq_spec(0, 0), freq_spec(0, 0)]
    else:
        near, near_specs = (wet, wet), [freq_spec(first - 1, step), freq_spec(first + 1, step)]
    rows = tiles // shares
    if joined:
        outs = [jax.ShapeDtypeStruct((shares, count * ND, rows, LANES), jnp.float32)]
        out_specs = [pl.BlockSpec((shares, ND, rows, LANES), lambda i: (0, i, 0, 0))]
    else:
        outs = [jax.ShapeDtypeStruct((count * ND, rows, LANES), jnp.float32)] * shares
        out_specs = [pl.BlockSpec((ND, rows, LANES), lambda i: (i, 0, 0))] * shares
    return pl.pallas_call(
        functools.partial(front_kernel, tiles, shares, nloc, kmin, kmax, chunk, bool(ends), joined),
        grid=(count,),
        out_shape=outs,
        in_specs=[smem] * 3
        + [whole(nbr.shape)] + [whole(p.shape) for p in par] + [halo_spec, halo_spec, freq_spec(first, step)]
        + near_specs,
        out_specs=out_specs,
        scratch_shapes=[pltpu.VMEM((ND * APART * (2 * tiles + ROWS), LANES), jnp.float32)],
        compiler_params=pltpu.CompilerParams(vmem_limit_bytes=VMEM_ASK),
        cost_estimate=pl.CostEstimate(flops=0, bytes_accessed=count * 22_000_000, transcendentals=0),
        name="front",
    )(speed, dirs, pos, nbr, *par, hs, hn, wet, *near)


def tail_kernel(nfreq, bins_dev, plan, spot_ref, wts_ref, ftab_ref, frs_ref, dir_ref, pos_ref, wind_ref, mask_ref, *refs):
    out_hbm, mv, base, a0, a1, a2, a3, dw, out_v, in_sem, out_sem = refs[-11:]
    parts = iter(refs[:-11])
    shares = nfreq * ND // bins_dev
    nbins = nfreq * ND
    loads = []
    for c, chunk in enumerate(plan):
        joined = c == 0
        whole = next(parts) if joined else None
        for d in range(shares):
            part = whole.at[d] if joined else next(parts)
            source = d if joined else lax.rem(pos_ref[0] + (shares - d), shares)
            for i, f in enumerate(freqs_of(chunk)):
                rows = pl.ds(source * bins_dev + f * ND, ND)
                copy = pltpu.make_async_copy(part.at[pl.ds(i * ND, ND)], mv.at[rows], in_sem.at[len(loads)])
                copy.start()
                loads.append(copy)
    zero = jnp.zeros((ROWS, LANES), jnp.float32)
    accs = (a0, a1, a2, a3)

    def clear(g, _):
        for acc in accs:
            acc[g] = zero
        return 0

    lax.fori_loop(0, nbins, clear, 0, unroll=8)
    for j in range(ND):
        dw[j] = wind_ref[0] * dir_ref[0, j] + wind_ref[1] * dir_ref[1, j]
    for copy in loads:
        copy.wait()

    def per_freq(f, steep):
        fr2, fr4, hspeed = ftab_ref[0, f], ftab_ref[1, f], ftab_ref[2, f]

        def per_group(t, total):
            j0 = t * GROUP
            g0 = f * ND + j0
            spots = [[spot_ref[4 * g0 + 4 * i + k] for k in range(4)] for i in range(GROUP)]
            own = [mv[g0 + i] for i in range(GROUP)]
            found = [[mv[b] for b in spots[i]] for i in range(GROUP)]
            adds = []
            for i in range(GROUP):
                m, (p0, p1, m0, m1) = own[i], found[i]
                wp, wm = wts_ref[2 * g0 + 2 * i], wts_ref[2 * g0 + 2 * i + 1]
                ep = p1 + wp * (p0 - p1)
                em = m1 + wm * (m0 - m1)
                mf = fr4 * m
                half = mf * (m * (ep * (1 / 1.25**4) + em * (1 / 0.75**4)) - ep * em * (2.0 / 0.9375**4))
                drive = jnp.maximum(0.0, dw[j0 + i] - hspeed)
                base[g0 + i] = m + 0.15 * (drive * drive) * m - 2.0 * half
                sp, sm = wp * half, wm * half
                adds.append((sp, half - sp, sm, half - sm))
                total = total + m
            for i in range(0, GROUP, 2):
                for acc, b0, b1, x0, x1 in zip(accs, spots[i], spots[i + 1], adds[i], adds[i + 1]):
                    old0, old1 = acc[b0], acc[b1]
                    acc[b0] = old0 + x0
                    acc[b1] = old1 + (x1 + jnp.where(b0 == b1, x0, zero))
            return total

        return steep + lax.fori_loop(0, ND // GROUP, per_group, zero, unroll=3) * fr2

    steep = lax.fori_loop(0, nfreq, per_freq, zero)
    steep = steep * (1.0 / nbins)
    mask = mask_ref[...].astype(jnp.float32)
    per = nbins // PIECES
    copies = []
    for p in range(PIECES):

        def finish(t, _):
            g0 = t * ROWS
            done = []
            for i in range(ROWS):
                g = g0 + i
                mine = base[g] - (frs_ref[g] * steep) * mv[g]
                done.append((mine + ((a0[g] + a1[g]) + (a2[g] + a3[g]))) * mask)
            turned = jnp.swapaxes(jnp.stack(done, axis=0), 0, 1)
            for c in range(ROWS):
                out_v[pl.ds(pl.multiple_of(g0, ROWS), ROWS), c * LANES : (c + 1) * LANES] = turned[c]
            return 0

        lax.fori_loop(p * per // ROWS, (p + 1) * per // ROWS, finish, 0, unroll=3)
        rows = pl.ds(p * per, per)
        copy = pltpu.make_async_copy(out_v.at[rows], out_hbm.at[rows], out_sem.at[p])
        copy.start()
        copies.append(copy)
    for copy in copies:
        copy.wait()


def tail(parts, plan, bins_dev, dia_bins, dia_wts, ftab, frs, dirs, pos, wind, mask):
    nbins = dia_bins.shape[1]
    nfreq = nbins // ND
    anywhere = pl.BlockSpec(memory_space=pl.ANY)
    smem = pl.BlockSpec(memory_space=pltpu.SMEM)
    vmem = pl.BlockSpec(memory_space=pltpu.VMEM)
    points = ROWS * LANES
    spots = dia_bins.T.reshape(-1)
    wts = dia_wts.T.reshape(-1)
    field = pltpu.VMEM((nbins, ROWS, LANES), jnp.float32)
    return pl.pallas_call(
        functools.partial(tail_kernel, nfreq, bins_dev, plan),
        out_shape=jax.ShapeDtypeStruct((nbins, points), jnp.float32),
        in_specs=[smem] * 6 + [vmem] * 2 + [anywhere] * len(parts),
        out_specs=anywhere,
        scratch_shapes=[field] * 6
        + [
            pltpu.VMEM((ND, ROWS, LANES), jnp.float32),
            pltpu.VMEM((nbins, points), jnp.float32),
            pltpu.SemaphoreType.DMA((nbins // ND,)),
            pltpu.SemaphoreType.DMA((PIECES,)),
        ],
        compiler_params=pltpu.CompilerParams(vmem_limit_bytes=VMEM_ASK),
        cost_estimate=pl.CostEstimate(flops=0, bytes_accessed=70_000_000, transcendentals=0),
        name="tail",
    )(spots, wts, ftab, frs, dirs, pos, wind, mask, *parts)


def fast_on_device(
    spectrum, wind, sea_mask, neighbours, metric_x, metric_y, refraction, freq_shift, dia_bins, dia_wts
):
    bins_dev, points = spectrum.shape
    nbins = dia_bins.shape[1]
    nfreq = nbins // ND
    nloc = bins_dev // ND
    tiles = points // LANES
    shares = lax.axis_size("bin")
    share = points // shares
    bin_pos = lax.axis_index("bin")
    space_pos = lax.axis_index("space")
    plan = chunk_plan(nloc)

    freqs = np.arange(nfreq, dtype=np.float32)
    speed = jnp.asarray(np.exp(-np.log(1.1) * freqs.astype(np.float64)).astype(np.float32))
    ratio = np.exp(np.log(1.1) * (freqs.astype(np.float64) - (nfreq - 1)))
    ftab = jnp.asarray(
        np.stack([ratio**2, 4.0 * ratio**4, 0.5 * np.exp(-np.log(1.1) * freqs)]).astype(np.float32)
    )
    frs = jnp.asarray(np.repeat(3.0 * ratio, ND).astype(np.float32))
    theta = 2.0 * np.pi * (np.arange(ND) + 0.5) / ND
    dirs = jnp.asarray(np.stack([np.cos(theta), np.sin(theta)]).astype(np.float32))

    groups = halo_groups(plan)
    early = runs_of(slots_of(groups[0]))
    mask_row = sea_mask.reshape(1, points)
    hs, hn, _ = prep(spectrum, mask_row, early, groups[:1], False)
    after, *_ = lax.optimization_barrier((spectrum, hs[0], hn[0]))
    whole_blocks = [(f, min(f + 2, nloc)) for f in range(0, nloc, 2)]
    hs_rest, hn_rest, (wet, low_out, high_out) = prep(after, mask_row, whole_blocks, groups[1:], True)
    wet = wet.reshape(nloc, ND, tiles, LANES)

    def line(array, axis, step):
        peers = lax.axis_size(axis)
        pairs = [(i, i + 1) for i in range(peers - 1)]
        if step < 0:
            pairs = [(b, a) for a, b in pairs]
        return lax.ppermute(array, axis, pairs)

    sends = list(zip(list(hs) + list(hs_rest), list(hn) + list(hn_rest)))
    halos = []

    def send_halos(*after):
        if len(halos) < len(sends):
            south, north = sends[len(halos)]
            if after:
                south, north, *_ = lax.optimization_barrier((south, north) + after)
            halos.append((line(south, "space", 1), line(north, "space", -1)))

    send_halos()
    send_halos(*halos[0])
    low_in = line(low_out, "bin", 1).reshape(1, ND, tiles, LANES)
    high_in = line(high_out, "bin", -1).reshape(1, ND, tiles, LANES)

    nbr = (neighbours - space_pos * points).reshape(4, tiles, LANES)
    par = [p.reshape(tiles, LANES) for p in (metric_x, metric_y, refraction, freq_shift)]
    pos = bin_pos.reshape(1)
    kmin, kmax = points // 2, points
    arrived = []
    order = pos
    for c, chunk in enumerate(plan):
        first, step, count = chunk
        joined = c == 0
        gi, slot = [(i, slots_of(g)[first]) for i, g in enumerate(groups) if chunk in g][0]
        ends = (low_in, high_in) if first == 0 else None
        blocks = front(speed, dirs, order, nbr, par, *halos[gi], slot, wet, ends, chunk, joined, shares, kmin, kmax)
        earlier = sum(halos, ()) if c == 0 else arrived[0] if c == 1 else []
        order, *_ = lax.optimization_barrier((pos, blocks[0], *earlier))
        if joined:
            blocks, *_ = lax.optimization_barrier((blocks[0], low_in, high_in))
            arrived.append([lax.all_to_all(blocks, "bin", split_axis=0, concat_axis=0, tiled=True)])
            continue
        here = [blocks[0]]
        for d in range(1, shares):
            rows = blocks[d]
            if c > 1:
                rows, _ = lax.optimization_barrier((rows, arrived[-1][d]))
            here.append(lax.ppermute(rows, "bin", [(i, (i + d) % shares) for i in range(shares)]))
        arrived.append(here)
    parts = sum(arrived, [])
    wind_part = lax.dynamic_slice_in_dim(wind, bin_pos * share, share, 1).reshape(2, ROWS, LANES)
    mask_part = lax.dynamic_slice_in_dim(sea_mask, bin_pos * share, share, 0).reshape(ROWS, LANES)
    return tail(parts, plan, bins_dev, dia_bins, dia_wts, ftab, frs, dirs, pos, wind_part, mask_part)


def pick_path(spectrum, *others):
    bins_dev, points = spectrum.shape
    fits = bins_dev % (2 * ND) == ND and bins_dev > ND and points // lax.axis_size("bin") == ROWS * LANES
    return (fast_on_device if fits else on_device)(spectrum, *others)


def solution(mesh):
    return jax.shard_map(
        pick_path,
        mesh=mesh,
        in_specs=(
            P("bin", ("ens", "space")),
            P(None, ("ens", "space")),
            P("space"),
            P(None, "space"),
            P("space"),
            P("space"),
            P("space"),
            P("space"),
            P(),
            P(),
        ),
        out_specs=P(None, ("ens", "space", "bin")),
        check_vma=False,
    )
```

```python
import functools
import itertools

import jax
import jax.numpy as jnp
import numpy as np
from jax import lax
from jax.experimental import pallas as pl
from jax.experimental.pallas import tpu as pltpu
from jax.sharding import PartitionSpec as P

ND = 36


def extended(array, sides, width):
    for axis, dim in sides:
        peers, length = (lax.axis_size(axis), array.shape[dim])
        up = [(i, (i + 1) % peers) for i in range(peers - 1)]
        down = [(j, i) for i, j in up]
        last = lax.slice_in_dim(array, length - width, length, axis=dim)
        initial = lax.slice_in_dim(array, 0, width, axis=dim)
        before = lax.ppermute(last, axis, up)
        after = lax.ppermute(initial, axis, down)
        array = jnp.concatenate([before, array, after], axis=dim)
    return array


def bin_tables(index, nfreq, ndir):
    freq = (index // ndir).astype(jnp.float32)
    direc = index % ndir
    fratio = jnp.exp(jnp.log(1.1) * (freq - (nfreq - 1)))
    speed = jnp.exp(-jnp.log(1.1) * freq)
    theta = 2.0 * jnp.pi * (direc.astype(jnp.float32) + 0.5) / ndir
    return (fratio, speed, jnp.cos(theta), jnp.sin(theta), direc == 0, direc == ndir - 1)


def spatial_term(wet, padded, local, metric_x, metric_y, speed, cosv, sinv):
    east = jnp.take(padded, local[0], axis=1)
    west = jnp.take(padded, local[1], axis=1)
    north = jnp.take(padded, local[2], axis=1)
    south = jnp.take(padded, local[3], axis=1)
    along_x = metric_x[None, :] * (speed * cosv)[:, None]
    along_y = metric_y[None, :] * (speed * sinv)[:, None]
    flux_x = jnp.abs(along_x) * (wet - jnp.where(along_x > 0, west, east))
    flux_y = jnp.abs(along_y) * (wet - jnp.where(along_y > 0, south, north))
    return flux_x + flux_y


def spectral_term(wet, padded, ndir, first, last, refraction, freq_shift, speed, cosv):
    rows = wet.shape[0]

    def moved_rows(offset):
        return lax.slice_in_dim(padded, ndir + offset, ndir + offset + rows, axis=0)

    prev_dir = jnp.where(first[:, None], moved_rows(ndir - 1), moved_rows(-1))
    next_dir = jnp.where(last[:, None], moved_rows(1 - ndir), moved_rows(1))
    lower = moved_rows(-ndir)
    upper = moved_rows(ndir)
    turning = refraction[None, :] * cosv[:, None]
    shifting = freq_shift[None, :] * speed[:, None]
    flux_t = jnp.abs(turning) * (wet - jnp.where(turning > 0, prev_dir, next_dir))
    flux_s = jnp.abs(shifting) * (wet - jnp.where(shifting > 0, lower, upper))
    return flux_t + flux_s


def source_step(
    moved, wind, maskf, fratio, speed, cosv, sinv, plus_fwd, minus_fwd, plus_back, minus_back
):
    steep = jnp.mean(moved * (fratio * fratio)[:, None], axis=0)
    drive = jnp.maximum(
        0.0,
        wind[0][None, :] * cosv[:, None] + wind[1][None, :] * sinv[:, None] - 0.5 * speed[:, None],
    )
    s_in = 0.3 * drive * drive * moved
    s_ds = -6.0 * fratio[:, None] * steep[None, :] * moved
    e_plus = plus_fwd(moved)
    e_minus = minus_fwd(moved)
    delta = (
        8.0
        * (fratio**4)[:, None]
        * (
            moved * moved * (e_plus / 1.25**4 + e_minus / 0.75**4)
            - 2.0 * moved * e_plus * e_minus / 0.9375**4
        )
    )
    s_nl = -2.0 * delta + plus_back(delta) + minus_back(delta)
    return (moved + 0.5 * (s_in + s_ds + s_nl)) * maskf[None, :]


def pair_matrix(first_bins, second_bins, weight, count):
    columns = jnp.arange(count, dtype=jnp.int32)[None, :]
    return weight[:, None] * (first_bins[:, None] == columns).astype(jnp.float32) + (1.0 - weight)[
        :, None
    ] * (second_bins[:, None] == columns).astype(jnp.float32)


def forward_product(matrix, values):
    return jnp.dot(
        matrix, values, precision=lax.Precision.HIGHEST, preferred_element_type=jnp.float32
    )


def backward_product(matrix, values):
    return lax.dot_general(
        matrix,
        values,
        (((0,), (0,)), ((), ())),
        precision=lax.Precision.HIGHEST,
        preferred_element_type=jnp.float32,
    )


def on_device(
    spectrum,
    wind,
    sea_mask,
    neighbours,
    metric_x,
    metric_y,
    refraction,
    freq_shift,
    dia_bins,
    dia_wts,
):
    bins_dev, points_dev = spectrum.shape
    nbins = dia_bins.shape[1]
    ndir = ND
    nfreq = nbins // ndir
    space_pos = lax.axis_index("space")
    bin_pos = lax.axis_index("bin")
    maskf = sea_mask.astype(jnp.float32)
    wet = spectrum * maskf[None, :]
    padded = extended(wet, (("space", 1),), points_dev)
    base = space_pos * points_dev - points_dev
    local = neighbours - base
    own_bins = bin_pos * bins_dev + jnp.arange(bins_dev, dtype=jnp.int32)
    fratio, speed, cosv, sinv, first, last = bin_tables(own_bins, nfreq, ndir)
    spatial = spatial_term(wet, padded, local, metric_x, metric_y, speed, cosv, sinv)
    share = points_dev // lax.axis_size("bin")
    start = bin_pos * share
    all_bins = jnp.arange(nbins, dtype=jnp.int32)
    fratio_all, speed_all, cos_all, sin_all, first_all, last_all = bin_tables(all_bins, nfreq, ndir)
    bin_pad = extended(wet, (("bin", 0),), ndir)
    spectral = spectral_term(wet, bin_pad, ndir, first, last, refraction, freq_shift, speed, cosv)
    moved_own = wet - spatial - spectral
    moved = lax.all_to_all(moved_own, "bin", split_axis=1, concat_axis=0, tiled=True)
    wind_part = lax.dynamic_slice_in_dim(wind, start, share, 1)
    mask_part = lax.dynamic_slice_in_dim(maskf, start, share, 0)
    plus_matrix = pair_matrix(dia_bins[0], dia_bins[1], dia_wts[0], nbins)
    minus_matrix = pair_matrix(dia_bins[2], dia_bins[3], dia_wts[1], nbins)
    result = source_step(
        moved,
        wind_part,
        mask_part,
        fratio_all,
        speed_all,
        cos_all,
        sin_all,
        lambda v: forward_product(plus_matrix, v),
        lambda v: forward_product(minus_matrix, v),
        lambda v: backward_product(plus_matrix, v),
        lambda v: backward_product(minus_matrix, v),
    )
    return result


LANES = 128
ROWS = 8
EDGE = 16
QUART = ND // 4
APART = 3
PIECES = 6
VMEM_ASK = 60 << 20
GROUP = 4


def chunk_plan(nloc):
    mid = nloc // 2
    plan = [(mid - d, 2 * d, 2) for d in range(1, mid + 1)]
    if mid > 3:
        plan[2] = (mid - 3, 3, 3)
    else:
        plan.insert(0, (mid, 1, 1))
    return plan


def freqs_of(chunk):
    first, step, count = chunk
    return [first + i * step for i in range(count)]


def halo_groups(plan):
    return [g for g in (plan[:1], plan[1:]) if g]


def slots_of(group):
    return {f: i for i, f in enumerate(f for chunk in group for f in freqs_of(chunk))}


def runs_of(freqs):
    runs = []
    for f in sorted(freqs):
        if runs and runs[-1][1] == f:
            runs[-1] = (runs[-1][0], f + 1)
        else:
            runs.append((f, f + 1))
    return runs


def prep_kernel(points, bins, blocks, groups, full, spec_hbm, mask_ref, *refs):
    ngr = len(groups)
    nloc = bins // ND
    hs_hbm, hn_hbm = refs[:ngr], refs[ngr : 2 * ngr]
    if full:
        wet_hbm, low_hbm, high_hbm = refs[2 * ngr : 2 * ngr + 3]
    spec_v, wet_v, edge_v, in_sem, out_sem = refs[-5:]
    tiles = points // LANES
    half = ND // 2
    where = {f: (i, k) for i, group in enumerate(groups) for f, k in slots_of(group).items()}
    loads = []
    spans = []
    for lo, hi in blocks:
        start = lo * ND // ROWS * ROWS
        stop = min(-(-hi * ND // ROWS) * ROWS, bins)
        spans.append((start, stop))
        rows = pl.ds(start, stop - start)
        copy = pltpu.make_async_copy(spec_hbm.at[rows], spec_v.at[rows], in_sem.at[len(loads)])
        copy.start()
        loads.append(copy)
    masks = [mask_ref[:, c * LANES : (c + 1) * LANES].astype(jnp.float32) for c in range(tiles)]
    copies = []

    def send(src, dst):
        copy = pltpu.make_async_copy(src, dst, out_sem.at[len(copies)])
        copy.start()
        copies.append(copy)

    for (lo, hi), (start, stop), load in zip(blocks, spans, loads):
        load.wait()

        def turn(g0, count):
            for c0 in range(0, tiles, ROWS):
                cols = range(c0, c0 + ROWS)
                block = jnp.stack(
                    [spec_v[pl.ds(g0, count), c * LANES : (c + 1) * LANES] * masks[c] for c in cols], axis=0
                )
                block = jnp.swapaxes(block, 0, 1)
                for i in range(count):
                    wet_v[pl.ds(pl.multiple_of((g0 + i) * tiles + c0, ROWS), ROWS), :] = block[i]

        def relayout(t, _):
            turn(pl.multiple_of(start + t * ROWS, ROWS), ROWS)
            return 0

        lax.fori_loop(0, (stop - start) // ROWS, relayout, 0)
        rest = (stop - start) % ROWS
        if rest:
            g0 = stop - rest
            for c in range(tiles):
                tile = spec_v[pl.ds(g0, rest), c * LANES : (c + 1) * LANES]
                wet_v[pl.ds(g0 * tiles + c, rest, stride=tiles), :] = tile * masks[c]
        for f in range(lo, hi):
            base = f * ND * tiles
            if f in where:
                i, k = where[f]
                for side, (j0, row) in enumerate(((3 * QUART, tiles - 1), (QUART, 0))):
                    at = base + j0 * tiles + row
                    edge_v[f, side, ROWS:EDGE, :] = jnp.zeros((EDGE - ROWS, LANES), jnp.float32)
                    edge_v[f, side, 0:ROWS, :] = wet_v[pl.ds(at, ROWS, stride=tiles), :]
                    edge_v[f, side, ROWS : ROWS + 1, :] = wet_v[pl.ds(at + ROWS * tiles, 1), :]
                span = half * tiles
                send(wet_v.at[pl.ds(base, span)], hs_hbm[i].at[k, pl.ds(0, span)])
                send(wet_v.at[pl.ds(base + span, span)], hn_hbm[i].at[k, pl.ds(0, span)])
                send(edge_v.at[f, 0], hs_hbm[i].at[k, pl.ds(span, EDGE)])
                send(edge_v.at[f, 1], hn_hbm[i].at[k, pl.ds(span, EDGE)])
            if full:
                own = pl.ds(base, ND * tiles)
                if f == nloc - 1:
                    send(wet_v.at[own], low_hbm)
                if f == 0:
                    send(wet_v.at[own], high_hbm)
                send(wet_v.at[own], wet_hbm.at[own])
    for copy in copies:
        copy.wait()


def prep(spectrum, mask, blocks, groups, full):
    bins, points = spectrum.shape
    nloc = bins // ND
    tiles = points // LANES
    halo_rows = ND // 2 * tiles + EDGE
    halos = [jax.ShapeDtypeStruct((len(slots_of(g)), halo_rows, LANES), jnp.float32) for g in groups]
    one = jax.ShapeDtypeStruct((ND * tiles, LANES), jnp.float32)
    outs = halos + halos
    if full:
        outs += [jax.ShapeDtypeStruct((bins * tiles, LANES), jnp.float32), one, one]
    anywhere = pl.BlockSpec(memory_space=pl.ANY)
    count = sum(hi - lo for lo, hi in blocks)
    sends = 4 * sum(len(slots_of(g)) for g in groups) + (nloc + 2 if full else 0)
    res = pl.pallas_call(
        functools.partial(prep_kernel, points, bins, blocks, groups, full),
        out_shape=outs,
        in_specs=[anywhere, pl.BlockSpec(memory_space=pltpu.VMEM)],
        out_specs=[anywhere] * len(outs),
        scratch_shapes=[
            pltpu.VMEM((bins, points), jnp.float32),
            pltpu.VMEM((bins * tiles, LANES), jnp.float32),
            pltpu.VMEM((nloc, 2, EDGE, LANES), jnp.float32),
            pltpu.SemaphoreType.DMA((len(blocks),)),
            pltpu.SemaphoreType.DMA((sends,)),
        ],
        compiler_params=pltpu.CompilerParams(vmem_limit_bytes=VMEM_ASK),
        cost_estimate=pl.CostEstimate(flops=0, bytes_accessed=count * 3_000_000, transcendentals=0),
        name="prep",
    )(spectrum, mask)
    ngr = len(groups)
    return res[:ngr], res[ngr : 2 * ngr], res[2 * ngr :]


def front_kernel(
    tiles, shares, nloc, kmin, kmax, chunk, edge, joined, tab_ref, dir_ref, pos_ref, nbr_ref, mx_ref, my_ref, rf_ref, fs_ref, hs_ref, hn_ref, wet_ref, *refs
):
    nout = 1 if joined else shares
    near, outs, ext_ref = refs[: -nout - 1], refs[-nout - 1 : -1], refs[-1]
    if joined:
        outs = [outs[0].at[d] for d in range(shares)]
    place = pl.program_id(0)
    speed = tab_ref[pos_ref[0] * nloc + chunk[0] + chunk[1] * place]
    first = place == 0
    half = ND // 2
    span = half * tiles
    south, north = tiles, ROWS
    pitch = APART * (2 * tiles + ROWS)

    def rows_at(j, row, count=ROWS):
        return pl.ds(j * pitch + APART * row, count, stride=APART)

    def extend(q, _):
        for t in range(0, tiles, ROWS):
            ext_ref[rows_at(q, t), :] = hs_ref[0, pl.ds(pl.multiple_of(q * tiles + t, ROWS), ROWS), :]
            ext_ref[rows_at(q, south + t), :] = wet_ref[0, q, t : t + ROWS, :]
            ext_ref[rows_at(half + q, north + t), :] = wet_ref[0, half + q, t : t + ROWS, :]
            ext_ref[rows_at(half + q, north + tiles + t), :] = hn_ref[
                0, pl.ds(pl.multiple_of(q * tiles + t, ROWS), ROWS), :
            ]
        return 0

    lax.fori_loop(0, half, extend, 0, unroll=2)
    for q in range(QUART):
        ext_ref[pl.ds((QUART + q) * pitch + APART * (south + tiles), 1), :] = hn_ref[0, span + q : span + q + 1, :]
        ext_ref[pl.ds((3 * QUART + q) * pitch + APART * (north - 1), 1), :] = hs_ref[0, span + q : span + q + 1, :]

    side = jnp.where(first, 1.0, -1.0)
    per_share = tiles // shares
    steps = [(d, k) for d in range(shares) for k in range(per_share // ROWS)]
    firsts = {}
    for d, k in steps:
        row = (d if joined else lax.rem(pos_ref[0] + d, shares)) * per_share + k * ROWS
        firsts[d, k] = row if joined else pl.multiple_of(row, ROWS)
    sub = lax.broadcasted_iota(jnp.int32, (ROWS, LANES), 0)
    lanes, rels = {}, {}
    for way in range(4):
        for step in steps:
            src = nbr_ref[way, pl.ds(firsts[step], ROWS), :]
            lanes[way, step] = src & (LANES - 1)
            rels[way, step] = (src >> 7) - (sub + firsts[step])

    def picked(j, own, step, way, offsets):
        out = None
        for r in offsets:
            window = ext_ref[rows_at(j, own + firsts[step] + r), :]
            got = jnp.take_along_axis(window, lanes[way, step], axis=1, mode="promise_in_bounds")
            out = got if out is None else jnp.where(rels[way, step] == r, got, out)
        return out

    for quad in range(4):
        cos_up = quad in (0, 3)
        own, way_y, off_y = (
            (south, 3, range(-(kmax // LANES), -(kmin // LANES) + 1))
            if quad < 2
            else (north, 2, range(kmin // LANES, kmax // LANES + 1))
        )
        way_x, off_x = (1, (-1, 0)) if cos_up else (0, (0, 1))

        def body(q, _):
            j = quad * QUART + q
            jprev = jnp.where(j == 0, ND - 1, j - 1)
            jnext = jnp.where(j == ND - 1, 0, j + 1)
            acos = jnp.abs(dir_ref[0, j])
            asin = jnp.abs(dir_ref[1, j])
            ax, ay = speed * acos, speed * asin
            for step in steps:
                at = pl.ds(firsts[step], ROWS)
                wet = wet_ref[0, j, at, :]
                e_y = picked(j, own, step, way_y, off_y)
                e_x = picked(j, own, step, way_x, off_x)
                rf, fs = rf_ref[at, :], fs_ref[at, :]
                e_prev, e_next = wet_ref[0, jprev, at, :], wet_ref[0, jnext, at, :]
                e_t = jnp.where(rf > 0, e_prev, e_next) if cos_up else jnp.where(rf < 0, e_prev, e_next)
                if edge:
                    inner, low, high = (ref[0, j, at, :] for ref in near)
                    outer = jnp.where(first, low, high)
                    e_s = jnp.where(fs * side > 0, outer, inner)
                else:
                    e_s = jnp.where(fs > 0, near[0][0, j, at, :], near[1][0, j, at, :])
                spatial = (mx_ref[at, :] * ax) * (wet - e_x) + (my_ref[at, :] * ay) * (wet - e_y)
                spectral = (jnp.abs(rf) * acos) * (wet - e_t) + (jnp.abs(fs) * speed) * (wet - e_s)
                d, k = step
                outs[d][j, k * ROWS : (k + 1) * ROWS, :] = wet - spatial - spectral
            return 0

        lax.fori_loop(0, QUART, body, 0, unroll=3)


def front(speed, dirs, pos, nbr, par, hs, hn, slot, wet, ends, chunk, joined, shares, kmin, kmax):
    first, step, count = chunk
    tiles = nbr.shape[1]
    nloc = wet.shape[0]
    smem = pl.BlockSpec(memory_space=pltpu.SMEM)

    def freq_spec(start, step):
        return pl.BlockSpec((1, ND, tiles, LANES), lambda i: (start + i * step, 0, 0, 0))

    halo_spec = pl.BlockSpec((1,) + hs.shape[1:], lambda i: (slot + i, 0, 0))

    def whole(shape):
        return pl.BlockSpec(shape, lambda i: (0,) * len(shape))

    if ends:
        near, near_specs = (wet,) + ends, [freq_spec(1, nloc - 3), freq_spec(0, 0), freq_spec(0, 0)]
    else:
        near, near_specs = (wet, wet), [freq_spec(first - 1, step), freq_spec(first + 1, step)]
    rows = tiles // shares
    if joined:
        outs = [jax.ShapeDtypeStruct((shares, count * ND, rows, LANES), jnp.float32)]
        out_specs = [pl.BlockSpec((shares, ND, rows, LANES), lambda i: (0, i, 0, 0))]
    else:
        outs = [jax.ShapeDtypeStruct((count * ND, rows, LANES), jnp.float32)] * shares
        out_specs = [pl.BlockSpec((ND, rows, LANES), lambda i: (i, 0, 0))] * shares
    return pl.pallas_call(
        functools.partial(front_kernel, tiles, shares, nloc, kmin, kmax, chunk, bool(ends), joined),
        grid=(count,),
        out_shape=outs,
        in_specs=[smem] * 3
        + [whole(nbr.shape)] + [whole(p.shape) for p in par] + [halo_spec, halo_spec, freq_spec(first, step)]
        + near_specs,
        out_specs=out_specs,
        scratch_shapes=[pltpu.VMEM((ND * APART * (2 * tiles + ROWS), LANES), jnp.float32)],
        compiler_params=pltpu.CompilerParams(vmem_limit_bytes=VMEM_ASK),
        cost_estimate=pl.CostEstimate(flops=0, bytes_accessed=count * 22_000_000, transcendentals=0),
        name="front",
    )(speed, dirs, pos, nbr, *par, hs, hn, wet, *near)


def tail_kernel(nfreq, bins_dev, plan, spot_ref, wts_ref, ftab_ref, frs_ref, dir_ref, pos_ref, wind_ref, mask_ref, *refs):
    out_hbm, mv, base, a0, a1, a2, a3, dw, out_v, in_sem, out_sem = refs[-11:]
    parts = iter(refs[:-11])
    shares = nfreq * ND // bins_dev
    nbins = nfreq * ND
    loads = []
    for c, chunk in enumerate(plan):
        joined = c == 0
        whole = next(parts) if joined else None
        for d in range(shares):
            part = whole.at[d] if joined else next(parts)
            source = d if joined else lax.rem(pos_ref[0] + (shares - d), shares)
            for i, f in enumerate(freqs_of(chunk)):
                rows = pl.ds(source * bins_dev + f * ND, ND)
                copy = pltpu.make_async_copy(part.at[pl.ds(i * ND, ND)], mv.at[rows], in_sem.at[len(loads)])
                copy.start()
                loads.append(copy)
    zero = jnp.zeros((ROWS, LANES), jnp.float32)
    accs = (a0, a1, a2, a3)

    def clear(g, _):
        for acc in accs:
            acc[g] = zero
        return 0

    lax.fori_loop(0, nbins, clear, 0, unroll=8)
    for j in range(ND):
        dw[j] = wind_ref[0] * dir_ref[0, j] + wind_ref[1] * dir_ref[1, j]
    for copy in loads:
        copy.wait()

    def per_freq(f, steep):
        fr2, fr4, hspeed = ftab_ref[0, f], ftab_ref[1, f], ftab_ref[2, f]

        def per_group(t, total):
            j0 = t * GROUP
            g0 = f * ND + j0
            spots = [[spot_ref[4 * g0 + 4 * i + k] for k in range(4)] for i in range(GROUP)]
            own = [mv[g0 + i] for i in range(GROUP)]
            found = [[mv[b] for b in spots[i]] for i in range(GROUP)]
            adds = []
            for i in range(GROUP):
                m, (p0, p1, m0, m1) = own[i], found[i]
                wp, wm = wts_ref[2 * g0 + 2 * i], wts_ref[2 * g0 + 2 * i + 1]
                ep = p1 + wp * (p0 - p1)
                em = m1 + wm * (m0 - m1)
                mf = fr4 * m
                half = mf * (m * (ep * (1 / 1.25**4) + em * (1 / 0.75**4)) - ep * em * (2.0 / 0.9375**4))
                drive = jnp.maximum(0.0, dw[j0 + i] - hspeed)
                base[g0 + i] = m + 0.15 * (drive * drive) * m - 2.0 * half
                sp, sm = wp * half, wm * half
                adds.append((sp, half - sp, sm, half - sm))
                total = total + m
            for i in range(0, GROUP, 2):
                for acc, b0, b1, x0, x1 in zip(accs, spots[i], spots[i + 1], adds[i], adds[i + 1]):
                    old0, old1 = acc[b0], acc[b1]
                    acc[b0] = old0 + x0
                    acc[b1] = old1 + (x1 + jnp.where(b0 == b1, x0, zero))
            return total

        return steep + lax.fori_loop(0, ND // GROUP, per_group, zero, unroll=3) * fr2

    steep = lax.fori_loop(0, nfreq, per_freq, zero)
    steep = steep * (1.0 / nbins)
    mask = mask_ref[...].astype(jnp.float32)
    per = nbins // PIECES
    copies = []
    for p in range(PIECES):

        def finish(t, _):
            g0 = t * ROWS
            done = []
            for i in range(ROWS):
                g = g0 + i
                mine = base[g] - (frs_ref[g] * steep) * mv[g]
                done.append((mine + ((a0[g] + a1[g]) + (a2[g] + a3[g]))) * mask)
            turned = jnp.swapaxes(jnp.stack(done, axis=0), 0, 1)
            for c in range(ROWS):
                out_v[pl.ds(pl.multiple_of(g0, ROWS), ROWS), c * LANES : (c + 1) * LANES] = turned[c]
            return 0

        lax.fori_loop(p * per // ROWS, (p + 1) * per // ROWS, finish, 0, unroll=3)
        rows = pl.ds(p * per, per)
        copy = pltpu.make_async_copy(out_v.at[rows], out_hbm.at[rows], out_sem.at[p])
        copy.start()
        copies.append(copy)
    for copy in copies:
        copy.wait()


def tail(parts, plan, bins_dev, dia_bins, dia_wts, ftab, frs, dirs, pos, wind, mask):
    nbins = dia_bins.shape[1]
    nfreq = nbins // ND
    anywhere = pl.BlockSpec(memory_space=pl.ANY)
    smem = pl.BlockSpec(memory_space=pltpu.SMEM)
    vmem = pl.BlockSpec(memory_space=pltpu.VMEM)
    points = ROWS * LANES
    spots = dia_bins.T.reshape(-1)
    wts = dia_wts.T.reshape(-1)
    field = pltpu.VMEM((nbins, ROWS, LANES), jnp.float32)
    return pl.pallas_call(
        functools.partial(tail_kernel, nfreq, bins_dev, plan),
        out_shape=jax.ShapeDtypeStruct((nbins, points), jnp.float32),
        in_specs=[smem] * 6 + [vmem] * 2 + [anywhere] * len(parts),
        out_specs=anywhere,
        scratch_shapes=[field] * 6
        + [
            pltpu.VMEM((ND, ROWS, LANES), jnp.float32),
            pltpu.VMEM((nbins, points), jnp.float32),
            pltpu.SemaphoreType.DMA((nbins // ND,)),
            pltpu.SemaphoreType.DMA((PIECES,)),
        ],
        compiler_params=pltpu.CompilerParams(vmem_limit_bytes=VMEM_ASK),
        cost_estimate=pl.CostEstimate(flops=0, bytes_accessed=70_000_000, transcendentals=0),
        name="tail",
    )(spots, wts, ftab, frs, dirs, pos, wind, mask, *parts)


def fast_on_device(
    spectrum, wind, sea_mask, neighbours, metric_x, metric_y, refraction, freq_shift, dia_bins, dia_wts
):
    bins_dev, points = spectrum.shape
    nbins = dia_bins.shape[1]
    nfreq = nbins // ND
    nloc = bins_dev // ND
    tiles = points // LANES
    shares = lax.axis_size("bin")
    share = points // shares
    bin_pos = lax.axis_index("bin")
    space_pos = lax.axis_index("space")
    plan = chunk_plan(nloc)

    freqs = np.arange(nfreq, dtype=np.float32)
    speed = jnp.asarray(np.exp(-np.log(1.1) * freqs.astype(np.float64)).astype(np.float32))
    ratio = np.exp(np.log(1.1) * (freqs.astype(np.float64) - (nfreq - 1)))
    ftab = jnp.asarray(
        np.stack([ratio**2, 4.0 * ratio**4, 0.5 * np.exp(-np.log(1.1) * freqs)]).astype(np.float32)
    )
    frs = jnp.asarray(np.repeat(3.0 * ratio, ND).astype(np.float32))
    theta = 2.0 * np.pi * (np.arange(ND) + 0.5) / ND
    dirs = jnp.asarray(np.stack([np.cos(theta), np.sin(theta)]).astype(np.float32))

    groups = halo_groups(plan)
    early = runs_of(slots_of(groups[0]))
    mask_row = sea_mask.reshape(1, points)
    hs, hn, _ = prep(spectrum, mask_row, early, groups[:1], False)
    after, *_ = lax.optimization_barrier((spectrum, hs[0], hn[0]))
    whole_blocks = [(f, min(f + 2, nloc)) for f in range(0, nloc, 2)]
    hs_rest, hn_rest, (wet, low_out, high_out) = prep(after, mask_row, whole_blocks, groups[1:], True)
    wet = wet.reshape(nloc, ND, tiles, LANES)

    def line(array, axis, step):
        peers = lax.axis_size(axis)
        pairs = [(i, i + 1) for i in range(peers - 1)]
        if step < 0:
            pairs = [(b, a) for a, b in pairs]
        return lax.ppermute(array, axis, pairs)

    sends = list(zip(list(hs) + list(hs_rest), list(hn) + list(hn_rest)))
    halos = []

    def send_halos(*after):
        if len(halos) < len(sends):
            south, north = sends[len(halos)]
            if after:
                south, north, *_ = lax.optimization_barrier((south, north) + after)
            halos.append((line(south, "space", 1), line(north, "space", -1)))

    send_halos()
    send_halos(*halos[0])
    low_in = line(low_out, "bin", 1).reshape(1, ND, tiles, LANES)
    high_in = line(high_out, "bin", -1).reshape(1, ND, tiles, LANES)

    nbr = (neighbours - space_pos * points).reshape(4, tiles, LANES)
    par = [p.reshape(tiles, LANES) for p in (metric_x, metric_y, refraction, freq_shift)]
    pos = bin_pos.reshape(1)
    kmin, kmax = points // 2, points
    arrived = []
    order = pos
    for c, chunk in enumerate(plan):
        first, step, count = chunk
        joined = c == 0
        gi, slot = [(i, slots_of(g)[first]) for i, g in enumerate(groups) if chunk in g][0]
        ends = (low_in, high_in) if first == 0 else None
        blocks = front(speed, dirs, order, nbr, par, *halos[gi], slot, wet, ends, chunk, joined, shares, kmin, kmax)
        earlier = sum(halos, ()) if c == 0 else arrived[0] if c == 1 else []
        order, *_ = lax.optimization_barrier((pos, blocks[0], *earlier))
        if joined:
            blocks, *_ = lax.optimization_barrier((blocks[0], low_in, high_in))
            arrived.append([lax.all_to_all(blocks, "bin", split_axis=0, concat_axis=0, tiled=True)])
            continue
        here = [blocks[0]]
        for d in range(1, shares):
            rows = blocks[d]
            rows, _ = lax.optimization_barrier((rows, arrived[-1][d if c > 1 else 0]))
            here.append(lax.ppermute(rows, "bin", [(i, (i + d) % shares) for i in range(shares)]))
        arrived.append(here)
    parts = sum(arrived, [])
    wind_part = lax.dynamic_slice_in_dim(wind, bin_pos * share, share, 1).reshape(2, ROWS, LANES)
    mask_part = lax.dynamic_slice_in_dim(sea_mask, bin_pos * share, share, 0).reshape(ROWS, LANES)
    return tail(parts, plan, bins_dev, dia_bins, dia_wts, ftab, frs, dirs, pos, wind_part, mask_part)


def pick_path(spectrum, *others):
    bins_dev, points = spectrum.shape
    fits = bins_dev % (2 * ND) == ND and bins_dev > ND and points // lax.axis_size("bin") == ROWS * LANES
    return (fast_on_device if fits else on_device)(spectrum, *others)


def solution(mesh):
    return jax.shard_map(
        pick_path,
        mesh=mesh,
        in_specs=(
            P("bin", ("ens", "space")),
            P(None, ("ens", "space")),
            P("space"),
            P(None, "space"),
            P("space"),
            P("space"),
            P("space"),
            P("space"),
            P(),
            P(),
        ),
        out_specs=P(None, ("ens", "space", "bin")),
        check_vma=False,
    )
```

```python
import functools
import itertools

import jax
import jax.numpy as jnp
import numpy as np
from jax import lax
from jax.experimental import pallas as pl
from jax.experimental.pallas import tpu as pltpu
from jax.sharding import PartitionSpec as P

ND = 36


def extended(array, sides, width):
    for axis, dim in sides:
        peers, length = (lax.axis_size(axis), array.shape[dim])
        up = [(i, (i + 1) % peers) for i in range(peers - 1)]
        down = [(j, i) for i, j in up]
        last = lax.slice_in_dim(array, length - width, length, axis=dim)
        initial = lax.slice_in_dim(array, 0, width, axis=dim)
        before = lax.ppermute(last, axis, up)
        after = lax.ppermute(initial, axis, down)
        array = jnp.concatenate([before, array, after], axis=dim)
    return array


def bin_tables(index, nfreq, ndir):
    freq = (index // ndir).astype(jnp.float32)
    direc = index % ndir
    fratio = jnp.exp(jnp.log(1.1) * (freq - (nfreq - 1)))
    speed = jnp.exp(-jnp.log(1.1) * freq)
    theta = 2.0 * jnp.pi * (direc.astype(jnp.float32) + 0.5) / ndir
    return (fratio, speed, jnp.cos(theta), jnp.sin(theta), direc == 0, direc == ndir - 1)


def spatial_term(wet, padded, local, metric_x, metric_y, speed, cosv, sinv):
    east = jnp.take(padded, local[0], axis=1)
    west = jnp.take(padded, local[1], axis=1)
    north = jnp.take(padded, local[2], axis=1)
    south = jnp.take(padded, local[3], axis=1)
    along_x = metric_x[None, :] * (speed * cosv)[:, None]
    along_y = metric_y[None, :] * (speed * sinv)[:, None]
    flux_x = jnp.abs(along_x) * (wet - jnp.where(along_x > 0, west, east))
    flux_y = jnp.abs(along_y) * (wet - jnp.where(along_y > 0, south, north))
    return flux_x + flux_y


def spectral_term(wet, padded, ndir, first, last, refraction, freq_shift, speed, cosv):
    rows = wet.shape[0]

    def moved_rows(offset):
        return lax.slice_in_dim(padded, ndir + offset, ndir + offset + rows, axis=0)

    prev_dir = jnp.where(first[:, None], moved_rows(ndir - 1), moved_rows(-1))
    next_dir = jnp.where(last[:, None], moved_rows(1 - ndir), moved_rows(1))
    lower = moved_rows(-ndir)
    upper = moved_rows(ndir)
    turning = refraction[None, :] * cosv[:, None]
    shifting = freq_shift[None, :] * speed[:, None]
    flux_t = jnp.abs(turning) * (wet - jnp.where(turning > 0, prev_dir, next_dir))
    flux_s = jnp.abs(shifting) * (wet - jnp.where(shifting > 0, lower, upper))
    return flux_t + flux_s


def source_step(
    moved, wind, maskf, fratio, speed, cosv, sinv, plus_fwd, minus_fwd, plus_back, minus_back
):
    steep = jnp.mean(moved * (fratio * fratio)[:, None], axis=0)
    drive = jnp.maximum(
        0.0,
        wind[0][None, :] * cosv[:, None] + wind[1][None, :] * sinv[:, None] - 0.5 * speed[:, None],
    )
    s_in = 0.3 * drive * drive * moved
    s_ds = -6.0 * fratio[:, None] * steep[None, :] * moved
    e_plus = plus_fwd(moved)
    e_minus = minus_fwd(moved)
    delta = (
        8.0
        * (fratio**4)[:, None]
        * (
            moved * moved * (e_plus / 1.25**4 + e_minus / 0.75**4)
            - 2.0 * moved * e_plus * e_minus / 0.9375**4
        )
    )
    s_nl = -2.0 * delta + plus_back(delta) + minus_back(delta)
    return (moved + 0.5 * (s_in + s_ds + s_nl)) * maskf[None, :]


def pair_matrix(first_bins, second_bins, weight, count):
    columns = jnp.arange(count, dtype=jnp.int32)[None, :]
    return weight[:, None] * (first_bins[:, None] == columns).astype(jnp.float32) + (1.0 - weight)[
        :, None
    ] * (second_bins[:, None] == columns).astype(jnp.float32)


def forward_product(matrix, values):
    return jnp.dot(
        matrix, values, precision=lax.Precision.HIGHEST, preferred_element_type=jnp.float32
    )


def backward_product(matrix, values):
    return lax.dot_general(
        matrix,
        values,
        (((0,), (0,)), ((), ())),
        precision=lax.Precision.HIGHEST,
        preferred_element_type=jnp.float32,
    )


def on_device(
    spectrum,
    wind,
    sea_mask,
    neighbours,
    metric_x,
    metric_y,
    refraction,
    freq_shift,
    dia_bins,
    dia_wts,
):
    bins_dev, points_dev = spectrum.shape
    nbins = dia_bins.shape[1]
    ndir = ND
    nfreq = nbins // ndir
    space_pos = lax.axis_index("space")
    bin_pos = lax.axis_index("bin")
    maskf = sea_mask.astype(jnp.float32)
    wet = spectrum * maskf[None, :]
    padded = extended(wet, (("space", 1),), points_dev)
    base = space_pos * points_dev - points_dev
    local = neighbours - base
    own_bins = bin_pos * bins_dev + jnp.arange(bins_dev, dtype=jnp.int32)
    fratio, speed, cosv, sinv, first, last = bin_tables(own_bins, nfreq, ndir)
    spatial = spatial_term(wet, padded, local, metric_x, metric_y, speed, cosv, sinv)
    share = points_dev // lax.axis_size("bin")
    start = bin_pos * share
    all_bins = jnp.arange(nbins, dtype=jnp.int32)
    fratio_all, speed_all, cos_all, sin_all, first_all, last_all = bin_tables(all_bins, nfreq, ndir)
    bin_pad = extended(wet, (("bin", 0),), ndir)
    spectral = spectral_term(wet, bin_pad, ndir, first, last, refraction, freq_shift, speed, cosv)
    moved_own = wet - spatial - spectral
    moved = lax.all_to_all(moved_own, "bin", split_axis=1, concat_axis=0, tiled=True)
    wind_part = lax.dynamic_slice_in_dim(wind, start, share, 1)
    mask_part = lax.dynamic_slice_in_dim(maskf, start, share, 0)
    plus_matrix = pair_matrix(dia_bins[0], dia_bins[1], dia_wts[0], nbins)
    minus_matrix = pair_matrix(dia_bins[2], dia_bins[3], dia_wts[1], nbins)
    result = source_step(
        moved,
        wind_part,
        mask_part,
        fratio_all,
        speed_all,
        cos_all,
        sin_all,
        lambda v: forward_product(plus_matrix, v),
        lambda v: forward_product(minus_matrix, v),
        lambda v: backward_product(plus_matrix, v),
        lambda v: backward_product(minus_matrix, v),
    )
    return result


LANES = 128
ROWS = 8
EDGE = 16
QUART = ND // 4
APART = 3
PIECES = 6
VMEM_ASK = 60 << 20
GROUP = 4


def chunk_plan(nloc):
    mid = nloc // 2
    return [(mid, 1, 1)] + [(mid - d, 2 * d, 2) for d in range(1, mid + 1)]


def freqs_of(chunk):
    first, step, count = chunk
    return [first + i * step for i in range(count)]


def halo_groups(plan):
    return [g for g in (plan[:1], plan[1:]) if g]


def slots_of(group):
    return {f: i for i, f in enumerate(f for chunk in group for f in freqs_of(chunk))}


def runs_of(freqs):
    runs = []
    for f in sorted(freqs):
        if runs and runs[-1][1] == f:
            runs[-1] = (runs[-1][0], f + 1)
        else:
            runs.append((f, f + 1))
    return runs


def prep_kernel(points, bins, blocks, groups, full, spec_hbm, mask_ref, *refs):
    ngr = len(groups)
    nloc = bins // ND
    hs_hbm, hn_hbm = refs[:ngr], refs[ngr : 2 * ngr]
    if full:
        wet_hbm, low_hbm, high_hbm = refs[2 * ngr : 2 * ngr + 3]
    spec_v, wet_v, edge_v, in_sem, out_sem = refs[-5:]
    tiles = points // LANES
    half = ND // 2
    where = {f: (i, k) for i, group in enumerate(groups) for f, k in slots_of(group).items()}
    loads = []
    spans = []
    for lo, hi in blocks:
        start = lo * ND // ROWS * ROWS
        stop = min(-(-hi * ND // ROWS) * ROWS, bins)
        spans.append((start, stop))
        rows = pl.ds(start, stop - start)
        copy = pltpu.make_async_copy(spec_hbm.at[rows], spec_v.at[rows], in_sem.at[len(loads)])
        copy.start()
        loads.append(copy)
    masks = [mask_ref[:, c * LANES : (c + 1) * LANES].astype(jnp.float32) for c in range(tiles)]
    copies = []

    def send(src, dst):
        copy = pltpu.make_async_copy(src, dst, out_sem.at[len(copies)])
        copy.start()
        copies.append(copy)

    for (lo, hi), (start, stop), load in zip(blocks, spans, loads):
        load.wait()

        def turn(g0, count):
            for c0 in range(0, tiles, ROWS):
                cols = range(c0, c0 + ROWS)
                block = jnp.stack(
                    [spec_v[pl.ds(g0, count), c * LANES : (c + 1) * LANES] * masks[c] for c in cols], axis=0
                )
                block = jnp.swapaxes(block, 0, 1)
                for i in range(count):
                    wet_v[pl.ds(pl.multiple_of((g0 + i) * tiles + c0, ROWS), ROWS), :] = block[i]

        def relayout(t, _):
            turn(pl.multiple_of(start + t * ROWS, ROWS), ROWS)
            return 0

        lax.fori_loop(0, (stop - start) // ROWS, relayout, 0)
        rest = (stop - start) % ROWS
        if rest:
            g0 = stop - rest
            for c in range(tiles):
                tile = spec_v[pl.ds(g0, rest), c * LANES : (c + 1) * LANES]
                wet_v[pl.ds(g0 * tiles + c, rest, stride=tiles), :] = tile * masks[c]
        for f in range(lo, hi):
            base = f * ND * tiles
            if f in where:
                i, k = where[f]
                for side, (j0, row) in enumerate(((3 * QUART, tiles - 1), (QUART, 0))):
                    at = base + j0 * tiles + row
                    edge_v[f, side, ROWS:EDGE, :] = jnp.zeros((EDGE - ROWS, LANES), jnp.float32)
                    edge_v[f, side, 0:ROWS, :] = wet_v[pl.ds(at, ROWS, stride=tiles), :]
                    edge_v[f, side, ROWS : ROWS + 1, :] = wet_v[pl.ds(at + ROWS * tiles, 1), :]
                span = half * tiles
                send(wet_v.at[pl.ds(base, span)], hs_hbm[i].at[k, pl.ds(0, span)])
                send(wet_v.at[pl.ds(base + span, span)], hn_hbm[i].at[k, pl.ds(0, span)])
                send(edge_v.at[f, 0], hs_hbm[i].at[k, pl.ds(span, EDGE)])
                send(edge_v.at[f, 1], hn_hbm[i].at[k, pl.ds(span, EDGE)])
            if full:
                own = pl.ds(base, ND * tiles)
                if f == nloc - 1:
                    send(wet_v.at[own], low_hbm)
                if f == 0:
                    send(wet_v.at[own], high_hbm)
                send(wet_v.at[own], wet_hbm.at[own])
    for copy in copies:
        copy.wait()


def prep(spectrum, mask, blocks, groups, full):
    bins, points = spectrum.shape
    nloc = bins // ND
    tiles = points // LANES
    halo_rows = ND // 2 * tiles + EDGE
    halos = [jax.ShapeDtypeStruct((len(slots_of(g)), halo_rows, LANES), jnp.float32) for g in groups]
    one = jax.ShapeDtypeStruct((ND * tiles, LANES), jnp.float32)
    outs = halos + halos
    if full:
        outs += [jax.ShapeDtypeStruct((bins * tiles, LANES), jnp.float32), one, one]
    anywhere = pl.BlockSpec(memory_space=pl.ANY)
    count = sum(hi - lo for lo, hi in blocks)
    sends = 4 * sum(len(slots_of(g)) for g in groups) + (nloc + 2 if full else 0)
    res = pl.pallas_call(
        functools.partial(prep_kernel, points, bins, blocks, groups, full),
        out_shape=outs,
        in_specs=[anywhere, pl.BlockSpec(memory_space=pltpu.VMEM)],
        out_specs=[anywhere] * len(outs),
        scratch_shapes=[
            pltpu.VMEM((bins, points), jnp.float32),
            pltpu.VMEM((bins * tiles, LANES), jnp.float32),
            pltpu.VMEM((nloc, 2, EDGE, LANES), jnp.float32),
            pltpu.SemaphoreType.DMA((len(blocks),)),
            pltpu.SemaphoreType.DMA((sends,)),
        ],
        compiler_params=pltpu.CompilerParams(vmem_limit_bytes=VMEM_ASK),
        cost_estimate=pl.CostEstimate(flops=0, bytes_accessed=count * 3_000_000, transcendentals=0),
        name="prep",
    )(spectrum, mask)
    ngr = len(groups)
    return res[:ngr], res[ngr : 2 * ngr], res[2 * ngr :]


def front_kernel(
    tiles, shares, nloc, kmin, kmax, chunk, edge, joined, tab_ref, dir_ref, pos_ref, nbr_ref, mx_ref, my_ref, rf_ref, fs_ref, hs_ref, hn_ref, wet_ref, *refs
):
    nout = 1 if joined else shares
    near, outs, ext_ref = refs[: -nout - 1], refs[-nout - 1 : -1], refs[-1]
    if joined:
        outs = [outs[0].at[d] for d in range(shares)]
    place = pl.program_id(0)
    speed = tab_ref[pos_ref[0] * nloc + chunk[0] + chunk[1] * place]
    first = place == 0
    half = ND // 2
    span = half * tiles
    south, north = tiles, ROWS
    pitch = APART * (2 * tiles + ROWS)

    def rows_at(j, row, count=ROWS):
        return pl.ds(j * pitch + APART * row, count, stride=APART)

    def extend(q, _):
        for t in range(0, tiles, ROWS):
            ext_ref[rows_at(q, t), :] = hs_ref[0, pl.ds(pl.multiple_of(q * tiles + t, ROWS), ROWS), :]
            ext_ref[rows_at(q, south + t), :] = wet_ref[0, q, t : t + ROWS, :]
            ext_ref[rows_at(half + q, north + t), :] = wet_ref[0, half + q, t : t + ROWS, :]
            ext_ref[rows_at(half + q, north + tiles + t), :] = hn_ref[
                0, pl.ds(pl.multiple_of(q * tiles + t, ROWS), ROWS), :
            ]
        return 0

    lax.fori_loop(0, half, extend, 0, unroll=2)
    for q in range(QUART):
        ext_ref[pl.ds((QUART + q) * pitch + APART * (south + tiles), 1), :] = hn_ref[0, span + q : span + q + 1, :]
        ext_ref[pl.ds((3 * QUART + q) * pitch + APART * (north - 1), 1), :] = hs_ref[0, span + q : span + q + 1, :]

    side = jnp.where(first, 1.0, -1.0)
    per_share = tiles // shares
    steps = [(d, k) for d in range(shares) for k in range(per_share // ROWS)]
    firsts = {}
    for d, k in steps:
        row = (d if joined else lax.rem(pos_ref[0] + d, shares)) * per_share + k * ROWS
        firsts[d, k] = row if joined else pl.multiple_of(row, ROWS)
    sub = lax.broadcasted_iota(jnp.int32, (ROWS, LANES), 0)
    lanes, rels = {}, {}
    for way in range(4):
        for step in steps:
            src = nbr_ref[way, pl.ds(firsts[step], ROWS), :]
            lanes[way, step] = src & (LANES - 1)
            rels[way, step] = (src >> 7) - (sub + firsts[step])

    def picked(j, own, step, way, offsets):
        out = None
        for r in offsets:
            window = ext_ref[rows_at(j, own + firsts[step] + r), :]
            got = jnp.take_along_axis(window, lanes[way, step], axis=1, mode="promise_in_bounds")
            out = got if out is None else jnp.where(rels[way, step] == r, got, out)
        return out

    for quad in range(4):
        cos_up = quad in (0, 3)
        own, way_y, off_y = (
            (south, 3, range(-(kmax // LANES), -(kmin // LANES) + 1))
            if quad < 2
            else (north, 2, range(kmin // LANES, kmax // LANES + 1))
        )
        way_x, off_x = (1, (-1, 0)) if cos_up else (0, (0, 1))

        def body(q, _):
            j = quad * QUART + q
            jprev = jnp.where(j == 0, ND - 1, j - 1)
            jnext = jnp.where(j == ND - 1, 0, j + 1)
            acos = jnp.abs(dir_ref[0, j])
            asin = jnp.abs(dir_ref[1, j])
            ax, ay = speed * acos, speed * asin
            for step in steps:
                at = pl.ds(firsts[step], ROWS)
                wet = wet_ref[0, j, at, :]
                e_y = picked(j, own, step, way_y, off_y)
                e_x = picked(j, own, step, way_x, off_x)
                rf, fs = rf_ref[at, :], fs_ref[at, :]
                e_prev, e_next = wet_ref[0, jprev, at, :], wet_ref[0, jnext, at, :]
                e_t = jnp.where(rf > 0, e_prev, e_next) if cos_up else jnp.where(rf < 0, e_prev, e_next)
                if edge:
                    inner, low, high = (ref[0, j, at, :] for ref in near)
                    outer = jnp.where(first, low, high)
                    e_s = jnp.where(fs * side > 0, outer, inner)
                else:
                    e_s = jnp.where(fs > 0, near[0][0, j, at, :], near[1][0, j, at, :])
                spatial = (mx_ref[at, :] * ax) * (wet - e_x) + (my_ref[at, :] * ay) * (wet - e_y)
                spectral = (jnp.abs(rf) * acos) * (wet - e_t) + (jnp.abs(fs) * speed) * (wet - e_s)
                d, k = step
                outs[d][j, k * ROWS : (k + 1) * ROWS, :] = wet - spatial - spectral
            return 0

        lax.fori_loop(0, QUART, body, 0, unroll=3)


def front(speed, dirs, pos, nbr, par, hs, hn, slot, wet, ends, chunk, joined, shares, kmin, kmax):
    first, step, count = chunk
    tiles = nbr.shape[1]
    nloc = wet.shape[0]
    smem = pl.BlockSpec(memory_space=pltpu.SMEM)

    def freq_spec(start, step):
        return pl.BlockSpec((1, ND, tiles, LANES), lambda i: (start + i * step, 0, 0, 0))

    halo_spec = pl.BlockSpec((1,) + hs.shape[1:], lambda i: (slot + i, 0, 0))

    def whole(shape):
        return pl.BlockSpec(shape, lambda i: (0,) * len(shape))

    if ends:
        near, near_specs = (wet,) + ends, [freq_spec(1, nloc - 3), freq_spec(0, 0), freq_spec(0, 0)]
    else:
        near, near_specs = (wet, wet), [freq_spec(first - 1, step), freq_spec(first + 1, step)]
    rows = tiles // shares
    if joined:
        outs = [jax.ShapeDtypeStruct((shares, count * ND, rows, LANES), jnp.float32)]
        out_specs = [pl.BlockSpec((shares, ND, rows, LANES), lambda i: (0, i, 0, 0))]
    else:
        outs = [jax.ShapeDtypeStruct((count * ND, rows, LANES), jnp.float32)] * shares
        out_specs = [pl.BlockSpec((ND, rows, LANES), lambda i: (i, 0, 0))] * shares
    return pl.pallas_call(
        functools.partial(front_kernel, tiles, shares, nloc, kmin, kmax, chunk, bool(ends), joined),
        grid=(count,),
        out_shape=outs,
        in_specs=[smem] * 3
        + [whole(nbr.shape)] + [whole(p.shape) for p in par] + [halo_spec, halo_spec, freq_spec(first, step)]
        + near_specs,
        out_specs=out_specs,
        scratch_shapes=[pltpu.VMEM((ND * APART * (2 * tiles + ROWS), LANES), jnp.float32)],
        compiler_params=pltpu.CompilerParams(vmem_limit_bytes=VMEM_ASK),
        cost_estimate=pl.CostEstimate(flops=0, bytes_accessed=count * 22_000_000, transcendentals=0),
        name="front",
    )(speed, dirs, pos, nbr, *par, hs, hn, wet, *near)


def tail_kernel(nfreq, bins_dev, plan, spot_ref, wts_ref, ftab_ref, frs_ref, dir_ref, pos_ref, wind_ref, mask_ref, *refs):
    out_hbm, mv, base, a0, a1, a2, a3, dw, out_v, in_sem, out_sem = refs[-11:]
    parts = iter(refs[:-11])
    shares = nfreq * ND // bins_dev
    nbins = nfreq * ND
    loads = []
    for c, chunk in enumerate(plan):
        joined = c == 0
        whole = next(parts) if joined else None
        for d in range(shares):
            part = whole.at[d] if joined else next(parts)
            source = d if joined else lax.rem(pos_ref[0] + (shares - d), shares)
            for i, f in enumerate(freqs_of(chunk)):
                rows = pl.ds(source * bins_dev + f * ND, ND)
                copy = pltpu.make_async_copy(part.at[pl.ds(i * ND, ND)], mv.at[rows], in_sem.at[len(loads)])
                copy.start()
                loads.append(copy)
    zero = jnp.zeros((ROWS, LANES), jnp.float32)
    accs = (a0, a1, a2, a3)

    def clear(g, _):
        for acc in accs:
            acc[g] = zero
        return 0

    lax.fori_loop(0, nbins, clear, 0, unroll=8)
    for j in range(ND):
        dw[j] = wind_ref[0] * dir_ref[0, j] + wind_ref[1] * dir_ref[1, j]
    for copy in loads:
        copy.wait()

    def per_freq(f, steep):
        fr2, fr4, hspeed = ftab_ref[0, f], ftab_ref[1, f], ftab_ref[2, f]

        def per_group(t, total):
            j0 = t * GROUP
            g0 = f * ND + j0
            spots = [[spot_ref[4 * g0 + 4 * i + k] for k in range(4)] for i in range(GROUP)]
            own = [mv[g0 + i] for i in range(GROUP)]
            found = [[mv[b] for b in spots[i]] for i in range(GROUP)]
            adds = []
            for i in range(GROUP):
                m, (p0, p1, m0, m1) = own[i], found[i]
                wp, wm = wts_ref[2 * g0 + 2 * i], wts_ref[2 * g0 + 2 * i + 1]
                ep = p1 + wp * (p0 - p1)
                em = m1 + wm * (m0 - m1)
                mf = fr4 * m
                half = mf * (m * (ep * (1 / 1.25**4) + em * (1 / 0.75**4)) - ep * em * (2.0 / 0.9375**4))
                drive = jnp.maximum(0.0, dw[j0 + i] - hspeed)
                base[g0 + i] = m + 0.15 * (drive * drive) * m - 2.0 * half
                sp, sm = wp * half, wm * half
                adds.append((sp, half - sp, sm, half - sm))
                total = total + m
            for i in range(0, GROUP, 2):
                for acc, b0, b1, x0, x1 in zip(accs, spots[i], spots[i + 1], adds[i], adds[i + 1]):
                    old0, old1 = acc[b0], acc[b1]
                    acc[b0] = old0 + x0
                    acc[b1] = old1 + (x1 + jnp.where(b0 == b1, x0, zero))
            return total

        return steep + lax.fori_loop(0, ND // GROUP, per_group, zero, unroll=3) * fr2

    steep = lax.fori_loop(0, nfreq, per_freq, zero)
    steep = steep * (1.0 / nbins)
    mask = mask_ref[...].astype(jnp.float32)
    per = nbins // PIECES
    copies = []
    for p in range(PIECES):

        def finish(t, _):
            g0 = t * ROWS
            done = []
            for i in range(ROWS):
                g = g0 + i
                mine = base[g] - (frs_ref[g] * steep) * mv[g]
                done.append((mine + ((a0[g] + a1[g]) + (a2[g] + a3[g]))) * mask)
            turned = jnp.swapaxes(jnp.stack(done, axis=0), 0, 1)
            for c in range(ROWS):
                out_v[pl.ds(pl.multiple_of(g0, ROWS), ROWS), c * LANES : (c + 1) * LANES] = turned[c]
            return 0

        lax.fori_loop(p * per // ROWS, (p + 1) * per // ROWS, finish, 0, unroll=3)
        rows = pl.ds(p * per, per)
        copy = pltpu.make_async_copy(out_v.at[rows], out_hbm.at[rows], out_sem.at[p])
        copy.start()
        copies.append(copy)
    for copy in copies:
        copy.wait()


def tail(parts, plan, bins_dev, dia_bins, dia_wts, ftab, frs, dirs, pos, wind, mask):
    nbins = dia_bins.shape[1]
    nfreq = nbins // ND
    anywhere = pl.BlockSpec(memory_space=pl.ANY)
    smem = pl.BlockSpec(memory_space=pltpu.SMEM)
    vmem = pl.BlockSpec(memory_space=pltpu.VMEM)
    points = ROWS * LANES
    spots = dia_bins.T.reshape(-1)
    wts = dia_wts.T.reshape(-1)
    field = pltpu.VMEM((nbins, ROWS, LANES), jnp.float32)
    return pl.pallas_call(
        functools.partial(tail_kernel, nfreq, bins_dev, plan),
        out_shape=jax.ShapeDtypeStruct((nbins, points), jnp.float32),
        in_specs=[smem] * 6 + [vmem] * 2 + [anywhere] * len(parts),
        out_specs=anywhere,
        scratch_shapes=[field] * 6
        + [
            pltpu.VMEM((ND, ROWS, LANES), jnp.float32),
            pltpu.VMEM((nbins, points), jnp.float32),
            pltpu.SemaphoreType.DMA((nbins // ND,)),
            pltpu.SemaphoreType.DMA((PIECES,)),
        ],
        compiler_params=pltpu.CompilerParams(vmem_limit_bytes=VMEM_ASK),
        cost_estimate=pl.CostEstimate(flops=0, bytes_accessed=70_000_000, transcendentals=0),
        name="tail",
    )(spots, wts, ftab, frs, dirs, pos, wind, mask, *parts)


def fast_on_device(
    spectrum, wind, sea_mask, neighbours, metric_x, metric_y, refraction, freq_shift, dia_bins, dia_wts
):
    bins_dev, points = spectrum.shape
    nbins = dia_bins.shape[1]
    nfreq = nbins // ND
    nloc = bins_dev // ND
    tiles = points // LANES
    shares = lax.axis_size("bin")
    share = points // shares
    bin_pos = lax.axis_index("bin")
    space_pos = lax.axis_index("space")
    plan = chunk_plan(nloc)

    freqs = np.arange(nfreq, dtype=np.float32)
    speed = jnp.asarray(np.exp(-np.log(1.1) * freqs.astype(np.float64)).astype(np.float32))
    ratio = np.exp(np.log(1.1) * (freqs.astype(np.float64) - (nfreq - 1)))
    ftab = jnp.asarray(
        np.stack([ratio**2, 4.0 * ratio**4, 0.5 * np.exp(-np.log(1.1) * freqs)]).astype(np.float32)
    )
    frs = jnp.asarray(np.repeat(3.0 * ratio, ND).astype(np.float32))
    theta = 2.0 * np.pi * (np.arange(ND) + 0.5) / ND
    dirs = jnp.asarray(np.stack([np.cos(theta), np.sin(theta)]).astype(np.float32))

    groups = halo_groups(plan)
    early = runs_of(slots_of(groups[0]))
    mask_row = sea_mask.reshape(1, points)
    hs, hn, _ = prep(spectrum, mask_row, early, groups[:1], False)
    after, *_ = lax.optimization_barrier((spectrum, hs[0], hn[0]))
    whole_blocks = [(f, min(f + 2, nloc)) for f in range(0, nloc, 2)]
    hs_rest, hn_rest, (wet, low_out, high_out) = prep(after, mask_row, whole_blocks, groups[1:], True)
    wet = wet.reshape(nloc, ND, tiles, LANES)

    def line(array, axis, step):
        peers = lax.axis_size(axis)
        pairs = [(i, i + 1) for i in range(peers - 1)]
        if step < 0:
            pairs = [(b, a) for a, b in pairs]
        return lax.ppermute(array, axis, pairs)

    sends = list(zip(list(hs) + list(hs_rest), list(hn) + list(hn_rest)))
    halos = []

    def send_halos(*after):
        if len(halos) < len(sends):
            south, north = sends[len(halos)]
            if after:
                south, north, *_ = lax.optimization_barrier((south, north) + after)
            halos.append((line(south, "space", 1), line(north, "space", -1)))

    send_halos()
    send_halos(*halos[0])
    low_in = line(low_out, "bin", 1).reshape(1, ND, tiles, LANES)
    high_in = line(high_out, "bin", -1).reshape(1, ND, tiles, LANES)

    nbr = (neighbours - space_pos * points).reshape(4, tiles, LANES)
    par = [p.reshape(tiles, LANES) for p in (metric_x, metric_y, refraction, freq_shift)]
    pos = bin_pos.reshape(1)
    kmin, kmax = points // 2, points
    arrived = []
    order = pos
    for c, chunk in enumerate(plan):
        first, step, count = chunk
        joined = c == 0
        gi, slot = [(i, slots_of(g)[first]) for i, g in enumerate(groups) if chunk in g][0]
        ends = (low_in, high_in) if first == 0 else None
        blocks = front(speed, dirs, order, nbr, par, *halos[gi], slot, wet, ends, chunk, joined, shares, kmin, kmax)
        earlier = sum(halos, ()) if c == 0 else arrived[0] if c == 1 else []
        order, *_ = lax.optimization_barrier((pos, blocks[0], *earlier))
        if joined:
            blocks, *_ = lax.optimization_barrier((blocks[0], low_in, high_in))
            arrived.append([lax.all_to_all(blocks, "bin", split_axis=0, concat_axis=0, tiled=True)])
            continue
        here = [blocks[0]]
        for d in range(1, shares):
            rows = blocks[d]
            rows, _ = lax.optimization_barrier((rows, arrived[-1][d if c > 1 else 0]))
            here.append(lax.ppermute(rows, "bin", [(i, (i + d) % shares) for i in range(shares)]))
        arrived.append(here)
    parts = sum(arrived, [])
    wind_part = lax.dynamic_slice_in_dim(wind, bin_pos * share, share, 1).reshape(2, ROWS, LANES)
    mask_part = lax.dynamic_slice_in_dim(sea_mask, bin_pos * share, share, 0).reshape(ROWS, LANES)
    return tail(parts, plan, bins_dev, dia_bins, dia_wts, ftab, frs, dirs, pos, wind_part, mask_part)


def pick_path(spectrum, *others):
    bins_dev, points = spectrum.shape
    fits = bins_dev % (2 * ND) == ND and bins_dev > ND and points // lax.axis_size("bin") == ROWS * LANES
    return (fast_on_device if fits else on_device)(spectrum, *others)


def solution(mesh):
    return jax.shard_map(
        pick_path,
        mesh=mesh,
        in_specs=(
            P("bin", ("ens", "space")),
            P(None, ("ens", "space")),
            P("space"),
            P(None, "space"),
            P("space"),
            P("space"),
            P("space"),
            P("space"),
            P(),
            P(),
        ),
        out_specs=P(None, ("ens", "space", "bin")),
        check_vma=False,
    )
```

```python
import functools
import itertools

import jax
import jax.numpy as jnp
import numpy as np
from jax import lax
from jax.experimental import pallas as pl
from jax.experimental.pallas import tpu as pltpu
from jax.sharding import PartitionSpec as P

ND = 36


def extended(array, sides, width):
    for axis, dim in sides:
        peers, length = (lax.axis_size(axis), array.shape[dim])
        up = [(i, (i + 1) % peers) for i in range(peers - 1)]
        down = [(j, i) for i, j in up]
        last = lax.slice_in_dim(array, length - width, length, axis=dim)
        initial = lax.slice_in_dim(array, 0, width, axis=dim)
        before = lax.ppermute(last, axis, up)
        after = lax.ppermute(initial, axis, down)
        array = jnp.concatenate([before, array, after], axis=dim)
    return array


def bin_tables(index, nfreq, ndir):
    freq = (index // ndir).astype(jnp.float32)
    direc = index % ndir
    fratio = jnp.exp(jnp.log(1.1) * (freq - (nfreq - 1)))
    speed = jnp.exp(-jnp.log(1.1) * freq)
    theta = 2.0 * jnp.pi * (direc.astype(jnp.float32) + 0.5) / ndir
    return (fratio, speed, jnp.cos(theta), jnp.sin(theta), direc == 0, direc == ndir - 1)


def spatial_term(wet, padded, local, metric_x, metric_y, speed, cosv, sinv):
    east = jnp.take(padded, local[0], axis=1)
    west = jnp.take(padded, local[1], axis=1)
    north = jnp.take(padded, local[2], axis=1)
    south = jnp.take(padded, local[3], axis=1)
    along_x = metric_x[None, :] * (speed * cosv)[:, None]
    along_y = metric_y[None, :] * (speed * sinv)[:, None]
    flux_x = jnp.abs(along_x) * (wet - jnp.where(along_x > 0, west, east))
    flux_y = jnp.abs(along_y) * (wet - jnp.where(along_y > 0, south, north))
    return flux_x + flux_y


def spectral_term(wet, padded, ndir, first, last, refraction, freq_shift, speed, cosv):
    rows = wet.shape[0]

    def moved_rows(offset):
        return lax.slice_in_dim(padded, ndir + offset, ndir + offset + rows, axis=0)

    prev_dir = jnp.where(first[:, None], moved_rows(ndir - 1), moved_rows(-1))
    next_dir = jnp.where(last[:, None], moved_rows(1 - ndir), moved_rows(1))
    lower = moved_rows(-ndir)
    upper = moved_rows(ndir)
    turning = refraction[None, :] * cosv[:, None]
    shifting = freq_shift[None, :] * speed[:, None]
    flux_t = jnp.abs(turning) * (wet - jnp.where(turning > 0, prev_dir, next_dir))
    flux_s = jnp.abs(shifting) * (wet - jnp.where(shifting > 0, lower, upper))
    return flux_t + flux_s


def source_step(
    moved, wind, maskf, fratio, speed, cosv, sinv, plus_fwd, minus_fwd, plus_back, minus_back
):
    steep = jnp.mean(moved * (fratio * fratio)[:, None], axis=0)
    drive = jnp.maximum(
        0.0,
        wind[0][None, :] * cosv[:, None] + wind[1][None, :] * sinv[:, None] - 0.5 * speed[:, None],
    )
    s_in = 0.3 * drive * drive * moved
    s_ds = -6.0 * fratio[:, None] * steep[None, :] * moved
    e_plus = plus_fwd(moved)
    e_minus = minus_fwd(moved)
    delta = (
        8.0
        * (fratio**4)[:, None]
        * (
            moved * moved * (e_plus / 1.25**4 + e_minus / 0.75**4)
            - 2.0 * moved * e_plus * e_minus / 0.9375**4
        )
    )
    s_nl = -2.0 * delta + plus_back(delta) + minus_back(delta)
    return (moved + 0.5 * (s_in + s_ds + s_nl)) * maskf[None, :]


def pair_matrix(first_bins, second_bins, weight, count):
    columns = jnp.arange(count, dtype=jnp.int32)[None, :]
    return weight[:, None] * (first_bins[:, None] == columns).astype(jnp.float32) + (1.0 - weight)[
        :, None
    ] * (second_bins[:, None] == columns).astype(jnp.float32)


def forward_product(matrix, values):
    return jnp.dot(
        matrix, values, precision=lax.Precision.HIGHEST, preferred_element_type=jnp.float32
    )


def backward_product(matrix, values):
    return lax.dot_general(
        matrix,
        values,
        (((0,), (0,)), ((), ())),
        precision=lax.Precision.HIGHEST,
        preferred_element_type=jnp.float32,
    )


def on_device(
    spectrum,
    wind,
    sea_mask,
    neighbours,
    metric_x,
    metric_y,
    refraction,
    freq_shift,
    dia_bins,
    dia_wts,
):
    bins_dev, points_dev = spectrum.shape
    nbins = dia_bins.shape[1]
    ndir = ND
    nfreq = nbins // ndir
    space_pos = lax.axis_index("space")
    bin_pos = lax.axis_index("bin")
    maskf = sea_mask.astype(jnp.float32)
    wet = spectrum * maskf[None, :]
    padded = extended(wet, (("space", 1),), points_dev)
    base = space_pos * points_dev - points_dev
    local = neighbours - base
    own_bins = bin_pos * bins_dev + jnp.arange(bins_dev, dtype=jnp.int32)
    fratio, speed, cosv, sinv, first, last = bin_tables(own_bins, nfreq, ndir)
    spatial = spatial_term(wet, padded, local, metric_x, metric_y, speed, cosv, sinv)
    share = points_dev // lax.axis_size("bin")
    start = bin_pos * share
    all_bins = jnp.arange(nbins, dtype=jnp.int32)
    fratio_all, speed_all, cos_all, sin_all, first_all, last_all = bin_tables(all_bins, nfreq, ndir)
    bin_pad = extended(wet, (("bin", 0),), ndir)
    spectral = spectral_term(wet, bin_pad, ndir, first, last, refraction, freq_shift, speed, cosv)
    moved_own = wet - spatial - spectral
    moved = lax.all_to_all(moved_own, "bin", split_axis=1, concat_axis=0, tiled=True)
    wind_part = lax.dynamic_slice_in_dim(wind, start, share, 1)
    mask_part = lax.dynamic_slice_in_dim(maskf, start, share, 0)
    plus_matrix = pair_matrix(dia_bins[0], dia_bins[1], dia_wts[0], nbins)
    minus_matrix = pair_matrix(dia_bins[2], dia_bins[3], dia_wts[1], nbins)
    result = source_step(
        moved,
        wind_part,
        mask_part,
        fratio_all,
        speed_all,
        cos_all,
        sin_all,
        lambda v: forward_product(plus_matrix, v),
        lambda v: forward_product(minus_matrix, v),
        lambda v: backward_product(plus_matrix, v),
        lambda v: backward_product(minus_matrix, v),
    )
    return result


LANES = 128
ROWS = 8
EDGE = 16
QUART = ND // 4
APART = 3
PIECES = 6
VMEM_ASK = 60 << 20
GROUP = 4


def chunk_plan(nloc):
    mid = nloc // 2
    plan = [(mid - d, 2 * d, 2) for d in range(1, mid + 1)]
    if mid > 3:
        plan[2] = (mid - 3, 3, 3)
    else:
        plan.insert(0, (mid, 1, 1))
    return plan


def freqs_of(chunk):
    first, step, count = chunk
    return [first + i * step for i in range(count)]


def halo_groups(plan):
    return [g for g in (plan[:1], plan[1:]) if g]


def slots_of(group):
    return {f: i for i, f in enumerate(f for chunk in group for f in freqs_of(chunk))}


def runs_of(freqs):
    runs = []
    for f in sorted(freqs):
        if runs and runs[-1][1] == f:
            runs[-1] = (runs[-1][0], f + 1)
        else:
            runs.append((f, f + 1))
    return runs


def prep_kernel(points, bins, blocks, groups, full, spec_hbm, mask_ref, *refs):
    ngr = len(groups)
    nloc = bins // ND
    hs_hbm, hn_hbm = refs[:ngr], refs[ngr : 2 * ngr]
    if full:
        wet_hbm, low_hbm, high_hbm = refs[2 * ngr : 2 * ngr + 3]
    spec_v, wet_v, edge_v, in_sem, out_sem = refs[-5:]
    tiles = points // LANES
    half = ND // 2
    where = {f: (i, k) for i, group in enumerate(groups) for f, k in slots_of(group).items()}
    loads = []
    spans = []
    for lo, hi in blocks:
        start = lo * ND // ROWS * ROWS
        stop = min(-(-hi * ND // ROWS) * ROWS, bins)
        spans.append((start, stop))
        rows = pl.ds(start, stop - start)
        copy = pltpu.make_async_copy(spec_hbm.at[rows], spec_v.at[rows], in_sem.at[len(loads)])
        copy.start()
        loads.append(copy)
    masks = [mask_ref[:, c * LANES : (c + 1) * LANES].astype(jnp.float32) for c in range(tiles)]
    copies = []

    def send(src, dst):
        copy = pltpu.make_async_copy(src, dst, out_sem.at[len(copies)])
        copy.start()
        copies.append(copy)

    for (lo, hi), (start, stop), load in zip(blocks, spans, loads):
        load.wait()

        def turn(g0, count):
            for c0 in range(0, tiles, ROWS):
                cols = range(c0, c0 + ROWS)
                block = jnp.stack(
                    [spec_v[pl.ds(g0, count), c * LANES : (c + 1) * LANES] * masks[c] for c in cols], axis=0
                )
                block = jnp.swapaxes(block, 0, 1)
                for i in range(count):
                    wet_v[pl.ds(pl.multiple_of((g0 + i) * tiles + c0, ROWS), ROWS), :] = block[i]

        def relayout(t, _):
            turn(pl.multiple_of(start + t * ROWS, ROWS), ROWS)
            return 0

        lax.fori_loop(0, (stop - start) // ROWS, relayout, 0)
        rest = (stop - start) % ROWS
        if rest:
            g0 = stop - rest
            for c in range(tiles):
                tile = spec_v[pl.ds(g0, rest), c * LANES : (c + 1) * LANES]
                wet_v[pl.ds(g0 * tiles + c, rest, stride=tiles), :] = tile * masks[c]
        for f in range(lo, hi):
            base = f * ND * tiles
            if f in where:
                i, k = where[f]
                for side, (j0, row) in enumerate(((3 * QUART, tiles - 1), (QUART, 0))):
                    at = base + j0 * tiles + row
                    edge_v[f, side, ROWS:EDGE, :] = jnp.zeros((EDGE - ROWS, LANES), jnp.float32)
                    edge_v[f, side, 0:ROWS, :] = wet_v[pl.ds(at, ROWS, stride=tiles), :]
                    edge_v[f, side, ROWS : ROWS + 1, :] = wet_v[pl.ds(at + ROWS * tiles, 1), :]
                span = half * tiles
                send(wet_v.at[pl.ds(base, span)], hs_hbm[i].at[k, pl.ds(0, span)])
                send(wet_v.at[pl.ds(base + span, span)], hn_hbm[i].at[k, pl.ds(0, span)])
                send(edge_v.at[f, 0], hs_hbm[i].at[k, pl.ds(span, EDGE)])
                send(edge_v.at[f, 1], hn_hbm[i].at[k, pl.ds(span, EDGE)])
            if full:
                own = pl.ds(base, ND * tiles)
                if f == nloc - 1:
                    send(wet_v.at[own], low_hbm)
                if f == 0:
                    send(wet_v.at[own], high_hbm)
                send(wet_v.at[own], wet_hbm.at[own])
    for copy in copies:
        copy.wait()


def prep(spectrum, mask, blocks, groups, full):
    bins, points = spectrum.shape
    nloc = bins // ND
    tiles = points // LANES
    halo_rows = ND // 2 * tiles + EDGE
    halos = [jax.ShapeDtypeStruct((len(slots_of(g)), halo_rows, LANES), jnp.float32) for g in groups]
    one = jax.ShapeDtypeStruct((ND * tiles, LANES), jnp.float32)
    outs = halos + halos
    if full:
        outs += [jax.ShapeDtypeStruct((bins * tiles, LANES), jnp.float32), one, one]
    anywhere = pl.BlockSpec(memory_space=pl.ANY)
    count = sum(hi - lo for lo, hi in blocks)
    sends = 4 * sum(len(slots_of(g)) for g in groups) + (nloc + 2 if full else 0)
    res = pl.pallas_call(
        functools.partial(prep_kernel, points, bins, blocks, groups, full),
        out_shape=outs,
        in_specs=[anywhere, pl.BlockSpec(memory_space=pltpu.VMEM)],
        out_specs=[anywhere] * len(outs),
        scratch_shapes=[
            pltpu.VMEM((bins, points), jnp.float32),
            pltpu.VMEM((bins * tiles, LANES), jnp.float32),
            pltpu.VMEM((nloc, 2, EDGE, LANES), jnp.float32),
            pltpu.SemaphoreType.DMA((len(blocks),)),
            pltpu.SemaphoreType.DMA((sends,)),
        ],
        compiler_params=pltpu.CompilerParams(vmem_limit_bytes=VMEM_ASK),
        cost_estimate=pl.CostEstimate(flops=0, bytes_accessed=count * 3_000_000, transcendentals=0),
        name="prep",
    )(spectrum, mask)
    ngr = len(groups)
    return res[:ngr], res[ngr : 2 * ngr], res[2 * ngr :]


def front_kernel(
    tiles, shares, nloc, kmin, kmax, chunk, edge, joined, tab_ref, dir_ref, pos_ref, nbr_ref, mx_ref, my_ref, rf_ref, fs_ref, hs_ref, hn_ref, wet_ref, *refs
):
    nout = 1 if joined else shares
    near, outs, ext_ref = refs[: -nout - 1], refs[-nout - 1 : -1], refs[-1]
    if joined:
        outs = [outs[0].at[d] for d in range(shares)]
    place = pl.program_id(0)
    speed = tab_ref[pos_ref[0] * nloc + chunk[0] + chunk[1] * place]
    first = place == 0
    half = ND // 2
    span = half * tiles
    south, north = tiles, ROWS
    pitch = APART * (2 * tiles + ROWS)

    def rows_at(j, row, count=ROWS):
        return pl.ds(j * pitch + APART * row, count, stride=APART)

    def extend(q, _):
        for t in range(0, tiles, ROWS):
            ext_ref[rows_at(q, t), :] = hs_ref[0, pl.ds(pl.multiple_of(q * tiles + t, ROWS), ROWS), :]
            ext_ref[rows_at(q, south + t), :] = wet_ref[0, q, t : t + ROWS, :]
            ext_ref[rows_at(half + q, north + t), :] = wet_ref[0, half + q, t : t + ROWS, :]
            ext_ref[rows_at(half + q, north + tiles + t), :] = hn_ref[
                0, pl.ds(pl.multiple_of(q * tiles + t, ROWS), ROWS), :
            ]
        return 0

    lax.fori_loop(0, half, extend, 0, unroll=2)
    for q in range(QUART):
        ext_ref[pl.ds((QUART + q) * pitch + APART * (south + tiles), 1), :] = hn_ref[0, span + q : span + q + 1, :]
        ext_ref[pl.ds((3 * QUART + q) * pitch + APART * (north - 1), 1), :] = hs_ref[0, span + q : span + q + 1, :]

    side = jnp.where(first, 1.0, -1.0)
    per_share = tiles // shares
    steps = [(d, k) for d in range(shares) for k in range(per_share // ROWS)]
    firsts = {}
    for d, k in steps:
        row = (d if joined else lax.rem(pos_ref[0] + d, shares)) * per_share + k * ROWS
        firsts[d, k] = row if joined else pl.multiple_of(row, ROWS)
    sub = lax.broadcasted_iota(jnp.int32, (ROWS, LANES), 0)
    lanes, rels = {}, {}
    for way in range(4):
        for step in steps:
            src = nbr_ref[way, pl.ds(firsts[step], ROWS), :]
            lanes[way, step] = src & (LANES - 1)
            rels[way, step] = (src >> 7) - (sub + firsts[step])

    def picked(j, own, step, way, offsets):
        out = None
        for r in offsets:
            window = ext_ref[rows_at(j, own + firsts[step] + r), :]
            got = jnp.take_along_axis(window, lanes[way, step], axis=1, mode="promise_in_bounds")
            out = got if out is None else jnp.where(rels[way, step] == r, got, out)
        return out

    for quad in range(4):
        cos_up = quad in (0, 3)
        own, way_y, off_y = (
            (south, 3, range(-(kmax // LANES), -(kmin // LANES) + 1))
            if quad < 2
            else (north, 2, range(kmin // LANES, kmax // LANES + 1))
        )
        way_x, off_x = (1, (-1, 0)) if cos_up else (0, (0, 1))

        def body(q, _):
            j = quad * QUART + q
            jprev = jnp.where(j == 0, ND - 1, j - 1)
            jnext = jnp.where(j == ND - 1, 0, j + 1)
            acos = jnp.abs(dir_ref[0, j])
            asin = jnp.abs(dir_ref[1, j])
            ax, ay = speed * acos, speed * asin
            for step in steps:
                at = pl.ds(firsts[step], ROWS)
                wet = wet_ref[0, j, at, :]
                e_y = picked(j, own, step, way_y, off_y)
                e_x = picked(j, own, step, way_x, off_x)
                rf, fs = rf_ref[at, :], fs_ref[at, :]
                e_prev, e_next = wet_ref[0, jprev, at, :], wet_ref[0, jnext, at, :]
                e_t = jnp.where(rf > 0, e_prev, e_next) if cos_up else jnp.where(rf < 0, e_prev, e_next)
                if edge:
                    inner, low, high = (ref[0, j, at, :] for ref in near)
                    outer = jnp.where(first, low, high)
                    e_s = jnp.where(fs * side > 0, outer, inner)
                else:
                    e_s = jnp.where(fs > 0, near[0][0, j, at, :], near[1][0, j, at, :])
                spatial = (mx_ref[at, :] * ax) * (wet - e_x) + (my_ref[at, :] * ay) * (wet - e_y)
                spectral = (jnp.abs(rf) * acos) * (wet - e_t) + (jnp.abs(fs) * speed) * (wet - e_s)
                d, k = step
                outs[d][j, k * ROWS : (k + 1) * ROWS, :] = wet - spatial - spectral
            return 0

        lax.fori_loop(0, QUART, body, 0, unroll=3)


def front(speed, dirs, pos, nbr, par, hs, hn, slot, wet, ends, chunk, joined, shares, kmin, kmax):
    first, step, count = chunk
    tiles = nbr.shape[1]
    nloc = wet.shape[0]
    smem = pl.BlockSpec(memory_space=pltpu.SMEM)

    def freq_spec(start, step):
        return pl.BlockSpec((1, ND, tiles, LANES), lambda i: (start + i * step, 0, 0, 0))

    halo_spec = pl.BlockSpec((1,) + hs.shape[1:], lambda i: (slot + i, 0, 0))

    def whole(shape):
        return pl.BlockSpec(shape, lambda i: (0,) * len(shape))

    if ends:
        near, near_specs = (wet,) + ends, [freq_spec(1, nloc - 3), freq_spec(0, 0), freq_spec(0, 0)]
    else:
        near, near_specs = (wet, wet), [freq_spec(first - 1, step), freq_spec(first + 1, step)]
    rows = tiles // shares
    if joined:
        outs = [jax.ShapeDtypeStruct((shares, count * ND, rows, LANES), jnp.float32)]
        out_specs = [pl.BlockSpec((shares, ND, rows, LANES), lambda i: (0, i, 0, 0))]
    else:
        outs = [jax.ShapeDtypeStruct((count * ND, rows, LANES), jnp.float32)] * shares
        out_specs = [pl.BlockSpec((ND, rows, LANES), lambda i: (i, 0, 0))] * shares
    return pl.pallas_call(
        functools.partial(front_kernel, tiles, shares, nloc, kmin, kmax, chunk, bool(ends), joined),
        grid=(count,),
        out_shape=outs,
        in_specs=[smem] * 3
        + [whole(nbr.shape)] + [whole(p.shape) for p in par] + [halo_spec, halo_spec, freq_spec(first, step)]
        + near_specs,
        out_specs=out_specs,
        scratch_shapes=[pltpu.VMEM((ND * APART * (2 * tiles + ROWS), LANES), jnp.float32)],
        compiler_params=pltpu.CompilerParams(vmem_limit_bytes=VMEM_ASK),
        cost_estimate=pl.CostEstimate(flops=0, bytes_accessed=count * 22_000_000, transcendentals=0),
        name="front",
    )(speed, dirs, pos, nbr, *par, hs, hn, wet, *near)


def tail_kernel(nfreq, bins_dev, plan, spot_ref, wts_ref, ftab_ref, frs_ref, dir_ref, pos_ref, wind_ref, mask_ref, *refs):
    out_hbm, mv, base, a0, a1, a2, a3, dw, out_v, in_sem, out_sem = refs[-11:]
    parts = iter(refs[:-11])
    shares = nfreq * ND // bins_dev
    nbins = nfreq * ND
    loads = []
    for c, chunk in enumerate(plan):
        joined = False
        whole = next(parts) if joined else None
        for d in range(shares):
            part = whole.at[d] if joined else next(parts)
            source = d if joined else lax.rem(pos_ref[0] + (shares - d), shares)
            for i, f in enumerate(freqs_of(chunk)):
                rows = pl.ds(source * bins_dev + f * ND, ND)
                copy = pltpu.make_async_copy(part.at[pl.ds(i * ND, ND)], mv.at[rows], in_sem.at[len(loads)])
                copy.start()
                loads.append(copy)
    zero = jnp.zeros((ROWS, LANES), jnp.float32)
    accs = (a0, a1, a2, a3)

    def clear(g, _):
        for acc in accs:
            acc[g] = zero
        return 0

    lax.fori_loop(0, nbins, clear, 0, unroll=8)
    for j in range(ND):
        dw[j] = wind_ref[0] * dir_ref[0, j] + wind_ref[1] * dir_ref[1, j]
    for copy in loads:
        copy.wait()

    def per_freq(f, steep):
        fr2, fr4, hspeed = ftab_ref[0, f], ftab_ref[1, f], ftab_ref[2, f]

        def per_group(t, total):
            j0 = t * GROUP
            g0 = f * ND + j0
            spots = [[spot_ref[4 * g0 + 4 * i + k] for k in range(4)] for i in range(GROUP)]
            own = [mv[g0 + i] for i in range(GROUP)]
            found = [[mv[b] for b in spots[i]] for i in range(GROUP)]
            adds = []
            for i in range(GROUP):
                m, (p0, p1, m0, m1) = own[i], found[i]
                wp, wm = wts_ref[2 * g0 + 2 * i], wts_ref[2 * g0 + 2 * i + 1]
                ep = p1 + wp * (p0 - p1)
                em = m1 + wm * (m0 - m1)
                mf = fr4 * m
                half = mf * (m * (ep * (1 / 1.25**4) + em * (1 / 0.75**4)) - ep * em * (2.0 / 0.9375**4))
                drive = jnp.maximum(0.0, dw[j0 + i] - hspeed)
                base[g0 + i] = m + 0.15 * (drive * drive) * m - 2.0 * half
                sp, sm = wp * half, wm * half
                adds.append((sp, half - sp, sm, half - sm))
                total = total + m
            for i in range(0, GROUP, 2):
                for acc, b0, b1, x0, x1 in zip(accs, spots[i], spots[i + 1], adds[i], adds[i + 1]):
                    old0, old1 = acc[b0], acc[b1]
                    acc[b0] = old0 + x0
                    acc[b1] = old1 + (x1 + jnp.where(b0 == b1, x0, zero))
            return total

        return steep + lax.fori_loop(0, ND // GROUP, per_group, zero, unroll=3) * fr2

    steep = lax.fori_loop(0, nfreq, per_freq, zero)
    steep = steep * (1.0 / nbins)
    mask = mask_ref[...].astype(jnp.float32)
    per = nbins // PIECES
    copies = []
    for p in range(PIECES):

        def finish(t, _):
            g0 = t * ROWS
            done = []
            for i in range(ROWS):
                g = g0 + i
                mine = base[g] - (frs_ref[g] * steep) * mv[g]
                done.append((mine + ((a0[g] + a1[g]) + (a2[g] + a3[g]))) * mask)
            turned = jnp.swapaxes(jnp.stack(done, axis=0), 0, 1)
            for c in range(ROWS):
                out_v[pl.ds(pl.multiple_of(g0, ROWS), ROWS), c * LANES : (c + 1) * LANES] = turned[c]
            return 0

        lax.fori_loop(p * per // ROWS, (p + 1) * per // ROWS, finish, 0, unroll=3)
        rows = pl.ds(p * per, per)
        copy = pltpu.make_async_copy(out_v.at[rows], out_hbm.at[rows], out_sem.at[p])
        copy.start()
        copies.append(copy)
    for copy in copies:
        copy.wait()


def tail(parts, plan, bins_dev, dia_bins, dia_wts, ftab, frs, dirs, pos, wind, mask):
    nbins = dia_bins.shape[1]
    nfreq = nbins // ND
    anywhere = pl.BlockSpec(memory_space=pl.ANY)
    smem = pl.BlockSpec(memory_space=pltpu.SMEM)
    vmem = pl.BlockSpec(memory_space=pltpu.VMEM)
    points = ROWS * LANES
    spots = dia_bins.T.reshape(-1)
    wts = dia_wts.T.reshape(-1)
    field = pltpu.VMEM((nbins, ROWS, LANES), jnp.float32)
    return pl.pallas_call(
        functools.partial(tail_kernel, nfreq, bins_dev, plan),
        out_shape=jax.ShapeDtypeStruct((nbins, points), jnp.float32),
        in_specs=[smem] * 6 + [vmem] * 2 + [anywhere] * len(parts),
        out_specs=anywhere,
        scratch_shapes=[field] * 6
        + [
            pltpu.VMEM((ND, ROWS, LANES), jnp.float32),
            pltpu.VMEM((nbins, points), jnp.float32),
            pltpu.SemaphoreType.DMA((nbins // ND,)),
            pltpu.SemaphoreType.DMA((PIECES,)),
        ],
        compiler_params=pltpu.CompilerParams(vmem_limit_bytes=VMEM_ASK),
        cost_estimate=pl.CostEstimate(flops=0, bytes_accessed=70_000_000, transcendentals=0),
        name="tail",
    )(spots, wts, ftab, frs, dirs, pos, wind, mask, *parts)


def fast_on_device(
    spectrum, wind, sea_mask, neighbours, metric_x, metric_y, refraction, freq_shift, dia_bins, dia_wts
):
    bins_dev, points = spectrum.shape
    nbins = dia_bins.shape[1]
    nfreq = nbins // ND
    nloc = bins_dev // ND
    tiles = points // LANES
    shares = lax.axis_size("bin")
    share = points // shares
    bin_pos = lax.axis_index("bin")
    space_pos = lax.axis_index("space")
    plan = chunk_plan(nloc)

    freqs = np.arange(nfreq, dtype=np.float32)
    speed = jnp.asarray(np.exp(-np.log(1.1) * freqs.astype(np.float64)).astype(np.float32))
    ratio = np.exp(np.log(1.1) * (freqs.astype(np.float64) - (nfreq - 1)))
    ftab = jnp.asarray(
        np.stack([ratio**2, 4.0 * ratio**4, 0.5 * np.exp(-np.log(1.1) * freqs)]).astype(np.float32)
    )
    frs = jnp.asarray(np.repeat(3.0 * ratio, ND).astype(np.float32))
    theta = 2.0 * np.pi * (np.arange(ND) + 0.5) / ND
    dirs = jnp.asarray(np.stack([np.cos(theta), np.sin(theta)]).astype(np.float32))

    groups = halo_groups(plan)
    early = runs_of(slots_of(groups[0]))
    mask_row = sea_mask.reshape(1, points)
    hs, hn, _ = prep(spectrum, mask_row, early, groups[:1], False)
    after, *_ = lax.optimization_barrier((spectrum, hs[0], hn[0]))
    whole_blocks = [(f, min(f + 2, nloc)) for f in range(0, nloc, 2)]
    hs_rest, hn_rest, (wet, low_out, high_out) = prep(after, mask_row, whole_blocks, groups[1:], True)
    wet = wet.reshape(nloc, ND, tiles, LANES)

    def line(array, axis, step):
        peers = lax.axis_size(axis)
        pairs = [(i, i + 1) for i in range(peers - 1)]
        if step < 0:
            pairs = [(b, a) for a, b in pairs]
        return lax.ppermute(array, axis, pairs)

    sends = list(zip(list(hs) + list(hs_rest), list(hn) + list(hn_rest)))
    halos = []

    def send_halos(*after):
        if len(halos) < len(sends):
            south, north = sends[len(halos)]
            if after:
                south, north, *_ = lax.optimization_barrier((south, north) + after)
            halos.append((line(south, "space", 1), line(north, "space", -1)))

    send_halos()
    send_halos(*halos[0])
    low_in = line(low_out, "bin", 1).reshape(1, ND, tiles, LANES)
    high_in = line(high_out, "bin", -1).reshape(1, ND, tiles, LANES)

    nbr = (neighbours - space_pos * points).reshape(4, tiles, LANES)
    par = [p.reshape(tiles, LANES) for p in (metric_x, metric_y, refraction, freq_shift)]
    pos = bin_pos.reshape(1)
    kmin, kmax = points // 2, points
    arrived = []
    order = pos
    for c, chunk in enumerate(plan):
        first, step, count = chunk
        joined = False
        gi, slot = [(i, slots_of(g)[first]) for i, g in enumerate(groups) if chunk in g][0]
        ends = (low_in, high_in) if first == 0 else None
        blocks = front(speed, dirs, order, nbr, par, *halos[gi], slot, wet, ends, chunk, joined, shares, kmin, kmax)
        earlier = sum(halos, ()) if c == 0 else arrived[0][1:] if c == 1 else []
        order, *_ = lax.optimization_barrier((pos, blocks[0], *earlier))
        if joined:
            blocks, *_ = lax.optimization_barrier((blocks[0], low_in, high_in))
            arrived.append([lax.all_to_all(blocks, "bin", split_axis=0, concat_axis=0, tiled=True)])
            continue
        here = [blocks[0]]
        for d in range(1, shares):
            rows = blocks[d]
            before = [low_in, high_in] if c == 0 else arrived[0][1:] if c == 1 else [arrived[-1][d]]
            rows, *_ = lax.optimization_barrier((rows, *before))
            here.append(lax.ppermute(rows, "bin", [(i, (i + d) % shares) for i in range(shares)]))
        arrived.append(here)
    parts = sum(arrived, [])
    wind_part = lax.dynamic_slice_in_dim(wind, bin_pos * share, share, 1).reshape(2, ROWS, LANES)
    mask_part = lax.dynamic_slice_in_dim(sea_mask, bin_pos * share, share, 0).reshape(ROWS, LANES)
    return tail(parts, plan, bins_dev, dia_bins, dia_wts, ftab, frs, dirs, pos, wind_part, mask_part)


def pick_path(spectrum, *others):
    bins_dev, points = spectrum.shape
    fits = bins_dev % (2 * ND) == ND and bins_dev > ND and points // lax.axis_size("bin") == ROWS * LANES
    return (fast_on_device if fits else on_device)(spectrum, *others)


def solution(mesh):
    return jax.shard_map(
        pick_path,
        mesh=mesh,
        in_specs=(
            P("bin", ("ens", "space")),
            P(None, ("ens", "space")),
            P("space"),
            P(None, "space"),
            P("space"),
            P("space"),
            P("space"),
            P("space"),
            P(),
            P(),
        ),
        out_specs=P(None, ("ens", "space", "bin")),
        check_vma=False,
    )
```
